32 devices in a mesh: group: 4 (over z), member: 8 (over y, x, core).
Axes of the slice: x: 2, y: 2, z: 4, core: 2. Of those that a mesh axis runs over, the one named last changes fastest.
Arguments:
- features: bfloat16 [256, 512], P(('group', 'member')), may hold values from -6 to 6
- labels: int32 [256], P('group'), may hold values from 0 to 4095, as said below
- centres: bfloat16 [16384, 512], P(('group', 'member')), may hold values from -6 to 6
- block_ids: int32 [4, 32], P(None, ('group', 'member')), may hold values from 0 to 3
- listed: int32 [4, 32], P(None, ('group', 'member')), may hold values from 0 to 1, as said below
Outputs:
- sample_loss: float32 [256], P(('group', 'member'))
- feature_grad: float32 [256, 512], P(('group', 'member'))
- centre_grad: float32 [16384, 512], P(('group', 'member'))
The draws below stay inside these ranges and needn't reach their ends.
Inputs may be any that keep to these rules, and one draw needn't show every extreme that they name: `listed`: every data group lists at least one block. `labels`: the label is a slot of an active block of the sample's group.
All inputs are finite; a program needn't handle non-finite values.
Results may differ from the reference program's by a relative error of at most 0.0042.
Values may be sent and summed in bfloat16 or wider, within the bound.
No kernel may reach another device: no remote copies, remote signals or barrier semaphores. Data moves between devices by JAX's collectives and lax.ppermute only.
A program may use at most 64 MiB of HBM per device.

```python
import jax
import jax.numpy as jnp
from jax import lax

D = 512
BLK = 128
BLK_DEV = 4
TOK_DEV = 8
IDS = 16384
TOKENS = 256
GROUP_TOK = 64
CANDS = 4096
N_GROUP = 4
N_MEMBER = 8


def listing(key):
    inner = jax.random.fold_in(key, 3)
    shape = (N_GROUP, N_GROUP * N_MEMBER)
    base = jax.random.randint(inner, shape, 0, 4)
    chosen = jax.random.randint(jax.random.fold_in(inner, 1), (N_GROUP,), 0, N_GROUP * N_MEMBER)
    places = jnp.arange(N_GROUP * N_MEMBER, dtype=jnp.int32)[None, :] == chosen[:, None]
    return jnp.where(places, 1, jnp.where(base != 0, 1, 0)).astype(jnp.int32)


def draw_listed(key, part):
    return listing(key)


def draw_labels(key, part):
    table = listing(key)
    slots = jnp.arange(CANDS, dtype=jnp.int32)
    member_of = slots // (N_GROUP * BLK)
    source = slots // BLK % N_GROUP
    owner_of = source * N_MEMBER + member_of
    group_keys = jax.random.split(jax.random.fold_in(key, 7), N_GROUP)

    def one_group(row, group_key):
        active = row[owner_of]
        order = jnp.argsort(1 - active, stable=True)
        number = jnp.sum(active) * 1
        pick = jax.random.randint(group_key, (GROUP_TOK,), 0, 2 ** 30) % number
        return order[pick].astype(jnp.int32)
    return jax.vmap(one_group)(table, group_keys).reshape(-1).astype(jnp.int32)


def with_ends(result, stream_key, smallest, high):
    extent = result.shape
    index_at = [jax.random.randint(jax.random.fold_in(stream_key, axis), (), 0, extent[axis]) for axis in range(len(extent))]
    result = result.at[tuple(index_at)].set(smallest)
    longest = extent.index(max(extent))
    index_at[longest] = (index_at[longest] + 1) % extent[longest]
    return result.at[tuple(index_at)].set(high)


def levels(rng, shape, cuts, smallest, top_value):
    factor_of, own = 1.0, jax.random.fold_in(rng, 6)
    for dim, parts in cuts:
        heights = jnp.exp(jax.random.uniform(jax.random.fold_in(own, dim), (parts,), jnp.float32, smallest / len(cuts), top_value / len(cuts)))
        factor_of = factor_of * jnp.repeat(heights, shape[dim] // parts).reshape([-1 if axis == dim else 1 for axis in range(len(shape))])
    return factor_of


def noise(stream_key, shape, scale, bound, cuts=(), kind=jnp.bfloat16):
    drawn = jax.random.normal(stream_key, shape, jnp.float32) * scale
    if len(cuts) > 0:
        drawn = levels(stream_key, shape, cuts, -0.22, 0.18) * drawn
    return jnp.clip(drawn, min=-bound, max=bound).astype(kind)


def setup_inputs(seed: int = 0) -> dict:
    key_list = jax.random.split(jax.random.key(seed), 6)
    features = noise(key_list[0], (TOKENS, D), 1.0, 6.0, ((0, 32),))
    labels = draw_labels(jax.random.fold_in(key_list[5], 71), 0)
    centres = noise(key_list[2], (IDS, D), 1.0, 6.0, ((0, 32),))
    block_ids = with_ends(jax.random.randint(key_list[3], (N_GROUP, N_GROUP * N_MEMBER), 0, BLK_DEV), jax.random.fold_in(key_list[3], 1), 0, BLK_DEV - 1).astype(jnp.int32)
    listed = draw_listed(jax.random.fold_in(key_list[5], 71), 0)
    return dict(features=features, labels=labels, centres=centres, block_ids=block_ids, listed=listed)


logit_scale = 32.0
cos_margin = 0.35
norm_epsilon = 1e-06

def reference(features, labels, centres, block_ids, listed):
    cand_count = N_GROUP * BLK
    group_tok = TOK_DEV * N_MEMBER
    vectors = features.astype(jnp.float32)
    inv_norm = lax.rsqrt(lax.optimization_barrier(jnp.sum(vectors * vectors, axis=1, keepdims=True)) + norm_epsilon)
    unit_rows = vectors * inv_norm
    unit_half = unit_rows.astype(jnp.bfloat16)
    table = centres.reshape(N_GROUP * N_MEMBER * BLK_DEV, BLK, D)
    owners = jnp.arange(N_GROUP, dtype=jnp.int32)[None, :] * N_MEMBER + jnp.arange(N_MEMBER, dtype=jnp.int32)[:, None]
    columns = jnp.arange(cand_count, dtype=jnp.int32)[None, :]
    member_ids = jnp.arange(N_MEMBER, dtype=jnp.int32)

    def per_group(grads, group):
        picked = block_ids[group][owners].astype(jnp.int32)
        flags = listed[group][owners].astype(jnp.float32)
        blocks = (owners * BLK_DEV + picked).astype(jnp.int32)
        cands = table[blocks].reshape(N_MEMBER, cand_count, D)
        active = jnp.repeat(flags, BLK, axis=1)
        start = (group * group_tok).astype(jnp.int32)
        rows = lax.dynamic_slice_in_dim(unit_half, start, group_tok, 0)
        rows_float = lax.dynamic_slice_in_dim(unit_rows, start, group_tok, 0)
        rows_inv = lax.dynamic_slice_in_dim(inv_norm, start, group_tok, 0)
        group_labels = lax.dynamic_slice_in_dim(labels, start, group_tok, 0)

        def member_logits(index, cand):
            cand_float = cand.astype(jnp.float32)
            inv_cand = lax.rsqrt(lax.optimization_barrier(jnp.sum(cand_float * cand_float, axis=1, keepdims=True)) + norm_epsilon)
            unit_cand = cand_float * inv_cand
            cand_half = unit_cand.astype(jnp.bfloat16)
            cosine = jnp.dot(rows, cand_half.T, preferred_element_type=jnp.float32)
            local_label = (group_labels - index * cand_count).astype(jnp.int32)
            onehot = (columns == local_label[:, None]).astype(jnp.float32)
            logits = logit_scale * (cosine - cos_margin * onehot)
            return (logits, onehot, unit_cand, inv_cand, cand_half)

        def forward(carry, items):
            index, cand, mask = items
            logits, onehot, unit_cand, inv_cand, cand_half = member_logits(index, cand)
            exp_logits = jnp.exp(logits) * mask[None, :]
            return ((carry[0] + lax.optimization_barrier(jnp.sum(exp_logits, axis=1)), carry[1] + lax.optimization_barrier(jnp.sum(logits * onehot, axis=1))), None)
        start_sums = (jnp.zeros((group_tok,), jnp.float32), jnp.zeros((group_tok,), jnp.float32))
        (totals, label_logit), unused = lax.scan(forward, start_sums, (member_ids, cands, active))

        def backward(carry, items):
            index, cand, mask = items
            logits, onehot, unit_cand, inv_cand, cand_half = member_logits(index, cand)
            exp_logits = jnp.exp(logits) * mask[None, :]
            weights = (logit_scale * (exp_logits / totals[:, None] - onehot)).astype(jnp.bfloat16)
            carry = carry + jnp.dot(weights, cand_half, preferred_element_type=jnp.float32)
            raw = jnp.dot(weights.T, rows, preferred_element_type=jnp.float32)
            cand_grad = (inv_cand * (raw - lax.optimization_barrier(jnp.sum(raw * unit_cand, axis=1, keepdims=True)) * unit_cand)).astype(jnp.bfloat16)
            return (carry, cand_grad)
        unit_grad, cand_grads = lax.scan(backward, jnp.zeros((group_tok, D), jnp.float32), (member_ids, cands, active))
        feature_grad = rows_inv * (unit_grad - lax.optimization_barrier(jnp.sum(unit_grad * rows_float, axis=1, keepdims=True)) * rows_float)
        row_index = (blocks[:, :, None] * BLK + jnp.arange(BLK, dtype=jnp.int32)[None, None, :]).reshape(-1).astype(jnp.int32)
        grads = grads.at[row_index].add(cand_grads.reshape(-1, D).astype(jnp.float32))
        return (grads, (jnp.log(totals) - label_logit, feature_grad))
    grads, (losses, feature_grads) = lax.scan(per_group, jnp.zeros((IDS, D), jnp.float32), jnp.arange(N_GROUP, dtype=jnp.int32))
    return (losses.reshape(-1), feature_grads.reshape(-1, D), grads)
```

```python
import jax
import jax.numpy as jnp
from jax import lax
from jax.sharding import PartitionSpec as P

BLK = 128
AXES = ("group", "member")

logit_scale = 32.0
cos_margin = 0.35
norm_epsilon = 1e-06


def sum_over_devices(values, devices):
    if devices * values.size > 1 << 20:
        return lax.psum(values, AXES)
    copies = jnp.broadcast_to(values[None], (devices, values.size))
    return jnp.sum(lax.all_to_all(copies, AXES, 0, 0, tiled=True), axis=0)


def on_device(features, labels, centres, block_ids, listed):
    groups = lax.axis_size("group")
    members = lax.axis_size("member")
    devices = groups * members
    group = lax.axis_index("group")
    member = lax.axis_index("member")
    tok_dev, width = features.shape
    group_tok = members * tok_dev
    held = centres.shape[0] // BLK

    vectors = features.astype(jnp.float32)
    inv_norm = lax.rsqrt(jnp.sum(vectors * vectors, axis=1, keepdims=True) + norm_epsilon)
    unit_rows = vectors * inv_norm
    own_labels = lax.dynamic_slice_in_dim(labels, member * tok_dev, tok_dev, 0)
    digits = jnp.stack([own_labels & 127, (own_labels >> 7) & 127, own_labels >> 14], axis=1)
    digits = jnp.pad(digits, ((0, 0), (0, 125))).astype(jnp.bfloat16)
    packed = jnp.concatenate([unit_rows.astype(jnp.bfloat16), digits], axis=1)
    gathered = lax.all_to_all(
        jnp.broadcast_to(packed[None], (devices, tok_dev, width + 128)), AXES, 0, 0, tiled=True
    )

    picked = centres.reshape(held, BLK, width)[block_ids[:, 0]].astype(jnp.float32)
    inv_cand = lax.rsqrt(jnp.sum(picked * picked, axis=2, keepdims=True) + norm_epsilon)
    unit_cand = picked * inv_cand
    cand_half = unit_cand.astype(jnp.bfloat16)

    gathered = gathered.reshape(groups, group_tok, width + 128)
    units = gathered[:, :, :width]
    digits = gathered[:, :, width : width + 3].astype(jnp.int32)
    all_labels = digits[:, :, 0] + (digits[:, :, 1] << 7) + (digits[:, :, 2] << 14)
    cosine = jnp.einsum("gsd,gcd->gsc", units, cand_half, preferred_element_type=jnp.float32)
    local_label = all_labels - (member * groups + group) * BLK
    onehot = (lax.broadcasted_iota(jnp.int32, (1, 1, BLK), 2) == local_label[:, :, None]).astype(
        jnp.float32
    )
    logits = logit_scale * (cosine - cos_margin * onehot)
    exp_logits = jnp.exp(logits) * listed.astype(jnp.float32)[:, :, None]
    sums = jnp.stack([jnp.sum(exp_logits, axis=2), jnp.sum(logits * onehot, axis=2)])
    both = sum_over_devices(sums.reshape(-1), devices).reshape(sums.shape)
    totals = both[0]
    loss_all = (jnp.log(totals) - both[1]).reshape(devices, tok_dev)
    sample_loss = lax.dynamic_slice_in_dim(loss_all, group * members + member, 1, 0)[0]

    weights = (logit_scale * (exp_logits / totals[:, :, None] - onehot)).astype(jnp.bfloat16)
    partial = jnp.einsum("gsc,gcd->gsd", weights, cand_half, preferred_element_type=jnp.float32)
    home = lax.all_to_all(
        partial.astype(jnp.bfloat16).reshape(devices, tok_dev, width), AXES, 0, 0, tiled=True
    )
    slot_grad = jnp.einsum("gsc,gsd->gcd", weights, units, preferred_element_type=jnp.float32)
    cand_grad = inv_cand * (
        slot_grad - jnp.sum(slot_grad * unit_cand, axis=2, keepdims=True) * unit_cand
    )
    cand_grad = cand_grad.astype(jnp.bfloat16).astype(jnp.float32)
    names = block_ids == jnp.arange(held, dtype=jnp.int32)[None, :]
    centre_grad = jnp.sum(
        jnp.where(names[:, :, None, None], cand_grad[:, None], 0.0), axis=0
    ).reshape(held * BLK, width)

    unit_grad = jnp.sum(home.astype(jnp.float32), axis=0)
    feature_grad = inv_norm * (
        unit_grad - jnp.sum(unit_grad * unit_rows, axis=1, keepdims=True) * unit_rows
    )
    return (sample_loss, feature_grad, centre_grad)


def solution(mesh):
    in_specs = (
        P(AXES, None),
        P("group"),
        P(AXES, None),
        P(None, AXES),
        P(None, AXES),
    )
    out_specs = (P(AXES), P(AXES, None), P(AXES, None))
    return jax.shard_map(
        on_device, mesh=mesh, in_specs=in_specs, out_specs=out_specs, check_vma=False
    )
```

```python
import jax
import jax.numpy as jnp
from jax import lax
from jax.sharding import PartitionSpec as P

BLK = 128
AXES = ("group", "member")

logit_scale = 32.0
cos_margin = 0.35
norm_epsilon = 1e-06


def from_ahead(value, axis, step):
    size = lax.axis_size(axis)
    if step % size == 0:
        return value
    return lax.ppermute(value, axis, [((i + step) % size, i) for i in range(size)])


def on_device(features, labels, centres, block_ids, listed):
    groups = lax.axis_size("group")
    members = lax.axis_size("member")
    group = lax.axis_index("group")
    member = lax.axis_index("member")
    tok_dev, width = features.shape
    group_tok = members * tok_dev
    held = centres.shape[0] // BLK

    vectors = features.astype(jnp.float32)
    inv_norm = lax.rsqrt(jnp.sum(vectors * vectors, axis=1, keepdims=True) + norm_epsilon)
    unit_rows = vectors * inv_norm
    digits = jnp.stack([labels & 127, (labels >> 7) & 127, labels >> 14], axis=0)
    digits = digits.reshape(3 * tok_dev, members)
    digits = jnp.pad(digits, ((0, 0), (0, 128 - members))).astype(jnp.bfloat16)
    digits = digits.reshape(3, tok_dev, 128).transpose(1, 0, 2).reshape(tok_dev, 3 * 128)
    packed = jnp.concatenate([unit_rows.astype(jnp.bfloat16), digits], axis=1)
    over_groups = jnp.stack([from_ahead(packed, "group", j) for j in range(groups)])
    digits = over_groups[:, :, width:].astype(jnp.int32).reshape(groups, tok_dev, 3, 128)
    digits = digits.transpose(0, 2, 1, 3)[..., :members].reshape(groups, 3, group_tok)
    all_labels = digits[:, 0] + (digits[:, 1] << 7) + (digits[:, 2] << 14)
    all_labels = jnp.roll(all_labels, -member * tok_dev, axis=1)
    columns = over_groups[:, :, :width]
    units = jnp.stack([from_ahead(columns, "member", i) for i in range(members)], axis=1)
    units = units.reshape(groups, group_tok, width)

    ids = jnp.roll(block_ids[:, 0], -group)
    flags = jnp.roll(listed[:, 0], -group).astype(jnp.float32)
    picked = centres.reshape(held, BLK, width)[ids].astype(jnp.float32)
    inv_cand = lax.rsqrt(jnp.sum(picked * picked, axis=2, keepdims=True) + norm_epsilon)
    unit_cand = picked * inv_cand
    cand_half = unit_cand.astype(jnp.bfloat16)

    cosine = jnp.einsum("gsd,gcd->gsc", units, cand_half, preferred_element_type=jnp.float32)
    local_label = all_labels - (member * groups + group) * BLK
    onehot = (lax.broadcasted_iota(jnp.int32, (1, 1, BLK), 2) == local_label[:, :, None]).astype(
        jnp.float32
    )
    logits = logit_scale * (cosine - cos_margin * onehot)
    exp_logits = jnp.exp(logits) * flags[:, None, None]
    sums = jnp.stack([jnp.sum(exp_logits, axis=2), jnp.sum(logits * onehot, axis=2)])
    sums = sums.reshape(2, groups, members, tok_dev)
    sums = sum(
        jnp.roll(from_ahead(sums, "member", i), i, axis=2) for i in range(members)
    )
    sums = sum(jnp.roll(from_ahead(sums, "group", j), j, axis=1) for j in range(groups))
    sample_loss = jnp.log(sums[0, 0, 0]) - sums[1, 0, 0]
    totals = sums[0].reshape(groups, group_tok)

    weights = (logit_scale * (exp_logits / totals[:, :, None] - onehot)).astype(jnp.bfloat16)
    partial = jnp.einsum("gsc,gcd->gsd", weights, cand_half, preferred_element_type=jnp.float32)
    partial = partial.astype(jnp.bfloat16).reshape(groups, members, tok_dev, width)
    home = sum(
        from_ahead(partial[:, i], "member", -i).astype(jnp.float32) for i in range(members)
    )
    home = home.astype(jnp.bfloat16)
    unit_grad = sum(
        from_ahead(home[j], "group", -j).astype(jnp.float32) for j in range(groups)
    )
    feature_grad = inv_norm * (
        unit_grad - jnp.sum(unit_grad * unit_rows, axis=1, keepdims=True) * unit_rows
    )

    slot_grad = jnp.einsum("gsc,gsd->gcd", weights, units, preferred_element_type=jnp.float32)
    cand_grad = inv_cand * (
        slot_grad - jnp.sum(slot_grad * unit_cand, axis=2, keepdims=True) * unit_cand
    )
    cand_grad = cand_grad.astype(jnp.bfloat16).astype(jnp.float32)
    names = ids[:, None] == jnp.arange(held, dtype=jnp.int32)[None, :]
    centre_grad = jnp.sum(
        jnp.where(names[:, :, None, None], cand_grad[:, None], 0.0), axis=0
    ).reshape(held * BLK, width)
    return (sample_loss, feature_grad, centre_grad)


def solution(mesh):
    in_specs = (
        P(AXES, None),
        P("group"),
        P(AXES, None),
        P(None, AXES),
        P(None, AXES),
    )
    out_specs = (P(AXES), P(AXES, None), P(AXES, None))
    return jax.shard_map(
        on_device, mesh=mesh, in_specs=in_specs, out_specs=out_specs, check_vma=False
    )
```

```python
import jax
import jax.numpy as jnp
from jax import lax
from jax.experimental import pallas as pl
from jax.experimental.pallas import tpu as pltpu
from jax.sharding import PartitionSpec as P

BLK = 128
AXES = ("group", "member")

logit_scale = 32.0
cos_margin = 0.35
norm_epsilon = 1e-06

VMEM = pl.BlockSpec(memory_space=pltpu.VMEM)
SMEM = pl.BlockSpec(memory_space=pltpu.SMEM)


def inverse_norm(rows):
    return lax.rsqrt(jnp.sum(rows * rows, axis=-1, keepdims=True) + norm_epsilon)


def contract(left, right, left_dim, right_dim):
    dims = (((left_dim,), (right_dim,)), ((), ()))
    return lax.dot_general(left, right, dims, preferred_element_type=jnp.float32)


def run(kernel, out_shape, in_specs, *operands):
    shapes = jax.tree.leaves(out_shape)
    return pl.pallas_call(
        kernel,
        out_shape=out_shape,
        in_specs=in_specs,
        out_specs=jax.tree.map(lambda _: VMEM, out_shape),
        compiler_params=pltpu.CompilerParams(vmem_limit_bytes=48 * 1024 * 1024),
        cost_estimate=pl.CostEstimate(
            flops=0,
            transcendentals=0,
            bytes_accessed=sum(a.size * a.dtype.itemsize for a in (*shapes, *operands)),
        ),
    )(*operands)


def pack_units(features, copies_out):
    rows = features[...].astype(jnp.float32)
    unit = (rows * inverse_norm(rows)).astype(jnp.bfloat16)
    copies_out[...] = jnp.broadcast_to(unit[None], copies_out.shape)


def own_slots(labels_row, group_tok, member, groups, group):
    first = (member * groups + group) * BLK
    return lax.broadcasted_iota(jnp.int32, (BLK, group_tok), 0) == labels_row - first


def prepare(ids, centres, labels, cand_out, label_rows_out):
    group, member = lax.axis_index("group"), lax.axis_index("member")
    groups, group_tok = labels.shape
    for g in range(groups):
        rows = centres[ids[g, 0]].astype(jnp.float32)
        cand = (rows * inverse_norm(rows)).astype(jnp.bfloat16)
        cand_out[g] = cand
        onehot = own_slots(labels[g : g + 1, :], group_tok, member, groups, group)
        label_rows_out[g] = contract(onehot.astype(jnp.bfloat16), cand, 0, 0).astype(jnp.bfloat16)


def forward(listed, units, cands, labels, expo_out, sums_out, shares_out):
    group, member = lax.axis_index("group"), lax.axis_index("member")
    groups, group_tok = labels.shape
    sums = []
    for g in range(groups):
        cand = cands[g]
        onehot = own_slots(labels[g : g + 1, :], group_tok, member, groups, group)
        cosine = contract(cand, units[g], 1, 1)
        logits = logit_scale * (cosine - jnp.where(onehot, cos_margin, 0.0))
        expo = jnp.exp(logits) * listed[g, 0].astype(jnp.float32)
        expo_out[g] = expo
        totals = jnp.sum(expo, axis=0, keepdims=True)
        label_logit = jnp.sum(jnp.where(onehot, logits, 0.0), axis=0, keepdims=True)
        sums.append(jnp.concatenate([totals, label_logit], axis=1))
        others = jnp.where(onehot, 0.0, expo).astype(jnp.bfloat16)
        shares_out[g] = contract(others, cand, 0, 0).astype(jnp.bfloat16)
    sums = jnp.concatenate(sums, axis=0)
    sums_out[...] = jnp.broadcast_to(sums[None], sums_out.shape)


def backward(
    ids, sums, expo, units, centres, labels, label_rows, grad_out, loss_out, scale_out, pull_out
):
    group, member = lax.axis_index("group"), lax.axis_index("member")
    groups, group_tok = labels.shape
    both = jnp.sum(sums[...], axis=0)
    grad_out[...] = jnp.zeros_like(grad_out)
    for g in range(groups):
        rows = centres[ids[g, 0]].astype(jnp.float32)
        inv_cand = inverse_norm(rows)
        unit_cand = rows * inv_cand
        onehot = own_slots(labels[g : g + 1, :], group_tok, member, groups, group)
        share = expo[g] / both[g : g + 1, :group_tok]
        weights = (logit_scale * (share - jnp.where(onehot, 1.0, 0.0))).astype(jnp.bfloat16)
        slot_grad = contract(weights, units[g], 1, 0)
        along = jnp.sum(slot_grad * unit_cand, axis=1, keepdims=True)
        cand_grad = (inv_cand * (slot_grad - along * unit_cand)).astype(jnp.bfloat16)
        grad_out[ids[g, 0]] += cand_grad.astype(jnp.float32)

    tok_dev = pull_out.shape[0]
    row = lax.broadcasted_iota(jnp.int32, (groups, 2 * group_tok), 0)
    mine = jnp.sum(jnp.where(row == group, both, 0.0), axis=0, keepdims=True)
    lane = lax.broadcasted_iota(jnp.int32, (tok_dev, 2 * group_tok), 1)
    sample = lax.broadcasted_iota(jnp.int32, (tok_dev, 2 * group_tok), 0) + member * tok_dev
    total = jnp.sum(jnp.where(lane == sample, mine, 0.0), axis=1, keepdims=True)
    label_logit = jnp.sum(
        jnp.where(lane == sample + group_tok, mine, 0.0), axis=1, keepdims=True
    )
    loss = jnp.log(total) - label_logit
    square = (tok_dev, tok_dev)
    diagonal = lax.broadcasted_iota(jnp.int32, square, 0) == lax.broadcasted_iota(
        jnp.int32, square, 1
    )
    loss_out[...] = jnp.sum(jnp.where(diagonal, loss, 0.0), axis=0, keepdims=True)
    scale = logit_scale / total
    scale_out[...] = jnp.broadcast_to(scale, scale_out.shape)
    label_row = jnp.sum(label_rows[...].astype(jnp.float32), axis=0)
    pull_out[...] = scale * (total - jnp.exp(label_logit)) * label_row


def finish(features, shares, scale, pull, grad_out):
    rows = features[...].astype(jnp.float32)
    inv_norm = inverse_norm(rows)
    unit = rows * inv_norm
    unit_grad = scale[:, :1] * jnp.sum(shares[...].astype(jnp.float32), axis=0) - pull[...]
    along = jnp.sum(unit_grad * unit, axis=1, keepdims=True)
    grad_out[...] = inv_norm * (unit_grad - along * unit)


def exchange(pieces, axes):
    return lax.all_to_all(pieces, axes, split_axis=0, concat_axis=0, tiled=True)


def on_device(features, labels, centres, block_ids, listed):
    groups = lax.axis_size("group")
    members = lax.axis_size("member")
    devices = groups * members
    tok_dev, width = features.shape
    group_tok = members * tok_dev
    held = centres.shape[0] // BLK
    blocks = centres.reshape(held, BLK, width)
    per_device = (devices, tok_dev, width)
    per_group = (groups, group_tok, width)
    bf16, f32 = jnp.bfloat16, jnp.float32
    shape = jax.ShapeDtypeStruct

    copies = run(pack_units, shape(per_device, bf16), [VMEM], features)
    units = exchange(copies, AXES).reshape(per_group)
    all_labels = exchange(jnp.broadcast_to(labels[None], (groups, group_tok)), "group")

    cands, label_rows = run(
        prepare,
        (shape((groups, BLK, width), bf16), shape(per_group, bf16)),
        [SMEM, VMEM, VMEM],
        block_ids,
        blocks,
        all_labels,
    )
    label_rows = exchange(label_rows.reshape(per_device), AXES)

    expo, sums, shares = run(
        forward,
        (
            shape((groups, BLK, group_tok), f32),
            shape((devices, groups, 2 * group_tok), f32),
            shape(per_group, bf16),
        ),
        [SMEM, VMEM, VMEM, VMEM],
        listed,
        units,
        cands,
        all_labels,
    )
    sums = exchange(sums, AXES)
    shares = exchange(shares.reshape(per_device), AXES)

    centre_grad, loss, scale, pull = run(
        backward,
        (
            shape((held, BLK, width), f32),
            shape((1, tok_dev), f32),
            shape((tok_dev, 128), f32),
            shape((tok_dev, width), f32),
        ),
        [SMEM] + [VMEM] * 6,
        block_ids,
        sums,
        expo,
        units,
        blocks,
        all_labels,
        label_rows,
    )
    feature_grad = run(
        finish, shape((tok_dev, width), f32), [VMEM] * 4, features, shares, scale, pull
    )
    return (loss.reshape(tok_dev), feature_grad, centre_grad.reshape(held * BLK, width))


def on_device_of_many(features, labels, centres, block_ids, listed):
    groups = lax.axis_size("group")
    members = lax.axis_size("member")
    devices = groups * members
    group = lax.axis_index("group")
    member = lax.axis_index("member")
    tok_dev, width = features.shape
    group_tok = members * tok_dev
    held = centres.shape[0] // BLK

    vectors = features.astype(jnp.float32)
    inv_norm = inverse_norm(vectors)
    unit_rows = vectors * inv_norm
    copies = jnp.broadcast_to(unit_rows.astype(jnp.bfloat16), (devices, tok_dev, width))
    units = exchange(copies, AXES).reshape(groups, group_tok, width)
    all_labels = exchange(jnp.broadcast_to(labels[None], (groups, group_tok)), "group")

    picked = centres.reshape(held, BLK, width)[block_ids[:, 0]].astype(jnp.float32)
    inv_cand = inverse_norm(picked)
    unit_cand = picked * inv_cand
    cand_half = unit_cand.astype(jnp.bfloat16)
    cosine = jnp.einsum("gsd,gcd->gsc", units, cand_half, preferred_element_type=jnp.float32)
    local_label = all_labels - (member * groups + group) * BLK
    onehot = (lax.broadcasted_iota(jnp.int32, (1, 1, BLK), 2) == local_label[:, :, None]).astype(
        jnp.float32
    )
    logits = logit_scale * (cosine - cos_margin * onehot)
    exp_logits = jnp.exp(logits) * listed.astype(jnp.float32)[:, :, None]
    totals, label_logit = lax.psum(
        (jnp.sum(exp_logits, axis=2), jnp.sum(logits * onehot, axis=2)), AXES
    )
    loss_all = (jnp.log(totals) - label_logit).reshape(devices, tok_dev)
    sample_loss = lax.dynamic_slice_in_dim(loss_all, group * members + member, 1, 0)[0]

    weights = (logit_scale * (exp_logits / totals[:, :, None] - onehot)).astype(jnp.bfloat16)
    partial = jnp.einsum("gsc,gcd->gsd", weights, cand_half, preferred_element_type=jnp.float32)
    home = exchange(partial.astype(jnp.bfloat16).reshape(devices, tok_dev, width), AXES)
    unit_grad = jnp.sum(home.astype(jnp.float32), axis=0)
    feature_grad = inv_norm * (
        unit_grad - jnp.sum(unit_grad * unit_rows, axis=1, keepdims=True) * unit_rows
    )
    slot_grad = jnp.einsum("gsc,gsd->gcd", weights, units, preferred_element_type=jnp.float32)
    cand_grad = inv_cand * (
        slot_grad - jnp.sum(slot_grad * unit_cand, axis=2, keepdims=True) * unit_cand
    )
    cand_grad = cand_grad.astype(jnp.bfloat16).astype(jnp.float32)
    names = block_ids == jnp.arange(held, dtype=jnp.int32)[None, :]
    centre_grad = jnp.sum(
        jnp.where(names[:, :, None, None], cand_grad[:, None], 0.0), axis=0
    ).reshape(held * BLK, width)
    return (sample_loss, feature_grad, centre_grad)


def solution(mesh):
    in_specs = (
        P(AXES, None),
        P("group"),
        P(AXES, None),
        P(None, AXES),
        P(None, AXES),
    )
    out_specs = (P(AXES), P(AXES, None), P(AXES, None))
    body = on_device if mesh.size <= 64 else on_device_of_many
    return jax.shard_map(
        body, mesh=mesh, in_specs=in_specs, out_specs=out_specs, check_vma=False
    )
```

```python
import jax
import jax.numpy as jnp
from jax import lax
from jax.experimental import pallas as pl
from jax.experimental.pallas import tpu as pltpu
from jax.sharding import PartitionSpec as P

BLK = 128
AXES = ("group", "member")

logit_scale = 32.0
cos_margin = 0.35
norm_epsilon = 1e-06

VMEM = pl.BlockSpec(memory_space=pltpu.VMEM)
SMEM = pl.BlockSpec(memory_space=pltpu.SMEM)


def inverse_norm(rows):
    return lax.rsqrt(jnp.sum(rows * rows, axis=-1, keepdims=True) + norm_epsilon)


def contract(left, right, left_dim, right_dim):
    dims = (((left_dim,), (right_dim,)), ((), ()))
    return lax.dot_general(left, right, dims, preferred_element_type=jnp.float32)


def run(kernel, out_shape, in_specs, *operands):
    shapes = jax.tree.leaves(out_shape)
    return pl.pallas_call(
        kernel,
        out_shape=out_shape,
        in_specs=in_specs,
        out_specs=jax.tree.map(lambda _: VMEM, out_shape),
        compiler_params=pltpu.CompilerParams(vmem_limit_bytes=48 * 1024 * 1024),
        cost_estimate=pl.CostEstimate(
            flops=0,
            transcendentals=0,
            bytes_accessed=sum(a.size * a.dtype.itemsize for a in (*shapes, *operands)),
        ),
    )(*operands)


def pack_units(features, labels, copies_out, labels_out):
    rows = features[...].astype(jnp.float32)
    unit = (rows * inverse_norm(rows)).astype(jnp.bfloat16)
    copies_out[...] = jnp.broadcast_to(unit[None], copies_out.shape)
    labels_out[...] = labels[...]


def own_slots(labels_row, group_tok, member, groups, group):
    first = (member * groups + group) * BLK
    return lax.broadcasted_iota(jnp.int32, (BLK, group_tok), 0) == labels_row - first


def prepare(ids, centres, cand_out):
    for g in range(cand_out.shape[0]):
        rows = centres[ids[g, 0]].astype(jnp.float32)
        cand_out[g] = (rows * inverse_norm(rows)).astype(jnp.bfloat16)


def forward(listed, units, cands, labels, expo_out, sums_out, shares_out):
    group, member = lax.axis_index("group"), lax.axis_index("member")
    groups, group_tok = labels.shape
    width = units.shape[2]
    for g in range(groups):
        cand = cands[g]
        onehot = own_slots(labels[g : g + 1, :], group_tok, member, groups, group)
        cosine = contract(cand, units[g], 1, 1)
        logits = logit_scale * (cosine - jnp.where(onehot, cos_margin, 0.0))
        expo = jnp.exp(logits) * listed[g, 0].astype(jnp.float32)
        expo_out[g] = expo
        totals = jnp.sum(expo, axis=0, keepdims=True)
        label_logit = jnp.sum(jnp.where(onehot, logits, 0.0), axis=0, keepdims=True)
        sums_out[g : g + 1, :] = jnp.concatenate([totals, label_logit], axis=1)
        others = jnp.where(onehot, 0.0, expo).astype(jnp.bfloat16)
        shares_out[g, :, :width] = contract(others, cand, 0, 0).astype(jnp.bfloat16)
        label_rows = contract(onehot.astype(jnp.bfloat16), cand, 0, 0)
        shares_out[g, :, width:] = label_rows.astype(jnp.bfloat16)


def backward(
    ids, sums, expo, units, centres, labels, grad_out, loss_out, scale_out, pull_out
):
    group, member = lax.axis_index("group"), lax.axis_index("member")
    groups, group_tok = labels.shape
    both = sums[...]
    grad_out[...] = jnp.zeros_like(grad_out)
    for g in range(groups):
        rows = centres[ids[g, 0]].astype(jnp.float32)
        inv_cand = inverse_norm(rows)
        unit_cand = rows * inv_cand
        onehot = own_slots(labels[g : g + 1, :], group_tok, member, groups, group)
        share = expo[g] / both[g : g + 1, :group_tok]
        weights = (logit_scale * (share - jnp.where(onehot, 1.0, 0.0))).astype(jnp.bfloat16)
        slot_grad = contract(weights, units[g], 1, 0)
        along = jnp.sum(slot_grad * unit_cand, axis=1, keepdims=True)
        cand_grad = (inv_cand * (slot_grad - along * unit_cand)).astype(jnp.bfloat16)
        grad_out[ids[g, 0]] += cand_grad.astype(jnp.float32)

    tok_dev = pull_out.shape[0]
    row = lax.broadcasted_iota(jnp.int32, (groups, 2 * group_tok), 0)
    mine = jnp.sum(jnp.where(row == group, both, 0.0), axis=0, keepdims=True)
    lane = lax.broadcasted_iota(jnp.int32, (tok_dev, 2 * group_tok), 1)
    sample = lax.broadcasted_iota(jnp.int32, (tok_dev, 2 * group_tok), 0) + member * tok_dev
    total = jnp.sum(jnp.where(lane == sample, mine, 0.0), axis=1, keepdims=True)
    label_logit = jnp.sum(
        jnp.where(lane == sample + group_tok, mine, 0.0), axis=1, keepdims=True
    )
    loss = jnp.log(total) - label_logit
    square = (tok_dev, tok_dev)
    diagonal = lax.broadcasted_iota(jnp.int32, square, 0) == lax.broadcasted_iota(
        jnp.int32, square, 1
    )
    loss_out[...] = jnp.sum(jnp.where(diagonal, loss, 0.0), axis=0, keepdims=True)
    scale = logit_scale / total
    scale_out[...] = jnp.broadcast_to(scale, scale_out.shape)
    pull_out[...] = jnp.broadcast_to(scale * (total - jnp.exp(label_logit)), pull_out.shape)


def finish(features, shares, scale, pull, grad_out):
    rows = features[...].astype(jnp.float32)
    inv_norm = inverse_norm(rows)
    unit = rows * inv_norm
    width = rows.shape[1]
    both = jnp.sum(shares[...].astype(jnp.float32), axis=0)
    unit_grad = scale[:, :1] * both[:, :width] - pull[:, :1] * both[:, width:]
    along = jnp.sum(unit_grad * unit, axis=1, keepdims=True)
    grad_out[...] = inv_norm * (unit_grad - along * unit)


def exchange(pieces, axes):
    return lax.all_to_all(pieces, axes, split_axis=0, concat_axis=0, tiled=True)


def gather_groups(row):
    groups = lax.axis_size("group")
    rows = [row] + [
        lax.ppermute(row, "group", [((i + step) % groups, i) for i in range(groups)])
        for step in range(1, groups)
    ]
    ahead = jnp.concatenate(rows, axis=0)
    return jnp.roll(ahead, lax.axis_index("group"), axis=0)


def on_device(features, labels, centres, block_ids, listed):
    groups = lax.axis_size("group")
    members = lax.axis_size("member")
    devices = groups * members
    tok_dev, width = features.shape
    group_tok = members * tok_dev
    held = centres.shape[0] // BLK
    blocks = centres.reshape(held, BLK, width)
    per_device = (devices, tok_dev, width)
    per_group = (groups, group_tok, width)
    bf16, f32 = jnp.bfloat16, jnp.float32
    shape = jax.ShapeDtypeStruct

    copies, own_labels = run(
        pack_units,
        (shape(per_device, bf16), shape((1, group_tok), labels.dtype)),
        [VMEM, VMEM],
        features,
        labels.reshape(1, group_tok),
    )
    units = exchange(copies, AXES).reshape(per_group)
    all_labels = gather_groups(own_labels)
    cands = run(prepare, shape((groups, BLK, width), bf16), [SMEM, VMEM], block_ids, blocks)

    expo, sums, shares = run(
        forward,
        (
            shape((groups, BLK, group_tok), f32),
            shape((groups, 2 * group_tok), f32),
            shape((groups, group_tok, 2 * width), bf16),
        ),
        [SMEM, VMEM, VMEM, VMEM],
        listed,
        units,
        cands,
        all_labels,
    )
    shares = exchange(shares.reshape(devices, tok_dev, 2 * width), AXES)
    sums = lax.psum(sums, AXES)

    centre_grad, loss, scale, pull = run(
        backward,
        (
            shape((held, BLK, width), f32),
            shape((1, tok_dev), f32),
            shape((tok_dev, 128), f32),
            shape((tok_dev, 128), f32),
        ),
        [SMEM] + [VMEM] * 5,
        block_ids,
        sums,
        expo,
        units,
        blocks,
        all_labels,
    )
    feature_grad = run(
        finish, shape((tok_dev, width), f32), [VMEM] * 4, features, shares, scale, pull
    )
    return (loss.reshape(tok_dev), feature_grad, centre_grad.reshape(held * BLK, width))


def on_device_of_many(features, labels, centres, block_ids, listed):
    groups = lax.axis_size("group")
    members = lax.axis_size("member")
    devices = groups * members
    group = lax.axis_index("group")
    member = lax.axis_index("member")
    tok_dev, width = features.shape
    group_tok = members * tok_dev
    held = centres.shape[0] // BLK

    vectors = features.astype(jnp.float32)
    inv_norm = inverse_norm(vectors)
    unit_rows = vectors * inv_norm
    copies = jnp.broadcast_to(unit_rows.astype(jnp.bfloat16), (devices, tok_dev, width))
    units = exchange(copies, AXES).reshape(groups, group_tok, width)
    all_labels = exchange(jnp.broadcast_to(labels[None], (groups, group_tok)), "group")

    picked = centres.reshape(held, BLK, width)[block_ids[:, 0]].astype(jnp.float32)
    inv_cand = inverse_norm(picked)
    unit_cand = picked * inv_cand
    cand_half = unit_cand.astype(jnp.bfloat16)
    cosine = jnp.einsum("gsd,gcd->gsc", units, cand_half, preferred_element_type=jnp.float32)
    local_label = all_labels - (member * groups + group) * BLK
    onehot = (lax.broadcasted_iota(jnp.int32, (1, 1, BLK), 2) == local_label[:, :, None]).astype(
        jnp.float32
    )
    logits = logit_scale * (cosine - cos_margin * onehot)
    exp_logits = jnp.exp(logits) * listed.astype(jnp.float32)[:, :, None]
    totals, label_logit = lax.psum(
        (jnp.sum(exp_logits, axis=2), jnp.sum(logits * onehot, axis=2)), AXES
    )
    loss_all = (jnp.log(totals) - label_logit).reshape(devices, tok_dev)
    sample_loss = lax.dynamic_slice_in_dim(loss_all, group * members + member, 1, 0)[0]

    weights = (logit_scale * (exp_logits / totals[:, :, None] - onehot)).astype(jnp.bfloat16)
    partial = jnp.einsum("gsc,gcd->gsd", weights, cand_half, preferred_element_type=jnp.float32)
    home = exchange(partial.astype(jnp.bfloat16).reshape(devices, tok_dev, width), AXES)
    unit_grad = jnp.sum(home.astype(jnp.float32), axis=0)
    feature_grad = inv_norm * (
        unit_grad - jnp.sum(unit_grad * unit_rows, axis=1, keepdims=True) * unit_rows
    )
    slot_grad = jnp.einsum("gsc,gsd->gcd", weights, units, preferred_element_type=jnp.float32)
    cand_grad = inv_cand * (
        slot_grad - jnp.sum(slot_grad * unit_cand, axis=2, keepdims=True) * unit_cand
    )
    cand_grad = cand_grad.astype(jnp.bfloat16).astype(jnp.float32)
    names = block_ids == jnp.arange(held, dtype=jnp.int32)[None, :]
    centre_grad = jnp.sum(
        jnp.where(names[:, :, None, None], cand_grad[:, None], 0.0), axis=0
    ).reshape(held * BLK, width)
    return (sample_loss, feature_grad, centre_grad)


def solution(mesh):
    in_specs = (
        P(AXES, None),
        P("group"),
        P(AXES, None),
        P(None, AXES),
        P(None, AXES),
    )
    out_specs = (P(AXES), P(AXES, None), P(AXES, None))
    body = on_device if mesh.size <= 64 else on_device_of_many
    return jax.shard_map(
        body, mesh=mesh, in_specs=in_specs, out_specs=out_specs, check_vma=False
    )
```

```python
import jax
import jax.numpy as jnp
from jax import lax
from jax.experimental import pallas as pl
from jax.experimental.pallas import tpu as pltpu
from jax.sharding import PartitionSpec as P

BLK = 128
AXES = ("group", "member")

logit_scale = 32.0
cos_margin = 0.35
norm_epsilon = 1e-06

VMEM = pl.BlockSpec(memory_space=pltpu.VMEM)
HBM = pl.BlockSpec(memory_space=pl.ANY)
SMEM = pl.BlockSpec(memory_space=pltpu.SMEM)


def inverse_norm(rows):
    return lax.rsqrt(jnp.sum(rows * rows, axis=-1, keepdims=True) + norm_epsilon)


def contract(left, right, left_dim, right_dim):
    dims = (((left_dim,), (right_dim,)), ((), ()))
    return lax.dot_general(left, right, dims, preferred_element_type=jnp.float32)


def run(kernel, out_shape, in_specs, *operands, scratch=()):
    shapes = jax.tree.leaves(out_shape)
    return pl.pallas_call(
        kernel,
        out_shape=out_shape,
        in_specs=in_specs,
        out_specs=jax.tree.map(lambda _: VMEM, out_shape),
        scratch_shapes=scratch,
        compiler_params=pltpu.CompilerParams(vmem_limit_bytes=48 * 1024 * 1024),
        cost_estimate=pl.CostEstimate(
            flops=0,
            transcendentals=0,
            bytes_accessed=sum(a.size * a.dtype.itemsize for a in (*shapes, *operands)),
        ),
    )(*operands)


def pack_units(features, labels, copies_out, labels_out, held, arrived):
    rows_copy = pltpu.make_async_copy(features, held, arrived.at[0])
    labels_copy = pltpu.make_async_copy(labels, labels_out, arrived.at[1])
    rows_copy.start()
    labels_copy.start()
    rows_copy.wait()
    rows = held[...].astype(jnp.float32)
    unit = (rows * inverse_norm(rows)).astype(jnp.bfloat16)
    copies_out[...] = jnp.broadcast_to(unit[None], copies_out.shape)
    labels_copy.wait()


def own_slots(labels_row, group_tok, member, groups, group):
    first = (member * groups + group) * BLK
    return lax.broadcasted_iota(jnp.int32, (BLK, group_tok), 0) == labels_row - first


def prepare(ids, centres, cand_out):
    for g in range(cand_out.shape[0]):
        rows = centres[ids[g, 0]].astype(jnp.float32)
        cand_out[g] = (rows * inverse_norm(rows)).astype(jnp.bfloat16)


def forward(listed, units, cands, labels, expo_out, sums_out, shares_out):
    group, member = lax.axis_index("group"), lax.axis_index("member")
    groups, group_tok = labels.shape
    width = units.shape[2]
    for g in range(groups):
        cand = cands[g]
        onehot = own_slots(labels[g : g + 1, :], group_tok, member, groups, group)
        cosine = contract(cand, units[g], 1, 1)
        logits = logit_scale * (cosine - jnp.where(onehot, cos_margin, 0.0))
        expo = jnp.exp(logits) * listed[g, 0].astype(jnp.float32)
        expo_out[g] = expo
        totals = jnp.sum(expo, axis=0, keepdims=True)
        label_logit = jnp.sum(jnp.where(onehot, logits, 0.0), axis=0, keepdims=True)
        sums_out[g : g + 1, :] = jnp.concatenate([totals, label_logit], axis=1)
        others = jnp.where(onehot, 0.0, expo)
        label = jnp.where(onehot, 1.0, 0.0)
        both = jnp.concatenate([others, label], axis=1).astype(jnp.bfloat16)
        both = contract(both, cand, 0, 0).astype(jnp.bfloat16)
        shares_out[g, :, :width] = both[:group_tok]
        shares_out[g, :, width:] = both[group_tok:]


def backward(
    ids, sums, expo, units, centres, labels, grad_out, loss_out, scale_out, pull_out
):
    group, member = lax.axis_index("group"), lax.axis_index("member")
    groups, group_tok = labels.shape
    both = sums[...]
    grad_out[...] = jnp.zeros_like(grad_out)
    for g in range(groups):
        rows = centres[ids[g, 0]].astype(jnp.float32)
        inv_cand = inverse_norm(rows)
        unit_cand = rows * inv_cand
        onehot = own_slots(labels[g : g + 1, :], group_tok, member, groups, group)
        share = expo[g] / both[g : g + 1, :group_tok]
        weights = (logit_scale * (share - jnp.where(onehot, 1.0, 0.0))).astype(jnp.bfloat16)
        slot_grad = contract(weights, units[g], 1, 0)
        along = jnp.sum(slot_grad * unit_cand, axis=1, keepdims=True)
        cand_grad = (inv_cand * (slot_grad - along * unit_cand)).astype(jnp.bfloat16)
        grad_out[ids[g, 0]] += cand_grad.astype(jnp.float32)

    tok_dev = pull_out.shape[0]
    row = lax.broadcasted_iota(jnp.int32, (groups, 2 * group_tok), 0)
    mine = jnp.sum(jnp.where(row == group, both, 0.0), axis=0, keepdims=True)
    lane = lax.broadcasted_iota(jnp.int32, (tok_dev, 2 * group_tok), 1)
    sample = lax.broadcasted_iota(jnp.int32, (tok_dev, 2 * group_tok), 0) + member * tok_dev
    total = jnp.sum(jnp.where(lane == sample, mine, 0.0), axis=1, keepdims=True)
    label_logit = jnp.sum(
        jnp.where(lane == sample + group_tok, mine, 0.0), axis=1, keepdims=True
    )
    loss = jnp.log(total) - label_logit
    square = (tok_dev, tok_dev)
    diagonal = lax.broadcasted_iota(jnp.int32, square, 0) == lax.broadcasted_iota(
        jnp.int32, square, 1
    )
    loss_out[...] = jnp.sum(jnp.where(diagonal, loss, 0.0), axis=0, keepdims=True)
    scale = logit_scale / total
    scale_out[...] = jnp.broadcast_to(scale, scale_out.shape)
    pull_out[...] = jnp.broadcast_to(scale * (total - jnp.exp(label_logit)), pull_out.shape)


def finish(features, shares, scale, pull, grad_out):
    rows = features[...].astype(jnp.float32)
    inv_norm = inverse_norm(rows)
    unit = rows * inv_norm
    width = rows.shape[1]
    both = jnp.sum(shares[...].astype(jnp.float32), axis=0)
    unit_grad = scale[:, :1] * both[:, :width] - pull[:, :1] * both[:, width:]
    along = jnp.sum(unit_grad * unit, axis=1, keepdims=True)
    grad_out[...] = inv_norm * (unit_grad - along * unit)


def exchange(pieces, axes):
    return lax.all_to_all(pieces, axes, split_axis=0, concat_axis=0, tiled=True)


def gather_groups(row):
    groups = lax.axis_size("group")
    rows = [row] + [
        lax.ppermute(row, "group", [((i + step) % groups, i) for i in range(groups)])
        for step in range(1, groups)
    ]
    ahead = jnp.concatenate(rows, axis=0)
    return jnp.roll(ahead, lax.axis_index("group"), axis=0)


def sum_over(value, axis):
    size = lax.axis_size(axis)
    if size & (size - 1):
        return lax.psum(value, axis)
    bit = 1
    while bit < size:
        value = value + lax.ppermute(value, axis, [(i, i ^ bit) for i in range(size)])
        bit *= 2
    return value


def on_device(features, labels, centres, block_ids, listed):
    groups = lax.axis_size("group")
    members = lax.axis_size("member")
    devices = groups * members
    tok_dev, width = features.shape
    group_tok = members * tok_dev
    held = centres.shape[0] // BLK
    blocks = centres.reshape(held, BLK, width)
    per_device = (devices, tok_dev, width)
    per_group = (groups, group_tok, width)
    bf16, f32 = jnp.bfloat16, jnp.float32
    shape = jax.ShapeDtypeStruct

    copies, own_labels = run(
        pack_units,
        (shape(per_device, bf16), shape((1, group_tok), labels.dtype)),
        [HBM, HBM],
        features,
        labels.reshape(1, group_tok),
        scratch=[pltpu.VMEM(features.shape, features.dtype), pltpu.SemaphoreType.DMA((2,))],
    )
    units = exchange(copies, AXES).reshape(per_group)
    all_labels = gather_groups(own_labels)
    cands = run(prepare, shape((groups, BLK, width), bf16), [SMEM, VMEM], block_ids, blocks)

    expo, sums, shares = run(
        forward,
        (
            shape((groups, BLK, group_tok), f32),
            shape((groups, 2 * group_tok), f32),
            shape((groups, group_tok, 2 * width), bf16),
        ),
        [SMEM, VMEM, VMEM, VMEM],
        listed,
        units,
        cands,
        all_labels,
    )
    shares = exchange(shares.reshape(devices, tok_dev, 2 * width), AXES)
    sums = sum_over(sum_over(sums, "member"), "group")

    centre_grad, loss, scale, pull = run(
        backward,
        (
            shape((held, BLK, width), f32),
            shape((1, tok_dev), f32),
            shape((tok_dev, 128), f32),
            shape((tok_dev, 128), f32),
        ),
        [SMEM] + [VMEM] * 5,
        block_ids,
        sums,
        expo,
        units,
        blocks,
        all_labels,
    )
    feature_grad = run(
        finish, shape((tok_dev, width), f32), [VMEM] * 4, features, shares, scale, pull
    )
    return (loss.reshape(tok_dev), feature_grad, centre_grad.reshape(held * BLK, width))


def on_device_of_many(features, labels, centres, block_ids, listed):
    groups = lax.axis_size("group")
    members = lax.axis_size("member")
    devices = groups * members
    group = lax.axis_index("group")
    member = lax.axis_index("member")
    tok_dev, width = features.shape
    group_tok = members * tok_dev
    held = centres.shape[0] // BLK

    vectors = features.astype(jnp.float32)
    inv_norm = inverse_norm(vectors)
    unit_rows = vectors * inv_norm
    copies = jnp.broadcast_to(unit_rows.astype(jnp.bfloat16), (devices, tok_dev, width))
    units = exchange(copies, AXES).reshape(groups, group_tok, width)
    all_labels = exchange(jnp.broadcast_to(labels[None], (groups, group_tok)), "group")

    picked = centres.reshape(held, BLK, width)[block_ids[:, 0]].astype(jnp.float32)
    inv_cand = inverse_norm(picked)
    unit_cand = picked * inv_cand
    cand_half = unit_cand.astype(jnp.bfloat16)
    cosine = jnp.einsum("gsd,gcd->gsc", units, cand_half, preferred_element_type=jnp.float32)
    local_label = all_labels - (member * groups + group) * BLK
    onehot = (lax.broadcasted_iota(jnp.int32, (1, 1, BLK), 2) == local_label[:, :, None]).astype(
        jnp.float32
    )
    logits = logit_scale * (cosine - cos_margin * onehot)
    exp_logits = jnp.exp(logits) * listed.astype(jnp.float32)[:, :, None]
    totals, label_logit = lax.psum(
        (jnp.sum(exp_logits, axis=2), jnp.sum(logits * onehot, axis=2)), AXES
    )
    loss_all = (jnp.log(totals) - label_logit).reshape(devices, tok_dev)
    sample_loss = lax.dynamic_slice_in_dim(loss_all, group * members + member, 1, 0)[0]

    weights = (logit_scale * (exp_logits / totals[:, :, None] - onehot)).astype(jnp.bfloat16)
    partial = jnp.einsum("gsc,gcd->gsd", weights, cand_half, preferred_element_type=jnp.float32)
    home = exchange(partial.astype(jnp.bfloat16).reshape(devices, tok_dev, width), AXES)
    unit_grad = jnp.sum(home.astype(jnp.float32), axis=0)
    feature_grad = inv_norm * (
        unit_grad - jnp.sum(unit_grad * unit_rows, axis=1, keepdims=True) * unit_rows
    )
    slot_grad = jnp.einsum("gsc,gsd->gcd", weights, units, preferred_element_type=jnp.float32)
    cand_grad = inv_cand * (
        slot_grad - jnp.sum(slot_grad * unit_cand, axis=2, keepdims=True) * unit_cand
    )
    cand_grad = cand_grad.astype(jnp.bfloat16).astype(jnp.float32)
    names = block_ids == jnp.arange(held, dtype=jnp.int32)[None, :]
    centre_grad = jnp.sum(
        jnp.where(names[:, :, None, None], cand_grad[:, None], 0.0), axis=0
    ).reshape(held * BLK, width)
    return (sample_loss, feature_grad, centre_grad)


def solution(mesh):
    in_specs = (
        P(AXES, None),
        P("group"),
        P(AXES, None),
        P(None, AXES),
        P(None, AXES),
    )
    out_specs = (P(AXES), P(AXES, None), P(AXES, None))
    body = on_device if mesh.size <= 64 else on_device_of_many
    return jax.shard_map(
        body, mesh=mesh, in_specs=in_specs, out_specs=out_specs, check_vma=False
    )
```

```python
import jax
import jax.numpy as jnp
from jax import lax
from jax.experimental import pallas as pl
from jax.experimental.pallas import tpu as pltpu
from jax.sharding import PartitionSpec as P

BLK = 128
AXES = ("group", "member")

logit_scale = 32.0
cos_margin = 0.35
norm_epsilon = 1e-06

VMEM = pl.BlockSpec(memory_space=pltpu.VMEM)
SMEM = pl.BlockSpec(memory_space=pltpu.SMEM)


def inverse_norm(rows):
    return lax.rsqrt(jnp.sum(rows * rows, axis=-1, keepdims=True) + norm_epsilon)


def contract(left, right, left_dim, right_dim):
    dims = (((left_dim,), (right_dim,)), ((), ()))
    return lax.dot_general(left, right, dims, preferred_element_type=jnp.float32)


def lanes(rows):
    return lax.broadcasted_iota(jnp.int32, (rows, 128), 1)


def run(kernel, out_shape, in_specs, *operands):
    shapes = jax.tree.leaves(out_shape)
    return pl.pallas_call(
        kernel,
        out_shape=out_shape,
        in_specs=in_specs,
        out_specs=jax.tree.map(lambda _: VMEM, out_shape),
        compiler_params=pltpu.CompilerParams(vmem_limit_bytes=48 * 1024 * 1024),
        cost_estimate=pl.CostEstimate(
            flops=0,
            transcendentals=0,
            bytes_accessed=sum(a.size * a.dtype.itemsize for a in (*shapes, *operands)),
        ),
    )(*operands)


def pack_units(features, labels, copies_out):
    group, member = lax.axis_index("group"), lax.axis_index("member")
    copies, tok_dev, _ = copies_out.shape
    width = features.shape[1]
    rows = features[...].astype(jnp.float32)
    unit = (rows * inverse_norm(rows)).astype(jnp.bfloat16)
    copies_out[:, :, :width] = jnp.broadcast_to(unit[None], (copies, tok_dev, width))

    pairs = lax.axis_size("member") // 2
    place = (group * pairs + member // 2) * tok_dev
    row = jnp.concatenate([labels[...], jnp.zeros((1, 128 - labels.shape[1]), jnp.int32)], axis=1)
    row = jnp.broadcast_to(row, (tok_dev, 128))
    row = pltpu.roll(row, lax.rem(place - member * tok_dev + 128, 128), 1)
    digit = lax.broadcasted_iota(jnp.int32, (tok_dev, 128), 0)
    digits = (row >> (7 * jnp.minimum(digit, 3))) & 127
    lane = lanes(tok_dev)
    digits = jnp.where((lane >= place) & (lane < place + tok_dev), digits, 0)
    copies_out[:, :, width:] = jnp.broadcast_to(
        digits.astype(jnp.float32).astype(jnp.bfloat16)[None], (copies, tok_dev, 128)
    )


def prepare(ids, centres, cand_out, unit_out, inverse_out):
    for g in range(ids.shape[0]):
        here = pl.ds(g * BLK, BLK)
        rows = centres[ids[g, 0]].astype(jnp.float32)
        inverse = inverse_norm(rows)
        unit = rows * inverse
        cand_out[here, :] = unit.astype(jnp.bfloat16)
        unit_out[here, :] = unit
        inverse_out[here, :] = jnp.broadcast_to(inverse, (BLK, 128))


def forward(listed, packed, cands, expo_out, sums_out, shares_out):
    group, member = lax.axis_index("group"), lax.axis_index("member")
    groups = listed.shape[0]
    width = cands.shape[1]
    tok_dev = packed.shape[0] * groups // 128
    per_group = 128 // groups
    units = packed[:, :width]
    digits = jnp.sum(
        packed[:, width:].astype(jnp.float32).reshape(128 // 8, 8, 128), axis=0
    ).astype(jnp.int32)
    labels = digits[0:1] + (digits[1:2] << 7) + (digits[2:3] << 14)
    first = (member * groups + group) * BLK
    onehot = lax.broadcasted_iota(jnp.int32, (BLK, 128), 0) == labels - first

    all_cosines = contract(cands[...], units, 1, 1)
    owner = lanes(1) // per_group
    cosine = jnp.zeros((BLK, 128), jnp.float32)
    active = jnp.zeros((1, 128), jnp.float32)
    for g in range(groups):
        cosine = jnp.where(owner == g, all_cosines[g * BLK : (g + 1) * BLK], cosine)
        active = jnp.where(owner == g, listed[g, 0].astype(jnp.float32), active)
    expo = jnp.exp(logit_scale * (cosine - jnp.where(onehot, cos_margin, 0.0))) * active
    others = jnp.where(onehot, 0.0, expo)
    expo_out[...] = jnp.where(onehot, -1.0, expo)
    sums_out[0:1, :] = jnp.sum(others, axis=0, keepdims=True)
    sums_out[1:2, :] = jnp.sum(jnp.where(onehot, expo, 0.0), axis=0, keepdims=True)

    others = others.T.astype(jnp.bfloat16)
    label = jnp.where(onehot, 1.0, 0.0).T.astype(jnp.bfloat16)
    for g in range(groups):
        here = slice(g * per_group, (g + 1) * per_group)
        cand = cands[g * BLK : (g + 1) * BLK, :]
        both = contract(jnp.concatenate([others[here], label[here]], axis=0), cand, 1, 0)
        both = both.astype(jnp.bfloat16)
        shares_out[here, :width] = both[:per_group]
        shares_out[here, width:] = both[per_group:]


def forward_other(own_sums, *refs):
    *ins, expo_out, sums_out, shares_out = refs
    forward(*ins, expo_out, sums_out.at[2:4], shares_out)
    sums_out[0:2, :] = own_sums[...]


def merge(shares, sums, partner_shares, partner_sums, sent_out):
    wide = shares.shape[1]
    both = shares[...].astype(jnp.float32) + partner_shares[...].astype(jnp.float32)
    sent_out[:, :wide] = both.astype(jnp.bfloat16)
    total = sums[...] + jnp.concatenate([partner_sums[2:4, :], partner_sums[0:2, :]], axis=0)
    high = total.astype(jnp.bfloat16)
    low = (total - high.astype(jnp.float32)).astype(jnp.bfloat16)
    tile = jnp.concatenate([high.astype(jnp.float32), low.astype(jnp.float32)], axis=0)
    tile = jnp.broadcast_to(tile[None], (shares.shape[0] // 8, 8, 128))
    sent_out[:, wide:] = tile.reshape(shares.shape[0], 128).astype(jnp.bfloat16)


def backward(
    ids,
    received,
    own_expo,
    other_expo,
    own_packed,
    other_packed,
    features,
    cand_unit,
    cand_inverse,
    grad_out,
    feature_out,
    loss_out,
):
    group, member = lax.axis_index("group"), lax.axis_index("member")
    groups = ids.shape[0]
    per_group = 128 // groups
    tok_dev, width = features.shape
    sums = received[0].astype(jnp.float32)
    for i in range(1, received.shape[0]):
        sums = sums + received[i].astype(jnp.float32)
    tile = sums[:, 2 * width :]
    tile = tile[:4] + tile[4:]
    own_rest, own_label = tile[0:1], tile[1:2]
    other_rest, other_label = tile[2:3], tile[3:4]

    units = jnp.concatenate([own_packed[:, :width], other_packed[:, :width]], axis=0)
    own_scale = logit_scale / (own_rest + own_label)
    other_scale = logit_scale / (other_rest + other_label)
    own = own_expo[...]
    other = other_expo[...]
    own = jnp.where(own < 0.0, -own_rest, own) * own_scale
    other = jnp.where(other < 0.0, -other_rest, other) * other_scale
    weights = jnp.concatenate([own, other], axis=1)
    owner = jnp.concatenate([lanes(1), lanes(1)], axis=1) // per_group
    grad_out[...] = jnp.zeros_like(grad_out)
    for g in range(groups):
        here = slice(g * BLK, (g + 1) * BLK)
        mine = jnp.where(owner == g, weights, 0.0).astype(jnp.bfloat16)
        slot_grad = contract(mine, units, 1, 0)
        unit = cand_unit[here, :]
        along = jnp.sum(slot_grad * unit, axis=1, keepdims=True)
        cand_grad = cand_inverse[here, :1] * (slot_grad - along * unit)
        grad_out[ids[g, 0]] += cand_grad.astype(jnp.bfloat16).astype(jnp.float32)

    place = (group * (lax.axis_size("member") // 2) + member // 2) * tok_dev
    sample = lax.broadcasted_iota(jnp.int32, (tok_dev, 128), 0) + place
    mine = lanes(tok_dev) == sample
    rest = jnp.sum(jnp.where(mine, own_rest, 0.0), axis=1, keepdims=True)
    label = jnp.sum(jnp.where(mine, own_label, 0.0), axis=1, keepdims=True)
    total = rest + label
    loss = jnp.log(total) - jnp.log(label)
    square = (tok_dev, tok_dev)
    diagonal = lax.broadcasted_iota(jnp.int32, square, 0) == lax.broadcasted_iota(
        jnp.int32, square, 1
    )
    loss_out[...] = jnp.sum(jnp.where(diagonal, loss, 0.0), axis=0, keepdims=True)
    rows = features[...].astype(jnp.float32)
    inv_norm = inverse_norm(rows)
    unit = rows * inv_norm
    unit_grad = logit_scale / total * (sums[:, :width] - rest * sums[:, width : 2 * width])
    along = jnp.sum(unit_grad * unit, axis=1, keepdims=True)
    feature_out[...] = inv_norm * (unit_grad - along * unit)


def exchange(pieces, axes, cores=1):
    groups = None
    if cores > 1:
        size = lax.axis_size(axes)
        groups = [list(range(core, size, cores)) for core in range(cores)]
    return lax.all_to_all(
        pieces, axes, split_axis=0, concat_axis=0, axis_index_groups=groups, tiled=True
    )


def with_partner(value):
    return lax.ppermute(value, "member", [(i, i ^ 1) for i in range(lax.axis_size("member"))])


def on_device(features, labels, centres, block_ids, listed):
    groups = lax.axis_size("group")
    chips = groups * lax.axis_size("member") // 2
    tok_dev, width = features.shape
    held = centres.shape[0] // BLK
    half = chips * tok_dev
    bf16, f32 = jnp.bfloat16, jnp.float32
    shape = jax.ShapeDtypeStruct

    copies = run(
        pack_units,
        shape((chips, tok_dev, width + 128), bf16),
        [VMEM, VMEM],
        features,
        labels.reshape(1, -1),
    )
    own_packed = exchange(copies, AXES, 2).reshape(half, width + 128)
    other_packed = with_partner(own_packed)
    cands, cand_unit, cand_inverse = run(
        prepare,
        (
            shape((groups * BLK, width), bf16),
            shape((groups * BLK, width), f32),
            shape((groups * BLK, 128), f32),
        ),
        [SMEM, VMEM],
        block_ids,
        centres.reshape(held, BLK, width),
    )
    own_expo, own_sums, shares = run(
        forward,
        (shape((BLK, half), f32), shape((2, half), f32), shape((half, 2 * width), bf16)),
        [SMEM, VMEM, VMEM],
        listed,
        own_packed,
        cands,
    )
    other_expo, sums, other_shares = run(
        forward_other,
        (shape((BLK, half), f32), shape((4, half), f32), shape((half, 2 * width), bf16)),
        [VMEM, SMEM, VMEM, VMEM],
        own_sums,
        listed,
        other_packed,
        cands,
    )
    sent = run(
        merge,
        shape((half, 2 * width + 128), bf16),
        [VMEM] * 4,
        shares,
        sums,
        with_partner(other_shares),
        with_partner(sums),
    )
    received = exchange(sent.reshape(chips, tok_dev, 2 * width + 128), AXES, 2)
    centre_grad, feature_grad, loss = run(
        backward,
        (shape((held, BLK, width), f32), shape((tok_dev, width), f32), shape((1, tok_dev), f32)),
        [SMEM] + [VMEM] * 8,
        block_ids,
        received,
        own_expo,
        other_expo,
        own_packed,
        other_packed,
        features,
        cand_unit,
        cand_inverse,
    )
    return (loss.reshape(tok_dev), feature_grad, centre_grad.reshape(held * BLK, width))


def on_device_of_many(features, labels, centres, block_ids, listed):
    groups = lax.axis_size("group")
    members = lax.axis_size("member")
    devices = groups * members
    group = lax.axis_index("group")
    member = lax.axis_index("member")
    tok_dev, width = features.shape
    group_tok = members * tok_dev
    held = centres.shape[0] // BLK

    vectors = features.astype(jnp.float32)
    inv_norm = inverse_norm(vectors)
    unit_rows = vectors * inv_norm
    copies = jnp.broadcast_to(unit_rows.astype(jnp.bfloat16), (devices, tok_dev, width))
    units = exchange(copies, AXES).reshape(groups, group_tok, width)
    all_labels = exchange(jnp.broadcast_to(labels[None], (groups, group_tok)), "group")

    picked = centres.reshape(held, BLK, width)[block_ids[:, 0]].astype(jnp.float32)
    inv_cand = inverse_norm(picked)
    unit_cand = picked * inv_cand
    cand_half = unit_cand.astype(jnp.bfloat16)
    cosine = jnp.einsum("gsd,gcd->gsc", units, cand_half, preferred_element_type=jnp.float32)
    local_label = all_labels - (member * groups + group) * BLK
    onehot = (lax.broadcasted_iota(jnp.int32, (1, 1, BLK), 2) == local_label[:, :, None]).astype(
        jnp.float32
    )
    logits = logit_scale * (cosine - cos_margin * onehot)
    exp_logits = jnp.exp(logits) * listed.astype(jnp.float32)[:, :, None]
    totals, label_logit = lax.psum(
        (jnp.sum(exp_logits, axis=2), jnp.sum(logits * onehot, axis=2)), AXES
    )
    loss_all = (jnp.log(totals) - label_logit).reshape(devices, tok_dev)
    sample_loss = lax.dynamic_slice_in_dim(loss_all, group * members + member, 1, 0)[0]

    weights = (logit_scale * (exp_logits / totals[:, :, None] - onehot)).astype(jnp.bfloat16)
    partial = jnp.einsum("gsc,gcd->gsd", weights, cand_half, preferred_element_type=jnp.float32)
    home = exchange(partial.astype(jnp.bfloat16).reshape(devices, tok_dev, width), AXES)
    unit_grad = jnp.sum(home.astype(jnp.float32), axis=0)
    feature_grad = inv_norm * (
        unit_grad - jnp.sum(unit_grad * unit_rows, axis=1, keepdims=True) * unit_rows
    )
    slot_grad = jnp.einsum("gsc,gsd->gcd", weights, units, preferred_element_type=jnp.float32)
    cand_grad = inv_cand * (
        slot_grad - jnp.sum(slot_grad * unit_cand, axis=2, keepdims=True) * unit_cand
    )
    cand_grad = cand_grad.astype(jnp.bfloat16).astype(jnp.float32)
    names = block_ids == jnp.arange(held, dtype=jnp.int32)[None, :]
    centre_grad = jnp.sum(
        jnp.where(names[:, :, None, None], cand_grad[:, None], 0.0), axis=0
    ).reshape(held * BLK, width)
    return (sample_loss, feature_grad, centre_grad)


def solution(mesh):
    in_specs = (
        P(AXES, None),
        P("group"),
        P(AXES, None),
        P(None, AXES),
        P(None, AXES),
    )
    out_specs = (P(AXES), P(AXES, None), P(AXES, None))

    def body(features, *others):
        half = mesh.size // 2 * features.shape[0]
        fits = half == 128 and 2 * mesh.shape["group"] == features.shape[0] == 8
        return (on_device if fits else on_device_of_many)(features, *others)

    return jax.shard_map(
        body, mesh=mesh, in_specs=in_specs, out_specs=out_specs, check_vma=False
    )
```

```python
import jax
import jax.numpy as jnp
from jax import lax
from jax.experimental import pallas as pl
from jax.experimental.pallas import tpu as pltpu
from jax.sharding import PartitionSpec as P

BLK = 128
AXES = ("group", "member")
CHIPS = ("group", "chip")

logit_scale = 32.0
cos_margin = 0.35
norm_epsilon = 1e-06

VMEM = pl.BlockSpec(memory_space=pltpu.VMEM)
SMEM = pl.BlockSpec(memory_space=pltpu.SMEM)


def inverse_norm(rows):
    return lax.rsqrt(jnp.sum(rows * rows, axis=-1, keepdims=True) + norm_epsilon)


def contract(left, right, left_dim, right_dim):
    dims = (((left_dim,), (right_dim,)), ((), ()))
    return lax.dot_general(left, right, dims, preferred_element_type=jnp.float32)


def lanes(rows):
    return lax.broadcasted_iota(jnp.int32, (rows, 128), 1)


def run(kernel, out_shape, in_specs, *operands):
    shapes = jax.tree.leaves(out_shape)
    return pl.pallas_call(
        kernel,
        out_shape=out_shape,
        in_specs=in_specs,
        out_specs=jax.tree.map(lambda _: VMEM, out_shape),
        compiler_params=pltpu.CompilerParams(vmem_limit_bytes=48 * 1024 * 1024),
        cost_estimate=pl.CostEstimate(
            flops=0,
            transcendentals=0,
            bytes_accessed=sum(a.size * a.dtype.itemsize for a in (*shapes, *operands)),
        ),
    )(*operands)


def pack_units(features, labels, copies_out):
    chip = lax.axis_index("chip")
    member = 2 * chip + lax.axis_index("core")
    copies, tok_dev, _ = copies_out.shape
    width = features.shape[1]
    rows = features[...].astype(jnp.float32)
    unit = (rows * inverse_norm(rows)).astype(jnp.bfloat16)
    copies_out[:, :, :width] = jnp.broadcast_to(unit[None], (copies, tok_dev, width))

    place = (lax.axis_index("group") * lax.axis_size("chip") + chip) * tok_dev
    row = jnp.concatenate([labels[...], jnp.zeros((1, 128 - labels.shape[1]), jnp.int32)], axis=1)
    row = jnp.broadcast_to(row, (tok_dev, 128))
    row = pltpu.roll(row, lax.rem(place - member * tok_dev + 128, 128), 1)
    digit = lax.broadcasted_iota(jnp.int32, (tok_dev, 128), 0)
    digits = (row >> (7 * jnp.minimum(digit, 3))) & 127
    lane = lanes(tok_dev)
    digits = jnp.where((lane >= place) & (lane < place + tok_dev), digits, 0)
    copies_out[:, :, width:] = jnp.broadcast_to(
        digits.astype(jnp.float32).astype(jnp.bfloat16)[None], (copies, tok_dev, 128)
    )


def prepare(ids, centres, cand_out, unit_out, inverse_out):
    for g in range(ids.shape[0]):
        here = pl.ds(g * BLK, BLK)
        rows = centres[ids[g, 0]].astype(jnp.float32)
        inverse = inverse_norm(rows)
        unit = rows * inverse
        cand_out[here, :] = unit.astype(jnp.bfloat16)
        unit_out[here, :] = unit
        inverse_out[here, :] = jnp.broadcast_to(inverse, (BLK, 128))


def forward(listed, packed, cands, expo_out, sums_out, shares_out):
    group = lax.axis_index("group")
    member = 2 * lax.axis_index("chip") + lax.axis_index("core")
    groups = listed.shape[0]
    width = cands.shape[1]
    tok_dev = packed.shape[0] * groups // 128
    per_group = 128 // groups
    units = packed[:, :width]
    digits = jnp.sum(
        packed[:, width:].astype(jnp.float32).reshape(128 // 8, 8, 128), axis=0
    ).astype(jnp.int32)
    labels = digits[0:1] + (digits[1:2] << 7) + (digits[2:3] << 14)
    first = (member * groups + group) * BLK
    onehot = lax.broadcasted_iota(jnp.int32, (BLK, 128), 0) == labels - first

    all_cosines = contract(cands[...], units, 1, 1)
    owner = lanes(1) // per_group
    cosine = jnp.zeros((BLK, 128), jnp.float32)
    active = jnp.zeros((1, 128), jnp.float32)
    for g in range(groups):
        cosine = jnp.where(owner == g, all_cosines[g * BLK : (g + 1) * BLK], cosine)
        active = jnp.where(owner == g, listed[g, 0].astype(jnp.float32), active)
    expo = jnp.exp(logit_scale * (cosine - jnp.where(onehot, cos_margin, 0.0))) * active
    others = jnp.where(onehot, 0.0, expo)
    expo_out[...] = jnp.where(onehot, -1.0, expo)
    sums_out[0:1, :] = jnp.sum(others, axis=0, keepdims=True)
    sums_out[1:2, :] = jnp.sum(jnp.where(onehot, expo, 0.0), axis=0, keepdims=True)

    others = others.T.astype(jnp.bfloat16)
    label = jnp.where(onehot, 1.0, 0.0).T.astype(jnp.bfloat16)
    for g in range(groups):
        here = slice(g * per_group, (g + 1) * per_group)
        cand = cands[g * BLK : (g + 1) * BLK, :]
        both = contract(jnp.concatenate([others[here], label[here]], axis=0), cand, 1, 0)
        both = both.astype(jnp.bfloat16)
        shares_out[here, :width] = both[:per_group]
        shares_out[here, width:] = both[per_group:]


def forward_other(own_sums, *refs):
    *ins, expo_out, sums_out, shares_out = refs
    forward(*ins, expo_out, sums_out.at[2:4], shares_out)
    sums_out[0:2, :] = own_sums[...]


def merge(shares, sums, partner_shares, partner_sums, sent_out):
    wide = shares.shape[1]
    both = shares[...].astype(jnp.float32) + partner_shares[...].astype(jnp.float32)
    sent_out[:, :wide] = both.astype(jnp.bfloat16)
    total = sums[...] + jnp.concatenate([partner_sums[2:4, :], partner_sums[0:2, :]], axis=0)
    high = total.astype(jnp.bfloat16)
    low = (total - high.astype(jnp.float32)).astype(jnp.bfloat16)
    tile = jnp.concatenate([high.astype(jnp.float32), low.astype(jnp.float32)], axis=0)
    tile = jnp.broadcast_to(tile[None], (shares.shape[0] // 8, 8, 128))
    sent_out[:, wide:] = tile.reshape(shares.shape[0], 128).astype(jnp.bfloat16)


def backward(
    ids,
    received,
    own_expo,
    other_expo,
    own_packed,
    other_packed,
    features,
    cand_unit,
    cand_inverse,
    grad_out,
    feature_out,
    loss_out,
):
    groups = ids.shape[0]
    per_group = 128 // groups
    tok_dev, width = features.shape
    sums = received[0].astype(jnp.float32)
    for i in range(1, received.shape[0]):
        sums = sums + received[i].astype(jnp.float32)
    tile = sums[:, 2 * width :]
    tile = tile[:4] + tile[4:]
    own_rest, own_label = tile[0:1], tile[1:2]
    other_rest, other_label = tile[2:3], tile[3:4]

    units = jnp.concatenate([own_packed[:, :width], other_packed[:, :width]], axis=0)
    own_scale = logit_scale / (own_rest + own_label)
    other_scale = logit_scale / (other_rest + other_label)
    own = own_expo[...]
    other = other_expo[...]
    own = jnp.where(own < 0.0, -own_rest, own) * own_scale
    other = jnp.where(other < 0.0, -other_rest, other) * other_scale
    weights = jnp.concatenate([own, other], axis=1)
    owner = jnp.concatenate([lanes(1), lanes(1)], axis=1) // per_group
    grad_out[...] = jnp.zeros_like(grad_out)
    for g in range(groups):
        here = slice(g * BLK, (g + 1) * BLK)
        mine = jnp.where(owner == g, weights, 0.0).astype(jnp.bfloat16)
        slot_grad = contract(mine, units, 1, 0)
        unit = cand_unit[here, :]
        along = jnp.sum(slot_grad * unit, axis=1, keepdims=True)
        cand_grad = cand_inverse[here, :1] * (slot_grad - along * unit)
        grad_out[ids[g, 0]] += cand_grad.astype(jnp.bfloat16).astype(jnp.float32)

    chip = lax.axis_index("group") * lax.axis_size("chip") + lax.axis_index("chip")
    place = chip * tok_dev
    sample = lax.broadcasted_iota(jnp.int32, (tok_dev, 128), 0) + place
    mine = lanes(tok_dev) == sample
    rest = jnp.sum(jnp.where(mine, own_rest, 0.0), axis=1, keepdims=True)
    label = jnp.sum(jnp.where(mine, own_label, 0.0), axis=1, keepdims=True)
    total = rest + label
    loss = jnp.log(total) - jnp.log(label)
    square = (tok_dev, tok_dev)
    diagonal = lax.broadcasted_iota(jnp.int32, square, 0) == lax.broadcasted_iota(
        jnp.int32, square, 1
    )
    loss_out[...] = jnp.sum(jnp.where(diagonal, loss, 0.0), axis=0, keepdims=True)
    rows = features[...].astype(jnp.float32)
    inv_norm = inverse_norm(rows)
    unit = rows * inv_norm
    unit_grad = logit_scale / total * (sums[:, :width] - rest * sums[:, width : 2 * width])
    along = jnp.sum(unit_grad * unit, axis=1, keepdims=True)
    feature_out[...] = inv_norm * (unit_grad - along * unit)


def exchange(pieces, axes):
    return lax.all_to_all(pieces, axes, split_axis=0, concat_axis=0, tiled=True)


def with_partner(value):
    return lax.ppermute(value, "core", [(0, 1), (1, 0)])


def on_device(features, labels, centres, block_ids, listed):
    groups = lax.axis_size("group")
    chips = groups * lax.axis_size("chip")
    tok_dev, width = features.shape
    held = centres.shape[0] // BLK
    half = chips * tok_dev
    bf16, f32 = jnp.bfloat16, jnp.float32
    shape = jax.ShapeDtypeStruct

    copies = run(
        pack_units,
        shape((chips, tok_dev, width + 128), bf16),
        [VMEM, VMEM],
        features,
        labels.reshape(1, -1),
    )
    own_packed = exchange(copies, CHIPS).reshape(half, width + 128)
    other_packed = with_partner(own_packed)
    cands, cand_unit, cand_inverse = run(
        prepare,
        (
            shape((groups * BLK, width), bf16),
            shape((groups * BLK, width), f32),
            shape((groups * BLK, 128), f32),
        ),
        [SMEM, VMEM],
        block_ids,
        centres.reshape(held, BLK, width),
    )
    own_expo, own_sums, shares = run(
        forward,
        (shape((BLK, half), f32), shape((2, half), f32), shape((half, 2 * width), bf16)),
        [SMEM, VMEM, VMEM],
        listed,
        own_packed,
        cands,
    )
    other_expo, sums, other_shares = run(
        forward_other,
        (shape((BLK, half), f32), shape((4, half), f32), shape((half, 2 * width), bf16)),
        [VMEM, SMEM, VMEM, VMEM],
        own_sums,
        listed,
        other_packed,
        cands,
    )
    sent = run(
        merge,
        shape((half, 2 * width + 128), bf16),
        [VMEM] * 4,
        shares,
        sums,
        with_partner(other_shares),
        with_partner(sums),
    )
    received = exchange(sent.reshape(chips, tok_dev, 2 * width + 128), CHIPS)
    centre_grad, feature_grad, loss = run(
        backward,
        (shape((held, BLK, width), f32), shape((tok_dev, width), f32), shape((1, tok_dev), f32)),
        [SMEM] + [VMEM] * 8,
        block_ids,
        received,
        own_expo,
        other_expo,
        own_packed,
        other_packed,
        features,
        cand_unit,
        cand_inverse,
    )
    return (loss.reshape(tok_dev), feature_grad, centre_grad.reshape(held * BLK, width))


def on_device_of_many(features, labels, centres, block_ids, listed):
    groups = lax.axis_size("group")
    members = lax.axis_size("member")
    devices = groups * members
    group = lax.axis_index("group")
    member = lax.axis_index("member")
    tok_dev, width = features.shape
    group_tok = members * tok_dev
    held = centres.shape[0] // BLK

    vectors = features.astype(jnp.float32)
    inv_norm = inverse_norm(vectors)
    unit_rows = vectors * inv_norm
    copies = jnp.broadcast_to(unit_rows.astype(jnp.bfloat16), (devices, tok_dev, width))
    units = exchange(copies, AXES).reshape(groups, group_tok, width)
    all_labels = exchange(jnp.broadcast_to(labels[None], (groups, group_tok)), "group")

    picked = centres.reshape(held, BLK, width)[block_ids[:, 0]].astype(jnp.float32)
    inv_cand = inverse_norm(picked)
    unit_cand = picked * inv_cand
    cand_half = unit_cand.astype(jnp.bfloat16)
    cosine = jnp.einsum("gsd,gcd->gsc", units, cand_half, preferred_element_type=jnp.float32)
    local_label = all_labels - (member * groups + group) * BLK
    onehot = (lax.broadcasted_iota(jnp.int32, (1, 1, BLK), 2) == local_label[:, :, None]).astype(
        jnp.float32
    )
    logits = logit_scale * (cosine - cos_margin * onehot)
    exp_logits = jnp.exp(logits) * listed.astype(jnp.float32)[:, :, None]
    totals, label_logit = lax.psum(
        (jnp.sum(exp_logits, axis=2), jnp.sum(logits * onehot, axis=2)), AXES
    )
    loss_all = (jnp.log(totals) - label_logit).reshape(devices, tok_dev)
    sample_loss = lax.dynamic_slice_in_dim(loss_all, group * members + member, 1, 0)[0]

    weights = (logit_scale * (exp_logits / totals[:, :, None] - onehot)).astype(jnp.bfloat16)
    partial = jnp.einsum("gsc,gcd->gsd", weights, cand_half, preferred_element_type=jnp.float32)
    home = exchange(partial.astype(jnp.bfloat16).reshape(devices, tok_dev, width), AXES)
    unit_grad = jnp.sum(home.astype(jnp.float32), axis=0)
    feature_grad = inv_norm * (
        unit_grad - jnp.sum(unit_grad * unit_rows, axis=1, keepdims=True) * unit_rows
    )
    slot_grad = jnp.einsum("gsc,gsd->gcd", weights, units, preferred_element_type=jnp.float32)
    cand_grad = inv_cand * (
        slot_grad - jnp.sum(slot_grad * unit_cand, axis=2, keepdims=True) * unit_cand
    )
    cand_grad = cand_grad.astype(jnp.bfloat16).astype(jnp.float32)
    names = block_ids == jnp.arange(held, dtype=jnp.int32)[None, :]
    centre_grad = jnp.sum(
        jnp.where(names[:, :, None, None], cand_grad[:, None], 0.0), axis=0
    ).reshape(held * BLK, width)
    return (sample_loss, feature_grad, centre_grad)


def on_axes(body, mesh, axes):
    split = P(axes)
    return jax.shard_map(
        body,
        mesh=mesh,
        in_specs=(split, P("group"), split, P(None, axes), P(None, axes)),
        out_specs=(split, split, split),
        check_vma=False,
    )


def solution(mesh):
    groups, members = mesh.shape["group"], mesh.shape["member"]
    by_core = jax.sharding.Mesh(
        mesh.devices.reshape(groups, members // 2, 2), ("group", "chip", "core")
    )

    def program(features, *others):
        half = features.shape[0] // 2
        if half == 128 and 2 * groups == features.shape[0] // mesh.size == 8:
            return on_axes(on_device, by_core, (*CHIPS, "core"))(features, *others)
        return on_axes(on_device_of_many, mesh, AXES)(features, *others)

    return program
```

```python
import jax
import jax.numpy as jnp
from jax import lax
from jax.experimental import pallas as pl
from jax.experimental.pallas import tpu as pltpu
from jax.sharding import PartitionSpec as P

BLK = 128
AXES = ("group", "member")
CHIPS = ("group", "chip")

logit_scale = 32.0
cos_margin = 0.35
norm_epsilon = 1e-06

VMEM = pl.BlockSpec(memory_space=pltpu.VMEM)
SMEM = pl.BlockSpec(memory_space=pltpu.SMEM)
HBM = pl.BlockSpec(memory_space=pltpu.HBM)


def inverse_norm(rows):
    return lax.rsqrt(jnp.sum(rows * rows, axis=-1, keepdims=True) + norm_epsilon)


def contract(left, right, left_dim, right_dim):
    dims = (((left_dim,), (right_dim,)), ((), ()))
    return lax.dot_general(left, right, dims, preferred_element_type=jnp.float32)


def lanes(rows):
    return lax.broadcasted_iota(jnp.int32, (rows, 128), 1)


def run(kernel, out_shape, in_specs, *operands, out_spec=VMEM, scratch=()):
    shapes = jax.tree.leaves(out_shape)
    return pl.pallas_call(
        kernel,
        out_shape=out_shape,
        in_specs=in_specs,
        out_specs=jax.tree.map(lambda _: out_spec, out_shape),
        scratch_shapes=scratch,
        compiler_params=pltpu.CompilerParams(vmem_limit_bytes=48 * 1024 * 1024),
        cost_estimate=pl.CostEstimate(
            flops=0,
            transcendentals=0,
            bytes_accessed=sum(a.size * a.dtype.itemsize for a in (*shapes, *operands)),
        ),
    )(*operands)


def load(
    features,
    labels,
    centres,
    ids,
    listed,
    copies_out,
    centres_out,
    ids_out,
    listed_out,
    held_features,
    held_labels,
    arrived,
):
    moves = [
        pltpu.make_async_copy(source, target, arrived.at[i])
        for i, (source, target) in enumerate(
            (
                (features, held_features),
                (labels, held_labels),
                (centres, centres_out),
                (ids, ids_out),
                (listed, listed_out),
            )
        )
    ]
    for move in moves:
        move.start()
    moves[0].wait()
    moves[1].wait()
    chip = lax.axis_index("chip")
    member = 2 * chip + lax.axis_index("core")
    copies, tok_dev, _ = copies_out.shape
    width = features.shape[1]
    rows = held_features[...].astype(jnp.float32)
    unit = (rows * inverse_norm(rows)).astype(jnp.bfloat16)
    copies_out[:, :, :width] = jnp.broadcast_to(unit[None], (copies, tok_dev, width))

    place = (lax.axis_index("group") * lax.axis_size("chip") + chip) * tok_dev
    row = held_labels[...]
    row = jnp.concatenate([row, jnp.zeros((1, 128 - row.shape[1]), jnp.int32)], axis=1)
    row = jnp.broadcast_to(row, (tok_dev, 128))
    row = pltpu.roll(row, lax.rem(place - member * tok_dev + 128, 128), 1)
    digit = lax.broadcasted_iota(jnp.int32, (tok_dev, 128), 0)
    digits = (row >> (7 * jnp.minimum(digit, 3))) & 127
    lane = lanes(tok_dev)
    digits = jnp.where((lane >= place) & (lane < place + tok_dev), digits, 0)
    copies_out[:, :, width:] = jnp.broadcast_to(
        digits.astype(jnp.float32).astype(jnp.bfloat16)[None], (copies, tok_dev, 128)
    )
    for move in moves[2:]:
        move.wait()


def select(parts, rows):
    owner = lanes(1) // (128 // len(parts))
    out = jnp.broadcast_to(parts[0], (rows, 128))
    for g in range(1, len(parts)):
        out = jnp.where(owner == g, parts[g], out)
    return out


def forward(ids, listed, packed, centres, inverse, expo_out, sums_out, shares_out):
    group = lax.axis_index("group")
    member = 2 * lax.axis_index("chip") + lax.axis_index("core")
    groups = ids.shape[1]
    width = centres.shape[2]
    per_group = 128 // groups
    units = packed[:, :width]
    digits = jnp.sum(
        packed[:, width:].astype(jnp.float32).reshape(128 // 8, 8, 128), axis=0
    ).astype(jnp.int32)
    labels = digits[0:1] + (digits[1:2] << 7) + (digits[2:3] << 14)
    first = (member * groups + group) * BLK
    onehot = lax.broadcasted_iota(jnp.int32, (BLK, 128), 0) == labels - first

    blocks = [centres[ids[0, g]] for g in range(groups)]
    cosine = select([contract(block, units, 1, 1) for block in blocks], BLK) * inverse
    active = select([listed[0, g].astype(jnp.float32) for g in range(groups)], 1)
    expo = jnp.exp(logit_scale * (cosine - jnp.where(onehot, cos_margin, 0.0))) * active
    others = jnp.where(onehot, 0.0, expo)
    expo_out[...] = jnp.where(onehot, -1.0, expo)
    sums_out[0:1, :] = jnp.sum(others, axis=0, keepdims=True)
    sums_out[1:2, :] = jnp.sum(jnp.where(onehot, expo, 0.0), axis=0, keepdims=True)

    others = (others * inverse).T.astype(jnp.bfloat16)
    label = jnp.where(onehot, 1.0, 0.0).T.astype(jnp.bfloat16)
    for g in range(groups):
        here = slice(g * per_group, (g + 1) * per_group)
        both = contract(jnp.concatenate([others[here], label[here]], axis=0), blocks[g], 1, 0)
        both = both.astype(jnp.bfloat16)
        shares_out[here, :width] = both[:per_group]
        shares_out[here, width:] = both[per_group:]


def forward_own(ids, listed, packed, centres, inverse_out, *outs):
    inverse = []
    for g in range(ids.shape[1]):
        inverse.append(inverse_norm(centres[ids[0, g]].astype(jnp.float32)))
    inverse = select(inverse, BLK)
    inverse_out[...] = inverse
    forward(ids, listed, packed, centres, inverse, *outs)


def forward_other(ids, listed, packed, centres, inverse, own_sums, expo_out, sums_out, shares_out):
    forward(ids, listed, packed, centres, inverse[...], expo_out, sums_out.at[2:4], shares_out)
    sums_out[0:2, :] = own_sums[...]


def merge(shares, sums, partner_shares, partner_sums, sent_out):
    wide = shares.shape[1]
    both = shares[...].astype(jnp.float32) + partner_shares[...].astype(jnp.float32)
    sent_out[:, :wide] = both.astype(jnp.bfloat16)
    total = sums[...] + jnp.concatenate([partner_sums[2:4, :], partner_sums[0:2, :]], axis=0)
    high = total.astype(jnp.bfloat16)
    low = (total - high.astype(jnp.float32)).astype(jnp.bfloat16)
    tile = jnp.concatenate([high.astype(jnp.float32), low.astype(jnp.float32)], axis=0)
    tile = jnp.broadcast_to(tile[None], (shares.shape[0] // 8, 8, 128))
    sent_out[:, wide:] = tile.reshape(shares.shape[0], 128).astype(jnp.bfloat16)


def backward(
    ids,
    received,
    own_expo,
    other_expo,
    own_packed,
    other_packed,
    features,
    centres,
    inverse,
    grad_out,
    feature_out,
    loss_out,
    grad,
    feature_grad,
    loss_row,
    left,
):
    groups = ids.shape[1]
    held = centres.shape[0]
    per_group = 128 // groups
    tok_dev, width = features.shape

    def leave(block):
        return pltpu.make_async_copy(grad.at[block], grad_out.at[block], left.at[block])

    grad[...] = jnp.zeros_like(grad)
    for block in range(held):
        named = ids[0, 0] == block
        for g in range(1, groups):
            named = named | (ids[0, g] == block)
        pl.when(jnp.logical_not(named))(leave(block).start)

    sums = received[0].astype(jnp.float32)
    for i in range(1, received.shape[0]):
        sums = sums + received[i].astype(jnp.float32)
    tile = sums[:, 2 * width :]
    tile = tile[:4] + tile[4:]
    own_rest, own_label = tile[0:1], tile[1:2]
    other_rest, other_label = tile[2:3], tile[3:4]

    units = jnp.concatenate([own_packed[:, :width], other_packed[:, :width]], axis=0)
    own_scale = logit_scale / (own_rest + own_label)
    other_scale = logit_scale / (other_rest + other_label)
    own = own_expo[...]
    other = other_expo[...]
    own = jnp.where(own < 0.0, -own_rest, own) * own_scale
    other = jnp.where(other < 0.0, -other_rest, other) * other_scale
    weights = jnp.concatenate([own, other], axis=1)
    owner = jnp.concatenate([lanes(1), lanes(1)], axis=1) // per_group
    for g in range(groups):
        block = ids[0, g]
        mine = jnp.where(owner == g, weights, 0.0).astype(jnp.bfloat16)
        slot_grad = contract(mine, units, 1, 0)
        factor = inverse[:, g * per_group : g * per_group + 1]
        unit = centres[block].astype(jnp.float32) * factor
        along = jnp.sum(slot_grad * unit, axis=1, keepdims=True)
        cand_grad = factor * (slot_grad - along * unit)
        grad[block] += cand_grad.astype(jnp.bfloat16).astype(jnp.float32)
        last = jnp.bool_(True)
        for later in range(g + 1, groups):
            last = last & (ids[0, later] != block)
        pl.when(last)(leave(block).start)

    chip = lax.axis_index("group") * lax.axis_size("chip") + lax.axis_index("chip")
    sample = lax.broadcasted_iota(jnp.int32, (tok_dev, 128), 0) + chip * tok_dev
    mine = lanes(tok_dev) == sample
    rest = jnp.sum(jnp.where(mine, own_rest, 0.0), axis=1, keepdims=True)
    label = jnp.sum(jnp.where(mine, own_label, 0.0), axis=1, keepdims=True)
    total = rest + label
    loss = jnp.log(total) - jnp.log(label)
    square = (tok_dev, tok_dev)
    diagonal = lax.broadcasted_iota(jnp.int32, square, 0) == lax.broadcasted_iota(
        jnp.int32, square, 1
    )
    loss_row[...] = jnp.sum(jnp.where(diagonal, loss, 0.0), axis=0, keepdims=True)
    rows = features[...].astype(jnp.float32)
    inv_norm = inverse_norm(rows)
    unit = rows * inv_norm
    cand = sums[:, width : 2 * width]
    cand = (cand * inverse_norm(cand)).astype(jnp.bfloat16).astype(jnp.float32)
    unit_grad = logit_scale / total * (sums[:, :width] - rest * cand)
    along = jnp.sum(unit_grad * unit, axis=1, keepdims=True)
    feature_grad[...] = inv_norm * (unit_grad - along * unit)
    ends = [
        pltpu.make_async_copy(feature_grad, feature_out, left.at[held]),
        pltpu.make_async_copy(loss_row, loss_out, left.at[held + 1]),
    ]
    for move in ends:
        move.start()
    for block in range(held):
        leave(block).wait()
    for move in ends:
        move.wait()


def exchange(pieces, axes):
    return lax.all_to_all(pieces, axes, split_axis=0, concat_axis=0, tiled=True)


def with_partner(value):
    return lax.ppermute(value, "core", [(0, 1), (1, 0)])


def on_device(features, labels, centres, block_ids, listed):
    groups = lax.axis_size("group")
    chips = groups * lax.axis_size("chip")
    tok_dev, width = features.shape
    held = centres.shape[0] // BLK
    half = chips * tok_dev
    bf16, f32 = jnp.bfloat16, jnp.float32
    shape = jax.ShapeDtypeStruct

    copies, blocks, ids, flags = run(
        load,
        (
            shape((chips, tok_dev, width + 128), bf16),
            shape((held, BLK, width), bf16),
            shape((1, groups), block_ids.dtype),
            shape((1, groups), listed.dtype),
        ),
        [HBM] * 5,
        *(
            pltpu.with_memory_space_constraint(array, pltpu.HBM)
            for array in (
                features,
                labels.reshape(1, -1),
                centres.reshape(held, BLK, width),
                block_ids.reshape(1, groups),
                listed.reshape(1, groups),
            )
        ),
        scratch=[
            pltpu.VMEM(features.shape, features.dtype),
            pltpu.VMEM((1, labels.shape[0]), labels.dtype),
            pltpu.SemaphoreType.DMA((5,)),
        ],
    )
    own_packed = exchange(copies, CHIPS).reshape(half, width + 128)
    other_packed = with_partner(own_packed)
    inverse, own_expo, own_sums, shares = run(
        forward_own,
        (
            shape((BLK, 128), f32),
            shape((BLK, half), f32),
            shape((2, half), f32),
            shape((half, 2 * width), bf16),
        ),
        [SMEM, SMEM, VMEM, VMEM],
        ids,
        flags,
        own_packed,
        blocks,
    )
    other_expo, sums, other_shares = run(
        forward_other,
        (shape((BLK, half), f32), shape((4, half), f32), shape((half, 2 * width), bf16)),
        [SMEM, SMEM, VMEM, VMEM, VMEM, VMEM],
        ids,
        flags,
        other_packed,
        blocks,
        inverse,
        own_sums,
    )
    sent = run(
        merge,
        shape((half, 2 * width + 128), bf16),
        [VMEM] * 4,
        shares,
        sums,
        with_partner(other_shares),
        with_partner(sums),
    )
    received = exchange(sent.reshape(chips, tok_dev, 2 * width + 128), CHIPS)
    outs = (shape((held, BLK, width), f32), shape((tok_dev, width), f32), shape((1, tok_dev), f32))
    centre_grad, feature_grad, loss = run(
        backward,
        outs,
        [SMEM] + [VMEM] * 8,
        ids,
        received,
        own_expo,
        other_expo,
        own_packed,
        other_packed,
        features,
        blocks,
        inverse,
        out_spec=HBM,
        scratch=[
            *(pltpu.VMEM(out.shape, out.dtype) for out in outs),
            pltpu.SemaphoreType.DMA((held + 2,)),
        ],
    )
    return (loss.reshape(tok_dev), feature_grad, centre_grad.reshape(held * BLK, width))


def on_device_of_many(features, labels, centres, block_ids, listed):
    groups = lax.axis_size("group")
    members = lax.axis_size("member")
    devices = groups * members
    group = lax.axis_index("group")
    member = lax.axis_index("member")
    tok_dev, width = features.shape
    group_tok = members * tok_dev
    held = centres.shape[0] // BLK

    vectors = features.astype(jnp.float32)
    inv_norm = inverse_norm(vectors)
    unit_rows = vectors * inv_norm
    copies = jnp.broadcast_to(unit_rows.astype(jnp.bfloat16), (devices, tok_dev, width))
    units = exchange(copies, AXES).reshape(groups, group_tok, width)
    all_labels = exchange(jnp.broadcast_to(labels[None], (groups, group_tok)), "group")

    picked = centres.reshape(held, BLK, width)[block_ids[:, 0]].astype(jnp.float32)
    inv_cand = inverse_norm(picked)
    unit_cand = picked * inv_cand
    cand_half = unit_cand.astype(jnp.bfloat16)
    cosine = jnp.einsum("gsd,gcd->gsc", units, cand_half, preferred_element_type=jnp.float32)
    local_label = all_labels - (member * groups + group) * BLK
    onehot = (lax.broadcasted_iota(jnp.int32, (1, 1, BLK), 2) == local_label[:, :, None]).astype(
        jnp.float32
    )
    logits = logit_scale * (cosine - cos_margin * onehot)
    exp_logits = jnp.exp(logits) * listed.astype(jnp.float32)[:, :, None]
    totals, label_logit = lax.psum(
        (jnp.sum(exp_logits, axis=2), jnp.sum(logits * onehot, axis=2)), AXES
    )
    loss_all = (jnp.log(totals) - label_logit).reshape(devices, tok_dev)
    sample_loss = lax.dynamic_slice_in_dim(loss_all, group * members + member, 1, 0)[0]

    weights = (logit_scale * (exp_logits / totals[:, :, None] - onehot)).astype(jnp.bfloat16)
    partial = jnp.einsum("gsc,gcd->gsd", weights, cand_half, preferred_element_type=jnp.float32)
    home = exchange(partial.astype(jnp.bfloat16).reshape(devices, tok_dev, width), AXES)
    unit_grad = jnp.sum(home.astype(jnp.float32), axis=0)
    feature_grad = inv_norm * (
        unit_grad - jnp.sum(unit_grad * unit_rows, axis=1, keepdims=True) * unit_rows
    )
    slot_grad = jnp.einsum("gsc,gsd->gcd", weights, units, preferred_element_type=jnp.float32)
    cand_grad = inv_cand * (
        slot_grad - jnp.sum(slot_grad * unit_cand, axis=2, keepdims=True) * unit_cand
    )
    cand_grad = cand_grad.astype(jnp.bfloat16).astype(jnp.float32)
    names = block_ids == jnp.arange(held, dtype=jnp.int32)[None, :]
    centre_grad = jnp.sum(
        jnp.where(names[:, :, None, None], cand_grad[:, None], 0.0), axis=0
    ).reshape(held * BLK, width)
    return (sample_loss, feature_grad, centre_grad)


def on_axes(body, mesh, axes):
    split = P(axes)
    return jax.shard_map(
        body,
        mesh=mesh,
        in_specs=(split, P("group"), split, P(None, axes), P(None, axes)),
        out_specs=(split, split, split),
        check_vma=False,
    )


def solution(mesh):
    groups, members = mesh.shape["group"], mesh.shape["member"]
    by_core = jax.sharding.Mesh(
        mesh.devices.reshape(groups, members // 2, 2), ("group", "chip", "core")
    )

    def program(features, *others):
        half = features.shape[0] // 2
        if half == 128 and 2 * groups == features.shape[0] // mesh.size == 8:
            return on_axes(on_device, by_core, (*CHIPS, "core"))(features, *others)
        return on_axes(on_device_of_many, mesh, AXES)(features, *others)

    return program
```

```python
import jax
import jax.numpy as jnp
from jax import lax
from jax.experimental import pallas as pl
from jax.experimental.pallas import tpu as pltpu
from jax.sharding import PartitionSpec as P

BLK = 128
AXES = ("group", "member")
CHIPS = ("group", "chip")

logit_scale = 32.0
cos_margin = 0.35
norm_epsilon = 1e-06
UNLISTED = 1e19

VMEM = pl.BlockSpec(memory_space=pltpu.VMEM)
SMEM = pl.BlockSpec(memory_space=pltpu.SMEM)
HBM = pl.BlockSpec(memory_space=pltpu.HBM)


def inverse_norm(rows):
    return lax.rsqrt(jnp.sum(rows * rows, axis=-1, keepdims=True) + norm_epsilon)


def contract(left, right, left_dim, right_dim):
    dims = (((left_dim,), (right_dim,)), ((), ()))
    return lax.dot_general(left, right, dims, preferred_element_type=jnp.float32)


def lanes(rows):
    return lax.broadcasted_iota(jnp.int32, (rows, 128), 1)


def run(kernel, out_shape, in_specs, *operands, out_spec=VMEM, scratch=()):
    shapes = jax.tree.leaves(out_shape)
    return pl.pallas_call(
        kernel,
        out_shape=out_shape,
        in_specs=in_specs,
        out_specs=jax.tree.map(lambda _: out_spec, out_shape),
        scratch_shapes=scratch,
        compiler_params=pltpu.CompilerParams(vmem_limit_bytes=48 * 1024 * 1024),
        cost_estimate=pl.CostEstimate(
            flops=0,
            transcendentals=0,
            bytes_accessed=sum(a.size * a.dtype.itemsize for a in (*shapes, *operands)),
        ),
    )(*operands)


def load(
    features,
    labels,
    centres,
    ids,
    listed,
    copies_out,
    blocks_out,
    ids_out,
    held_features,
    held_labels,
    held_centres,
    held_ids,
    held_listed,
    arrived,
):
    moves = [
        pltpu.make_async_copy(source, target, arrived.at[i])
        for i, (source, target) in enumerate(
            (
                (features, held_features),
                (labels, held_labels),
                (ids, held_ids),
                (listed, held_listed),
                (ids, ids_out),
                (centres, held_centres),
            )
        )
    ]
    for move in moves:
        move.start()
    moves[0].wait()
    moves[1].wait()
    chip = lax.axis_index("chip")
    member = 2 * chip + lax.axis_index("core")
    copies, tok_dev, _ = copies_out.shape
    width = features.shape[1]
    rows = held_features[...].astype(jnp.float32)
    unit = (rows * inverse_norm(rows)).astype(jnp.bfloat16)
    copies_out[:, :, :width] = jnp.broadcast_to(unit[None], (copies, tok_dev, width))

    place = (lax.axis_index("group") * lax.axis_size("chip") + chip) * tok_dev
    row = held_labels[...]
    row = jnp.concatenate([row, jnp.zeros((1, 128 - row.shape[1]), jnp.int32)], axis=1)
    row = jnp.broadcast_to(row, (tok_dev, 128))
    row = pltpu.roll(row, lax.rem(place - member * tok_dev + 128, 128), 1)
    digit = lax.broadcasted_iota(jnp.int32, (tok_dev, 128), 0)
    digits = (row >> (7 * jnp.minimum(digit, 3))) & 127
    lane = lanes(tok_dev)
    digits = jnp.where((lane >= place) & (lane < place + tok_dev), digits, 0)
    copies_out[:, :, width:] = jnp.broadcast_to(
        digits.astype(jnp.float32).astype(jnp.bfloat16)[None], (copies, tok_dev, 128)
    )
    for move in moves[2:]:
        move.wait()
    for g in range(blocks_out.shape[0]):
        block = held_centres[held_ids[0, g]]
        blocks_out[g] = jnp.where(held_listed[0, g] > 0, block, jnp.full_like(block, UNLISTED))


def select(parts, rows):
    owner = lanes(1) // (128 // len(parts))
    out = jnp.broadcast_to(parts[0], (rows, 128))
    for g in range(1, len(parts)):
        out = jnp.where(owner == g, parts[g], out)
    return out


def exponentials(packed, own_blocks, pair_blocks, expo_out, pair_expo_out, inverse_out, sums_out):
    group, core = lax.axis_index("group"), lax.axis_index("core")
    groups, _, width = own_blocks.shape
    units = packed[:, :width]
    digits = jnp.sum(
        packed[:, width:].astype(jnp.float32).reshape(128 // 8, 8, 128), axis=0
    ).astype(jnp.int32)
    labels = digits[0:1] + (digits[1:2] << 7) + (digits[2:3] << 14)
    rest = jnp.zeros((1, 128), jnp.float32)
    at_label = jnp.zeros((1, 128), jnp.float32)
    for k, (blocks, out) in enumerate(((own_blocks, expo_out), (pair_blocks, pair_expo_out))):
        member = 2 * lax.axis_index("chip") + (core if k == 0 else 1 - core)
        first = (member * groups + group) * BLK
        onehot = lax.broadcasted_iota(jnp.int32, (BLK, 128), 0) == labels - first
        inverse = select(
            [inverse_norm(blocks[g].astype(jnp.float32)) for g in range(groups)], BLK
        )
        inverse_out[k] = inverse
        cosine = inverse * select([contract(blocks[g], units, 1, 1) for g in range(groups)], BLK)
        expo = jnp.exp(logit_scale * (cosine - jnp.where(onehot, cos_margin, 0.0)))
        expo = jnp.where(inverse > 0.0, expo, 0.0)
        out[...] = jnp.where(onehot, -1.0, expo)
        rest += jnp.sum(jnp.where(onehot, 0.0, expo), axis=0, keepdims=True)
        at_label += jnp.sum(jnp.where(onehot, expo, 0.0), axis=0, keepdims=True)
    sums_out[0:1, :] = rest
    sums_out[1:2, :] = at_label


def shares(own_expo, pair_expo, inverse, own_blocks, pair_blocks, shares_out):
    groups, _, width = own_blocks.shape
    per_group = 128 // groups
    others, label = [], []
    for k, expo in enumerate((own_expo[...], pair_expo[...])):
        others.append((jnp.maximum(expo, 0.0) * inverse[k]).T.astype(jnp.bfloat16))
        label.append(jnp.where(expo < 0.0, 1.0, 0.0).T.astype(jnp.bfloat16))
    others = jnp.concatenate(others, axis=1)
    label = jnp.concatenate(label, axis=1)
    for g in range(groups):
        here = slice(g * per_group, (g + 1) * per_group)
        blocks = jnp.concatenate([own_blocks[g], pair_blocks[g]], axis=0)
        both = contract(jnp.concatenate([others[here], label[here]], axis=0), blocks, 1, 0)
        both = both.astype(jnp.bfloat16)
        shares_out[here, :width] = both[:per_group]
        shares_out[here, width:] = both[per_group:]


def with_sums(shares, own_sums, other_sums, sent_out):
    rows, wide = shares.shape
    sent_out[:, :wide] = shares[...]
    total = jnp.concatenate([own_sums[...], other_sums[...]], axis=0)
    high = total.astype(jnp.bfloat16)
    low = (total - high.astype(jnp.float32)).astype(jnp.bfloat16)
    tile = jnp.concatenate([high.astype(jnp.float32), low.astype(jnp.float32)], axis=0)
    tile = jnp.broadcast_to(tile[None], (rows // 8, 8, 128))
    sent_out[:, wide:] = tile.reshape(rows, 128).astype(jnp.bfloat16)


def backward(
    ids,
    received,
    own_expo,
    other_expo,
    own_packed,
    other_packed,
    features,
    blocks,
    inverse,
    grad_out,
    feature_out,
    loss_out,
    grad,
    feature_grad,
    loss_row,
    left,
):
    groups = ids.shape[1]
    held = grad.shape[0]
    per_group = 128 // groups
    tok_dev, width = features.shape

    def leave(block):
        return pltpu.make_async_copy(grad.at[block], grad_out.at[block], left.at[block])

    grad[...] = jnp.zeros_like(grad)
    for block in range(held):
        named = ids[0, 0] == block
        for g in range(1, groups):
            named = named | (ids[0, g] == block)
        pl.when(jnp.logical_not(named))(leave(block).start)

    sums = received[0].astype(jnp.float32)
    for i in range(1, received.shape[0]):
        sums = sums + received[i].astype(jnp.float32)
    tile = sums[:, 2 * width :]
    tile = tile[:4] + tile[4:]
    own_rest, own_label = tile[0:1], tile[1:2]
    other_rest, other_label = tile[2:3], tile[3:4]

    units = jnp.concatenate([own_packed[:, :width], other_packed[:, :width]], axis=0)
    own_scale = logit_scale / (own_rest + own_label)
    other_scale = logit_scale / (other_rest + other_label)
    own = own_expo[...]
    other = other_expo[...]
    own = jnp.where(own < 0.0, -own_rest, own) * own_scale
    other = jnp.where(other < 0.0, -other_rest, other) * other_scale
    weights = jnp.concatenate([own, other], axis=1)
    owner = jnp.concatenate([lanes(1), lanes(1)], axis=1) // per_group
    for g in range(groups):
        block = ids[0, g]
        mine = jnp.where(owner == g, weights, 0.0).astype(jnp.bfloat16)
        slot_grad = contract(mine, units, 1, 0)
        factor = inverse[0, :, g * per_group : g * per_group + 1]
        unit = blocks[g].astype(jnp.float32) * factor
        along = jnp.sum(slot_grad * unit, axis=1, keepdims=True)
        cand_grad = factor * (slot_grad - along * unit)
        grad[block] += cand_grad.astype(jnp.bfloat16).astype(jnp.float32)
        last = jnp.bool_(True)
        for later in range(g + 1, groups):
            last = last & (ids[0, later] != block)
        pl.when(last)(leave(block).start)

    chip = lax.axis_index("group") * lax.axis_size("chip") + lax.axis_index("chip")
    sample = lax.broadcasted_iota(jnp.int32, (tok_dev, 128), 0) + chip * tok_dev
    mine = lanes(tok_dev) == sample
    rest = jnp.sum(jnp.where(mine, own_rest, 0.0), axis=1, keepdims=True)
    label = jnp.sum(jnp.where(mine, own_label, 0.0), axis=1, keepdims=True)
    total = rest + label
    loss = jnp.log(total) - jnp.log(label)
    square = (tok_dev, tok_dev)
    diagonal = lax.broadcasted_iota(jnp.int32, square, 0) == lax.broadcasted_iota(
        jnp.int32, square, 1
    )
    loss_row[...] = jnp.sum(jnp.where(diagonal, loss, 0.0), axis=0, keepdims=True)
    rows = features[...].astype(jnp.float32)
    inv_norm = inverse_norm(rows)
    unit = rows * inv_norm
    cand = sums[:, width : 2 * width]
    cand = (cand * inverse_norm(cand)).astype(jnp.bfloat16).astype(jnp.float32)
    unit_grad = logit_scale / total * (sums[:, :width] - rest * cand)
    along = jnp.sum(unit_grad * unit, axis=1, keepdims=True)
    feature_grad[...] = inv_norm * (unit_grad - along * unit)
    ends = [
        pltpu.make_async_copy(feature_grad, feature_out, left.at[held]),
        pltpu.make_async_copy(loss_row, loss_out, left.at[held + 1]),
    ]
    for move in ends:
        move.start()
    for block in range(held):
        leave(block).wait()
    for move in ends:
        move.wait()


def exchange(pieces, axes):
    return lax.all_to_all(pieces, axes, split_axis=0, concat_axis=0, tiled=True)


def with_partner(value):
    return lax.ppermute(value, "core", [(0, 1), (1, 0)])


def on_device(features, labels, centres, block_ids, listed):
    groups = lax.axis_size("group")
    chips = groups * lax.axis_size("chip")
    tok_dev, width = features.shape
    held = centres.shape[0] // BLK
    half = chips * tok_dev
    bf16, f32 = jnp.bfloat16, jnp.float32
    shape = jax.ShapeDtypeStruct

    copies, own_blocks, ids = run(
        load,
        (
            shape((chips, tok_dev, width + 128), bf16),
            shape((groups, BLK, width), bf16),
            shape((1, groups), block_ids.dtype),
        ),
        [HBM] * 5,
        *(
            pltpu.with_memory_space_constraint(array, pltpu.HBM)
            for array in (
                features,
                labels.reshape(1, -1),
                centres.reshape(held, BLK, width),
                block_ids.reshape(1, groups),
                listed.reshape(1, groups),
            )
        ),
        scratch=[
            pltpu.VMEM(features.shape, features.dtype),
            pltpu.VMEM((1, labels.shape[0]), labels.dtype),
            pltpu.VMEM((held, BLK, width), centres.dtype),
            pltpu.SMEM((1, groups), block_ids.dtype),
            pltpu.SMEM((1, groups), listed.dtype),
            pltpu.SemaphoreType.DMA((6,)),
        ],
    )
    pair_blocks = with_partner(own_blocks)
    own_packed = exchange(copies, CHIPS).reshape(half, width + 128)
    other_packed = with_partner(own_packed)
    own_expo, pair_expo, inverse, sums = run(
        exponentials,
        (
            shape((BLK, half), f32),
            shape((BLK, half), f32),
            shape((2, BLK, 128), f32),
            shape((2, half), f32),
        ),
        [VMEM] * 3,
        own_packed,
        own_blocks,
        pair_blocks,
    )
    other_expo = with_partner(pair_expo)
    other_sums = with_partner(sums)
    going = run(
        shares,
        shape((half, 2 * width), bf16),
        [VMEM] * 5,
        own_expo,
        pair_expo,
        inverse,
        own_blocks,
        pair_blocks,
    )
    sent = run(
        with_sums, shape((half, 2 * width + 128), bf16), [VMEM] * 3, going, sums, other_sums
    )
    received = exchange(sent.reshape(chips, tok_dev, 2 * width + 128), CHIPS)
    outs = (shape((held, BLK, width), f32), shape((tok_dev, width), f32), shape((1, tok_dev), f32))
    centre_grad, feature_grad, loss = run(
        backward,
        outs,
        [SMEM] + [VMEM] * 8,
        ids,
        received,
        own_expo,
        other_expo,
        own_packed,
        other_packed,
        features,
        own_blocks,
        inverse,
        out_spec=HBM,
        scratch=[
            *(pltpu.VMEM(out.shape, out.dtype) for out in outs),
            pltpu.SemaphoreType.DMA((held + 2,)),
        ],
    )
    return (loss.reshape(tok_dev), feature_grad, centre_grad.reshape(held * BLK, width))


def on_device_of_many(features, labels, centres, block_ids, listed):
    groups = lax.axis_size("group")
    members = lax.axis_size("member")
    devices = groups * members
    group = lax.axis_index("group")
    member = lax.axis_index("member")
    tok_dev, width = features.shape
    group_tok = members * tok_dev
    held = centres.shape[0] // BLK

    vectors = features.astype(jnp.float32)
    inv_norm = inverse_norm(vectors)
    unit_rows = vectors * inv_norm
    copies = jnp.broadcast_to(unit_rows.astype(jnp.bfloat16), (devices, tok_dev, width))
    units = exchange(copies, AXES).reshape(groups, group_tok, width)
    all_labels = exchange(jnp.broadcast_to(labels[None], (groups, group_tok)), "group")

    picked = centres.reshape(held, BLK, width)[block_ids[:, 0]].astype(jnp.float32)
    inv_cand = inverse_norm(picked)
    unit_cand = picked * inv_cand
    cand_half = unit_cand.astype(jnp.bfloat16)
    cosine = jnp.einsum("gsd,gcd->gsc", units, cand_half, preferred_element_type=jnp.float32)
    local_label = all_labels - (member * groups + group) * BLK
    onehot = (lax.broadcasted_iota(jnp.int32, (1, 1, BLK), 2) == local_label[:, :, None]).astype(
        jnp.float32
    )
    logits = logit_scale * (cosine - cos_margin * onehot)
    exp_logits = jnp.exp(logits) * listed.astype(jnp.float32)[:, :, None]
    totals, label_logit = lax.psum(
        (jnp.sum(exp_logits, axis=2), jnp.sum(logits * onehot, axis=2)), AXES
    )
    loss_all = (jnp.log(totals) - label_logit).reshape(devices, tok_dev)
    sample_loss = lax.dynamic_slice_in_dim(loss_all, group * members + member, 1, 0)[0]

    weights = (logit_scale * (exp_logits / totals[:, :, None] - onehot)).astype(jnp.bfloat16)
    partial = jnp.einsum("gsc,gcd->gsd", weights, cand_half, preferred_element_type=jnp.float32)
    home = exchange(partial.astype(jnp.bfloat16).reshape(devices, tok_dev, width), AXES)
    unit_grad = jnp.sum(home.astype(jnp.float32), axis=0)
    feature_grad = inv_norm * (
        unit_grad - jnp.sum(unit_grad * unit_rows, axis=1, keepdims=True) * unit_rows
    )
    slot_grad = jnp.einsum("gsc,gsd->gcd", weights, units, preferred_element_type=jnp.float32)
    cand_grad = inv_cand * (
        slot_grad - jnp.sum(slot_grad * unit_cand, axis=2, keepdims=True) * unit_cand
    )
    cand_grad = cand_grad.astype(jnp.bfloat16).astype(jnp.float32)
    names = block_ids == jnp.arange(held, dtype=jnp.int32)[None, :]
    centre_grad = jnp.sum(
        jnp.where(names[:, :, None, None], cand_grad[:, None], 0.0), axis=0
    ).reshape(held * BLK, width)
    return (sample_loss, feature_grad, centre_grad)


def on_axes(body, mesh, axes):
    split = P(axes)
    return jax.shard_map(
        body,
        mesh=mesh,
        in_specs=(split, P("group"), split, P(None, axes), P(None, axes)),
        out_specs=(split, split, split),
        check_vma=False,
    )


def solution(mesh):
    groups, members = mesh.shape["group"], mesh.shape["member"]
    by_core = jax.sharding.Mesh(
        mesh.devices.reshape(groups, members // 2, 2), ("group", "chip", "core")
    )

    def program(features, *others):
        half = features.shape[0] // 2
        if half == 128 and 2 * groups == features.shape[0] // mesh.size == 8:
            return on_axes(on_device, by_core, (*CHIPS, "core"))(features, *others)
        return on_axes(on_device_of_many, mesh, AXES)(features, *others)

    return program
```

```python
import jax
import jax.numpy as jnp
from jax import lax
from jax.experimental import pallas as pl
from jax.experimental.pallas import tpu as pltpu
from jax.sharding import PartitionSpec as P

BLK = 128
AXES = ("group", "member")
CHIPS = ("group", "chip")

logit_scale = 32.0
cos_margin = 0.35
norm_epsilon = 1e-06
UNLISTED = 1e19

VMEM = pl.BlockSpec(memory_space=pltpu.VMEM)
SMEM = pl.BlockSpec(memory_space=pltpu.SMEM)
HBM = pl.BlockSpec(memory_space=pltpu.HBM)


def inverse_norm(rows):
    return lax.rsqrt(jnp.sum(rows * rows, axis=-1, keepdims=True) + norm_epsilon)


def contract(left, right, left_dim, right_dim):
    dims = (((left_dim,), (right_dim,)), ((), ()))
    return lax.dot_general(left, right, dims, preferred_element_type=jnp.float32)


def lanes(rows):
    return lax.broadcasted_iota(jnp.int32, (rows, 128), 1)


def run(kernel, out_shape, in_specs, *operands, out_spec=VMEM, scratch=()):
    shapes = jax.tree.leaves(out_shape)
    return pl.pallas_call(
        kernel,
        out_shape=out_shape,
        in_specs=in_specs,
        out_specs=jax.tree.map(lambda _: out_spec, out_shape),
        scratch_shapes=scratch,
        compiler_params=pltpu.CompilerParams(vmem_limit_bytes=48 * 1024 * 1024),
        cost_estimate=pl.CostEstimate(
            flops=0,
            transcendentals=0,
            bytes_accessed=sum(a.size * a.dtype.itemsize for a in (*shapes, *operands)),
        ),
    )(*operands)


def load(
    features,
    labels,
    centres,
    ids,
    listed,
    copies_out,
    blocks_out,
    ids_out,
    held_features,
    held_labels,
    held_centres,
    held_ids,
    held_listed,
    arrived,
):
    moves = [
        pltpu.make_async_copy(source, target, arrived.at[i])
        for i, (source, target) in enumerate(
            (
                (features, held_features),
                (labels, held_labels),
                (ids, held_ids),
                (listed, held_listed),
                (ids, ids_out),
                (centres, held_centres),
            )
        )
    ]
    for move in moves:
        move.start()
    moves[0].wait()
    moves[1].wait()
    chip = lax.axis_index("chip")
    member = 2 * chip + lax.axis_index("core")
    copies, tok_dev, _ = copies_out.shape
    width = features.shape[1]
    rows = held_features[...].astype(jnp.float32)
    unit = (rows * inverse_norm(rows)).astype(jnp.bfloat16)
    copies_out[:, :, :width] = jnp.broadcast_to(unit[None], (copies, tok_dev, width))

    place = (lax.axis_index("group") * lax.axis_size("chip") + chip) * tok_dev
    row = held_labels[...]
    row = jnp.concatenate([row, jnp.zeros((1, 128 - row.shape[1]), jnp.int32)], axis=1)
    row = jnp.broadcast_to(row, (tok_dev, 128))
    row = pltpu.roll(row, lax.rem(place - member * tok_dev + 128, 128), 1)
    digit = lax.broadcasted_iota(jnp.int32, (tok_dev, 128), 0)
    digits = (row >> (7 * jnp.minimum(digit, 3))) & 127
    lane = lanes(tok_dev)
    digits = jnp.where((lane >= place) & (lane < place + tok_dev), digits, 0)
    copies_out[:, :, width:] = jnp.broadcast_to(
        digits.astype(jnp.float32).astype(jnp.bfloat16)[None], (copies, tok_dev, 128)
    )
    for move in moves[2:]:
        move.wait()
    for g in range(blocks_out.shape[0]):
        block = held_centres[held_ids[0, g]]
        blocks_out[g] = jnp.where(held_listed[0, g] > 0, block, jnp.full_like(block, UNLISTED))


def select(parts, rows):
    owner = lanes(1) // (128 // len(parts))
    out = jnp.broadcast_to(parts[0], (rows, 128))
    for g in range(1, len(parts)):
        out = jnp.where(owner == g, parts[g], out)
    return out


def exponentials(packed, own_blocks, pair_blocks, expo_out, pair_expo_out, inverse_out, sums_out):
    group, core = lax.axis_index("group"), lax.axis_index("core")
    groups, _, width = own_blocks.shape
    units = packed[:, :width]
    digits = jnp.sum(
        packed[:, width:].astype(jnp.float32).reshape(128 // 8, 8, 128), axis=0
    ).astype(jnp.int32)
    labels = digits[0:1] + (digits[1:2] << 7) + (digits[2:3] << 14)
    rest = jnp.zeros((1, 128), jnp.float32)
    at_label = jnp.zeros((1, 128), jnp.float32)
    for k, (blocks, out) in enumerate(((own_blocks, expo_out), (pair_blocks, pair_expo_out))):
        member = 2 * lax.axis_index("chip") + (core if k == 0 else 1 - core)
        first = (member * groups + group) * BLK
        onehot = lax.broadcasted_iota(jnp.int32, (BLK, 128), 0) == labels - first
        inverse = select(
            [inverse_norm(blocks[g].astype(jnp.float32)) for g in range(groups)], BLK
        )
        inverse_out[k] = inverse
        cosine = inverse * select([contract(blocks[g], units, 1, 1) for g in range(groups)], BLK)
        expo = jnp.exp(logit_scale * (cosine - jnp.where(onehot, cos_margin, 0.0)))
        expo = jnp.where(inverse > 0.0, expo, 0.0)
        out[...] = jnp.where(onehot, -1.0, expo)
        rest += jnp.sum(jnp.where(onehot, 0.0, expo), axis=0, keepdims=True)
        at_label += jnp.sum(jnp.where(onehot, expo, 0.0), axis=0, keepdims=True)
    sums_out[0:1, :] = rest
    sums_out[1:2, :] = at_label


def shares(own_expo, pair_expo, inverse, own_blocks, pair_blocks, shares_out):
    groups, _, width = own_blocks.shape
    per_group = 128 // groups
    others, label = [], []
    for k, expo in enumerate((own_expo[...], pair_expo[...])):
        others.append((jnp.maximum(expo, 0.0) * inverse[k]).T.astype(jnp.bfloat16))
        label.append(jnp.where(expo < 0.0, 1.0, 0.0).T.astype(jnp.bfloat16))
    others = jnp.concatenate(others, axis=1)
    label = jnp.concatenate(label, axis=1)
    for g in range(groups):
        here = slice(g * per_group, (g + 1) * per_group)
        blocks = jnp.concatenate([own_blocks[g], pair_blocks[g]], axis=0)
        both = contract(jnp.concatenate([others[here], label[here]], axis=0), blocks, 1, 0)
        both = both.astype(jnp.bfloat16)
        shares_out[here, :width] = both[:per_group]
        shares_out[here, width:] = both[per_group:]


def with_sums(shares, own_sums, other_sums, other_packed, other_expo, sent_out):
    del other_packed, other_expo
    rows, wide = shares.shape
    sent_out[:, :wide] = shares[...]
    total = jnp.concatenate([own_sums[...], other_sums[...]], axis=0)
    high = total.astype(jnp.bfloat16)
    low = (total - high.astype(jnp.float32)).astype(jnp.bfloat16)
    tile = jnp.concatenate([high.astype(jnp.float32), low.astype(jnp.float32)], axis=0)
    tile = jnp.broadcast_to(tile[None], (rows // 8, 8, 128))
    sent_out[:, wide:] = tile.reshape(rows, 128).astype(jnp.bfloat16)


def backward(
    ids,
    received,
    own_expo,
    other_expo,
    own_packed,
    other_packed,
    features,
    blocks,
    inverse,
    grad_out,
    feature_out,
    loss_out,
    grad,
    feature_grad,
    loss_row,
    left,
):
    groups = ids.shape[1]
    held = grad.shape[0]
    per_group = 128 // groups
    tok_dev, width = features.shape

    grad[...] = jnp.zeros_like(grad)
    sums = received[0].astype(jnp.float32)
    for i in range(1, received.shape[0]):
        sums = sums + received[i].astype(jnp.float32)
    tile = sums[:, 2 * width :]
    tile = tile[:4] + tile[4:]
    own_rest, own_label = tile[0:1], tile[1:2]
    other_rest, other_label = tile[2:3], tile[3:4]

    chip = lax.axis_index("group") * lax.axis_size("chip") + lax.axis_index("chip")
    sample = lax.broadcasted_iota(jnp.int32, (tok_dev, 128), 0) + chip * tok_dev
    mine = lanes(tok_dev) == sample
    rest = jnp.sum(jnp.where(mine, own_rest, 0.0), axis=1, keepdims=True)
    label = jnp.sum(jnp.where(mine, own_label, 0.0), axis=1, keepdims=True)
    total = rest + label
    loss = jnp.log(total) - jnp.log(label)
    square = (tok_dev, tok_dev)
    diagonal = lax.broadcasted_iota(jnp.int32, square, 0) == lax.broadcasted_iota(
        jnp.int32, square, 1
    )
    loss_row[...] = jnp.sum(jnp.where(diagonal, loss, 0.0), axis=0, keepdims=True)
    rows = features[...].astype(jnp.float32)
    inv_norm = inverse_norm(rows)
    unit = rows * inv_norm
    cand = sums[:, width : 2 * width]
    cand = (cand * inverse_norm(cand)).astype(jnp.bfloat16).astype(jnp.float32)
    unit_grad = logit_scale / total * (sums[:, :width] - rest * cand)
    along = jnp.sum(unit_grad * unit, axis=1, keepdims=True)
    feature_grad[...] = inv_norm * (unit_grad - along * unit)
    moves = [
        pltpu.make_async_copy(feature_grad, feature_out, left.at[held]),
        pltpu.make_async_copy(loss_row, loss_out, left.at[held + 1]),
    ]
    for move in moves:
        move.start()

    units = jnp.concatenate([own_packed[:, :width], other_packed[:, :width]], axis=0)
    own_scale = logit_scale / (own_rest + own_label)
    other_scale = logit_scale / (other_rest + other_label)
    own = own_expo[...]
    other = other_expo[...]
    own = jnp.where(own < 0.0, -own_rest, own) * own_scale
    other = jnp.where(other < 0.0, -other_rest, other) * other_scale
    weights = jnp.concatenate([own, other], axis=1)
    owner = jnp.concatenate([lanes(1), lanes(1)], axis=1) // per_group
    for g in range(groups):
        mine = jnp.where(owner == g, weights, 0.0).astype(jnp.bfloat16)
        slot_grad = contract(mine, units, 1, 0)
        factor = inverse[0, :, g * per_group : g * per_group + 1]
        unit = blocks[g].astype(jnp.float32) * factor
        along = jnp.sum(slot_grad * unit, axis=1, keepdims=True)
        cand_grad = factor * (slot_grad - along * unit)
        grad[ids[0, g]] += cand_grad.astype(jnp.bfloat16).astype(jnp.float32)
    for block in range(held):
        move = pltpu.make_async_copy(grad.at[block], grad_out.at[block], left.at[block])
        move.start()
        moves.append(move)
    for move in moves:
        move.wait()


def exchange(pieces, axes):
    return lax.all_to_all(pieces, axes, split_axis=0, concat_axis=0, tiled=True)


def with_partner(value):
    return lax.ppermute(value, "core", [(0, 1), (1, 0)])


def on_device(features, labels, centres, block_ids, listed):
    groups = lax.axis_size("group")
    chips = groups * lax.axis_size("chip")
    tok_dev, width = features.shape
    held = centres.shape[0] // BLK
    half = chips * tok_dev
    bf16, f32 = jnp.bfloat16, jnp.float32
    shape = jax.ShapeDtypeStruct

    copies, own_blocks, ids = run(
        load,
        (
            shape((chips, tok_dev, width + 128), bf16),
            shape((groups, BLK, width), bf16),
            shape((1, groups), block_ids.dtype),
        ),
        [HBM] * 5,
        *(
            pltpu.with_memory_space_constraint(array, pltpu.HBM)
            for array in (
                features,
                labels.reshape(1, -1),
                centres.reshape(held, BLK, width),
                block_ids.reshape(1, groups),
                listed.reshape(1, groups),
            )
        ),
        scratch=[
            pltpu.VMEM(features.shape, features.dtype),
            pltpu.VMEM((1, labels.shape[0]), labels.dtype),
            pltpu.VMEM((held, BLK, width), centres.dtype),
            pltpu.SMEM((1, groups), block_ids.dtype),
            pltpu.SMEM((1, groups), listed.dtype),
            pltpu.SemaphoreType.DMA((6,)),
        ],
    )
    pair_blocks = with_partner(own_blocks)
    own_packed = exchange(copies, CHIPS).reshape(half, width + 128)
    other_packed = with_partner(own_packed)
    own_expo, pair_expo, inverse, sums = run(
        exponentials,
        (
            shape((BLK, half), f32),
            shape((BLK, half), f32),
            shape((2, BLK, 128), f32),
            shape((2, half), f32),
        ),
        [VMEM] * 3,
        own_packed,
        own_blocks,
        pair_blocks,
    )
    other_expo = with_partner(pair_expo)
    other_sums = with_partner(sums)
    going = run(
        shares,
        shape((half, 2 * width), bf16),
        [VMEM] * 5,
        own_expo,
        pair_expo,
        inverse,
        own_blocks,
        pair_blocks,
    )
    sent = run(
        with_sums,
        shape((half, 2 * width + 128), bf16),
        [VMEM] * 3 + [pl.BlockSpec(memory_space=pl.ANY)] * 2,
        going,
        sums,
        other_sums,
        other_packed,
        other_expo,
    )
    received = exchange(sent.reshape(chips, tok_dev, 2 * width + 128), CHIPS)
    outs = (shape((held, BLK, width), f32), shape((tok_dev, width), f32), shape((1, tok_dev), f32))
    centre_grad, feature_grad, loss = run(
        backward,
        outs,
        [SMEM] + [VMEM] * 8,
        ids,
        received,
        own_expo,
        other_expo,
        own_packed,
        other_packed,
        features,
        own_blocks,
        inverse,
        out_spec=HBM,
        scratch=[
            *(pltpu.VMEM(out.shape, out.dtype) for out in outs),
            pltpu.SemaphoreType.DMA((held + 2,)),
        ],
    )
    return (loss.reshape(tok_dev), feature_grad, centre_grad.reshape(held * BLK, width))


def on_device_of_many(features, labels, centres, block_ids, listed):
    groups = lax.axis_size("group")
    members = lax.axis_size("member")
    devices = groups * members
    group = lax.axis_index("group")
    member = lax.axis_index("member")
    tok_dev, width = features.shape
    group_tok = members * tok_dev
    held = centres.shape[0] // BLK

    vectors = features.astype(jnp.float32)
    inv_norm = inverse_norm(vectors)
    unit_rows = vectors * inv_norm
    copies = jnp.broadcast_to(unit_rows.astype(jnp.bfloat16), (devices, tok_dev, width))
    units = exchange(copies, AXES).reshape(groups, group_tok, width)
    all_labels = exchange(jnp.broadcast_to(labels[None], (groups, group_tok)), "group")

    picked = centres.reshape(held, BLK, width)[block_ids[:, 0]].astype(jnp.float32)
    inv_cand = inverse_norm(picked)
    unit_cand = picked * inv_cand
    cand_half = unit_cand.astype(jnp.bfloat16)
    cosine = jnp.einsum("gsd,gcd->gsc", units, cand_half, preferred_element_type=jnp.float32)
    local_label = all_labels - (member * groups + group) * BLK
    onehot = (lax.broadcasted_iota(jnp.int32, (1, 1, BLK), 2) == local_label[:, :, None]).astype(
        jnp.float32
    )
    logits = logit_scale * (cosine - cos_margin * onehot)
    exp_logits = jnp.exp(logits) * listed.astype(jnp.float32)[:, :, None]
    totals, label_logit = lax.psum(
        (jnp.sum(exp_logits, axis=2), jnp.sum(logits * onehot, axis=2)), AXES
    )
    loss_all = (jnp.log(totals) - label_logit).reshape(devices, tok_dev)
    sample_loss = lax.dynamic_slice_in_dim(loss_all, group * members + member, 1, 0)[0]

    weights = (logit_scale * (exp_logits / totals[:, :, None] - onehot)).astype(jnp.bfloat16)
    partial = jnp.einsum("gsc,gcd->gsd", weights, cand_half, preferred_element_type=jnp.float32)
    home = exchange(partial.astype(jnp.bfloat16).reshape(devices, tok_dev, width), AXES)
    unit_grad = jnp.sum(home.astype(jnp.float32), axis=0)
    feature_grad = inv_norm * (
        unit_grad - jnp.sum(unit_grad * unit_rows, axis=1, keepdims=True) * unit_rows
    )
    slot_grad = jnp.einsum("gsc,gsd->gcd", weights, units, preferred_element_type=jnp.float32)
    cand_grad = inv_cand * (
        slot_grad - jnp.sum(slot_grad * unit_cand, axis=2, keepdims=True) * unit_cand
    )
    cand_grad = cand_grad.astype(jnp.bfloat16).astype(jnp.float32)
    names = block_ids == jnp.arange(held, dtype=jnp.int32)[None, :]
    centre_grad = jnp.sum(
        jnp.where(names[:, :, None, None], cand_grad[:, None], 0.0), axis=0
    ).reshape(held * BLK, width)
    return (sample_loss, feature_grad, centre_grad)


def on_axes(body, mesh, axes):
    split = P(axes)
    return jax.shard_map(
        body,
        mesh=mesh,
        in_specs=(split, P("group"), split, P(None, axes), P(None, axes)),
        out_specs=(split, split, split),
        check_vma=False,
    )


def solution(mesh):
    groups, members = mesh.shape["group"], mesh.shape["member"]
    by_core = jax.sharding.Mesh(
        mesh.devices.reshape(groups, members // 2, 2), ("group", "chip", "core")
    )

    def program(features, *others):
        half = features.shape[0] // 2
        if half == 128 and 2 * groups == features.shape[0] // mesh.size == 8:
            return on_axes(on_device, by_core, (*CHIPS, "core"))(features, *others)
        return on_axes(on_device_of_many, mesh, AXES)(features, *others)

    return program
```

```python
import jax
import jax.numpy as jnp
from jax import lax
from jax.experimental import pallas as pl
from jax.experimental.pallas import tpu as pltpu
from jax.sharding import PartitionSpec as P

BLK = 128
AXES = ("group", "member")
CHIPS = ("group", "chip")

logit_scale = 32.0
cos_margin = 0.35
norm_epsilon = 1e-06
UNLISTED = 1e19

VMEM = pl.BlockSpec(memory_space=pltpu.VMEM)
SMEM = pl.BlockSpec(memory_space=pltpu.SMEM)
HBM = pl.BlockSpec(memory_space=pltpu.HBM)


def inverse_norm(rows):
    return lax.rsqrt(jnp.sum(rows * rows, axis=-1, keepdims=True) + norm_epsilon)


def contract(left, right, left_dim, right_dim):
    dims = (((left_dim,), (right_dim,)), ((), ()))
    return lax.dot_general(left, right, dims, preferred_element_type=jnp.float32)


def lanes(rows):
    return lax.broadcasted_iota(jnp.int32, (rows, 128), 1)


def run(kernel, out_shape, in_specs, *operands, out_spec=VMEM, scratch=()):
    shapes = jax.tree.leaves(out_shape)
    return pl.pallas_call(
        kernel,
        out_shape=out_shape,
        in_specs=in_specs,
        out_specs=jax.tree.map(lambda _: out_spec, out_shape),
        scratch_shapes=scratch,
        compiler_params=pltpu.CompilerParams(vmem_limit_bytes=48 * 1024 * 1024),
        cost_estimate=pl.CostEstimate(
            flops=0,
            transcendentals=0,
            bytes_accessed=sum(a.size * a.dtype.itemsize for a in (*shapes, *operands)),
        ),
    )(*operands)


def load(
    features,
    labels,
    centres,
    ids,
    listed,
    copies_out,
    blocks_out,
    centres_out,
    ids_out,
    held_features,
    held_labels,
    held_ids,
    held_listed,
    arrived,
):
    moves = [
        pltpu.make_async_copy(source, target, arrived.at[i])
        for i, (source, target) in enumerate(
            (
                (features, held_features),
                (labels, held_labels),
                (ids, held_ids),
                (listed, held_listed),
                (ids, ids_out),
                (centres, centres_out),
            )
        )
    ]
    for move in moves:
        move.start()
    moves[0].wait()
    moves[1].wait()
    chip = lax.axis_index("chip")
    member = 2 * chip + lax.axis_index("core")
    copies, tok_dev, _ = copies_out.shape
    width = features.shape[1]
    rows = held_features[...].astype(jnp.float32)
    unit = (rows * inverse_norm(rows)).astype(jnp.bfloat16)
    copies_out[:, :, :width] = jnp.broadcast_to(unit[None], (copies, tok_dev, width))

    place = (lax.axis_index("group") * lax.axis_size("chip") + chip) * tok_dev
    row = held_labels[...]
    row = jnp.concatenate([row, jnp.zeros((1, 128 - row.shape[1]), jnp.int32)], axis=1)
    row = jnp.broadcast_to(row, (tok_dev, 128))
    row = pltpu.roll(row, lax.rem(place - member * tok_dev + 128, 128), 1)
    digit = lax.broadcasted_iota(jnp.int32, (tok_dev, 128), 0)
    digits = (row >> (7 * jnp.minimum(digit, 3))) & 127
    lane = lanes(tok_dev)
    digits = jnp.where((lane >= place) & (lane < place + tok_dev), digits, 0)
    copies_out[:, :, width:] = jnp.broadcast_to(
        digits.astype(jnp.float32).astype(jnp.bfloat16)[None], (copies, tok_dev, 128)
    )
    for move in moves[2:]:
        move.wait()
    for g in range(blocks_out.shape[0]):
        block = centres_out[held_ids[0, g]]
        blocks_out[g] = jnp.where(held_listed[0, g] > 0, block, jnp.full_like(block, UNLISTED))


def select(parts, rows):
    owner = lanes(1) // (128 // len(parts))
    out = jnp.broadcast_to(parts[0], (rows, 128))
    for g in range(1, len(parts)):
        out = jnp.where(owner == g, parts[g], out)
    return out


def exponentials(packed, own_blocks, pair_blocks, expo_out, pair_expo_out, inverse_out, sums_out):
    group, core = lax.axis_index("group"), lax.axis_index("core")
    groups, _, width = own_blocks.shape
    units = packed[:, :width]
    digits = jnp.sum(
        packed[:, width:].astype(jnp.float32).reshape(128 // 8, 8, 128), axis=0
    ).astype(jnp.int32)
    labels = digits[0:1] + (digits[1:2] << 7) + (digits[2:3] << 14)
    rest = jnp.zeros((1, 128), jnp.float32)
    at_label = jnp.zeros((1, 128), jnp.float32)
    for k, (blocks, out) in enumerate(((own_blocks, expo_out), (pair_blocks, pair_expo_out))):
        member = 2 * lax.axis_index("chip") + (core if k == 0 else 1 - core)
        first = (member * groups + group) * BLK
        onehot = lax.broadcasted_iota(jnp.int32, (BLK, 128), 0) == labels - first
        inverse = select(
            [inverse_norm(blocks[g].astype(jnp.float32)) for g in range(groups)], BLK
        )
        inverse_out[k] = inverse
        cosine = inverse * select([contract(blocks[g], units, 1, 1) for g in range(groups)], BLK)
        expo = jnp.exp(logit_scale * (cosine - jnp.where(onehot, cos_margin, 0.0)))
        expo = jnp.where(inverse > 0.0, expo, 0.0)
        out[...] = jnp.where(onehot, -1.0, expo)
        rest += jnp.sum(jnp.where(onehot, 0.0, expo), axis=0, keepdims=True)
        at_label += jnp.sum(jnp.where(onehot, expo, 0.0), axis=0, keepdims=True)
    sums_out[0:1, :] = rest
    sums_out[1:2, :] = at_label


def shares(own_expo, pair_expo, inverse, own_blocks, pair_blocks, centres, shares_out, norms_out):
    groups, _, width = own_blocks.shape
    per_group = 128 // groups
    others, label = [], []
    for k, expo in enumerate((own_expo[...], pair_expo[...])):
        others.append((jnp.maximum(expo, 0.0) * inverse[k]).T.astype(jnp.bfloat16))
        label.append(jnp.where(expo < 0.0, 1.0, 0.0).T.astype(jnp.bfloat16))
    others = jnp.concatenate(others, axis=1)
    label = jnp.concatenate(label, axis=1)
    for g in range(groups):
        here = slice(g * per_group, (g + 1) * per_group)
        blocks = jnp.concatenate([own_blocks[g], pair_blocks[g]], axis=0)
        both = contract(jnp.concatenate([others[here], label[here]], axis=0), blocks, 1, 0)
        both = both.astype(jnp.bfloat16)
        shares_out[here, :width] = both[:per_group]
        shares_out[here, width:] = both[per_group:]
    held = centres.shape[0]
    norms_out[...] = select(
        [inverse_norm(centres[b].astype(jnp.float32)) for b in range(held)], BLK
    )


def with_sums(shares, own_sums, other_sums, other_packed, other_expo, sent_out):
    del other_packed, other_expo
    rows, wide = shares.shape
    sent_out[:, :wide] = shares[...]
    total = jnp.concatenate([own_sums[...], other_sums[...]], axis=0)
    high = total.astype(jnp.bfloat16)
    low = (total - high.astype(jnp.float32)).astype(jnp.bfloat16)
    tile = jnp.concatenate([high.astype(jnp.float32), low.astype(jnp.float32)], axis=0)
    tile = jnp.broadcast_to(tile[None], (rows // 8, 8, 128))
    sent_out[:, wide:] = tile.reshape(rows, 128).astype(jnp.bfloat16)


def backward(
    ids,
    received,
    own_expo,
    other_expo,
    own_packed,
    other_packed,
    features,
    centres,
    norms,
    grad_out,
    feature_out,
    loss_out,
    grad,
    feature_grad,
    loss_row,
    left,
):
    groups = ids.shape[1]
    held = centres.shape[0]
    tok_dev, width = features.shape

    sums = received[0].astype(jnp.float32)
    for i in range(1, received.shape[0]):
        sums = sums + received[i].astype(jnp.float32)
    tile = sums[:, 2 * width :]
    tile = tile[:4] + tile[4:]
    own_rest, own_label = tile[0:1], tile[1:2]
    other_rest, other_label = tile[2:3], tile[3:4]

    chip = lax.axis_index("group") * lax.axis_size("chip") + lax.axis_index("chip")
    sample = lax.broadcasted_iota(jnp.int32, (tok_dev, 128), 0) + chip * tok_dev
    mine = lanes(tok_dev) == sample
    rest = jnp.sum(jnp.where(mine, own_rest, 0.0), axis=1, keepdims=True)
    label = jnp.sum(jnp.where(mine, own_label, 0.0), axis=1, keepdims=True)
    total = rest + label
    loss = jnp.log(total) - jnp.log(label)
    square = (tok_dev, tok_dev)
    diagonal = lax.broadcasted_iota(jnp.int32, square, 0) == lax.broadcasted_iota(
        jnp.int32, square, 1
    )
    loss_row[...] = jnp.sum(jnp.where(diagonal, loss, 0.0), axis=0, keepdims=True)
    rows = features[...].astype(jnp.float32)
    inv_norm = inverse_norm(rows)
    unit = rows * inv_norm
    cand = sums[:, width : 2 * width]
    cand = (cand * inverse_norm(cand)).astype(jnp.bfloat16).astype(jnp.float32)
    unit_grad = logit_scale / total * (sums[:, :width] - rest * cand)
    along = jnp.sum(unit_grad * unit, axis=1, keepdims=True)
    feature_grad[...] = inv_norm * (unit_grad - along * unit)

    units = jnp.concatenate([own_packed[:, :width], other_packed[:, :width]], axis=0)
    own_scale = logit_scale / (own_rest + own_label)
    other_scale = logit_scale / (other_rest + other_label)
    own = own_expo[...]
    other = other_expo[...]
    own = jnp.where(own < 0.0, -own_rest, own) * own_scale
    other = jnp.where(other < 0.0, -other_rest, other) * other_scale
    weights = jnp.concatenate([own, other], axis=1)
    named = select([ids[0, g] for g in range(groups)], 1)
    named = jnp.concatenate([named, named], axis=1)
    for b in range(held):
        mine = jnp.where(named == b, weights, 0.0).astype(jnp.bfloat16)
        grad[b] = contract(mine, units, 1, 0)
    moves = [
        pltpu.make_async_copy(feature_grad, feature_out, left.at[held]),
        pltpu.make_async_copy(loss_row, loss_out, left.at[held + 1]),
    ]
    for move in moves:
        move.start()
    per_block = 128 // held
    for b in range(held):
        slot_grad = grad[b]
        factor = norms[:, b * per_block : b * per_block + 1]
        unit = centres[b].astype(jnp.float32) * factor
        along = jnp.sum(slot_grad * unit, axis=1, keepdims=True)
        grad[b] = factor * (slot_grad - along * unit)
        move = pltpu.make_async_copy(grad.at[b], grad_out.at[b], left.at[b])
        move.start()
        moves.append(move)
    for move in moves:
        move.wait()


def exchange(pieces, axes):
    return lax.all_to_all(pieces, axes, split_axis=0, concat_axis=0, tiled=True)


def with_partner(value):
    return lax.ppermute(value, "core", [(0, 1), (1, 0)])


def on_device(features, labels, centres, block_ids, listed):
    groups = lax.axis_size("group")
    chips = groups * lax.axis_size("chip")
    tok_dev, width = features.shape
    held = centres.shape[0] // BLK
    half = chips * tok_dev
    bf16, f32 = jnp.bfloat16, jnp.float32
    shape = jax.ShapeDtypeStruct

    copies, own_blocks, blocks, ids = run(
        load,
        (
            shape((chips, tok_dev, width + 128), bf16),
            shape((groups, BLK, width), bf16),
            shape((held, BLK, width), bf16),
            shape((1, groups), block_ids.dtype),
        ),
        [HBM] * 5,
        *(
            pltpu.with_memory_space_constraint(array, pltpu.HBM)
            for array in (
                features,
                labels.reshape(1, -1),
                centres.reshape(held, BLK, width),
                block_ids.reshape(1, groups),
                listed.reshape(1, groups),
            )
        ),
        scratch=[
            pltpu.VMEM(features.shape, features.dtype),
            pltpu.VMEM((1, labels.shape[0]), labels.dtype),
            pltpu.SMEM((1, groups), block_ids.dtype),
            pltpu.SMEM((1, groups), listed.dtype),
            pltpu.SemaphoreType.DMA((6,)),
        ],
    )
    pair_blocks = with_partner(own_blocks)
    own_packed = exchange(copies, CHIPS).reshape(half, width + 128)
    other_packed = with_partner(own_packed)
    own_expo, pair_expo, inverse, sums = run(
        exponentials,
        (
            shape((BLK, half), f32),
            shape((BLK, half), f32),
            shape((2, BLK, 128), f32),
            shape((2, half), f32),
        ),
        [VMEM] * 3,
        own_packed,
        own_blocks,
        pair_blocks,
    )
    other_expo = with_partner(pair_expo)
    other_sums = with_partner(sums)
    going, norms = run(
        shares,
        (shape((half, 2 * width), bf16), shape((BLK, 128), f32)),
        [VMEM] * 6,
        own_expo,
        pair_expo,
        inverse,
        own_blocks,
        pair_blocks,
        blocks,
    )
    sent = run(
        with_sums,
        shape((half, 2 * width + 128), bf16),
        [VMEM] * 3 + [pl.BlockSpec(memory_space=pl.ANY)] * 2,
        going,
        sums,
        other_sums,
        other_packed,
        other_expo,
    )
    received = exchange(sent.reshape(chips, tok_dev, 2 * width + 128), CHIPS)
    outs = (shape((held, BLK, width), f32), shape((tok_dev, width), f32), shape((1, tok_dev), f32))
    centre_grad, feature_grad, loss = run(
        backward,
        outs,
        [SMEM] + [VMEM] * 8,
        ids,
        received,
        own_expo,
        other_expo,
        own_packed,
        other_packed,
        features,
        blocks,
        norms,
        out_spec=HBM,
        scratch=[
            *(pltpu.VMEM(out.shape, out.dtype) for out in outs),
            pltpu.SemaphoreType.DMA((held + 2,)),
        ],
    )
    return (loss.reshape(tok_dev), feature_grad, centre_grad.reshape(held * BLK, width))


def on_device_of_many(features, labels, centres, block_ids, listed):
    groups = lax.axis_size("group")
    members = lax.axis_size("member")
    devices = groups * members
    group = lax.axis_index("group")
    member = lax.axis_index("member")
    tok_dev, width = features.shape
    group_tok = members * tok_dev
    held = centres.shape[0] // BLK

    vectors = features.astype(jnp.float32)
    inv_norm = inverse_norm(vectors)
    unit_rows = vectors * inv_norm
    copies = jnp.broadcast_to(unit_rows.astype(jnp.bfloat16), (devices, tok_dev, width))
    units = exchange(copies, AXES).reshape(groups, group_tok, width)
    all_labels = exchange(jnp.broadcast_to(labels[None], (groups, group_tok)), "group")

    picked = centres.reshape(held, BLK, width)[block_ids[:, 0]].astype(jnp.float32)
    inv_cand = inverse_norm(picked)
    unit_cand = picked * inv_cand
    cand_half = unit_cand.astype(jnp.bfloat16)
    cosine = jnp.einsum("gsd,gcd->gsc", units, cand_half, preferred_element_type=jnp.float32)
    local_label = all_labels - (member * groups + group) * BLK
    onehot = (lax.broadcasted_iota(jnp.int32, (1, 1, BLK), 2) == local_label[:, :, None]).astype(
        jnp.float32
    )
    logits = logit_scale * (cosine - cos_margin * onehot)
    exp_logits = jnp.exp(logits) * listed.astype(jnp.float32)[:, :, None]
    totals, label_logit = lax.psum(
        (jnp.sum(exp_logits, axis=2), jnp.sum(logits * onehot, axis=2)), AXES
    )
    loss_all = (jnp.log(totals) - label_logit).reshape(devices, tok_dev)
    sample_loss = lax.dynamic_slice_in_dim(loss_all, group * members + member, 1, 0)[0]

    weights = (logit_scale * (exp_logits / totals[:, :, None] - onehot)).astype(jnp.bfloat16)
    partial = jnp.einsum("gsc,gcd->gsd", weights, cand_half, preferred_element_type=jnp.float32)
    home = exchange(partial.astype(jnp.bfloat16).reshape(devices, tok_dev, width), AXES)
    unit_grad = jnp.sum(home.astype(jnp.float32), axis=0)
    feature_grad = inv_norm * (
        unit_grad - jnp.sum(unit_grad * unit_rows, axis=1, keepdims=True) * unit_rows
    )
    slot_grad = jnp.einsum("gsc,gsd->gcd", weights, units, preferred_element_type=jnp.float32)
    cand_grad = inv_cand * (
        slot_grad - jnp.sum(slot_grad * unit_cand, axis=2, keepdims=True) * unit_cand
    )
    cand_grad = cand_grad.astype(jnp.bfloat16).astype(jnp.float32)
    names = block_ids == jnp.arange(held, dtype=jnp.int32)[None, :]
    centre_grad = jnp.sum(
        jnp.where(names[:, :, None, None], cand_grad[:, None], 0.0), axis=0
    ).reshape(held * BLK, width)
    return (sample_loss, feature_grad, centre_grad)


def on_axes(body, mesh, axes):
    split = P(axes)
    return jax.shard_map(
        body,
        mesh=mesh,
        in_specs=(split, P("group"), split, P(None, axes), P(None, axes)),
        out_specs=(split, split, split),
        check_vma=False,
    )


def solution(mesh):
    groups, members = mesh.shape["group"], mesh.shape["member"]
    by_core = jax.sharding.Mesh(
        mesh.devices.reshape(groups, members // 2, 2), ("group", "chip", "core")
    )

    def program(features, *others):
        half = features.shape[0] // 2
        if half == 128 and 2 * groups == features.shape[0] // mesh.size == 8:
            return on_axes(on_device, by_core, (*CHIPS, "core"))(features, *others)
        return on_axes(on_device_of_many, mesh, AXES)(features, *others)

    return program
```

```python
import jax
import jax.numpy as jnp
from jax import lax
from jax.experimental import pallas as pl
from jax.experimental.pallas import tpu as pltpu
from jax.sharding import PartitionSpec as P

BLK = 128
AXES = ("group", "member")
CHIPS = ("group", "chip")

logit_scale = 32.0
cos_margin = 0.35
norm_epsilon = 1e-06
FIRST_GROUP = 1
UNLISTED = 1e19

VMEM = pl.BlockSpec(memory_space=pltpu.VMEM)
SMEM = pl.BlockSpec(memory_space=pltpu.SMEM)
HBM = pl.BlockSpec(memory_space=pltpu.HBM)


def inverse_norm(rows):
    return lax.rsqrt(jnp.sum(rows * rows, axis=-1, keepdims=True) + norm_epsilon)


def contract(left, right, left_dim, right_dim):
    dims = (((left_dim,), (right_dim,)), ((), ()))
    return lax.dot_general(left, right, dims, preferred_element_type=jnp.float32)


def lanes(rows):
    return lax.broadcasted_iota(jnp.int32, (rows, 128), 1)


def run(kernel, out_shape, in_specs, *operands, out_spec=VMEM, scratch=()):
    shapes = jax.tree.leaves(out_shape)
    return pl.pallas_call(
        kernel,
        out_shape=out_shape,
        in_specs=in_specs,
        out_specs=jax.tree.map(lambda _: out_spec, out_shape),
        scratch_shapes=scratch,
        compiler_params=pltpu.CompilerParams(vmem_limit_bytes=48 * 1024 * 1024),
        cost_estimate=pl.CostEstimate(
            flops=0,
            transcendentals=0,
            bytes_accessed=sum(a.size * a.dtype.itemsize for a in (*shapes, *operands)),
        ),
    )(*operands)


def load(
    features,
    labels,
    centres,
    ids,
    listed,
    copies_out,
    blocks_out,
    centres_out,
    ids_out,
    held_features,
    held_labels,
    held_ids,
    held_listed,
    arrived,
):
    moves = [
        pltpu.make_async_copy(source, target, arrived.at[i])
        for i, (source, target) in enumerate(
            (
                (features, held_features),
                (labels, held_labels),
                (ids, held_ids),
                (listed, held_listed),
                (ids, ids_out),
                (centres, centres_out),
            )
        )
    ]
    for move in moves:
        move.start()
    moves[0].wait()
    moves[1].wait()
    chip = lax.axis_index("chip")
    member = 2 * chip + lax.axis_index("core")
    copies, tok_dev, _ = copies_out.shape
    width = features.shape[1]
    rows = held_features[...].astype(jnp.float32)
    unit = (rows * inverse_norm(rows)).astype(jnp.bfloat16)
    copies_out[:, :, :width] = jnp.broadcast_to(unit[None], (copies, tok_dev, width))

    place = own_place() * tok_dev
    row = held_labels[...]
    row = jnp.concatenate([row, jnp.zeros((1, 128 - row.shape[1]), jnp.int32)], axis=1)
    row = jnp.broadcast_to(row, (tok_dev, 128))
    row = pltpu.roll(row, lax.rem(place - member * tok_dev + 128, 128), 1)
    digit = lax.broadcasted_iota(jnp.int32, (tok_dev, 128), 0)
    digits = (row >> (7 * jnp.minimum(digit, 3))) & 127
    lane = lanes(tok_dev)
    digits = jnp.where((lane >= place) & (lane < place + tok_dev), digits, 0)
    copies_out[:, :, width:] = jnp.broadcast_to(
        digits.astype(jnp.float32).astype(jnp.bfloat16)[None], (copies, tok_dev, 128)
    )
    for move in moves[2:]:
        move.wait()
    for g in range(blocks_out.shape[0]):
        group = group_at(g)
        block = centres_out[held_ids[0, group]]
        blocks_out[g] = jnp.where(held_listed[0, group] > 0, block, jnp.full_like(block, UNLISTED))


def group_at(place):
    return (place + FIRST_GROUP) % lax.axis_size("group")


def own_place():
    groups = lax.axis_size("group")
    group = lax.rem(lax.axis_index("group") + groups - FIRST_GROUP, groups)
    return group * lax.axis_size("chip") + lax.axis_index("chip")


def select(parts, rows):
    owner = lanes(1) // (128 // len(parts))
    out = jnp.broadcast_to(parts[0], (rows, 128))
    for g in range(1, len(parts)):
        out = jnp.where(owner == g, parts[g], out)
    return out


def exponentials(packed, own_blocks, pair_blocks, expo_out, pair_expo_out, inverse_out, sums_out):
    group, core = lax.axis_index("group"), lax.axis_index("core")
    groups, _, width = own_blocks.shape
    units = packed[:, :width]
    digits = jnp.sum(
        packed[:, width:].astype(jnp.float32).reshape(128 // 8, 8, 128), axis=0
    ).astype(jnp.int32)
    labels = digits[0:1] + (digits[1:2] << 7) + (digits[2:3] << 14)
    rest = jnp.zeros((1, 128), jnp.float32)
    at_label = jnp.zeros((1, 128), jnp.float32)
    for k, (blocks, out) in enumerate(((own_blocks, expo_out), (pair_blocks, pair_expo_out))):
        member = 2 * lax.axis_index("chip") + (core if k == 0 else 1 - core)
        first = (member * groups + group) * BLK
        onehot = lax.broadcasted_iota(jnp.int32, (BLK, 128), 0) == labels - first
        inverse = select(
            [inverse_norm(blocks[g].astype(jnp.float32)) for g in range(groups)], BLK
        )
        inverse_out[k] = inverse
        cosine = inverse * select([contract(blocks[g], units, 1, 1) for g in range(groups)], BLK)
        expo = jnp.exp(logit_scale * (cosine - jnp.where(onehot, cos_margin, 0.0)))
        expo = jnp.where(inverse > 0.0, expo, 0.0)
        out[...] = jnp.where(onehot, -1.0, expo)
        rest += jnp.sum(jnp.where(onehot, 0.0, expo), axis=0, keepdims=True)
        at_label += jnp.sum(jnp.where(onehot, expo, 0.0), axis=0, keepdims=True)
    sums_out[0:1, :] = rest
    sums_out[1:2, :] = at_label


def shares(own_expo, pair_expo, inverse, own_blocks, pair_blocks, centres, shares_out, norms_out):
    groups, _, width = own_blocks.shape
    per_group = 128 // groups
    others, label = [], []
    for k, expo in enumerate((own_expo[...], pair_expo[...])):
        others.append((jnp.maximum(expo, 0.0) * inverse[k]).T.astype(jnp.bfloat16))
        label.append(jnp.where(expo < 0.0, 1.0, 0.0).T.astype(jnp.bfloat16))
    others = jnp.concatenate(others, axis=1)
    label = jnp.concatenate(label, axis=1)
    for g in range(groups):
        here = slice(g * per_group, (g + 1) * per_group)
        blocks = jnp.concatenate([own_blocks[g], pair_blocks[g]], axis=0)
        both = contract(jnp.concatenate([others[here], label[here]], axis=0), blocks, 1, 0)
        both = both.astype(jnp.bfloat16)
        shares_out[here, :width] = both[:per_group]
        shares_out[here, width:] = both[per_group:]
    held = centres.shape[0]
    norms_out[...] = select(
        [inverse_norm(centres[b].astype(jnp.float32)) for b in range(held)], BLK
    )


def with_sums(shares, own_sums, other_sums, other_packed, other_expo, sent_out):
    del other_packed, other_expo
    rows, wide = shares.shape
    sent_out[:, :wide] = shares[...]
    total = jnp.concatenate([own_sums[...], other_sums[...]], axis=0)
    high = total.astype(jnp.bfloat16)
    low = (total - high.astype(jnp.float32)).astype(jnp.bfloat16)
    tile = jnp.concatenate([high.astype(jnp.float32), low.astype(jnp.float32)], axis=0)
    tile = jnp.broadcast_to(tile[None], (rows // 8, 8, 128))
    sent_out[:, wide:] = tile.reshape(rows, 128).astype(jnp.bfloat16)


def backward(
    ids,
    received,
    own_expo,
    other_expo,
    own_packed,
    other_packed,
    features,
    centres,
    norms,
    grad_out,
    feature_out,
    loss_out,
    grad,
    feature_grad,
    loss_row,
    left,
):
    groups = ids.shape[1]
    held = centres.shape[0]
    tok_dev, width = features.shape

    sums = received[0].astype(jnp.float32)
    for i in range(1, received.shape[0]):
        sums = sums + received[i].astype(jnp.float32)
    tile = sums[:, 2 * width :]
    tile = tile[:4] + tile[4:]
    own_rest, own_label = tile[0:1], tile[1:2]
    other_rest, other_label = tile[2:3], tile[3:4]

    units = jnp.concatenate([own_packed[:, :width], other_packed[:, :width]], axis=0)
    own_scale = logit_scale / (own_rest + own_label)
    other_scale = logit_scale / (other_rest + other_label)
    own = own_expo[...]
    other = other_expo[...]
    own = jnp.where(own < 0.0, -own_rest, own) * own_scale
    other = jnp.where(other < 0.0, -other_rest, other) * other_scale
    weights = jnp.concatenate([own, other], axis=1)
    named = select([ids[0, group_at(g)] for g in range(groups)], 1)
    named = jnp.concatenate([named, named], axis=1)
    mine = [jnp.where(named == b, weights, 0.0).astype(jnp.bfloat16) for b in range(held)]
    slot_grad = contract(jnp.concatenate(mine, axis=0), units, 1, 0)
    moves = []

    def leave(source, target):
        move = pltpu.make_async_copy(source, target, left.at[len(moves)])
        move.start()
        moves.append(move)

    def block_out(b):
        here = slot_grad[b * BLK : (b + 1) * BLK]
        factor = norms[:, b * (128 // held) : b * (128 // held) + 1]
        unit = centres[b].astype(jnp.float32) * factor
        along = jnp.sum(here * unit, axis=1, keepdims=True)
        grad[b] = factor * (here - along * unit)
        for part in (pl.ds(0, BLK // 2), pl.ds(BLK // 2, BLK // 2)):
            leave(grad.at[b, part], grad_out.at[b, part])

    for b in range(held // 2):
        block_out(b)

    sample = lax.broadcasted_iota(jnp.int32, (tok_dev, 128), 0) + own_place() * tok_dev
    mine = lanes(tok_dev) == sample
    rest = jnp.sum(jnp.where(mine, own_rest, 0.0), axis=1, keepdims=True)
    label = jnp.sum(jnp.where(mine, own_label, 0.0), axis=1, keepdims=True)
    total = rest + label
    loss = jnp.log(total) - jnp.log(label)
    square = (tok_dev, tok_dev)
    diagonal = lax.broadcasted_iota(jnp.int32, square, 0) == lax.broadcasted_iota(
        jnp.int32, square, 1
    )
    loss_row[...] = jnp.sum(jnp.where(diagonal, loss, 0.0), axis=0, keepdims=True)
    rows = features[...].astype(jnp.float32)
    inv_norm = inverse_norm(rows)
    unit = rows * inv_norm
    cand = sums[:, width : 2 * width]
    cand = (cand * inverse_norm(cand)).astype(jnp.bfloat16).astype(jnp.float32)
    unit_grad = logit_scale / total * (sums[:, :width] - rest * cand)
    along = jnp.sum(unit_grad * unit, axis=1, keepdims=True)
    feature_grad[...] = inv_norm * (unit_grad - along * unit)

    leave(feature_grad, feature_out)
    leave(loss_row, loss_out)
    for b in range(held // 2, held):
        block_out(b)
    for move in moves:
        move.wait()


def exchange(pieces, axes, order=None):
    return lax.all_to_all(
        pieces, axes, split_axis=0, concat_axis=0, axis_index_groups=order, tiled=True
    )


def exchange_chips(pieces):
    groups, chips = lax.axis_size("group"), lax.axis_size("chip")
    order = [group_at(g) * chips + chip for g in range(groups) for chip in range(chips)]
    return exchange(pieces, CHIPS, [order])


def with_partner(value):
    return lax.ppermute(value, "core", [(0, 1), (1, 0)])


def on_device(features, labels, centres, block_ids, listed):
    groups = lax.axis_size("group")
    chips = groups * lax.axis_size("chip")
    tok_dev, width = features.shape
    held = centres.shape[0] // BLK
    half = chips * tok_dev
    bf16, f32 = jnp.bfloat16, jnp.float32
    shape = jax.ShapeDtypeStruct

    copies, own_blocks, blocks, ids = run(
        load,
        (
            shape((chips, tok_dev, width + 128), bf16),
            shape((groups, BLK, width), bf16),
            shape((held, BLK, width), bf16),
            shape((1, groups), block_ids.dtype),
        ),
        [HBM] * 5,
        *(
            pltpu.with_memory_space_constraint(array, pltpu.HBM)
            for array in (
                features,
                labels.reshape(1, -1),
                centres.reshape(held, BLK, width),
                block_ids.reshape(1, groups),
                listed.reshape(1, groups),
            )
        ),
        scratch=[
            pltpu.VMEM(features.shape, features.dtype),
            pltpu.VMEM((1, labels.shape[0]), labels.dtype),
            pltpu.SMEM((1, groups), block_ids.dtype),
            pltpu.SMEM((1, groups), listed.dtype),
            pltpu.SemaphoreType.DMA((6,)),
        ],
    )
    pair_blocks = with_partner(own_blocks)
    own_packed = exchange_chips(copies).reshape(half, width + 128)
    other_packed = with_partner(own_packed)
    own_expo, pair_expo, inverse, sums = run(
        exponentials,
        (
            shape((BLK, half), f32),
            shape((BLK, half), f32),
            shape((2, BLK, 128), f32),
            shape((2, half), f32),
        ),
        [VMEM] * 3,
        own_packed,
        own_blocks,
        pair_blocks,
    )
    other_expo = with_partner(pair_expo)
    other_sums = with_partner(sums)
    going, norms = run(
        shares,
        (shape((half, 2 * width), bf16), shape((BLK, 128), f32)),
        [VMEM] * 6,
        own_expo,
        pair_expo,
        inverse,
        own_blocks,
        pair_blocks,
        blocks,
    )
    sent = run(
        with_sums,
        shape((half, 2 * width + 128), bf16),
        [VMEM] * 3 + [pl.BlockSpec(memory_space=pl.ANY)] * 2,
        going,
        sums,
        other_sums,
        other_packed,
        other_expo,
    )
    received = exchange_chips(sent.reshape(chips, tok_dev, 2 * width + 128))
    outs = (shape((held, BLK, width), f32), shape((tok_dev, width), f32), shape((1, tok_dev), f32))
    centre_grad, feature_grad, loss = run(
        backward,
        outs,
        [SMEM] + [VMEM] * 8,
        ids,
        received,
        own_expo,
        other_expo,
        own_packed,
        other_packed,
        features,
        blocks,
        norms,
        out_spec=HBM,
        scratch=[
            *(pltpu.VMEM(out.shape, out.dtype) for out in outs),
            pltpu.SemaphoreType.DMA((2 * held + 2,)),
        ],
    )
    return (loss.reshape(tok_dev), feature_grad, centre_grad.reshape(held * BLK, width))


def on_device_of_many(features, labels, centres, block_ids, listed):
    groups = lax.axis_size("group")
    members = lax.axis_size("member")
    devices = groups * members
    group = lax.axis_index("group")
    member = lax.axis_index("member")
    tok_dev, width = features.shape
    group_tok = members * tok_dev
    held = centres.shape[0] // BLK

    vectors = features.astype(jnp.float32)
    inv_norm = inverse_norm(vectors)
    unit_rows = vectors * inv_norm
    copies = jnp.broadcast_to(unit_rows.astype(jnp.bfloat16), (devices, tok_dev, width))
    units = exchange(copies, AXES).reshape(groups, group_tok, width)
    all_labels = exchange(jnp.broadcast_to(labels[None], (groups, group_tok)), "group")

    picked = centres.reshape(held, BLK, width)[block_ids[:, 0]].astype(jnp.float32)
    inv_cand = inverse_norm(picked)
    unit_cand = picked * inv_cand
    cand_half = unit_cand.astype(jnp.bfloat16)
    cosine = jnp.einsum("gsd,gcd->gsc", units, cand_half, preferred_element_type=jnp.float32)
    local_label = all_labels - (member * groups + group) * BLK
    onehot = (lax.broadcasted_iota(jnp.int32, (1, 1, BLK), 2) == local_label[:, :, None]).astype(
        jnp.float32
    )
    logits = logit_scale * (cosine - cos_margin * onehot)
    exp_logits = jnp.exp(logits) * listed.astype(jnp.float32)[:, :, None]
    totals, label_logit = lax.psum(
        (jnp.sum(exp_logits, axis=2), jnp.sum(logits * onehot, axis=2)), AXES
    )
    loss_all = (jnp.log(totals) - label_logit).reshape(devices, tok_dev)
    sample_loss = lax.dynamic_slice_in_dim(loss_all, group * members + member, 1, 0)[0]

    weights = (logit_scale * (exp_logits / totals[:, :, None] - onehot)).astype(jnp.bfloat16)
    partial = jnp.einsum("gsc,gcd->gsd", weights, cand_half, preferred_element_type=jnp.float32)
    home = exchange(partial.astype(jnp.bfloat16).reshape(devices, tok_dev, width), AXES)
    unit_grad = jnp.sum(home.astype(jnp.float32), axis=0)
    feature_grad = inv_norm * (
        unit_grad - jnp.sum(unit_grad * unit_rows, axis=1, keepdims=True) * unit_rows
    )
    slot_grad = jnp.einsum("gsc,gsd->gcd", weights, units, preferred_element_type=jnp.float32)
    cand_grad = inv_cand * (
        slot_grad - jnp.sum(slot_grad * unit_cand, axis=2, keepdims=True) * unit_cand
    )
    cand_grad = cand_grad.astype(jnp.bfloat16).astype(jnp.float32)
    names = block_ids == jnp.arange(held, dtype=jnp.int32)[None, :]
    centre_grad = jnp.sum(
        jnp.where(names[:, :, None, None], cand_grad[:, None], 0.0), axis=0
    ).reshape(held * BLK, width)
    return (sample_loss, feature_grad, centre_grad)


def on_axes(body, mesh, axes):
    split = P(axes)
    return jax.shard_map(
        body,
        mesh=mesh,
        in_specs=(split, P("group"), split, P(None, axes), P(None, axes)),
        out_specs=(split, split, split),
        check_vma=False,
    )


def solution(mesh):
    groups, members = mesh.shape["group"], mesh.shape["member"]
    by_core = jax.sharding.Mesh(
        mesh.devices.reshape(groups, members // 2, 2), ("group", "chip", "core")
    )

    def program(features, *others):
        half = features.shape[0] // 2
        if half == 128 and 2 * groups == features.shape[0] // mesh.size == 8:
            return on_axes(on_device, by_core, (*CHIPS, "core"))(features, *others)
        return on_axes(on_device_of_many, mesh, AXES)(features, *others)

    return program
```

```python
import jax
import jax.numpy as jnp
from jax import lax
from jax.experimental import pallas as pl
from jax.experimental.pallas import tpu as pltpu
from jax.sharding import PartitionSpec as P

BLK = 128
AXES = ("group", "member")
CHIPS = ("group", "chip")

logit_scale = 32.0
cos_margin = 0.35
norm_epsilon = 1e-06
FIRST_GROUP = 1
UNLISTED = 1e19

VMEM = pl.BlockSpec(memory_space=pltpu.VMEM)
HBM = pl.BlockSpec(memory_space=pltpu.HBM)


def inverse_norm(rows):
    return lax.rsqrt(jnp.sum(rows * rows, axis=-1, keepdims=True) + norm_epsilon)


def contract(left, right, left_dim, right_dim):
    dims = (((left_dim,), (right_dim,)), ((), ()))
    return lax.dot_general(left, right, dims, preferred_element_type=jnp.float32)


def lanes(rows):
    return lax.broadcasted_iota(jnp.int32, (rows, 128), 1)


def run(kernel, out_shape, in_specs, *operands, out_spec=VMEM, scratch=()):
    shapes = jax.tree.leaves(out_shape)
    return pl.pallas_call(
        kernel,
        out_shape=out_shape,
        in_specs=in_specs,
        out_specs=jax.tree.map(lambda _: out_spec, out_shape),
        scratch_shapes=scratch,
        compiler_params=pltpu.CompilerParams(vmem_limit_bytes=48 * 1024 * 1024),
        cost_estimate=pl.CostEstimate(
            flops=0,
            transcendentals=0,
            bytes_accessed=sum(a.size * a.dtype.itemsize for a in (*shapes, *operands)),
        ),
    )(*operands)


def load(
    features,
    labels,
    centres,
    ids,
    listed,
    copies_out,
    blocks_out,
    centres_out,
    named_out,
    held_features,
    held_labels,
    held_ids,
    held_listed,
    arrived,
):
    moves = [
        pltpu.make_async_copy(source, target, arrived.at[i])
        for i, (source, target) in enumerate(
            (
                (features, held_features),
                (labels, held_labels),
                (ids, held_ids),
                (listed, held_listed),
                *((centres.at[b], centres_out.at[b]) for b in range(centres.shape[0])),
            )
        )
    ]
    for move in moves:
        move.start()
    moves[0].wait()
    moves[1].wait()
    chip = lax.axis_index("chip")
    member = 2 * chip + lax.axis_index("core")
    copies, tok_dev, _ = copies_out.shape
    width = features.shape[1]
    rows = held_features[...].astype(jnp.float32)
    unit = (rows * inverse_norm(rows)).astype(jnp.bfloat16)
    copies_out[:, :, :width] = jnp.broadcast_to(unit[None], (copies, tok_dev, width))

    place = own_place() * tok_dev
    row = held_labels[...]
    row = jnp.concatenate([row, jnp.zeros((1, 128 - row.shape[1]), jnp.int32)], axis=1)
    row = jnp.broadcast_to(row, (tok_dev, 128))
    row = pltpu.roll(row, lax.rem(place - member * tok_dev + 128, 128), 1)
    digit = lax.broadcasted_iota(jnp.int32, (tok_dev, 128), 0)
    digits = (row >> (7 * jnp.minimum(digit, 3))) & 127
    lane = lanes(tok_dev)
    digits = jnp.where((lane >= place) & (lane < place + tok_dev), digits, 0)
    copies_out[:, :, width:] = jnp.broadcast_to(
        digits.astype(jnp.float32).astype(jnp.bfloat16)[None], (copies, tok_dev, 128)
    )
    for move in moves[2:]:
        move.wait()
    groups = blocks_out.shape[0]
    named_out[...] = select([held_ids[0, group_at(g)] for g in range(groups)], 1)
    for g in range(groups):
        group = group_at(g)
        block = centres_out[held_ids[0, group]]
        blocks_out[g] = jnp.where(held_listed[0, group] > 0, block, jnp.full_like(block, UNLISTED))


def group_at(place):
    return (place + FIRST_GROUP) % lax.axis_size("group")


def own_place():
    groups = lax.axis_size("group")
    group = lax.rem(lax.axis_index("group") + groups - FIRST_GROUP, groups)
    return group * lax.axis_size("chip") + lax.axis_index("chip")


def select(parts, rows):
    owner = lanes(1) // (128 // len(parts))
    out = jnp.broadcast_to(parts[0], (rows, 128))
    for g in range(1, len(parts)):
        out = jnp.where(owner == g, parts[g], out)
    return out


def exponentials(packed, own_blocks, pair_blocks, expo_out, pair_expo_out, inverse_out, sums_out):
    group, core = lax.axis_index("group"), lax.axis_index("core")
    groups, _, width = own_blocks.shape
    units = packed[:, :width]
    digits = jnp.sum(
        packed[:, width:].astype(jnp.float32).reshape(128 // 8, 8, 128), axis=0
    ).astype(jnp.int32)
    labels = digits[0:1] + (digits[1:2] << 7) + (digits[2:3] << 14)
    rest = jnp.zeros((1, 128), jnp.float32)
    at_label = jnp.zeros((1, 128), jnp.float32)
    for k, (blocks, out) in enumerate(((own_blocks, expo_out), (pair_blocks, pair_expo_out))):
        member = 2 * lax.axis_index("chip") + (core if k == 0 else 1 - core)
        first = (member * groups + group) * BLK
        onehot = lax.broadcasted_iota(jnp.int32, (BLK, 128), 0) == labels - first
        inverse = select(
            [inverse_norm(blocks[g].astype(jnp.float32)) for g in range(groups)], BLK
        )
        inverse_out[k] = inverse
        cosine = inverse * select([contract(blocks[g], units, 1, 1) for g in range(groups)], BLK)
        expo = jnp.exp(logit_scale * (cosine - jnp.where(onehot, cos_margin, 0.0)))
        expo = jnp.where(inverse > 0.0, expo, 0.0)
        out[...] = jnp.where(onehot, -1.0, expo)
        rest += jnp.sum(jnp.where(onehot, 0.0, expo), axis=0, keepdims=True)
        at_label += jnp.sum(jnp.where(onehot, expo, 0.0), axis=0, keepdims=True)
    sums_out[0:1, :] = rest
    sums_out[1:2, :] = at_label


def shares(own_expo, pair_expo, inverse, own_blocks, pair_blocks, centres, shares_out, norms_out):
    groups, _, width = own_blocks.shape
    per_group = 128 // groups
    others, label = [], []
    for k, expo in enumerate((own_expo[...], pair_expo[...])):
        others.append((jnp.maximum(expo, 0.0) * inverse[k]).T.astype(jnp.bfloat16))
        label.append(jnp.where(expo < 0.0, 1.0, 0.0).T.astype(jnp.bfloat16))
    others = jnp.concatenate(others, axis=1)
    label = jnp.concatenate(label, axis=1)
    for g in range(groups):
        here = slice(g * per_group, (g + 1) * per_group)
        blocks = jnp.concatenate([own_blocks[g], pair_blocks[g]], axis=0)
        both = contract(jnp.concatenate([others[here], label[here]], axis=0), blocks, 1, 0)
        both = both.astype(jnp.bfloat16)
        shares_out[here, :width] = both[:per_group]
        shares_out[here, width:] = both[per_group:]
    held = centres.shape[0]
    norms_out[...] = select(
        [inverse_norm(centres[b].astype(jnp.float32)) for b in range(held)], BLK
    )


def with_sums(shares, own_sums, other_sums, other_packed, other_expo, sent_out):
    del other_packed, other_expo
    rows, wide = shares.shape
    sent_out[:, :wide] = shares[...]
    total = jnp.concatenate([own_sums[...], other_sums[...]], axis=0)
    high = total.astype(jnp.bfloat16)
    low = (total - high.astype(jnp.float32)).astype(jnp.bfloat16)
    tile = jnp.concatenate([high.astype(jnp.float32), low.astype(jnp.float32)], axis=0)
    tile = jnp.broadcast_to(tile[None], (rows // 8, 8, 128))
    sent_out[:, wide:] = tile.reshape(rows, 128).astype(jnp.bfloat16)


def backward(
    named,
    received,
    own_expo,
    other_expo,
    own_packed,
    other_packed,
    features,
    centres,
    norms,
    grad_out,
    feature_out,
    loss_out,
    grad,
    feature_grad,
    loss_row,
    left,
):
    held = centres.shape[0]
    tok_dev, width = features.shape

    sums = received[0].astype(jnp.float32)
    for i in range(1, received.shape[0]):
        sums = sums + received[i].astype(jnp.float32)
    tile = sums[:, 2 * width :]
    tile = tile[:4] + tile[4:]
    own_rest, own_label = tile[0:1], tile[1:2]
    other_rest, other_label = tile[2:3], tile[3:4]

    units = jnp.concatenate([own_packed[:, :width], other_packed[:, :width]], axis=0)
    own_scale = logit_scale / (own_rest + own_label)
    other_scale = logit_scale / (other_rest + other_label)
    own = own_expo[...]
    other = other_expo[...]
    own = jnp.where(own < 0.0, -own_rest, own) * own_scale
    other = jnp.where(other < 0.0, -other_rest, other) * other_scale
    weights = jnp.concatenate([own, other], axis=1)
    named = jnp.concatenate([named[...], named[...]], axis=1)
    mine = [jnp.where(named == b, weights, 0.0).astype(jnp.bfloat16) for b in range(held)]
    slot_grad = contract(jnp.concatenate(mine, axis=0), units, 1, 0)
    moves = []

    def leave(source, target):
        move = pltpu.make_async_copy(source, target, left.at[len(moves)])
        move.start()
        moves.append(move)

    def block_out(b):
        here = slot_grad[b * BLK : (b + 1) * BLK]
        factor = norms[:, b * (128 // held) : b * (128 // held) + 1]
        unit = centres[b].astype(jnp.float32) * factor
        along = jnp.sum(here * unit, axis=1, keepdims=True)
        grad[b] = factor * (here - along * unit)
        for part in (pl.ds(0, BLK // 2), pl.ds(BLK // 2, BLK // 2)):
            leave(grad.at[b, part], grad_out.at[b, part])

    for b in range(held // 2):
        block_out(b)

    sample = lax.broadcasted_iota(jnp.int32, (tok_dev, 128), 0) + own_place() * tok_dev
    mine = lanes(tok_dev) == sample
    rest = jnp.sum(jnp.where(mine, own_rest, 0.0), axis=1, keepdims=True)
    label = jnp.sum(jnp.where(mine, own_label, 0.0), axis=1, keepdims=True)
    total = rest + label
    loss = jnp.log(total) - jnp.log(label)
    square = (tok_dev, tok_dev)
    diagonal = lax.broadcasted_iota(jnp.int32, square, 0) == lax.broadcasted_iota(
        jnp.int32, square, 1
    )
    loss_row[...] = jnp.sum(jnp.where(diagonal, loss, 0.0), axis=0, keepdims=True)
    rows = features[...].astype(jnp.float32)
    inv_norm = inverse_norm(rows)
    unit = rows * inv_norm
    cand = sums[:, width : 2 * width]
    cand = (cand * inverse_norm(cand)).astype(jnp.bfloat16).astype(jnp.float32)
    unit_grad = logit_scale / total * (sums[:, :width] - rest * cand)
    along = jnp.sum(unit_grad * unit, axis=1, keepdims=True)
    feature_grad[...] = inv_norm * (unit_grad - along * unit)

    leave(feature_grad, feature_out)
    leave(loss_row, loss_out)
    for b in range(held // 2, held):
        block_out(b)
    for move in moves:
        move.wait()


def exchange(pieces, axes, order=None):
    return lax.all_to_all(
        pieces, axes, split_axis=0, concat_axis=0, axis_index_groups=order, tiled=True
    )


def exchange_chips(pieces):
    groups, chips = lax.axis_size("group"), lax.axis_size("chip")
    order = [group_at(g) * chips + chip for g in range(groups) for chip in range(chips)]
    return exchange(pieces, CHIPS, [order])


def with_partner(value):
    return lax.ppermute(value, "core", [(0, 1), (1, 0)])


def on_device(features, labels, centres, block_ids, listed):
    groups = lax.axis_size("group")
    chips = groups * lax.axis_size("chip")
    tok_dev, width = features.shape
    held = centres.shape[0] // BLK
    half = chips * tok_dev
    bf16, f32 = jnp.bfloat16, jnp.float32
    shape = jax.ShapeDtypeStruct

    copies, own_blocks, blocks, named = run(
        load,
        (
            shape((chips, tok_dev, width + 128), bf16),
            shape((groups, BLK, width), bf16),
            shape((held, BLK, width), bf16),
            shape((1, 128), block_ids.dtype),
        ),
        [HBM] * 5,
        *(
            pltpu.with_memory_space_constraint(array, pltpu.HBM)
            for array in (
                features,
                labels.reshape(1, -1),
                centres.reshape(held, BLK, width),
                block_ids.reshape(1, groups),
                listed.reshape(1, groups),
            )
        ),
        scratch=[
            pltpu.VMEM(features.shape, features.dtype),
            pltpu.VMEM((1, labels.shape[0]), labels.dtype),
            pltpu.SMEM((1, groups), block_ids.dtype),
            pltpu.SMEM((1, groups), listed.dtype),
            pltpu.SemaphoreType.DMA((4 + held,)),
        ],
    )
    pair_blocks = with_partner(own_blocks)
    own_packed = exchange_chips(copies).reshape(half, width + 128)
    other_packed = with_partner(own_packed)
    own_expo, pair_expo, inverse, sums = run(
        exponentials,
        (
            shape((BLK, half), f32),
            shape((BLK, half), f32),
            shape((2, BLK, 128), f32),
            shape((2, half), f32),
        ),
        [VMEM] * 3,
        own_packed,
        own_blocks,
        pair_blocks,
    )
    other_expo = with_partner(pair_expo)
    other_sums = with_partner(sums)
    going, norms = run(
        shares,
        (shape((half, 2 * width), bf16), shape((BLK, 128), f32)),
        [VMEM] * 6,
        own_expo,
        pair_expo,
        inverse,
        own_blocks,
        pair_blocks,
        blocks,
    )
    sent = run(
        with_sums,
        shape((half, 2 * width + 128), bf16),
        [VMEM] * 3 + [pl.BlockSpec(memory_space=pl.ANY)] * 2,
        going,
        sums,
        other_sums,
        other_packed,
        other_expo,
    )
    received = exchange_chips(sent.reshape(chips, tok_dev, 2 * width + 128))
    outs = (shape((held, BLK, width), f32), shape((tok_dev, width), f32), shape((1, tok_dev), f32))
    centre_grad, feature_grad, loss = run(
        backward,
        outs,
        [VMEM] * 9,
        named,
        received,
        own_expo,
        other_expo,
        own_packed,
        other_packed,
        features,
        blocks,
        norms,
        out_spec=HBM,
        scratch=[
            *(pltpu.VMEM(out.shape, out.dtype) for out in outs),
            pltpu.SemaphoreType.DMA((2 * held + 2,)),
        ],
    )
    return (loss.reshape(tok_dev), feature_grad, centre_grad.reshape(held * BLK, width))


def on_device_of_many(features, labels, centres, block_ids, listed):
    groups = lax.axis_size("group")
    members = lax.axis_size("member")
    devices = groups * members
    group = lax.axis_index("group")
    member = lax.axis_index("member")
    tok_dev, width = features.shape
    group_tok = members * tok_dev
    held = centres.shape[0] // BLK

    vectors = features.astype(jnp.float32)
    inv_norm = inverse_norm(vectors)
    unit_rows = vectors * inv_norm
    copies = jnp.broadcast_to(unit_rows.astype(jnp.bfloat16), (devices, tok_dev, width))
    units = exchange(copies, AXES).reshape(groups, group_tok, width)
    all_labels = exchange(jnp.broadcast_to(labels[None], (groups, group_tok)), "group")

    picked = centres.reshape(held, BLK, width)[block_ids[:, 0]].astype(jnp.float32)
    inv_cand = inverse_norm(picked)
    unit_cand = picked * inv_cand
    cand_half = unit_cand.astype(jnp.bfloat16)
    cosine = jnp.einsum("gsd,gcd->gsc", units, cand_half, preferred_element_type=jnp.float32)
    local_label = all_labels - (member * groups + group) * BLK
    onehot = (lax.broadcasted_iota(jnp.int32, (1, 1, BLK), 2) == local_label[:, :, None]).astype(
        jnp.float32
    )
    logits = logit_scale * (cosine - cos_margin * onehot)
    exp_logits = jnp.exp(logits) * listed.astype(jnp.float32)[:, :, None]
    totals, label_logit = lax.psum(
        (jnp.sum(exp_logits, axis=2), jnp.sum(logits * onehot, axis=2)), AXES
    )
    loss_all = (jnp.log(totals) - label_logit).reshape(devices, tok_dev)
    sample_loss = lax.dynamic_slice_in_dim(loss_all, group * members + member, 1, 0)[0]

    weights = (logit_scale * (exp_logits / totals[:, :, None] - onehot)).astype(jnp.bfloat16)
    partial = jnp.einsum("gsc,gcd->gsd", weights, cand_half, preferred_element_type=jnp.float32)
    home = exchange(partial.astype(jnp.bfloat16).reshape(devices, tok_dev, width), AXES)
    unit_grad = jnp.sum(home.astype(jnp.float32), axis=0)
    feature_grad = inv_norm * (
        unit_grad - jnp.sum(unit_grad * unit_rows, axis=1, keepdims=True) * unit_rows
    )
    slot_grad = jnp.einsum("gsc,gsd->gcd", weights, units, preferred_element_type=jnp.float32)
    cand_grad = inv_cand * (
        slot_grad - jnp.sum(slot_grad * unit_cand, axis=2, keepdims=True) * unit_cand
    )
    cand_grad = cand_grad.astype(jnp.bfloat16).astype(jnp.float32)
    names = block_ids == jnp.arange(held, dtype=jnp.int32)[None, :]
    centre_grad = jnp.sum(
        jnp.where(names[:, :, None, None], cand_grad[:, None], 0.0), axis=0
    ).reshape(held * BLK, width)
    return (sample_loss, feature_grad, centre_grad)


def on_axes(body, mesh, axes):
    split = P(axes)
    return jax.shard_map(
        body,
        mesh=mesh,
        in_specs=(split, P("group"), split, P(None, axes), P(None, axes)),
        out_specs=(split, split, split),
        check_vma=False,
    )


def solution(mesh):
    groups, members = mesh.shape["group"], mesh.shape["member"]
    by_core = jax.sharding.Mesh(
        mesh.devices.reshape(groups, members // 2, 2), ("group", "chip", "core")
    )

    def program(features, *others):
        half = features.shape[0] // 2
        if half == 128 and 2 * groups == features.shape[0] // mesh.size == 8:
            return on_axes(on_device, by_core, (*CHIPS, "core"))(features, *others)
        return on_axes(on_device_of_many, mesh, AXES)(features, *others)

    return program
```

```python
import jax
import jax.numpy as jnp
from jax import lax
from jax.experimental import pallas as pl
from jax.experimental.pallas import tpu as pltpu
from jax.sharding import PartitionSpec as P

BLK = 128
AXES = ("group", "member")
CHIPS = ("group", "chip")

logit_scale = 32.0
cos_margin = 0.35
norm_epsilon = 1e-06
FIRST_GROUP = 1
UNLISTED = 1e19

VMEM = pl.BlockSpec(memory_space=pltpu.VMEM)
HBM = pl.BlockSpec(memory_space=pltpu.HBM)


def inverse_norm(rows):
    return lax.rsqrt(jnp.sum(rows * rows, axis=-1, keepdims=True) + norm_epsilon)


def contract(left, right, left_dim, right_dim):
    dims = (((left_dim,), (right_dim,)), ((), ()))
    return lax.dot_general(left, right, dims, preferred_element_type=jnp.float32)


def lanes(rows):
    return lax.broadcasted_iota(jnp.int32, (rows, 128), 1)


def run(kernel, out_shape, in_specs, *operands, out_spec=VMEM, scratch=()):
    shapes = jax.tree.leaves(out_shape)
    return pl.pallas_call(
        kernel,
        out_shape=out_shape,
        in_specs=in_specs,
        out_specs=jax.tree.map(lambda _: out_spec, out_shape),
        scratch_shapes=scratch,
        compiler_params=pltpu.CompilerParams(vmem_limit_bytes=48 * 1024 * 1024),
        cost_estimate=pl.CostEstimate(
            flops=0,
            transcendentals=0,
            bytes_accessed=sum(a.size * a.dtype.itemsize for a in (*shapes, *operands)),
        ),
    )(*operands)


def load(
    features,
    labels,
    centres,
    ids,
    listed,
    copies_out,
    blocks_out,
    centres_out,
    named_out,
    held_features,
    held_labels,
    held_ids,
    held_listed,
    arrived,
):
    moves = [
        pltpu.make_async_copy(source, target, arrived.at[i])
        for i, (source, target) in enumerate(
            (
                (features, held_features),
                (labels, held_labels),
                (ids, held_ids),
                (listed, held_listed),
                *((centres.at[b], centres_out.at[b]) for b in range(centres.shape[0])),
            )
        )
    ]
    for move in moves:
        move.start()
    moves[0].wait()
    moves[1].wait()
    chip = lax.axis_index("chip")
    member = 2 * chip + lax.axis_index("core")
    copies, tok_dev, _ = copies_out.shape
    width = features.shape[1]
    rows = held_features[...].astype(jnp.float32)
    unit = (rows * inverse_norm(rows)).astype(jnp.bfloat16)
    copies_out[:, :, :width] = jnp.broadcast_to(unit[None], (copies, tok_dev, width))

    place = own_place() * tok_dev
    row = held_labels[...]
    row = jnp.concatenate([row, jnp.zeros((1, 128 - row.shape[1]), jnp.int32)], axis=1)
    row = jnp.broadcast_to(row, (tok_dev, 128))
    row = pltpu.roll(row, lax.rem(place - member * tok_dev + 128, 128), 1)
    digit = lax.broadcasted_iota(jnp.int32, (tok_dev, 128), 0)
    digits = (row >> (7 * jnp.minimum(digit, 3))) & 127
    lane = lanes(tok_dev)
    digits = jnp.where((lane >= place) & (lane < place + tok_dev), digits, 0)
    copies_out[:, :, width:] = jnp.broadcast_to(
        digits.astype(jnp.float32).astype(jnp.bfloat16)[None], (copies, tok_dev, 128)
    )
    for move in moves[2:]:
        move.wait()
    groups, held = blocks_out.shape[0], centres_out.shape[0]
    order = [group_at(g) for g in range(groups)]
    named = [held_ids[:, group : group + 1] for group in order]
    named_out[...] = select(named, 1)
    for g, group in enumerate(order):
        block = jnp.full(blocks_out.shape[1:], UNLISTED, jnp.bfloat16)
        block_id = jnp.where(held_listed[:, group : group + 1] > 0, named[g], -1)
        for b in range(held):
            here = jnp.broadcast_to(block_id, (BLK, 1)) == b
            block = jnp.where(here, centres_out[b], block)
        blocks_out[g] = block


def group_at(place):
    return (place + FIRST_GROUP) % lax.axis_size("group")


def own_place():
    groups = lax.axis_size("group")
    group = lax.rem(lax.axis_index("group") + groups - FIRST_GROUP, groups)
    return group * lax.axis_size("chip") + lax.axis_index("chip")


def select(parts, rows):
    owner = lanes(1) // (128 // len(parts))
    out = jnp.broadcast_to(parts[0], (rows, 128))
    for g in range(1, len(parts)):
        out = jnp.where(owner == g, parts[g], out)
    return out


def exponentials(packed, own_blocks, pair_blocks, expo_out, inverse_out, swap_out):
    group, core = lax.axis_index("group"), lax.axis_index("core")
    groups, _, width = own_blocks.shape
    units = packed[:, :width]
    digits = jnp.sum(
        packed[:, width:].astype(jnp.float32).reshape(128 // 8, 8, 128), axis=0
    ).astype(jnp.int32)
    labels = digits[0:1] + (digits[1:2] << 7) + (digits[2:3] << 14)
    rest = jnp.zeros((1, 128), jnp.float32)
    at_label = jnp.zeros((1, 128), jnp.float32)
    for k, (blocks, out) in enumerate(((own_blocks, expo_out), (pair_blocks, swap_out))):
        member = 2 * lax.axis_index("chip") + (core if k == 0 else 1 - core)
        first = (member * groups + group) * BLK
        onehot = lax.broadcasted_iota(jnp.int32, (BLK, 128), 0) == labels - first
        inverse = select(
            [inverse_norm(blocks[g].astype(jnp.float32)) for g in range(groups)], BLK
        )
        inverse_out[k] = inverse
        cosine = inverse * select([contract(blocks[g], units, 1, 1) for g in range(groups)], BLK)
        expo = jnp.exp(logit_scale * (cosine - jnp.where(onehot, cos_margin, 0.0)))
        expo = jnp.where(inverse > 0.0, expo, 0.0)
        out[:BLK, :] = jnp.where(onehot, -1.0, expo)
        rest += jnp.sum(jnp.where(onehot, 0.0, expo), axis=0, keepdims=True)
        at_label += jnp.sum(jnp.where(onehot, expo, 0.0), axis=0, keepdims=True)
    row = lax.broadcasted_iota(jnp.int32, (8, 128), 0)
    swap_out[BLK:, :] = jnp.where(row == 0, rest, jnp.where(row == 1, at_label, 0.0))


def shares(own_expo, swap, inverse, own_blocks, pair_blocks, centres, shares_out, norms_out):
    groups, _, width = own_blocks.shape
    per_group = 128 // groups
    others, label = [], []
    for k, expo in enumerate((own_expo[...], swap[:BLK, :])):
        others.append((jnp.maximum(expo, 0.0) * inverse[k]).T.astype(jnp.bfloat16))
        label.append(jnp.where(expo < 0.0, 1.0, 0.0).T.astype(jnp.bfloat16))
    others = jnp.concatenate(others, axis=1)
    label = jnp.concatenate(label, axis=1)
    for g in range(groups):
        here = slice(g * per_group, (g + 1) * per_group)
        blocks = jnp.concatenate([own_blocks[g], pair_blocks[g]], axis=0)
        both = contract(jnp.concatenate([others[here], label[here]], axis=0), blocks, 1, 0)
        both = both.astype(jnp.bfloat16)
        shares_out[here, :width] = both[:per_group]
        shares_out[here, width:] = both[per_group:]
    held = centres.shape[0]
    norms_out[...] = select(
        [inverse_norm(centres[b].astype(jnp.float32)) for b in range(held)], BLK
    )


def with_sums(shares, swap, swapped, other_packed, sent_out):
    del other_packed
    rows, wide = shares.shape
    sent_out[:, :wide] = shares[...]
    total = jnp.concatenate([swap[BLK : BLK + 2, :], swapped[BLK : BLK + 2, :]], axis=0)
    high = total.astype(jnp.bfloat16)
    low = (total - high.astype(jnp.float32)).astype(jnp.bfloat16)
    tile = jnp.concatenate([high.astype(jnp.float32), low.astype(jnp.float32)], axis=0)
    tile = jnp.broadcast_to(tile[None], (rows // 8, 8, 128))
    sent_out[:, wide:] = tile.reshape(rows, 128).astype(jnp.bfloat16)


def backward(
    named,
    received,
    own_expo,
    swapped,
    own_packed,
    other_packed,
    features,
    centres,
    norms,
    grad_out,
    feature_out,
    loss_out,
    grad,
    feature_grad,
    loss_row,
    left,
):
    held = centres.shape[0]
    tok_dev, width = features.shape

    sums = received[0].astype(jnp.float32)
    for i in range(1, received.shape[0]):
        sums = sums + received[i].astype(jnp.float32)
    tile = sums[:, 2 * width :]
    tile = tile[:4] + tile[4:]
    own_rest, own_label = tile[0:1], tile[1:2]
    other_rest, other_label = tile[2:3], tile[3:4]

    units = jnp.concatenate([own_packed[:, :width], other_packed[:, :width]], axis=0)
    own_scale = logit_scale / (own_rest + own_label)
    other_scale = logit_scale / (other_rest + other_label)
    own = own_expo[...]
    other = swapped[:BLK, :]
    own = jnp.where(own < 0.0, -own_rest, own) * own_scale
    other = jnp.where(other < 0.0, -other_rest, other) * other_scale
    weights = jnp.concatenate([own, other], axis=1)
    named = jnp.concatenate([named[...], named[...]], axis=1)
    mine = [jnp.where(named == b, weights, 0.0).astype(jnp.bfloat16) for b in range(held)]
    slot_grad = contract(jnp.concatenate(mine, axis=0), units, 1, 0)
    moves = []

    def leave(source, target):
        move = pltpu.make_async_copy(source, target, left.at[len(moves)])
        move.start()
        moves.append(move)

    def block_out(b):
        here = slot_grad[b * BLK : (b + 1) * BLK]
        factor = norms[:, b * (128 // held) : b * (128 // held) + 1]
        unit = centres[b].astype(jnp.float32) * factor
        along = jnp.sum(here * unit, axis=1, keepdims=True)
        grad[b] = factor * (here - along * unit)
        for part in (pl.ds(0, BLK // 2), pl.ds(BLK // 2, BLK // 2)):
            leave(grad.at[b, part], grad_out.at[b, part])

    for b in range(held // 2):
        block_out(b)

    sample = lax.broadcasted_iota(jnp.int32, (tok_dev, 128), 0) + own_place() * tok_dev
    mine = lanes(tok_dev) == sample
    rest = jnp.sum(jnp.where(mine, own_rest, 0.0), axis=1, keepdims=True)
    label = jnp.sum(jnp.where(mine, own_label, 0.0), axis=1, keepdims=True)
    total = rest + label
    loss = jnp.log(total) - jnp.log(label)
    square = (tok_dev, tok_dev)
    diagonal = lax.broadcasted_iota(jnp.int32, square, 0) == lax.broadcasted_iota(
        jnp.int32, square, 1
    )
    loss_row[...] = jnp.sum(jnp.where(diagonal, loss, 0.0), axis=0, keepdims=True)
    rows = features[...].astype(jnp.float32)
    inv_norm = inverse_norm(rows)
    unit = rows * inv_norm
    cand = sums[:, width : 2 * width]
    cand = (cand * inverse_norm(cand)).astype(jnp.bfloat16).astype(jnp.float32)
    unit_grad = logit_scale / total * (sums[:, :width] - rest * cand)
    along = jnp.sum(unit_grad * unit, axis=1, keepdims=True)
    feature_grad[...] = inv_norm * (unit_grad - along * unit)

    leave(feature_grad, feature_out)
    leave(loss_row, loss_out)
    for b in range(held // 2, held):
        block_out(b)
    for move in moves:
        move.wait()


def exchange(pieces, axes, order=None):
    return lax.all_to_all(
        pieces, axes, split_axis=0, concat_axis=0, axis_index_groups=order, tiled=True
    )


def exchange_chips(pieces):
    groups, chips = lax.axis_size("group"), lax.axis_size("chip")
    order = [group_at(g) * chips + chip for g in range(groups) for chip in range(chips)]
    return exchange(pieces, CHIPS, [order])


def with_partner(value):
    return lax.ppermute(value, "core", [(0, 1), (1, 0)])


def on_device(features, labels, centres, block_ids, listed):
    groups = lax.axis_size("group")
    chips = groups * lax.axis_size("chip")
    tok_dev, width = features.shape
    held = centres.shape[0] // BLK
    half = chips * tok_dev
    bf16, f32 = jnp.bfloat16, jnp.float32
    shape = jax.ShapeDtypeStruct

    copies, own_blocks, blocks, named = run(
        load,
        (
            shape((chips, tok_dev, width + 128), bf16),
            shape((groups, BLK, width), bf16),
            shape((held, BLK, width), bf16),
            shape((1, 128), block_ids.dtype),
        ),
        [HBM] * 5,
        *(
            pltpu.with_memory_space_constraint(array, pltpu.HBM)
            for array in (
                features,
                labels.reshape(1, -1),
                centres.reshape(held, BLK, width),
                block_ids.reshape(1, groups),
                listed.reshape(1, groups),
            )
        ),
        scratch=[
            pltpu.VMEM(features.shape, features.dtype),
            pltpu.VMEM((1, labels.shape[0]), labels.dtype),
            pltpu.VMEM((1, groups), block_ids.dtype),
            pltpu.VMEM((1, groups), listed.dtype),
            pltpu.SemaphoreType.DMA((4 + held,)),
        ],
    )
    pair_blocks = with_partner(own_blocks)
    own_packed = exchange_chips(copies).reshape(half, width + 128)
    other_packed = with_partner(own_packed)
    own_expo, inverse, swap = run(
        exponentials,
        (shape((BLK, half), f32), shape((2, BLK, 128), f32), shape((BLK + 8, half), f32)),
        [VMEM] * 3,
        own_packed,
        own_blocks,
        pair_blocks,
    )
    swapped = with_partner(swap)
    going, norms = run(
        shares,
        (shape((half, 2 * width), bf16), shape((BLK, 128), f32)),
        [VMEM] * 6,
        own_expo,
        swap,
        inverse,
        own_blocks,
        pair_blocks,
        blocks,
    )
    sent = run(
        with_sums,
        shape((half, 2 * width + 128), bf16),
        [VMEM] * 3 + [pl.BlockSpec(memory_space=pl.ANY)],
        going,
        swap,
        swapped,
        other_packed,
    )
    received = exchange_chips(sent.reshape(chips, tok_dev, 2 * width + 128))
    outs = (shape((held, BLK, width), f32), shape((tok_dev, width), f32), shape((1, tok_dev), f32))
    centre_grad, feature_grad, loss = run(
        backward,
        outs,
        [VMEM] * 9,
        named,
        received,
        own_expo,
        swapped,
        own_packed,
        other_packed,
        features,
        blocks,
        norms,
        out_spec=HBM,
        scratch=[
            *(pltpu.VMEM(out.shape, out.dtype) for out in outs),
            pltpu.SemaphoreType.DMA((2 * held + 2,)),
        ],
    )
    return (loss.reshape(tok_dev), feature_grad, centre_grad.reshape(held * BLK, width))


def on_device_of_many(features, labels, centres, block_ids, listed):
    groups = lax.axis_size("group")
    members = lax.axis_size("member")
    devices = groups * members
    group = lax.axis_index("group")
    member = lax.axis_index("member")
    tok_dev, width = features.shape
    group_tok = members * tok_dev
    held = centres.shape[0] // BLK

    vectors = features.astype(jnp.float32)
    inv_norm = inverse_norm(vectors)
    unit_rows = vectors * inv_norm
    copies = jnp.broadcast_to(unit_rows.astype(jnp.bfloat16), (devices, tok_dev, width))
    units = exchange(copies, AXES).reshape(groups, group_tok, width)
    all_labels = exchange(jnp.broadcast_to(labels[None], (groups, group_tok)), "group")

    picked = centres.reshape(held, BLK, width)[block_ids[:, 0]].astype(jnp.float32)
    inv_cand = inverse_norm(picked)
    unit_cand = picked * inv_cand
    cand_half = unit_cand.astype(jnp.bfloat16)
    cosine = jnp.einsum("gsd,gcd->gsc", units, cand_half, preferred_element_type=jnp.float32)
    local_label = all_labels - (member * groups + group) * BLK
    onehot = (lax.broadcasted_iota(jnp.int32, (1, 1, BLK), 2) == local_label[:, :, None]).astype(
        jnp.float32
    )
    logits = logit_scale * (cosine - cos_margin * onehot)
    exp_logits = jnp.exp(logits) * listed.astype(jnp.float32)[:, :, None]
    totals, label_logit = lax.psum(
        (jnp.sum(exp_logits, axis=2), jnp.sum(logits * onehot, axis=2)), AXES
    )
    loss_all = (jnp.log(totals) - label_logit).reshape(devices, tok_dev)
    sample_loss = lax.dynamic_slice_in_dim(loss_all, group * members + member, 1, 0)[0]

    weights = (logit_scale * (exp_logits / totals[:, :, None] - onehot)).astype(jnp.bfloat16)
    partial = jnp.einsum("gsc,gcd->gsd", weights, cand_half, preferred_element_type=jnp.float32)
    home = exchange(partial.astype(jnp.bfloat16).reshape(devices, tok_dev, width), AXES)
    unit_grad = jnp.sum(home.astype(jnp.float32), axis=0)
    feature_grad = inv_norm * (
        unit_grad - jnp.sum(unit_grad * unit_rows, axis=1, keepdims=True) * unit_rows
    )
    slot_grad = jnp.einsum("gsc,gsd->gcd", weights, units, preferred_element_type=jnp.float32)
    cand_grad = inv_cand * (
        slot_grad - jnp.sum(slot_grad * unit_cand, axis=2, keepdims=True) * unit_cand
    )
    cand_grad = cand_grad.astype(jnp.bfloat16).astype(jnp.float32)
    names = block_ids == jnp.arange(held, dtype=jnp.int32)[None, :]
    centre_grad = jnp.sum(
        jnp.where(names[:, :, None, None], cand_grad[:, None], 0.0), axis=0
    ).reshape(held * BLK, width)
    return (sample_loss, feature_grad, centre_grad)


def on_axes(body, mesh, axes):
    split = P(axes)
    return jax.shard_map(
        body,
        mesh=mesh,
        in_specs=(split, P("group"), split, P(None, axes), P(None, axes)),
        out_specs=(split, split, split),
        check_vma=False,
    )


def solution(mesh):
    groups, members = mesh.shape["group"], mesh.shape["member"]
    by_core = jax.sharding.Mesh(
        mesh.devices.reshape(groups, members // 2, 2), ("group", "chip", "core")
    )

    def program(features, *others):
        half = features.shape[0] // 2
        if half == 128 and 2 * groups == features.shape[0] // mesh.size == 8:
            return on_axes(on_device, by_core, (*CHIPS, "core"))(features, *others)
        return on_axes(on_device_of_many, mesh, AXES)(features, *others)

    return program
```

```python
import jax
import jax.numpy as jnp
from jax import lax
from jax.experimental import pallas as pl
from jax.experimental.pallas import tpu as pltpu
from jax.sharding import PartitionSpec as P

BLK = 128
AXES = ("group", "member")
CHIPS = ("group", "chip")

logit_scale = 32.0
cos_margin = 0.35
norm_epsilon = 1e-06
UNLISTED = 1e19

VMEM = pl.BlockSpec(memory_space=pltpu.VMEM)
HBM = pl.BlockSpec(memory_space=pltpu.HBM)


def inverse_norm(rows):
    return lax.rsqrt(jnp.sum(rows * rows, axis=-1, keepdims=True) + norm_epsilon)


def contract(left, right, left_dim, right_dim):
    dims = (((left_dim,), (right_dim,)), ((), ()))
    return lax.dot_general(left, right, dims, preferred_element_type=jnp.float32)


def lanes(rows):
    return lax.broadcasted_iota(jnp.int32, (rows, 128), 1)


def run(kernel, out_shape, in_specs, *operands, out_spec=VMEM, scratch=()):
    shapes = jax.tree.leaves(out_shape)
    return pl.pallas_call(
        kernel,
        out_shape=out_shape,
        in_specs=in_specs,
        out_specs=jax.tree.map(lambda _: out_spec, out_shape),
        scratch_shapes=scratch,
        compiler_params=pltpu.CompilerParams(vmem_limit_bytes=48 * 1024 * 1024),
        cost_estimate=pl.CostEstimate(
            flops=0,
            transcendentals=0,
            bytes_accessed=sum(a.size * a.dtype.itemsize for a in (*shapes, *operands)),
        ),
    )(*operands)


def load(
    features,
    labels,
    centres,
    ids,
    listed,
    copies_out,
    blocks_out,
    centres_out,
    named_out,
    held_features,
    held_labels,
    held_ids,
    held_listed,
    arrived,
):
    moves = [
        pltpu.make_async_copy(source, target, arrived.at[i])
        for i, (source, target) in enumerate(
            (
                (features, held_features),
                (labels, held_labels),
                (ids, held_ids),
                (listed, held_listed),
                *((centres.at[b], centres_out.at[b]) for b in range(centres.shape[0])),
            )
        )
    ]
    for move in moves:
        move.start()
    moves[0].wait()
    moves[1].wait()
    chip = lax.axis_index("chip")
    member = 2 * chip + lax.axis_index("core")
    copies, tok_dev, _ = copies_out.shape
    width = features.shape[1]
    rows = held_features[...].astype(jnp.float32)
    unit = (rows * inverse_norm(rows)).astype(jnp.bfloat16)
    copies_out[:, :, :width] = jnp.broadcast_to(unit[None], (copies, tok_dev, width))

    place = own_place() * tok_dev
    row = held_labels[...]
    row = jnp.concatenate([row, jnp.zeros((1, 128 - row.shape[1]), jnp.int32)], axis=1)
    row = jnp.broadcast_to(row, (tok_dev, 128))
    row = pltpu.roll(row, lax.rem(place - member * tok_dev + 128, 128), 1)
    digit = lax.broadcasted_iota(jnp.int32, (tok_dev, 128), 0)
    digits = (row >> (7 * jnp.minimum(digit, 3))) & 127
    lane = lanes(tok_dev)
    digits = jnp.where((lane >= place) & (lane < place + tok_dev), digits, 0)
    copies_out[:, :, width:] = jnp.broadcast_to(
        digits.astype(jnp.float32).astype(jnp.bfloat16)[None], (copies, tok_dev, 128)
    )
    for move in moves[2:]:
        move.wait()
    groups = blocks_out.shape[0]
    named_out[...] = select([held_ids[0, group_at(g)] for g in range(groups)], 1)
    for g in range(groups):
        group = group_at(g)
        block = centres_out[held_ids[0, group]]
        blocks_out[g] = jnp.where(held_listed[0, group] > 0, block, jnp.full_like(block, UNLISTED))


def group_at(place):
    return lax.axis_size("group") - 1 - place


def own_place():
    chips = lax.axis_size("chip")
    own = lax.axis_index("group") * chips + lax.axis_index("chip")
    return lax.axis_size("group") * chips - 1 - own


def select(parts, rows):
    owner = lanes(1) // (128 // len(parts))
    out = jnp.broadcast_to(parts[0], (rows, 128))
    for g in range(1, len(parts)):
        out = jnp.where(owner == g, parts[g], out)
    return out


def exponentials(packed, own_blocks, pair_blocks, expo_out, inverse_out, swap_out):
    group, core = lax.axis_index("group"), lax.axis_index("core")
    groups, _, width = own_blocks.shape
    units = packed[:, :width]
    digits = jnp.sum(
        packed[:, width:].astype(jnp.float32).reshape(128 // 8, 8, 128), axis=0
    ).astype(jnp.int32)
    labels = digits[0:1] + (digits[1:2] << 7) + (digits[2:3] << 14)
    rest = jnp.zeros((1, 128), jnp.float32)
    at_label = jnp.zeros((1, 128), jnp.float32)
    for k, (blocks, out) in enumerate(((own_blocks, expo_out), (pair_blocks, swap_out))):
        member = 2 * lax.axis_index("chip") + (core if k == 0 else 1 - core)
        first = (member * groups + group) * BLK
        onehot = lax.broadcasted_iota(jnp.int32, (BLK, 128), 0) == labels - first
        inverse = select(
            [inverse_norm(blocks[g].astype(jnp.float32)) for g in range(groups)], BLK
        )
        inverse_out[k] = inverse
        cosine = inverse * select([contract(blocks[g], units, 1, 1) for g in range(groups)], BLK)
        expo = jnp.exp(logit_scale * (cosine - jnp.where(onehot, cos_margin, 0.0)))
        expo = jnp.where(inverse > 0.0, expo, 0.0)
        out[:BLK, :] = jnp.where(onehot, -1.0, expo)
        rest += jnp.sum(jnp.where(onehot, 0.0, expo), axis=0, keepdims=True)
        at_label += jnp.sum(jnp.where(onehot, expo, 0.0), axis=0, keepdims=True)
    row = lax.broadcasted_iota(jnp.int32, (8, 128), 0)
    swap_out[BLK:, :] = jnp.where(row == 0, rest, jnp.where(row == 1, at_label, 0.0))


def shares(own_expo, swap, inverse, own_blocks, pair_blocks, centres, shares_out, norms_out):
    groups, _, width = own_blocks.shape
    per_group = 128 // groups
    others, label = [], []
    for k, expo in enumerate((own_expo[...], swap[:BLK, :])):
        others.append((jnp.maximum(expo, 0.0) * inverse[k]).T.astype(jnp.bfloat16))
        label.append(jnp.where(expo < 0.0, 1.0, 0.0).T.astype(jnp.bfloat16))
    others = jnp.concatenate(others, axis=1)
    label = jnp.concatenate(label, axis=1)
    for g in range(groups):
        here = slice(g * per_group, (g + 1) * per_group)
        blocks = jnp.concatenate([own_blocks[g], pair_blocks[g]], axis=0)
        both = contract(jnp.concatenate([others[here], label[here]], axis=0), blocks, 1, 0)
        both = both.astype(jnp.bfloat16)
        shares_out[here, :width] = both[:per_group]
        shares_out[here, width:] = both[per_group:]
    held = centres.shape[0]
    norms_out[...] = select(
        [inverse_norm(centres[b].astype(jnp.float32)) for b in range(held)], BLK
    )


def with_sums(shares, swap, swapped, other_packed, sent_out):
    del other_packed
    rows, wide = shares.shape
    sent_out[:, :wide] = shares[...]
    total = jnp.concatenate([swap[BLK : BLK + 2, :], swapped[BLK : BLK + 2, :]], axis=0)
    high = total.astype(jnp.bfloat16)
    low = (total - high.astype(jnp.float32)).astype(jnp.bfloat16)
    tile = jnp.concatenate([high.astype(jnp.float32), low.astype(jnp.float32)], axis=0)
    tile = jnp.broadcast_to(tile[None], (rows // 8, 8, 128))
    sent_out[:, wide:] = tile.reshape(rows, 128).astype(jnp.bfloat16)


def backward(
    named,
    received,
    own_expo,
    swapped,
    own_packed,
    other_packed,
    features,
    centres,
    norms,
    grad_out,
    feature_out,
    loss_out,
    grad,
    feature_grad,
    loss_row,
    left,
):
    held = centres.shape[0]
    tok_dev, width = features.shape

    sums = received[0].astype(jnp.float32)
    for i in range(1, received.shape[0]):
        sums = sums + received[i].astype(jnp.float32)
    tile = sums[:, 2 * width :]
    tile = tile[:4] + tile[4:]
    own_rest, own_label = tile[0:1], tile[1:2]
    other_rest, other_label = tile[2:3], tile[3:4]

    units = jnp.concatenate([own_packed[:, :width], other_packed[:, :width]], axis=0)
    own_scale = logit_scale / (own_rest + own_label)
    other_scale = logit_scale / (other_rest + other_label)
    own = own_expo[...]
    other = swapped[:BLK, :]
    own = jnp.where(own < 0.0, -own_rest, own) * own_scale
    other = jnp.where(other < 0.0, -other_rest, other) * other_scale
    weights = jnp.concatenate([own, other], axis=1)
    named = jnp.concatenate([named[...], named[...]], axis=1)
    mine = [jnp.where(named == b, weights, 0.0).astype(jnp.bfloat16) for b in range(held)]
    slot_grad = contract(jnp.concatenate(mine, axis=0), units, 1, 0)
    moves = []

    def leave(source, target):
        move = pltpu.make_async_copy(source, target, left.at[len(moves)])
        move.start()
        moves.append(move)

    def block_out(b):
        here = slot_grad[b * BLK : (b + 1) * BLK]
        factor = norms[:, b * (128 // held) : b * (128 // held) + 1]
        unit = centres[b].astype(jnp.float32) * factor
        along = jnp.sum(here * unit, axis=1, keepdims=True)
        grad[b] = factor * (here - along * unit)
        for part in (pl.ds(0, BLK // 2), pl.ds(BLK // 2, BLK // 2)):
            leave(grad.at[b, part], grad_out.at[b, part])

    for b in range(held // 2):
        block_out(b)

    sample = lax.broadcasted_iota(jnp.int32, (tok_dev, 128), 0) + own_place() * tok_dev
    mine = lanes(tok_dev) == sample
    rest = jnp.sum(jnp.where(mine, own_rest, 0.0), axis=1, keepdims=True)
    label = jnp.sum(jnp.where(mine, own_label, 0.0), axis=1, keepdims=True)
    total = rest + label
    loss = jnp.log(total) - jnp.log(label)
    square = (tok_dev, tok_dev)
    diagonal = lax.broadcasted_iota(jnp.int32, square, 0) == lax.broadcasted_iota(
        jnp.int32, square, 1
    )
    loss_row[...] = jnp.sum(jnp.where(diagonal, loss, 0.0), axis=0, keepdims=True)
    rows = features[...].astype(jnp.float32)
    inv_norm = inverse_norm(rows)
    unit = rows * inv_norm
    cand = sums[:, width : 2 * width]
    cand = (cand * inverse_norm(cand)).astype(jnp.bfloat16).astype(jnp.float32)
    unit_grad = logit_scale / total * (sums[:, :width] - rest * cand)
    along = jnp.sum(unit_grad * unit, axis=1, keepdims=True)
    feature_grad[...] = inv_norm * (unit_grad - along * unit)

    leave(feature_grad, feature_out)
    leave(loss_row, loss_out)
    for b in range(held // 2, held):
        block_out(b)
    for move in moves:
        move.wait()


def exchange(pieces, axes, order=None):
    return lax.all_to_all(
        pieces, axes, split_axis=0, concat_axis=0, axis_index_groups=order, tiled=True
    )


def exchange_chips(pieces):
    return exchange(pieces, CHIPS, [list(reversed(range(pieces.shape[0])))])


def with_partner(value):
    return lax.ppermute(value, "core", [(0, 1), (1, 0)])


def on_device(features, labels, centres, block_ids, listed):
    groups = lax.axis_size("group")
    chips = groups * lax.axis_size("chip")
    tok_dev, width = features.shape
    held = centres.shape[0] // BLK
    half = chips * tok_dev
    bf16, f32 = jnp.bfloat16, jnp.float32
    shape = jax.ShapeDtypeStruct

    copies, own_blocks, blocks, named = run(
        load,
        (
            shape((chips, tok_dev, width + 128), bf16),
            shape((groups, BLK, width), bf16),
            shape((held, BLK, width), bf16),
            shape((1, 128), block_ids.dtype),
        ),
        [HBM] * 5,
        *(
            pltpu.with_memory_space_constraint(array, pltpu.HBM)
            for array in (
                features,
                labels.reshape(1, -1),
                centres.reshape(held, BLK, width),
                block_ids.reshape(1, groups),
                listed.reshape(1, groups),
            )
        ),
        scratch=[
            pltpu.VMEM(features.shape, features.dtype),
            pltpu.VMEM((1, labels.shape[0]), labels.dtype),
            pltpu.SMEM((1, groups), block_ids.dtype),
            pltpu.SMEM((1, groups), listed.dtype),
            pltpu.SemaphoreType.DMA((4 + held,)),
        ],
    )
    pair_blocks = with_partner(own_blocks)
    own_packed = exchange_chips(copies).reshape(half, width + 128)
    other_packed = with_partner(own_packed)
    own_expo, inverse, swap = run(
        exponentials,
        (shape((BLK, half), f32), shape((2, BLK, 128), f32), shape((BLK + 8, half), f32)),
        [VMEM] * 3,
        own_packed,
        own_blocks,
        pair_blocks,
    )
    swapped = with_partner(swap)
    going, norms = run(
        shares,
        (shape((half, 2 * width), bf16), shape((BLK, 128), f32)),
        [VMEM] * 6,
        own_expo,
        swap,
        inverse,
        own_blocks,
        pair_blocks,
        blocks,
    )
    sent = run(
        with_sums,
        shape((half, 2 * width + 128), bf16),
        [VMEM] * 3 + [pl.BlockSpec(memory_space=pl.ANY)],
        going,
        swap,
        swapped,
        other_packed,
    )
    received = exchange_chips(sent.reshape(chips, tok_dev, 2 * width + 128))
    outs = (shape((held, BLK, width), f32), shape((tok_dev, width), f32), shape((1, tok_dev), f32))
    centre_grad, feature_grad, loss = run(
        backward,
        outs,
        [VMEM] * 9,
        named,
        received,
        own_expo,
        swapped,
        own_packed,
        other_packed,
        features,
        blocks,
        norms,
        out_spec=HBM,
        scratch=[
            *(pltpu.VMEM(out.shape, out.dtype) for out in outs),
            pltpu.SemaphoreType.DMA((2 * held + 2,)),
        ],
    )
    return (loss.reshape(tok_dev), feature_grad, centre_grad.reshape(held * BLK, width))


def on_device_of_many(features, labels, centres, block_ids, listed):
    groups = lax.axis_size("group")
    members = lax.axis_size("member")
    devices = groups * members
    group = lax.axis_index("group")
    member = lax.axis_index("member")
    tok_dev, width = features.shape
    group_tok = members * tok_dev
    held = centres.shape[0] // BLK

    vectors = features.astype(jnp.float32)
    inv_norm = inverse_norm(vectors)
    unit_rows = vectors * inv_norm
    copies = jnp.broadcast_to(unit_rows.astype(jnp.bfloat16), (devices, tok_dev, width))
    units = exchange(copies, AXES).reshape(groups, group_tok, width)
    all_labels = exchange(jnp.broadcast_to(labels[None], (groups, group_tok)), "group")

    picked = centres.reshape(held, BLK, width)[block_ids[:, 0]].astype(jnp.float32)
    inv_cand = inverse_norm(picked)
    unit_cand = picked * inv_cand
    cand_half = unit_cand.astype(jnp.bfloat16)
    cosine = jnp.einsum("gsd,gcd->gsc", units, cand_half, preferred_element_type=jnp.float32)
    local_label = all_labels - (member * groups + group) * BLK
    onehot = (lax.broadcasted_iota(jnp.int32, (1, 1, BLK), 2) == local_label[:, :, None]).astype(
        jnp.float32
    )
    logits = logit_scale * (cosine - cos_margin * onehot)
    exp_logits = jnp.exp(logits) * listed.astype(jnp.float32)[:, :, None]
    totals, label_logit = lax.psum(
        (jnp.sum(exp_logits, axis=2), jnp.sum(logits * onehot, axis=2)), AXES
    )
    loss_all = (jnp.log(totals) - label_logit).reshape(devices, tok_dev)
    sample_loss = lax.dynamic_slice_in_dim(loss_all, group * members + member, 1, 0)[0]

    weights = (logit_scale * (exp_logits / totals[:, :, None] - onehot)).astype(jnp.bfloat16)
    partial = jnp.einsum("gsc,gcd->gsd", weights, cand_half, preferred_element_type=jnp.float32)
    home = exchange(partial.astype(jnp.bfloat16).reshape(devices, tok_dev, width), AXES)
    unit_grad = jnp.sum(home.astype(jnp.float32), axis=0)
    feature_grad = inv_norm * (
        unit_grad - jnp.sum(unit_grad * unit_rows, axis=1, keepdims=True) * unit_rows
    )
    slot_grad = jnp.einsum("gsc,gsd->gcd", weights, units, preferred_element_type=jnp.float32)
    cand_grad = inv_cand * (
        slot_grad - jnp.sum(slot_grad * unit_cand, axis=2, keepdims=True) * unit_cand
    )
    cand_grad = cand_grad.astype(jnp.bfloat16).astype(jnp.float32)
    names = block_ids == jnp.arange(held, dtype=jnp.int32)[None, :]
    centre_grad = jnp.sum(
        jnp.where(names[:, :, None, None], cand_grad[:, None], 0.0), axis=0
    ).reshape(held * BLK, width)
    return (sample_loss, feature_grad, centre_grad)


def on_axes(body, mesh, axes):
    split = P(axes)
    return jax.shard_map(
        body,
        mesh=mesh,
        in_specs=(split, P("group"), split, P(None, axes), P(None, axes)),
        out_specs=(split, split, split),
        check_vma=False,
    )


def solution(mesh):
    groups, members = mesh.shape["group"], mesh.shape["member"]
    by_core = jax.sharding.Mesh(
        mesh.devices.reshape(groups, members // 2, 2), ("group", "chip", "core")
    )

    def program(features, *others):
        half = features.shape[0] // 2
        if half == 128 and 2 * groups == features.shape[0] // mesh.size == 8:
            return on_axes(on_device, by_core, (*CHIPS, "core"))(features, *others)
        return on_axes(on_device_of_many, mesh, AXES)(features, *others)

    return program
```

```python
import jax
import jax.numpy as jnp
from jax import lax
from jax.experimental import pallas as pl
from jax.experimental.pallas import tpu as pltpu
from jax.sharding import PartitionSpec as P

BLK = 128
AXES = ("group", "member")
CHIPS = ("group", "chip")

logit_scale = 32.0
cos_margin = 0.35
norm_epsilon = 1e-06
UNLISTED = 1e19

VMEM = pl.BlockSpec(memory_space=pltpu.VMEM)
HBM = pl.BlockSpec(memory_space=pltpu.HBM)


def inverse_norm(rows):
    return lax.rsqrt(jnp.sum(rows * rows, axis=-1, keepdims=True) + norm_epsilon)


def contract(left, right, left_dim, right_dim):
    dims = (((left_dim,), (right_dim,)), ((), ()))
    return lax.dot_general(left, right, dims, preferred_element_type=jnp.float32)


def lanes(rows):
    return lax.broadcasted_iota(jnp.int32, (rows, 128), 1)


def run(kernel, out_shape, in_specs, *operands, out_spec=VMEM, scratch=()):
    shapes = jax.tree.leaves(out_shape)
    return pl.pallas_call(
        kernel,
        out_shape=out_shape,
        in_specs=in_specs,
        out_specs=jax.tree.map(lambda _: out_spec, out_shape),
        scratch_shapes=scratch,
        compiler_params=pltpu.CompilerParams(vmem_limit_bytes=48 * 1024 * 1024),
        cost_estimate=pl.CostEstimate(
            flops=0,
            transcendentals=0,
            bytes_accessed=sum(a.size * a.dtype.itemsize for a in (*shapes, *operands)),
        ),
    )(*operands)


def load(
    features,
    labels,
    centres,
    ids,
    listed,
    copies_out,
    blocks_out,
    centres_out,
    named_out,
    held_features,
    held_labels,
    held_ids,
    held_listed,
    arrived,
):
    moves = [
        pltpu.make_async_copy(source, target, arrived.at[i])
        for i, (source, target) in enumerate(
            (
                (features, held_features),
                (labels, held_labels),
                (ids, held_ids),
                (listed, held_listed),
                *((centres.at[b], centres_out.at[b]) for b in range(centres.shape[0])),
            )
        )
    ]
    for move in moves:
        move.start()
    moves[0].wait()
    moves[1].wait()
    chip = lax.axis_index("chip")
    member = 2 * chip + lax.axis_index("core")
    copies, tok_dev, _ = copies_out.shape
    width = features.shape[1]
    rows = held_features[...].astype(jnp.float32)
    unit = (rows * inverse_norm(rows)).astype(jnp.bfloat16)
    copies_out[:, :, :width] = jnp.broadcast_to(unit[None], (copies, tok_dev, width))

    place = own_place() * tok_dev
    row = held_labels[...]
    row = jnp.concatenate([row, jnp.zeros((1, 128 - row.shape[1]), jnp.int32)], axis=1)
    row = jnp.broadcast_to(row, (tok_dev, 128))
    row = pltpu.roll(row, lax.rem(place - member * tok_dev + 128, 128), 1)
    digit = lax.broadcasted_iota(jnp.int32, (tok_dev, 128), 0)
    digits = (row >> (7 * jnp.minimum(digit, 3))) & 127
    lane = lanes(tok_dev)
    digits = jnp.where((lane >= place) & (lane < place + tok_dev), digits, 0)
    copies_out[:, :, width:] = jnp.broadcast_to(
        digits.astype(jnp.float32).astype(jnp.bfloat16)[None], (copies, tok_dev, 128)
    )
    for move in moves[2:]:
        move.wait()
    groups = blocks_out.shape[0]
    named_out[...] = select([held_ids[0, group_at(g)] for g in range(groups)], 1)
    for g in range(groups):
        group = group_at(g)
        block = centres_out[held_ids[0, group]]
        blocks_out[g] = jnp.where(held_listed[0, group] > 0, block, jnp.full_like(block, UNLISTED))


def group_at(place):
    groups = lax.axis_size("group")
    return (groups - 2 - place) % groups


def own_place():
    groups, chips = lax.axis_size("group"), lax.axis_size("chip")
    own = lax.axis_index("group") * chips + lax.axis_index("chip")
    return lax.rem((2 * groups - 1) * chips - 1 - own, groups * chips)


def select(parts, rows):
    owner = lanes(1) // (128 // len(parts))
    out = jnp.broadcast_to(parts[0], (rows, 128))
    for g in range(1, len(parts)):
        out = jnp.where(owner == g, parts[g], out)
    return out


def exponentials(packed, core, blocks, inverse):
    groups, _, width = blocks.shape
    digits = jnp.sum(
        packed[:, width:].astype(jnp.float32).reshape(128 // 8, 8, 128), axis=0
    ).astype(jnp.int32)
    labels = digits[0:1] + (digits[1:2] << 7) + (digits[2:3] << 14)
    member = 2 * lax.axis_index("chip") + core
    first = (member * groups + lax.axis_index("group")) * BLK
    onehot = lax.broadcasted_iota(jnp.int32, (BLK, 128), 0) == labels - first
    units = packed[:, :width]
    cosine = inverse * select([contract(blocks[g], units, 1, 1) for g in range(groups)], BLK)
    expo = jnp.exp(logit_scale * (cosine - jnp.where(onehot, cos_margin, 0.0)))
    return jnp.where(inverse > 0.0, expo, 0.0), onehot


def sums(parts):
    rest = [jnp.where(onehot, 0.0, expo) for expo, onehot in parts]
    at_label = [jnp.where(onehot, expo, 0.0) for expo, onehot in parts]
    return [jnp.sum(sum(part), axis=0, keepdims=True) for part in (rest, at_label)]


def forward(packed, own_blocks, pair_blocks, own_expo_out, pair_expo_out, inverse_out, sums_out):
    core = lax.axis_index("core")
    parts = []
    for k, (blocks, out) in enumerate(((own_blocks, own_expo_out), (pair_blocks, pair_expo_out))):
        norms = [inverse_norm(blocks[g].astype(jnp.float32)) for g in range(blocks.shape[0])]
        inverse = select(norms, BLK)
        inverse_out[k] = inverse
        expo, onehot = exponentials(packed, core if k == 0 else 1 - core, blocks, inverse)
        out[...] = jnp.where(onehot, -1.0, expo)
        parts.append((expo, onehot))
    sums_out[0:1, :], sums_out[1:2, :] = sums(parts)


def forward_other(
    packed, own_blocks, pair_blocks, inverse, own_sums, shares, expo_out, sent_out
):
    core = lax.axis_index("core")
    own = exponentials(packed, core, own_blocks, inverse[0])
    pair = exponentials(packed, 1 - core, pair_blocks, inverse[1])
    expo_out[...] = jnp.where(own[1], -1.0, own[0])
    rows, wide = shares.shape
    sent_out[:, :wide] = shares[...]
    total = jnp.concatenate([own_sums[...], *sums([own, pair])], axis=0)
    high = total.astype(jnp.bfloat16)
    low = (total - high.astype(jnp.float32)).astype(jnp.bfloat16)
    tile = jnp.concatenate([high.astype(jnp.float32), low.astype(jnp.float32)], axis=0)
    tile = jnp.broadcast_to(tile[None], (rows // 8, 8, 128))
    sent_out[:, wide:] = tile.reshape(rows, 128).astype(jnp.bfloat16)


def shares(own_expo, pair_expo, inverse, own_blocks, pair_blocks, centres, shares_out, norms_out):
    groups, _, width = own_blocks.shape
    per_group = 128 // groups
    others, label = [], []
    for k, expo in enumerate((own_expo[...], pair_expo[...])):
        others.append((jnp.maximum(expo, 0.0) * inverse[k]).T.astype(jnp.bfloat16))
        label.append(jnp.where(expo < 0.0, 1.0, 0.0).T.astype(jnp.bfloat16))
    others = jnp.concatenate(others, axis=1)
    label = jnp.concatenate(label, axis=1)
    for g in range(groups):
        here = slice(g * per_group, (g + 1) * per_group)
        blocks = jnp.concatenate([own_blocks[g], pair_blocks[g]], axis=0)
        both = contract(jnp.concatenate([others[here], label[here]], axis=0), blocks, 1, 0)
        both = both.astype(jnp.bfloat16)
        shares_out[here, :width] = both[:per_group]
        shares_out[here, width:] = both[per_group:]
    held = centres.shape[0]
    norms_out[...] = select(
        [inverse_norm(centres[b].astype(jnp.float32)) for b in range(held)], BLK
    )


def backward(
    named,
    received,
    own_expo,
    other_expo,
    own_packed,
    other_packed,
    features,
    centres,
    norms,
    grad_out,
    feature_out,
    loss_out,
    grad,
    feature_grad,
    loss_row,
    left,
):
    held = centres.shape[0]
    tok_dev, width = features.shape

    sums = received[0].astype(jnp.float32)
    for i in range(1, received.shape[0]):
        sums = sums + received[i].astype(jnp.float32)
    tile = sums[:, 2 * width :]
    tile = tile[:4] + tile[4:]
    own_rest, own_label = tile[0:1], tile[1:2]
    other_rest, other_label = tile[2:3], tile[3:4]

    units = jnp.concatenate([own_packed[:, :width], other_packed[:, :width]], axis=0)
    own_scale = logit_scale / (own_rest + own_label)
    other_scale = logit_scale / (other_rest + other_label)
    own = own_expo[...]
    other = other_expo[...]
    own = jnp.where(own < 0.0, -own_rest, own) * own_scale
    other = jnp.where(other < 0.0, -other_rest, other) * other_scale
    weights = jnp.concatenate([own, other], axis=1)
    named = jnp.concatenate([named[...], named[...]], axis=1)
    mine = [jnp.where(named == b, weights, 0.0).astype(jnp.bfloat16) for b in range(held)]
    slot_grad = contract(jnp.concatenate(mine, axis=0), units, 1, 0)
    moves = []

    def leave(source, target):
        move = pltpu.make_async_copy(source, target, left.at[len(moves)])
        move.start()
        moves.append(move)

    def block_out(b):
        here = slot_grad[b * BLK : (b + 1) * BLK]
        factor = norms[:, b * (128 // held) : b * (128 // held) + 1]
        unit = centres[b].astype(jnp.float32) * factor
        along = jnp.sum(here * unit, axis=1, keepdims=True)
        grad[b] = factor * (here - along * unit)
        for part in (pl.ds(0, BLK // 2), pl.ds(BLK // 2, BLK // 2)):
            leave(grad.at[b, part], grad_out.at[b, part])

    for b in range(held // 2):
        block_out(b)

    sample = lax.broadcasted_iota(jnp.int32, (tok_dev, 128), 0) + own_place() * tok_dev
    mine = lanes(tok_dev) == sample
    rest = jnp.sum(jnp.where(mine, own_rest, 0.0), axis=1, keepdims=True)
    label = jnp.sum(jnp.where(mine, own_label, 0.0), axis=1, keepdims=True)
    total = rest + label
    loss = jnp.log(total) - jnp.log(label)
    square = (tok_dev, tok_dev)
    diagonal = lax.broadcasted_iota(jnp.int32, square, 0) == lax.broadcasted_iota(
        jnp.int32, square, 1
    )
    loss_row[...] = jnp.sum(jnp.where(diagonal, loss, 0.0), axis=0, keepdims=True)
    rows = features[...].astype(jnp.float32)
    inv_norm = inverse_norm(rows)
    unit = rows * inv_norm
    cand = sums[:, width : 2 * width]
    cand = (cand * inverse_norm(cand)).astype(jnp.bfloat16).astype(jnp.float32)
    unit_grad = logit_scale / total * (sums[:, :width] - rest * cand)
    along = jnp.sum(unit_grad * unit, axis=1, keepdims=True)
    feature_grad[...] = inv_norm * (unit_grad - along * unit)

    leave(feature_grad, feature_out)
    leave(loss_row, loss_out)
    for b in range(held // 2, held):
        block_out(b)
    for move in moves:
        move.wait()


def exchange(pieces, axes, order=None):
    return lax.all_to_all(
        pieces, axes, split_axis=0, concat_axis=0, axis_index_groups=order, tiled=True
    )


def exchange_chips(pieces):
    size, last = pieces.shape[0], lax.axis_size("chip") + 1
    return exchange(pieces, CHIPS, [[(size - last - i) % size for i in range(size)]])


def with_partner(value):
    return lax.ppermute(value, "core", [(0, 1), (1, 0)])


def on_device(features, labels, centres, block_ids, listed):
    groups = lax.axis_size("group")
    chips = groups * lax.axis_size("chip")
    tok_dev, width = features.shape
    held = centres.shape[0] // BLK
    half = chips * tok_dev
    bf16, f32 = jnp.bfloat16, jnp.float32
    shape = jax.ShapeDtypeStruct

    copies, own_blocks, blocks, named = run(
        load,
        (
            shape((chips, tok_dev, width + 128), bf16),
            shape((groups, BLK, width), bf16),
            shape((held, BLK, width), bf16),
            shape((1, 128), block_ids.dtype),
        ),
        [HBM] * 5,
        *(
            pltpu.with_memory_space_constraint(array, pltpu.HBM)
            for array in (
                features,
                labels.reshape(1, -1),
                centres.reshape(held, BLK, width),
                block_ids.reshape(1, groups),
                listed.reshape(1, groups),
            )
        ),
        scratch=[
            pltpu.VMEM(features.shape, features.dtype),
            pltpu.VMEM((1, labels.shape[0]), labels.dtype),
            pltpu.SMEM((1, groups), block_ids.dtype),
            pltpu.SMEM((1, groups), listed.dtype),
            pltpu.SemaphoreType.DMA((4 + held,)),
        ],
    )
    pair_blocks = with_partner(own_blocks)
    own_packed = exchange_chips(copies).reshape(half, width + 128)
    other_packed = with_partner(own_packed)
    own_expo, pair_expo, inverse, own_sums = run(
        forward,
        (
            shape((BLK, half), f32),
            shape((BLK, half), f32),
            shape((2, BLK, 128), f32),
            shape((2, half), f32),
        ),
        [VMEM] * 3,
        own_packed,
        own_blocks,
        pair_blocks,
    )
    going, norms = run(
        shares,
        (shape((half, 2 * width), bf16), shape((BLK, 128), f32)),
        [VMEM] * 6,
        own_expo,
        pair_expo,
        inverse,
        own_blocks,
        pair_blocks,
        blocks,
    )
    other_expo, sent = run(
        forward_other,
        (shape((BLK, half), f32), shape((half, 2 * width + 128), bf16)),
        [VMEM] * 6,
        other_packed,
        own_blocks,
        pair_blocks,
        inverse,
        own_sums,
        going,
    )
    received = exchange_chips(sent.reshape(chips, tok_dev, 2 * width + 128))
    outs = (shape((held, BLK, width), f32), shape((tok_dev, width), f32), shape((1, tok_dev), f32))
    centre_grad, feature_grad, loss = run(
        backward,
        outs,
        [VMEM] * 9,
        named,
        received,
        own_expo,
        other_expo,
        own_packed,
        other_packed,
        features,
        blocks,
        norms,
        out_spec=HBM,
        scratch=[
            *(pltpu.VMEM(out.shape, out.dtype) for out in outs),
            pltpu.SemaphoreType.DMA((2 * held + 2,)),
        ],
    )
    return (loss.reshape(tok_dev), feature_grad, centre_grad.reshape(held * BLK, width))


def on_device_of_many(features, labels, centres, block_ids, listed):
    groups = lax.axis_size("group")
    members = lax.axis_size("member")
    devices = groups * members
    group = lax.axis_index("group")
    member = lax.axis_index("member")
    tok_dev, width = features.shape
    group_tok = members * tok_dev
    held = centres.shape[0] // BLK

    vectors = features.astype(jnp.float32)
    inv_norm = inverse_norm(vectors)
    unit_rows = vectors * inv_norm
    copies = jnp.broadcast_to(unit_rows.astype(jnp.bfloat16), (devices, tok_dev, width))
    units = exchange(copies, AXES).reshape(groups, group_tok, width)
    all_labels = exchange(jnp.broadcast_to(labels[None], (groups, group_tok)), "group")

    picked = centres.reshape(held, BLK, width)[block_ids[:, 0]].astype(jnp.float32)
    inv_cand = inverse_norm(picked)
    unit_cand = picked * inv_cand
    cand_half = unit_cand.astype(jnp.bfloat16)
    cosine = jnp.einsum("gsd,gcd->gsc", units, cand_half, preferred_element_type=jnp.float32)
    local_label = all_labels - (member * groups + group) * BLK
    onehot = (lax.broadcasted_iota(jnp.int32, (1, 1, BLK), 2) == local_label[:, :, None]).astype(
        jnp.float32
    )
    logits = logit_scale * (cosine - cos_margin * onehot)
    exp_logits = jnp.exp(logits) * listed.astype(jnp.float32)[:, :, None]
    totals, label_logit = lax.psum(
        (jnp.sum(exp_logits, axis=2), jnp.sum(logits * onehot, axis=2)), AXES
    )
    loss_all = (jnp.log(totals) - label_logit).reshape(devices, tok_dev)
    sample_loss = lax.dynamic_slice_in_dim(loss_all, group * members + member, 1, 0)[0]

    weights = (logit_scale * (exp_logits / totals[:, :, None] - onehot)).astype(jnp.bfloat16)
    partial = jnp.einsum("gsc,gcd->gsd", weights, cand_half, preferred_element_type=jnp.float32)
    home = exchange(partial.astype(jnp.bfloat16).reshape(devices, tok_dev, width), AXES)
    unit_grad = jnp.sum(home.astype(jnp.float32), axis=0)
    feature_grad = inv_norm * (
        unit_grad - jnp.sum(unit_grad * unit_rows, axis=1, keepdims=True) * unit_rows
    )
    slot_grad = jnp.einsum("gsc,gsd->gcd", weights, units, preferred_element_type=jnp.float32)
    cand_grad = inv_cand * (
        slot_grad - jnp.sum(slot_grad * unit_cand, axis=2, keepdims=True) * unit_cand
    )
    cand_grad = cand_grad.astype(jnp.bfloat16).astype(jnp.float32)
    names = block_ids == jnp.arange(held, dtype=jnp.int32)[None, :]
    centre_grad = jnp.sum(
        jnp.where(names[:, :, None, None], cand_grad[:, None], 0.0), axis=0
    ).reshape(held * BLK, width)
    return (sample_loss, feature_grad, centre_grad)


def on_axes(body, mesh, axes):
    split = P(axes)
    return jax.shard_map(
        body,
        mesh=mesh,
        in_specs=(split, P("group"), split, P(None, axes), P(None, axes)),
        out_specs=(split, split, split),
        check_vma=False,
    )


def solution(mesh):
    groups, members = mesh.shape["group"], mesh.shape["member"]
    by_core = jax.sharding.Mesh(
        mesh.devices.reshape(groups, members // 2, 2), ("group", "chip", "core")
    )

    def program(features, *others):
        half = features.shape[0] // 2
        if half == 128 and 2 * groups == features.shape[0] // mesh.size == 8:
            return on_axes(on_device, by_core, (*CHIPS, "core"))(features, *others)
        return on_axes(on_device_of_many, mesh, AXES)(features, *others)

    return program
```

```python
import jax
import jax.numpy as jnp
from jax import lax
from jax.experimental import pallas as pl
from jax.experimental.pallas import tpu as pltpu
from jax.sharding import PartitionSpec as P

BLK = 128
AXES = ("group", "member")
CHIPS = ("group", "chip")

logit_scale = 32.0
cos_margin = 0.35
norm_epsilon = 1e-06
GROUP_ORDER = (2, 0, 3, 1)
UNLISTED = 1e19

VMEM = pl.BlockSpec(memory_space=pltpu.VMEM)
HBM = pl.BlockSpec(memory_space=pltpu.HBM)


def inverse_norm(rows):
    return lax.rsqrt(jnp.sum(rows * rows, axis=-1, keepdims=True) + norm_epsilon)


def contract(left, right, left_dim, right_dim):
    dims = (((left_dim,), (right_dim,)), ((), ()))
    return lax.dot_general(left, right, dims, preferred_element_type=jnp.float32)


def lanes(rows):
    return lax.broadcasted_iota(jnp.int32, (rows, 128), 1)


def run(kernel, out_shape, in_specs, *operands, out_spec=VMEM, scratch=()):
    shapes = jax.tree.leaves(out_shape)
    return pl.pallas_call(
        kernel,
        out_shape=out_shape,
        in_specs=in_specs,
        out_specs=jax.tree.map(lambda _: out_spec, out_shape),
        scratch_shapes=scratch,
        compiler_params=pltpu.CompilerParams(vmem_limit_bytes=48 * 1024 * 1024),
        cost_estimate=pl.CostEstimate(
            flops=0,
            transcendentals=0,
            bytes_accessed=sum(a.size * a.dtype.itemsize for a in (*shapes, *operands)),
        ),
    )(*operands)


def load(
    features,
    labels,
    centres,
    ids,
    listed,
    copies_out,
    blocks_out,
    centres_out,
    named_out,
    held_features,
    held_labels,
    held_ids,
    held_listed,
    arrived,
):
    moves = [
        pltpu.make_async_copy(source, target, arrived.at[i])
        for i, (source, target) in enumerate(
            (
                (features, held_features),
                (labels, held_labels),
                (ids, held_ids),
                (listed, held_listed),
                *((centres.at[b], centres_out.at[b]) for b in range(centres.shape[0])),
            )
        )
    ]
    for move in moves:
        move.start()
    moves[0].wait()
    moves[1].wait()
    chip = lax.axis_index("chip")
    member = 2 * chip + lax.axis_index("core")
    copies, tok_dev, _ = copies_out.shape
    width = features.shape[1]
    rows = held_features[...].astype(jnp.float32)
    unit = (rows * inverse_norm(rows)).astype(jnp.bfloat16)
    copies_out[:, :, :width] = jnp.broadcast_to(unit[None], (copies, tok_dev, width))

    place = own_place() * tok_dev
    row = held_labels[...]
    row = jnp.concatenate([row, jnp.zeros((1, 128 - row.shape[1]), jnp.int32)], axis=1)
    row = jnp.broadcast_to(row, (tok_dev, 128))
    row = pltpu.roll(row, lax.rem(place - member * tok_dev + 128, 128), 1)
    digit = lax.broadcasted_iota(jnp.int32, (tok_dev, 128), 0)
    digits = (row >> (7 * jnp.minimum(digit, 3))) & 127
    lane = lanes(tok_dev)
    digits = jnp.where((lane >= place) & (lane < place + tok_dev), digits, 0)
    copies_out[:, :, width:] = jnp.broadcast_to(
        digits.astype(jnp.float32).astype(jnp.bfloat16)[None], (copies, tok_dev, 128)
    )
    for move in moves[2:]:
        move.wait()
    named_out[...] = select([held_ids[0, group] for group in GROUP_ORDER], 1)
    for g, group in enumerate(GROUP_ORDER):
        block = centres_out[held_ids[0, group]]
        blocks_out[g] = jnp.where(held_listed[0, group] > 0, block, jnp.full_like(block, UNLISTED))


def own_place():
    groups, chips = lax.axis_size("group"), lax.axis_size("chip")
    group = lax.axis_index("group")
    place = sum(jnp.where(group == g, k, 0) for k, g in enumerate(GROUP_ORDER))
    return (chips - 1 - lax.axis_index("chip")) * groups + place


def select(parts, rows):
    owner = lax.rem(lanes(1) // 8, len(parts))
    out = jnp.broadcast_to(parts[0], (rows, 128))
    for g in range(1, len(parts)):
        out = jnp.where(owner == g, parts[g], out)
    return out


def exponentials(packed, core, blocks, inverse):
    groups, _, width = blocks.shape
    digits = jnp.sum(
        packed[:, width:].astype(jnp.float32).reshape(128 // 8, 8, 128), axis=0
    ).astype(jnp.int32)
    labels = digits[0:1] + (digits[1:2] << 7) + (digits[2:3] << 14)
    member = 2 * lax.axis_index("chip") + core
    first = (member * groups + lax.axis_index("group")) * BLK
    onehot = lax.broadcasted_iota(jnp.int32, (BLK, 128), 0) == labels - first
    units = packed[:, :width]
    cosine = inverse * select([contract(blocks[g], units, 1, 1) for g in range(groups)], BLK)
    expo = jnp.exp(logit_scale * (cosine - jnp.where(onehot, cos_margin, 0.0)))
    return jnp.where(inverse > 0.0, expo, 0.0), onehot


def sums(parts):
    rest = [jnp.where(onehot, 0.0, expo) for expo, onehot in parts]
    at_label = [jnp.where(onehot, expo, 0.0) for expo, onehot in parts]
    return [jnp.sum(sum(part), axis=0, keepdims=True) for part in (rest, at_label)]


def forward(packed, own_blocks, pair_blocks, own_expo_out, pair_expo_out, inverse_out, sums_out):
    core = lax.axis_index("core")
    parts = []
    for k, (blocks, out) in enumerate(((own_blocks, own_expo_out), (pair_blocks, pair_expo_out))):
        norms = [inverse_norm(blocks[g].astype(jnp.float32)) for g in range(blocks.shape[0])]
        inverse = select(norms, BLK)
        inverse_out[k] = inverse
        expo, onehot = exponentials(packed, core if k == 0 else 1 - core, blocks, inverse)
        out[...] = jnp.where(onehot, -1.0, expo)
        parts.append((expo, onehot))
    sums_out[0:1, :], sums_out[1:2, :] = sums(parts)


def forward_other(
    packed, own_blocks, pair_blocks, inverse, own_sums, shares, expo_out, sent_out
):
    core = lax.axis_index("core")
    own = exponentials(packed, core, own_blocks, inverse[0])
    pair = exponentials(packed, 1 - core, pair_blocks, inverse[1])
    expo_out[...] = jnp.where(own[1], -1.0, own[0])
    rows, wide = shares.shape
    sent_out[:, :wide] = shares[...]
    total = jnp.concatenate([own_sums[...], *sums([own, pair])], axis=0)
    high = total.astype(jnp.bfloat16)
    low = (total - high.astype(jnp.float32)).astype(jnp.bfloat16)
    tile = jnp.concatenate([high.astype(jnp.float32), low.astype(jnp.float32)], axis=0)
    tile = jnp.broadcast_to(tile[None], (rows // 8, 8, 128))
    sent_out[:, wide:] = tile.reshape(rows, 128).astype(jnp.bfloat16)


def shares(own_expo, pair_expo, inverse, own_blocks, pair_blocks, centres, shares_out, norms_out):
    groups, _, width = own_blocks.shape
    others, label = [], []
    for k, expo in enumerate((own_expo[...], pair_expo[...])):
        others.append((jnp.maximum(expo, 0.0) * inverse[k]).T)
        label.append(jnp.where(expo < 0.0, 1.0, 0.0).T)
    others = jnp.concatenate(others, axis=1)
    label = jnp.concatenate(label, axis=1)
    places = [[] for _ in range(groups)]
    for g in range(groups):
        rows = [part[p * 8 : p * 8 + 8] for part in (others, label) for p in range(g, 16, groups)]
        blocks = jnp.concatenate([own_blocks[g], pair_blocks[g]], axis=0)
        both = contract(jnp.concatenate(rows, axis=0).astype(jnp.bfloat16), blocks, 1, 0)
        places[g] = [both[i * 8 : i * 8 + 8] for i in range(len(rows))]
    for part in range(2):
        count = 16 // groups
        rows = [places[g][part * count + i] for i in range(count) for g in range(groups)]
        rows = jnp.concatenate(rows, axis=0).astype(jnp.bfloat16)
        shares_out[:, part * width : (part + 1) * width] = rows
    held = centres.shape[0]
    norms_out[...] = select(
        [inverse_norm(centres[b].astype(jnp.float32)) for b in range(held)], BLK
    )


def backward(
    named,
    received,
    own_expo,
    other_expo,
    own_packed,
    other_packed,
    features,
    centres,
    norms,
    grad_out,
    feature_out,
    loss_out,
    grad,
    feature_grad,
    loss_row,
    left,
):
    held = centres.shape[0]
    tok_dev, width = features.shape


    def total_of(columns):
        total = received[0, :, columns].astype(jnp.float32)
        for i in range(1, received.shape[0]):
            total = total + received[i, :, columns].astype(jnp.float32)
        return total

    tile = total_of(pl.ds(2 * width, 128))
    tile = tile[:4] + tile[4:]
    own_rest, own_label = tile[0:1], tile[1:2]
    other_rest, other_label = tile[2:3], tile[3:4]

    units = jnp.concatenate([own_packed[:, :width], other_packed[:, :width]], axis=0)
    own_scale = logit_scale / (own_rest + own_label)
    other_scale = logit_scale / (other_rest + other_label)
    own = own_expo[...]
    other = other_expo[...]
    own = jnp.where(own < 0.0, -own_rest, own) * own_scale
    other = jnp.where(other < 0.0, -other_rest, other) * other_scale
    weights = jnp.concatenate([own, other], axis=1)
    named = jnp.concatenate([named[...], named[...]], axis=1)
    moves = []

    def leave(source, target):
        move = pltpu.make_async_copy(source, target, left.at[len(moves)])
        move.start()
        moves.append(move)

    def block_out(b):
        mine = jnp.where(named == b, weights, 0.0).astype(jnp.bfloat16)
        here = contract(mine, units, 1, 0)
        factor = norms[:, b * 8 : b * 8 + 1]
        unit = centres[b].astype(jnp.float32) * factor
        along = jnp.sum(here * unit, axis=1, keepdims=True)
        grad[b] = factor * (here - along * unit)
        for part in (pl.ds(0, BLK // 2), pl.ds(BLK // 2, BLK // 2)):
            leave(grad.at[b, part], grad_out.at[b, part])

    for b in range(held // 2):
        block_out(b)

    sums = total_of(pl.ds(0, 2 * width))
    sample = lax.broadcasted_iota(jnp.int32, (tok_dev, 128), 0) + own_place() * tok_dev
    mine = lanes(tok_dev) == sample
    rest = jnp.sum(jnp.where(mine, own_rest, 0.0), axis=1, keepdims=True)
    label = jnp.sum(jnp.where(mine, own_label, 0.0), axis=1, keepdims=True)
    total = rest + label
    loss = jnp.log(total) - jnp.log(label)
    square = (tok_dev, tok_dev)
    diagonal = lax.broadcasted_iota(jnp.int32, square, 0) == lax.broadcasted_iota(
        jnp.int32, square, 1
    )
    loss_row[...] = jnp.sum(jnp.where(diagonal, loss, 0.0), axis=0, keepdims=True)
    rows = features[...].astype(jnp.float32)
    inv_norm = inverse_norm(rows)
    unit = rows * inv_norm
    cand = sums[:, width : 2 * width]
    cand = (cand * inverse_norm(cand)).astype(jnp.bfloat16).astype(jnp.float32)
    unit_grad = logit_scale / total * (sums[:, :width] - rest * cand)
    along = jnp.sum(unit_grad * unit, axis=1, keepdims=True)
    feature_grad[...] = inv_norm * (unit_grad - along * unit)

    leave(feature_grad, feature_out)
    leave(loss_row, loss_out)
    for b in range(held // 2, held):
        block_out(b)
    for move in moves:
        move.wait()


def exchange(pieces, axes, order=None):
    return lax.all_to_all(
        pieces, axes, split_axis=0, concat_axis=0, axis_index_groups=order, tiled=True
    )


def exchange_chips(pieces):
    chips = lax.axis_size("chip")
    order = [g * chips + chip for chip in reversed(range(chips)) for g in GROUP_ORDER]
    return exchange(pieces, CHIPS, [order])


def with_partner(value):
    return lax.ppermute(value, "core", [(0, 1), (1, 0)])


def on_device(features, labels, centres, block_ids, listed):
    groups = lax.axis_size("group")
    chips = groups * lax.axis_size("chip")
    tok_dev, width = features.shape
    held = centres.shape[0] // BLK
    half = chips * tok_dev
    bf16, f32 = jnp.bfloat16, jnp.float32
    shape = jax.ShapeDtypeStruct

    copies, own_blocks, blocks, named = run(
        load,
        (
            shape((chips, tok_dev, width + 128), bf16),
            shape((groups, BLK, width), bf16),
            shape((held, BLK, width), bf16),
            shape((1, 128), block_ids.dtype),
        ),
        [HBM] * 5,
        *(
            pltpu.with_memory_space_constraint(array, pltpu.HBM)
            for array in (
                features,
                labels.reshape(1, -1),
                centres.reshape(held, BLK, width),
                block_ids.reshape(1, groups),
                listed.reshape(1, groups),
            )
        ),
        scratch=[
            pltpu.VMEM(features.shape, features.dtype),
            pltpu.VMEM((1, labels.shape[0]), labels.dtype),
            pltpu.SMEM((1, groups), block_ids.dtype),
            pltpu.SMEM((1, groups), listed.dtype),
            pltpu.SemaphoreType.DMA((4 + held,)),
        ],
    )
    pair_blocks = with_partner(own_blocks)
    own_packed = exchange_chips(copies).reshape(half, width + 128)
    other_packed = with_partner(own_packed)
    own_expo, pair_expo, inverse, own_sums = run(
        forward,
        (
            shape((BLK, half), f32),
            shape((BLK, half), f32),
            shape((2, BLK, 128), f32),
            shape((2, half), f32),
        ),
        [VMEM] * 3,
        own_packed,
        own_blocks,
        pair_blocks,
    )
    going, norms = run(
        shares,
        (shape((half, 2 * width), bf16), shape((BLK, 128), f32)),
        [VMEM] * 6,
        own_expo,
        pair_expo,
        inverse,
        own_blocks,
        pair_blocks,
        blocks,
    )
    other_expo, sent = run(
        forward_other,
        (shape((BLK, half), f32), shape((half, 2 * width + 128), bf16)),
        [VMEM] * 6,
        other_packed,
        own_blocks,
        pair_blocks,
        inverse,
        own_sums,
        going,
    )
    received = exchange_chips(sent.reshape(chips, tok_dev, 2 * width + 128))
    outs = (shape((held, BLK, width), f32), shape((tok_dev, width), f32), shape((1, tok_dev), f32))
    centre_grad, feature_grad, loss = run(
        backward,
        outs,
        [VMEM] * 9,
        named,
        received,
        own_expo,
        other_expo,
        own_packed,
        other_packed,
        features,
        blocks,
        norms,
        out_spec=HBM,
        scratch=[
            *(pltpu.VMEM(out.shape, out.dtype) for out in outs),
            pltpu.SemaphoreType.DMA((2 * held + 2,)),
        ],
    )
    return (loss.reshape(tok_dev), feature_grad, centre_grad.reshape(held * BLK, width))


def on_device_of_many(features, labels, centres, block_ids, listed):
    groups = lax.axis_size("group")
    members = lax.axis_size("member")
    devices = groups * members
    group = lax.axis_index("group")
    member = lax.axis_index("member")
    tok_dev, width = features.shape
    group_tok = members * tok_dev
    held = centres.shape[0] // BLK

    vectors = features.astype(jnp.float32)
    inv_norm = inverse_norm(vectors)
    unit_rows = vectors * inv_norm
    copies = jnp.broadcast_to(unit_rows.astype(jnp.bfloat16), (devices, tok_dev, width))
    units = exchange(copies, AXES).reshape(groups, group_tok, width)
    all_labels = exchange(jnp.broadcast_to(labels[None], (groups, group_tok)), "group")

    picked = centres.reshape(held, BLK, width)[block_ids[:, 0]].astype(jnp.float32)
    inv_cand = inverse_norm(picked)
    unit_cand = picked * inv_cand
    cand_half = unit_cand.astype(jnp.bfloat16)
    cosine = jnp.einsum("gsd,gcd->gsc", units, cand_half, preferred_element_type=jnp.float32)
    local_label = all_labels - (member * groups + group) * BLK
    onehot = (lax.broadcasted_iota(jnp.int32, (1, 1, BLK), 2) == local_label[:, :, None]).astype(
        jnp.float32
    )
    logits = logit_scale * (cosine - cos_margin * onehot)
    exp_logits = jnp.exp(logits) * listed.astype(jnp.float32)[:, :, None]
    totals, label_logit = lax.psum(
        (jnp.sum(exp_logits, axis=2), jnp.sum(logits * onehot, axis=2)), AXES
    )
    loss_all = (jnp.log(totals) - label_logit).reshape(devices, tok_dev)
    sample_loss = lax.dynamic_slice_in_dim(loss_all, group * members + member, 1, 0)[0]

    weights = (logit_scale * (exp_logits / totals[:, :, None] - onehot)).astype(jnp.bfloat16)
    partial = jnp.einsum("gsc,gcd->gsd", weights, cand_half, preferred_element_type=jnp.float32)
    home = exchange(partial.astype(jnp.bfloat16).reshape(devices, tok_dev, width), AXES)
    unit_grad = jnp.sum(home.astype(jnp.float32), axis=0)
    feature_grad = inv_norm * (
        unit_grad - jnp.sum(unit_grad * unit_rows, axis=1, keepdims=True) * unit_rows
    )
    slot_grad = jnp.einsum("gsc,gsd->gcd", weights, units, preferred_element_type=jnp.float32)
    cand_grad = inv_cand * (
        slot_grad - jnp.sum(slot_grad * unit_cand, axis=2, keepdims=True) * unit_cand
    )
    cand_grad = cand_grad.astype(jnp.bfloat16).astype(jnp.float32)
    names = block_ids == jnp.arange(held, dtype=jnp.int32)[None, :]
    centre_grad = jnp.sum(
        jnp.where(names[:, :, None, None], cand_grad[:, None], 0.0), axis=0
    ).reshape(held * BLK, width)
    return (sample_loss, feature_grad, centre_grad)


def on_axes(body, mesh, axes):
    split = P(axes)
    return jax.shard_map(
        body,
        mesh=mesh,
        in_specs=(split, P("group"), split, P(None, axes), P(None, axes)),
        out_specs=(split, split, split),
        check_vma=False,
    )


def solution(mesh):
    groups, members = mesh.shape["group"], mesh.shape["member"]
    by_core = jax.sharding.Mesh(
        mesh.devices.reshape(groups, members // 2, 2), ("group", "chip", "core")
    )

    def program(features, *others):
        half = features.shape[0] // 2
        if half == 128 and 2 * groups == features.shape[0] // mesh.size == 8:
            return on_axes(on_device, by_core, (*CHIPS, "core"))(features, *others)
        return on_axes(on_device_of_many, mesh, AXES)(features, *others)

    return program
```

```python
import jax
import jax.numpy as jnp
from jax import lax
from jax.experimental import pallas as pl
from jax.experimental.pallas import tpu as pltpu
from jax.sharding import PartitionSpec as P

BLK = 128
AXES = ("group", "member")
CHIPS = ("group", "chip")

logit_scale = 32.0
cos_margin = 0.35
norm_epsilon = 1e-06
GROUP_ORDER = (2, 0, 3, 1)
UNLISTED = 1e19

VMEM = pl.BlockSpec(memory_space=pltpu.VMEM)
HBM = pl.BlockSpec(memory_space=pltpu.HBM)


def inverse_norm(rows):
    return lax.rsqrt(jnp.sum(rows * rows, axis=-1, keepdims=True) + norm_epsilon)


def contract(left, right, left_dim, right_dim):
    dims = (((left_dim,), (right_dim,)), ((), ()))
    return lax.dot_general(left, right, dims, preferred_element_type=jnp.float32)


def lanes(rows):
    return lax.broadcasted_iota(jnp.int32, (rows, 128), 1)


def run(kernel, out_shape, in_specs, *operands, out_spec=VMEM, scratch=()):
    shapes = jax.tree.leaves(out_shape)
    return pl.pallas_call(
        kernel,
        out_shape=out_shape,
        in_specs=in_specs,
        out_specs=jax.tree.map(lambda _: out_spec, out_shape),
        scratch_shapes=scratch,
        compiler_params=pltpu.CompilerParams(vmem_limit_bytes=48 * 1024 * 1024),
        cost_estimate=pl.CostEstimate(
            flops=0,
            transcendentals=0,
            bytes_accessed=sum(a.size * a.dtype.itemsize for a in (*shapes, *operands)),
        ),
    )(*operands)


def load(
    features,
    labels,
    centres,
    ids,
    listed,
    copies_out,
    blocks_out,
    centres_out,
    named_out,
    held_features,
    held_labels,
    held_ids,
    held_listed,
    arrived,
):
    moves = [
        pltpu.make_async_copy(source, target, arrived.at[i])
        for i, (source, target) in enumerate(
            (
                (features, held_features),
                (labels, held_labels),
                (ids, held_ids),
                (listed, held_listed),
                *((centres.at[b], centres_out.at[b]) for b in range(centres.shape[0])),
            )
        )
    ]
    for move in moves:
        move.start()
    moves[0].wait()
    moves[1].wait()
    chip = lax.axis_index("chip")
    member = 2 * chip + lax.axis_index("core")
    copies, tok_dev, _ = copies_out.shape
    width = features.shape[1]
    rows = held_features[...].astype(jnp.float32)
    unit = (rows * inverse_norm(rows)).astype(jnp.bfloat16)
    copies_out[:, :, :width] = jnp.broadcast_to(unit[None], (copies, tok_dev, width))

    place = own_place() * tok_dev
    row = held_labels[...]
    row = jnp.concatenate([row, jnp.zeros((1, 128 - row.shape[1]), jnp.int32)], axis=1)
    row = jnp.broadcast_to(row, (tok_dev, 128))
    row = pltpu.roll(row, lax.rem(place - member * tok_dev + 128, 128), 1)
    digit = lax.broadcasted_iota(jnp.int32, (tok_dev, 128), 0)
    digits = (row >> (7 * jnp.minimum(digit, 3))) & 127
    lane = lanes(tok_dev)
    digits = jnp.where((lane >= place) & (lane < place + tok_dev), digits, 0)
    copies_out[:, :, width:] = jnp.broadcast_to(
        digits.astype(jnp.float32).astype(jnp.bfloat16)[None], (copies, tok_dev, 128)
    )
    for move in moves[2:]:
        move.wait()
    named_out[...] = select([held_ids[0, group] for group in GROUP_ORDER], 1)
    for g, group in enumerate(GROUP_ORDER):
        block = centres_out[held_ids[0, group]]
        blocks_out[g] = jnp.where(held_listed[0, group] > 0, block, jnp.full_like(block, UNLISTED))


def own_place():
    groups, chips = lax.axis_size("group"), lax.axis_size("chip")
    group = lax.axis_index("group")
    place = sum(jnp.where(group == g, k, 0) for k, g in enumerate(GROUP_ORDER))
    return (chips - 1 - lax.axis_index("chip")) * groups + place


def select(parts, rows):
    owner = lax.rem(lanes(1) // 8, len(parts))
    out = jnp.broadcast_to(parts[0], (rows, 128))
    for g in range(1, len(parts)):
        out = jnp.where(owner == g, parts[g], out)
    return out


def exponentials(packed, core, blocks, inverse):
    groups, _, width = blocks.shape
    digits = jnp.sum(
        packed[:, width:].astype(jnp.float32).reshape(128 // 8, 8, 128), axis=0
    ).astype(jnp.int32)
    labels = digits[0:1] + (digits[1:2] << 7) + (digits[2:3] << 14)
    member = 2 * lax.axis_index("chip") + core
    first = (member * groups + lax.axis_index("group")) * BLK
    onehot = lax.broadcasted_iota(jnp.int32, (BLK, 128), 0) == labels - first
    units = packed[:, :width]
    dots = contract(blocks[...].reshape(groups * BLK, width), units, 1, 1)
    cosine = inverse * select([dots[g * BLK : (g + 1) * BLK] for g in range(groups)], BLK)
    expo = jnp.exp(logit_scale * (cosine - jnp.where(onehot, cos_margin, 0.0)))
    return jnp.where(inverse > 0.0, expo, 0.0), onehot, cosine * inverse


def sums(parts):
    rest = [jnp.where(onehot, 0.0, expo) for expo, onehot, _ in parts]
    at_label = [jnp.where(onehot, expo, 0.0) for expo, onehot, _ in parts]
    return [jnp.sum(sum(part), axis=0, keepdims=True) for part in (rest, at_label)]


def forward(packed, own_blocks, pair_blocks, expo_out, scaled_out, inverse_out, sums_out):
    core = lax.axis_index("core")
    parts = []
    for k, blocks in enumerate((own_blocks, pair_blocks)):
        norms = [inverse_norm(blocks[g].astype(jnp.float32)) for g in range(blocks.shape[0])]
        inverse = select(norms, BLK)
        inverse_out[k] = inverse
        part = exponentials(packed, core if k == 0 else 1 - core, blocks, inverse)
        expo_out[k] = jnp.where(part[1], -1.0, part[0])
        parts.append(part)
    scaled_out[...] = parts[0][2]
    sums_out[0:1, :], sums_out[1:2, :] = sums(parts)


def forward_other(
    packed, own_blocks, pair_blocks, inverse, own_sums, shares, expo_out, scaled_out, sent_out
):
    core = lax.axis_index("core")
    own = exponentials(packed, core, own_blocks, inverse[0])
    pair = exponentials(packed, 1 - core, pair_blocks, inverse[1])
    expo_out[...] = jnp.where(own[1], -1.0, own[0])
    scaled_out[...] = own[2]
    rows, wide = shares.shape
    sent_out[:, :wide] = shares[...]
    total = jnp.concatenate([own_sums[...], *sums([own, pair])], axis=0)
    high = total.astype(jnp.bfloat16)
    low = (total - high.astype(jnp.float32)).astype(jnp.bfloat16)
    tile = jnp.concatenate([high.astype(jnp.float32), low.astype(jnp.float32)], axis=0)
    tile = jnp.broadcast_to(tile[None], (rows // 8, 8, 128))
    sent_out[:, wide:] = tile.reshape(rows, 128).astype(jnp.bfloat16)


def shares(expo, inverse, own_blocks, pair_blocks, shares_out):
    groups, _, width = own_blocks.shape
    others, label = [], []
    for k in range(2):
        others.append((jnp.maximum(expo[k], 0.0) * inverse[k]).T)
        label.append(jnp.where(expo[k] < 0.0, 1.0, 0.0).T)
    others = jnp.concatenate(others, axis=1)
    label = jnp.concatenate(label, axis=1)
    places = [[] for _ in range(groups)]
    for g in range(groups):
        rows = [part[p * 8 : p * 8 + 8] for part in (others, label) for p in range(g, 16, groups)]
        blocks = jnp.concatenate([own_blocks[g], pair_blocks[g]], axis=0)
        both = contract(jnp.concatenate(rows, axis=0).astype(jnp.bfloat16), blocks, 1, 0)
        places[g] = [both[i * 8 : i * 8 + 8] for i in range(len(rows))]
    for part in range(2):
        count = 16 // groups
        rows = [places[g][part * count + i] for i in range(count) for g in range(groups)]
        rows = jnp.concatenate(rows, axis=0).astype(jnp.bfloat16)
        shares_out[:, part * width : (part + 1) * width] = rows


def backward(
    named,
    received,
    expo,
    other_expo,
    scaled,
    other_scaled,
    inverse,
    own_packed,
    other_packed,
    features,
    centres,
    grad_out,
    feature_out,
    loss_out,
    grad,
    feature_grad,
    loss_row,
    left,
):
    held = centres.shape[0]
    tok_dev, width = features.shape

    def total_of(columns):
        total = received[0, :, columns].astype(jnp.float32)
        for i in range(1, received.shape[0]):
            total = total + received[i, :, columns].astype(jnp.float32)
        return total

    tile = total_of(pl.ds(2 * width, 128))
    tile = tile[:4] + tile[4:]
    own_rest, own_label = tile[0:1], tile[1:2]
    other_rest, other_label = tile[2:3], tile[3:4]

    units = jnp.concatenate([own_packed[:, :width], other_packed[:, :width]], axis=0)
    own_scale = logit_scale / (own_rest + own_label)
    other_scale = logit_scale / (other_rest + other_label)
    own = expo[0]
    other = other_expo[...]
    own = jnp.where(own < 0.0, -own_rest, own) * (own_scale * inverse[0])
    other = jnp.where(other < 0.0, -other_rest, other) * (other_scale * inverse[0])
    weights = jnp.concatenate([own, other], axis=1)
    pulls = weights * jnp.concatenate([scaled[...], other_scaled[...]], axis=1)
    named = jnp.concatenate([named[...], named[...]], axis=1)
    moves = []

    def leave(source, target):
        move = pltpu.make_async_copy(source, target, left.at[len(moves)])
        move.start()
        moves.append(move)

    def block_out(b):
        mine = jnp.where(named == b, weights, 0.0).astype(jnp.bfloat16)
        back = jnp.sum(jnp.where(named == b, pulls, 0.0), axis=1, keepdims=True)
        grad[b] = contract(mine, units, 1, 0) - back * centres[b].astype(jnp.float32)
        for part in (pl.ds(0, BLK // 2), pl.ds(BLK // 2, BLK // 2)):
            leave(grad.at[b, part], grad_out.at[b, part])

    for b in range(held // 2):
        block_out(b)

    sums = total_of(pl.ds(0, 2 * width))
    sample = lax.broadcasted_iota(jnp.int32, (tok_dev, 128), 0) + own_place() * tok_dev
    mine = lanes(tok_dev) == sample
    rest = jnp.sum(jnp.where(mine, own_rest, 0.0), axis=1, keepdims=True)
    label = jnp.sum(jnp.where(mine, own_label, 0.0), axis=1, keepdims=True)
    total = rest + label
    loss = jnp.log(total) - jnp.log(label)
    square = (tok_dev, tok_dev)
    diagonal = lax.broadcasted_iota(jnp.int32, square, 0) == lax.broadcasted_iota(
        jnp.int32, square, 1
    )
    loss_row[...] = jnp.sum(jnp.where(diagonal, loss, 0.0), axis=0, keepdims=True)
    rows = features[...].astype(jnp.float32)
    inv_norm = inverse_norm(rows)
    unit = rows * inv_norm
    cand = sums[:, width : 2 * width]
    cand = (cand * inverse_norm(cand)).astype(jnp.bfloat16).astype(jnp.float32)
    unit_grad = logit_scale / total * (sums[:, :width] - rest * cand)
    along = jnp.sum(unit_grad * unit, axis=1, keepdims=True)
    feature_grad[...] = inv_norm * (unit_grad - along * unit)

    leave(feature_grad, feature_out)
    leave(loss_row, loss_out)
    for b in range(held // 2, held):
        block_out(b)
    for move in moves:
        move.wait()


def exchange(pieces, axes, order=None):
    return lax.all_to_all(
        pieces, axes, split_axis=0, concat_axis=0, axis_index_groups=order, tiled=True
    )


def exchange_chips(pieces):
    chips = lax.axis_size("chip")
    order = [g * chips + chip for chip in reversed(range(chips)) for g in GROUP_ORDER]
    return exchange(pieces, CHIPS, [order])


def with_partner(value):
    return lax.ppermute(value, "core", [(0, 1), (1, 0)])


def on_device(features, labels, centres, block_ids, listed):
    groups = lax.axis_size("group")
    chips = groups * lax.axis_size("chip")
    tok_dev, width = features.shape
    held = centres.shape[0] // BLK
    half = chips * tok_dev
    bf16, f32 = jnp.bfloat16, jnp.float32
    shape = jax.ShapeDtypeStruct

    copies, own_blocks, blocks, named = run(
        load,
        (
            shape((chips, tok_dev, width + 128), bf16),
            shape((groups, BLK, width), bf16),
            shape((held, BLK, width), bf16),
            shape((1, 128), block_ids.dtype),
        ),
        [HBM] * 5,
        *(
            pltpu.with_memory_space_constraint(array, pltpu.HBM)
            for array in (
                features,
                labels.reshape(1, -1),
                centres.reshape(held, BLK, width),
                block_ids.reshape(1, groups),
                listed.reshape(1, groups),
            )
        ),
        scratch=[
            pltpu.VMEM(features.shape, features.dtype),
            pltpu.VMEM((1, labels.shape[0]), labels.dtype),
            pltpu.SMEM((1, groups), block_ids.dtype),
            pltpu.SMEM((1, groups), listed.dtype),
            pltpu.SemaphoreType.DMA((4 + held,)),
        ],
    )
    pair_blocks = with_partner(own_blocks)
    own_packed = exchange_chips(copies).reshape(half, width + 128)
    other_packed = with_partner(own_packed)
    expo, scaled, inverse, own_sums = run(
        forward,
        (
            shape((2, BLK, half), f32),
            shape((BLK, half), f32),
            shape((2, BLK, half), f32),
            shape((2, half), f32),
        ),
        [VMEM] * 3,
        own_packed,
        own_blocks,
        pair_blocks,
    )
    going = run(
        shares,
        shape((half, 2 * width), bf16),
        [VMEM] * 4,
        expo,
        inverse,
        own_blocks,
        pair_blocks,
    )
    other_expo, other_scaled, sent = run(
        forward_other,
        (
            shape((BLK, half), f32),
            shape((BLK, half), f32),
            shape((half, 2 * width + 128), bf16),
        ),
        [VMEM] * 6,
        other_packed,
        own_blocks,
        pair_blocks,
        inverse,
        own_sums,
        going,
    )
    received = exchange_chips(sent.reshape(chips, tok_dev, 2 * width + 128))
    outs = (shape((held, BLK, width), f32), shape((tok_dev, width), f32), shape((1, tok_dev), f32))
    centre_grad, feature_grad, loss = run(
        backward,
        outs,
        [VMEM] * 11,
        named,
        received,
        expo,
        other_expo,
        scaled,
        other_scaled,
        inverse,
        own_packed,
        other_packed,
        features,
        blocks,
        out_spec=HBM,
        scratch=[
            *(pltpu.VMEM(out.shape, out.dtype) for out in outs),
            pltpu.SemaphoreType.DMA((2 * held + 2,)),
        ],
    )
    return (loss.reshape(tok_dev), feature_grad, centre_grad.reshape(held * BLK, width))


def on_device_of_many(features, labels, centres, block_ids, listed):
    groups = lax.axis_size("group")
    members = lax.axis_size("member")
    devices = groups * members
    group = lax.axis_index("group")
    member = lax.axis_index("member")
    tok_dev, width = features.shape
    group_tok = members * tok_dev
    held = centres.shape[0] // BLK

    vectors = features.astype(jnp.float32)
    inv_norm = inverse_norm(vectors)
    unit_rows = vectors * inv_norm
    copies = jnp.broadcast_to(unit_rows.astype(jnp.bfloat16), (devices, tok_dev, width))
    units = exchange(copies, AXES).reshape(groups, group_tok, width)
    all_labels = exchange(jnp.broadcast_to(labels[None], (groups, group_tok)), "group")

    picked = centres.reshape(held, BLK, width)[block_ids[:, 0]].astype(jnp.float32)
    inv_cand = inverse_norm(picked)
    unit_cand = picked * inv_cand
    cand_half = unit_cand.astype(jnp.bfloat16)
    cosine = jnp.einsum("gsd,gcd->gsc", units, cand_half, preferred_element_type=jnp.float32)
    local_label = all_labels - (member * groups + group) * BLK
    onehot = (lax.broadcasted_iota(jnp.int32, (1, 1, BLK), 2) == local_label[:, :, None]).astype(
        jnp.float32
    )
    logits = logit_scale * (cosine - cos_margin * onehot)
    exp_logits = jnp.exp(logits) * listed.astype(jnp.float32)[:, :, None]
    totals, label_logit = lax.psum(
        (jnp.sum(exp_logits, axis=2), jnp.sum(logits * onehot, axis=2)), AXES
    )
    loss_all = (jnp.log(totals) - label_logit).reshape(devices, tok_dev)
    sample_loss = lax.dynamic_slice_in_dim(loss_all, group * members + member, 1, 0)[0]

    weights = (logit_scale * (exp_logits / totals[:, :, None] - onehot)).astype(jnp.bfloat16)
    partial = jnp.einsum("gsc,gcd->gsd", weights, cand_half, preferred_element_type=jnp.float32)
    home = exchange(partial.astype(jnp.bfloat16).reshape(devices, tok_dev, width), AXES)
    unit_grad = jnp.sum(home.astype(jnp.float32), axis=0)
    feature_grad = inv_norm * (
        unit_grad - jnp.sum(unit_grad * unit_rows, axis=1, keepdims=True) * unit_rows
    )
    slot_grad = jnp.einsum("gsc,gsd->gcd", weights, units, preferred_element_type=jnp.float32)
    cand_grad = inv_cand * (
        slot_grad - jnp.sum(slot_grad * unit_cand, axis=2, keepdims=True) * unit_cand
    )
    cand_grad = cand_grad.astype(jnp.bfloat16).astype(jnp.float32)
    names = block_ids == jnp.arange(held, dtype=jnp.int32)[None, :]
    centre_grad = jnp.sum(
        jnp.where(names[:, :, None, None], cand_grad[:, None], 0.0), axis=0
    ).reshape(held * BLK, width)
    return (sample_loss, feature_grad, centre_grad)


def on_axes(body, mesh, axes):
    split = P(axes)
    return jax.shard_map(
        body,
        mesh=mesh,
        in_specs=(split, P("group"), split, P(None, axes), P(None, axes)),
        out_specs=(split, split, split),
        check_vma=False,
    )


def solution(mesh):
    groups, members = mesh.shape["group"], mesh.shape["member"]
    by_core = jax.sharding.Mesh(
        mesh.devices.reshape(groups, members // 2, 2), ("group", "chip", "core")
    )

    def program(features, *others):
        half = features.shape[0] // 2
        if half == 128 and 2 * groups == features.shape[0] // mesh.size == 8:
            return on_axes(on_device, by_core, (*CHIPS, "core"))(features, *others)
        return on_axes(on_device_of_many, mesh, AXES)(features, *others)

    return program
```

```python
import jax
import jax.numpy as jnp
from jax import lax
from jax.experimental import pallas as pl
from jax.experimental.pallas import tpu as pltpu
from jax.sharding import PartitionSpec as P

BLK = 128
AXES = ("group", "member")
CHIPS = ("group", "chip")

logit_scale = 32.0
cos_margin = 0.35
norm_epsilon = 1e-06
GROUP_ORDER = (2, 0, 3, 1)
UNLISTED = 1e19

VMEM = pl.BlockSpec(memory_space=pltpu.VMEM)
HBM = pl.BlockSpec(memory_space=pltpu.HBM)


def inverse_norm(rows):
    return lax.rsqrt(jnp.sum(rows * rows, axis=-1, keepdims=True) + norm_epsilon)


def contract(left, right, left_dim, right_dim):
    dims = (((left_dim,), (right_dim,)), ((), ()))
    return lax.dot_general(left, right, dims, preferred_element_type=jnp.float32)


def lanes(rows):
    return lax.broadcasted_iota(jnp.int32, (rows, 128), 1)


def run(kernel, out_shape, in_specs, *operands, out_spec=VMEM, scratch=()):
    shapes = jax.tree.leaves(out_shape)
    return pl.pallas_call(
        kernel,
        out_shape=out_shape,
        in_specs=in_specs,
        out_specs=jax.tree.map(lambda _: out_spec, out_shape),
        scratch_shapes=scratch,
        compiler_params=pltpu.CompilerParams(vmem_limit_bytes=48 * 1024 * 1024),
        cost_estimate=pl.CostEstimate(
            flops=0,
            transcendentals=0,
            bytes_accessed=sum(a.size * a.dtype.itemsize for a in (*shapes, *operands)),
        ),
    )(*operands)


def load(
    features,
    labels,
    centres,
    ids,
    listed,
    copies_out,
    blocks_out,
    centres_out,
    named_out,
    held_features,
    held_labels,
    held_ids,
    held_listed,
    arrived,
):
    moves = [
        pltpu.make_async_copy(source, target, arrived.at[i])
        for i, (source, target) in enumerate(
            (
                (features, held_features),
                (labels, held_labels),
                (ids, held_ids),
                (listed, held_listed),
                (centres, centres_out),
            )
        )
    ]
    for move in moves:
        move.start()
    moves[0].wait()
    moves[1].wait()
    chip = lax.axis_index("chip")
    member = 2 * chip + lax.axis_index("core")
    copies, tok_dev, _ = copies_out.shape
    width = features.shape[1]
    rows = held_features[...].astype(jnp.float32)
    unit = (rows * inverse_norm(rows)).astype(jnp.bfloat16)
    copies_out[:, :, :width] = jnp.broadcast_to(unit[None], (copies, tok_dev, width))

    place = own_place() * tok_dev
    row = held_labels[...]
    row = jnp.concatenate([row, jnp.zeros((1, 128 - row.shape[1]), jnp.int32)], axis=1)
    row = jnp.broadcast_to(row, (tok_dev, 128))
    row = pltpu.roll(row, lax.rem(place - member * tok_dev + 128, 128), 1)
    digit = lax.broadcasted_iota(jnp.int32, (tok_dev, 128), 0)
    digits = (row >> (7 * jnp.minimum(digit, 3))) & 127
    lane = lanes(tok_dev)
    digits = jnp.where((lane >= place) & (lane < place + tok_dev), digits, 0)
    copies_out[:, :, width:] = jnp.broadcast_to(
        digits.astype(jnp.float32).astype(jnp.bfloat16)[None], (copies, tok_dev, 128)
    )
    for move in moves[2:]:
        move.wait()
    named_out[...] = select([held_ids[0, group] for group in GROUP_ORDER], 1)
    for g, group in enumerate(GROUP_ORDER):
        block = centres_out[held_ids[0, group]]
        blocks_out[g] = jnp.where(held_listed[0, group] > 0, block, jnp.full_like(block, UNLISTED))


def own_place():
    groups, chips = lax.axis_size("group"), lax.axis_size("chip")
    group = lax.axis_index("group")
    place = sum(jnp.where(group == g, k, 0) for k, g in enumerate(GROUP_ORDER))
    return (chips - 1 - lax.axis_index("chip")) * groups + place


def select(parts, rows):
    owner = lax.rem(lanes(1) // 8, len(parts))
    out = jnp.broadcast_to(parts[0], (rows, 128))
    for g in range(1, len(parts)):
        out = jnp.where(owner == g, parts[g], out)
    return out


def exponentials(packed, core, blocks, inverse):
    groups, _, width = blocks.shape
    digits = jnp.sum(
        packed[:, width:].astype(jnp.float32).reshape(128 // 8, 8, 128), axis=0
    ).astype(jnp.int32)
    labels = digits[0:1] + (digits[1:2] << 7) + (digits[2:3] << 14)
    member = 2 * lax.axis_index("chip") + core
    first = (member * groups + lax.axis_index("group")) * BLK
    onehot = lax.broadcasted_iota(jnp.int32, (BLK, 128), 0) == labels - first
    units = packed[:, :width]
    dots = contract(blocks[...].reshape(groups * BLK, width), units, 1, 1)
    cosine = inverse * select([dots[g * BLK : (g + 1) * BLK] for g in range(groups)], BLK)
    expo = jnp.exp(logit_scale * (cosine - jnp.where(onehot, cos_margin, 0.0)))
    return jnp.where(inverse > 0.0, expo, 0.0), onehot, cosine * inverse


def sums(parts):
    rest = [jnp.where(onehot, 0.0, expo) for expo, onehot, _ in parts]
    at_label = [jnp.where(onehot, expo, 0.0) for expo, onehot, _ in parts]
    return [jnp.sum(sum(part), axis=0, keepdims=True) for part in (rest, at_label)]


def forward(packed, own_blocks, pair_blocks, expo_out, scaled_out, inverse_out, sums_out):
    core = lax.axis_index("core")
    parts = []
    for k, blocks in enumerate((own_blocks, pair_blocks)):
        norms = [inverse_norm(blocks[g].astype(jnp.float32)) for g in range(blocks.shape[0])]
        inverse = select(norms, BLK)
        inverse_out[k] = inverse
        part = exponentials(packed, core if k == 0 else 1 - core, blocks, inverse)
        expo_out[k] = jnp.where(part[1], -1.0, part[0])
        parts.append(part)
    scaled_out[...] = parts[0][2]
    sums_out[0:1, :], sums_out[1:2, :] = sums(parts)


def forward_other(
    packed, own_blocks, pair_blocks, inverse, own_sums, shares, expo_out, scaled_out, sent_out
):
    core = lax.axis_index("core")
    own = exponentials(packed, core, own_blocks, inverse[0])
    pair = exponentials(packed, 1 - core, pair_blocks, inverse[1])
    expo_out[...] = jnp.where(own[1], -1.0, own[0])
    scaled_out[...] = own[2]
    rows, wide = shares.shape
    sent_out[:, :wide] = shares[...]
    total = jnp.concatenate([own_sums[...], *sums([own, pair])], axis=0)
    high = total.astype(jnp.bfloat16)
    low = (total - high.astype(jnp.float32)).astype(jnp.bfloat16)
    tile = jnp.concatenate([high.astype(jnp.float32), low.astype(jnp.float32)], axis=0)
    tile = jnp.broadcast_to(tile[None], (rows // 8, 8, 128))
    sent_out[:, wide:] = tile.reshape(rows, 128).astype(jnp.bfloat16)


def shares(expo, inverse, own_blocks, pair_blocks, shares_out):
    groups, _, width = own_blocks.shape
    others, label = [], []
    for k in range(2):
        others.append((jnp.maximum(expo[k], 0.0) * inverse[k]).T)
        label.append(jnp.where(expo[k] < 0.0, 1.0, 0.0).T)
    others = jnp.concatenate(others, axis=1)
    label = jnp.concatenate(label, axis=1)
    places = [[] for _ in range(groups)]
    for g in range(groups):
        rows = [part[p * 8 : p * 8 + 8] for part in (others, label) for p in range(g, 16, groups)]
        blocks = jnp.concatenate([own_blocks[g], pair_blocks[g]], axis=0)
        both = contract(jnp.concatenate(rows, axis=0).astype(jnp.bfloat16), blocks, 1, 0)
        places[g] = [both[i * 8 : i * 8 + 8] for i in range(len(rows))]
    for part in range(2):
        count = 16 // groups
        rows = [places[g][part * count + i] for i in range(count) for g in range(groups)]
        rows = jnp.concatenate(rows, axis=0).astype(jnp.bfloat16)
        shares_out[:, part * width : (part + 1) * width] = rows


def backward(
    named,
    received,
    expo,
    other_expo,
    scaled,
    other_scaled,
    inverse,
    own_packed,
    other_packed,
    features,
    centres,
    grad_out,
    feature_out,
    loss_out,
    grad,
    feature_grad,
    loss_row,
    left,
):
    held = centres.shape[0]
    tok_dev, width = features.shape

    def total_of(columns):
        total = received[0, :, columns].astype(jnp.float32)
        for i in range(1, received.shape[0]):
            total = total + received[i, :, columns].astype(jnp.float32)
        return total

    tile = total_of(pl.ds(2 * width, 128))
    tile = tile[:4] + tile[4:]
    own_rest, own_label = tile[0:1], tile[1:2]
    other_rest, other_label = tile[2:3], tile[3:4]

    units = jnp.concatenate([own_packed[:, :width], other_packed[:, :width]], axis=0)
    own_scale = logit_scale / (own_rest + own_label)
    other_scale = logit_scale / (other_rest + other_label)
    own = expo[0]
    other = other_expo[...]
    own = jnp.where(own < 0.0, -own_rest, own) * (own_scale * inverse[0])
    other = jnp.where(other < 0.0, -other_rest, other) * (other_scale * inverse[0])
    weights = jnp.concatenate([own, other], axis=1)
    pulls = weights * jnp.concatenate([scaled[...], other_scaled[...]], axis=1)
    named = jnp.concatenate([named[...], named[...]], axis=1)
    moves = []

    def leave(source, target):
        move = pltpu.make_async_copy(source, target, left.at[len(moves)])
        move.start()
        moves.append(move)

    def block_out(b):
        mine = jnp.where(named == b, weights, 0.0).astype(jnp.bfloat16)
        back = jnp.sum(jnp.where(named == b, pulls, 0.0), axis=1, keepdims=True)
        grad[b] = contract(mine, units, 1, 0) - back * centres[b].astype(jnp.float32)
        for part in (pl.ds(0, BLK // 2), pl.ds(BLK // 2, BLK // 2)):
            leave(grad.at[b, part], grad_out.at[b, part])

    for b in range(held // 2):
        block_out(b)

    sums = total_of(pl.ds(0, 2 * width))
    sample = lax.broadcasted_iota(jnp.int32, (tok_dev, 128), 0) + own_place() * tok_dev
    mine = lanes(tok_dev) == sample
    rest = jnp.sum(jnp.where(mine, own_rest, 0.0), axis=1, keepdims=True)
    label = jnp.sum(jnp.where(mine, own_label, 0.0), axis=1, keepdims=True)
    total = rest + label
    loss = jnp.log(total) - jnp.log(label)
    square = (tok_dev, tok_dev)
    diagonal = lax.broadcasted_iota(jnp.int32, square, 0) == lax.broadcasted_iota(
        jnp.int32, square, 1
    )
    loss_row[...] = jnp.sum(jnp.where(diagonal, loss, 0.0), axis=0, keepdims=True)
    rows = features[...].astype(jnp.float32)
    inv_norm = inverse_norm(rows)
    unit = rows * inv_norm
    cand = sums[:, width : 2 * width]
    cand = (cand * inverse_norm(cand)).astype(jnp.bfloat16).astype(jnp.float32)
    unit_grad = logit_scale / total * (sums[:, :width] - rest * cand)
    along = jnp.sum(unit_grad * unit, axis=1, keepdims=True)
    feature_grad[...] = inv_norm * (unit_grad - along * unit)

    leave(feature_grad, feature_out)
    leave(loss_row, loss_out)
    for b in range(held // 2, held):
        block_out(b)
    for move in moves:
        move.wait()


def exchange(pieces, axes, order=None):
    return lax.all_to_all(
        pieces, axes, split_axis=0, concat_axis=0, axis_index_groups=order, tiled=True
    )


def exchange_chips(pieces):
    chips = lax.axis_size("chip")
    order = [g * chips + chip for chip in reversed(range(chips)) for g in GROUP_ORDER]
    return exchange(pieces, CHIPS, [order])


def with_partner(value):
    return lax.ppermute(value, "core", [(0, 1), (1, 0)])


def on_device(features, labels, centres, block_ids, listed):
    groups = lax.axis_size("group")
    chips = groups * lax.axis_size("chip")
    tok_dev, width = features.shape
    held = centres.shape[0] // BLK
    half = chips * tok_dev
    bf16, f32 = jnp.bfloat16, jnp.float32
    shape = jax.ShapeDtypeStruct

    copies, own_blocks, blocks, named, own_features = run(
        load,
        (
            shape((chips, tok_dev, width + 128), bf16),
            shape((groups, BLK, width), bf16),
            shape((held, BLK, width), bf16),
            shape((1, 128), block_ids.dtype),
            shape(features.shape, bf16),
        ),
        [HBM] * 5,
        *(
            pltpu.with_memory_space_constraint(array, pltpu.HBM)
            for array in (
                features,
                labels.reshape(1, -1),
                centres.reshape(held, BLK, width),
                block_ids.reshape(1, groups),
                listed.reshape(1, groups),
            )
        ),
        scratch=[
            pltpu.VMEM((1, labels.shape[0]), labels.dtype),
            pltpu.SMEM((1, groups), block_ids.dtype),
            pltpu.SMEM((1, groups), listed.dtype),
            pltpu.SemaphoreType.DMA((5,)),
        ],
    )
    pair_blocks = with_partner(own_blocks)
    own_packed = exchange_chips(copies).reshape(half, width + 128)
    other_packed = with_partner(own_packed)
    expo, scaled, inverse, own_sums = run(
        forward,
        (
            shape((2, BLK, half), f32),
            shape((BLK, half), f32),
            shape((2, BLK, half), f32),
            shape((2, half), f32),
        ),
        [VMEM] * 3,
        own_packed,
        own_blocks,
        pair_blocks,
    )
    going = run(
        shares,
        shape((half, 2 * width), bf16),
        [VMEM] * 4,
        expo,
        inverse,
        own_blocks,
        pair_blocks,
    )
    other_expo, other_scaled, sent = run(
        forward_other,
        (
            shape((BLK, half), f32),
            shape((BLK, half), f32),
            shape((half, 2 * width + 128), bf16),
        ),
        [VMEM] * 6,
        other_packed,
        own_blocks,
        pair_blocks,
        inverse,
        own_sums,
        going,
    )
    received = exchange_chips(sent.reshape(chips, tok_dev, 2 * width + 128))
    outs = (shape((held, BLK, width), f32), shape((tok_dev, width), f32), shape((1, tok_dev), f32))
    centre_grad, feature_grad, loss = run(
        backward,
        outs,
        [VMEM] * 11,
        named,
        received,
        expo,
        other_expo,
        scaled,
        other_scaled,
        inverse,
        own_packed,
        other_packed,
        own_features,
        blocks,
        out_spec=HBM,
        scratch=[
            *(pltpu.VMEM(out.shape, out.dtype) for out in outs),
            pltpu.SemaphoreType.DMA((2 * held + 2,)),
        ],
    )
    return (loss.reshape(tok_dev), feature_grad, centre_grad.reshape(held * BLK, width))


def on_device_of_many(features, labels, centres, block_ids, listed):
    groups = lax.axis_size("group")
    members = lax.axis_size("member")
    devices = groups * members
    group = lax.axis_index("group")
    member = lax.axis_index("member")
    tok_dev, width = features.shape
    group_tok = members * tok_dev
    held = centres.shape[0] // BLK

    vectors = features.astype(jnp.float32)
    inv_norm = inverse_norm(vectors)
    unit_rows = vectors * inv_norm
    copies = jnp.broadcast_to(unit_rows.astype(jnp.bfloat16), (devices, tok_dev, width))
    units = exchange(copies, AXES).reshape(groups, group_tok, width)
    all_labels = exchange(jnp.broadcast_to(labels[None], (groups, group_tok)), "group")

    picked = centres.reshape(held, BLK, width)[block_ids[:, 0]].astype(jnp.float32)
    inv_cand = inverse_norm(picked)
    unit_cand = picked * inv_cand
    cand_half = unit_cand.astype(jnp.bfloat16)
    cosine = jnp.einsum("gsd,gcd->gsc", units, cand_half, preferred_element_type=jnp.float32)
    local_label = all_labels - (member * groups + group) * BLK
    onehot = (lax.broadcasted_iota(jnp.int32, (1, 1, BLK), 2) == local_label[:, :, None]).astype(
        jnp.float32
    )
    logits = logit_scale * (cosine - cos_margin * onehot)
    exp_logits = jnp.exp(logits) * listed.astype(jnp.float32)[:, :, None]
    totals, label_logit = lax.psum(
        (jnp.sum(exp_logits, axis=2), jnp.sum(logits * onehot, axis=2)), AXES
    )
    loss_all = (jnp.log(totals) - label_logit).reshape(devices, tok_dev)
    sample_loss = lax.dynamic_slice_in_dim(loss_all, group * members + member, 1, 0)[0]

    weights = (logit_scale * (exp_logits / totals[:, :, None] - onehot)).astype(jnp.bfloat16)
    partial = jnp.einsum("gsc,gcd->gsd", weights, cand_half, preferred_element_type=jnp.float32)
    home = exchange(partial.astype(jnp.bfloat16).reshape(devices, tok_dev, width), AXES)
    unit_grad = jnp.sum(home.astype(jnp.float32), axis=0)
    feature_grad = inv_norm * (
        unit_grad - jnp.sum(unit_grad * unit_rows, axis=1, keepdims=True) * unit_rows
    )
    slot_grad = jnp.einsum("gsc,gsd->gcd", weights, units, preferred_element_type=jnp.float32)
    cand_grad = inv_cand * (
        slot_grad - jnp.sum(slot_grad * unit_cand, axis=2, keepdims=True) * unit_cand
    )
    cand_grad = cand_grad.astype(jnp.bfloat16).astype(jnp.float32)
    names = block_ids == jnp.arange(held, dtype=jnp.int32)[None, :]
    centre_grad = jnp.sum(
        jnp.where(names[:, :, None, None], cand_grad[:, None], 0.0), axis=0
    ).reshape(held * BLK, width)
    return (sample_loss, feature_grad, centre_grad)


def on_axes(body, mesh, axes):
    split = P(axes)
    return jax.shard_map(
        body,
        mesh=mesh,
        in_specs=(split, P("group"), split, P(None, axes), P(None, axes)),
        out_specs=(split, split, split),
        check_vma=False,
    )


def solution(mesh):
    groups, members = mesh.shape["group"], mesh.shape["member"]
    by_core = jax.sharding.Mesh(
        mesh.devices.reshape(groups, members // 2, 2), ("group", "chip", "core")
    )

    def program(features, *others):
        half = features.shape[0] // 2
        if half == 128 and 2 * groups == features.shape[0] // mesh.size == 8:
            return on_axes(on_device, by_core, (*CHIPS, "core"))(features, *others)
        return on_axes(on_device_of_many, mesh, AXES)(features, *others)

    return program
```

```python
import jax
import jax.numpy as jnp
from jax import lax
from jax.experimental import pallas as pl
from jax.experimental.pallas import tpu as pltpu
from jax.sharding import PartitionSpec as P

BLK = 128
AXES = ("group", "member")
CHIPS = ("group", "chip")

logit_scale = 32.0
cos_margin = 0.35
norm_epsilon = 1e-06
GROUP_ORDER = (1, 3, 0, 2)
UNLISTED = 1e19

VMEM = pl.BlockSpec(memory_space=pltpu.VMEM)
HBM = pl.BlockSpec(memory_space=pltpu.HBM)


def inverse_norm(rows):
    return lax.rsqrt(jnp.sum(rows * rows, axis=-1, keepdims=True) + norm_epsilon)


def contract(left, right, left_dim, right_dim):
    dims = (((left_dim,), (right_dim,)), ((), ()))
    return lax.dot_general(left, right, dims, preferred_element_type=jnp.float32)


def lanes(rows):
    return lax.broadcasted_iota(jnp.int32, (rows, 128), 1)


def run(kernel, out_shape, in_specs, *operands, out_spec=VMEM, scratch=()):
    shapes = jax.tree.leaves(out_shape)
    return pl.pallas_call(
        kernel,
        out_shape=out_shape,
        in_specs=in_specs,
        out_specs=jax.tree.map(lambda _: out_spec, out_shape),
        scratch_shapes=scratch,
        compiler_params=pltpu.CompilerParams(vmem_limit_bytes=48 * 1024 * 1024),
        cost_estimate=pl.CostEstimate(
            flops=0,
            transcendentals=0,
            bytes_accessed=sum(a.size * a.dtype.itemsize for a in (*shapes, *operands)),
        ),
    )(*operands)


def load(
    features,
    labels,
    centres,
    ids,
    listed,
    copies_out,
    blocks_out,
    centres_out,
    named_out,
    held_features,
    held_labels,
    held_ids,
    held_listed,
    arrived,
):
    moves = [
        pltpu.make_async_copy(source, target, arrived.at[i])
        for i, (source, target) in enumerate(
            (
                (features, held_features),
                (labels, held_labels),
                (ids, held_ids),
                (listed, held_listed),
                (centres, centres_out),
            )
        )
    ]
    for move in moves:
        move.start()
    moves[0].wait()
    moves[1].wait()
    chip = lax.axis_index("chip")
    member = 2 * chip + lax.axis_index("core")
    copies, tok_dev, _ = copies_out.shape
    width = features.shape[1]
    rows = held_features[...].astype(jnp.float32)
    unit = (rows * inverse_norm(rows)).astype(jnp.bfloat16)
    copies_out[:, :, :width] = jnp.broadcast_to(unit[None], (copies, tok_dev, width))

    place = own_place() * tok_dev
    row = held_labels[...]
    row = jnp.concatenate([row, jnp.zeros((1, 128 - row.shape[1]), jnp.int32)], axis=1)
    row = jnp.broadcast_to(row, (tok_dev, 128))
    row = pltpu.roll(row, lax.rem(place - member * tok_dev + 128, 128), 1)
    digit = lax.broadcasted_iota(jnp.int32, (tok_dev, 128), 0)
    digits = (row >> (7 * jnp.minimum(digit, 3))) & 127
    lane = lanes(tok_dev)
    digits = jnp.where((lane >= place) & (lane < place + tok_dev), digits, 0)
    copies_out[:, :, width:] = jnp.broadcast_to(
        digits.astype(jnp.float32).astype(jnp.bfloat16)[None], (copies, tok_dev, 128)
    )
    for move in moves[2:]:
        move.wait()
    named_out[...] = select([held_ids[0, group] for group in GROUP_ORDER], 1)
    for g, group in enumerate(GROUP_ORDER):
        block = centres_out[held_ids[0, group]]
        blocks_out[g] = jnp.where(held_listed[0, group] > 0, block, jnp.full_like(block, UNLISTED))


def own_place():
    groups, chips = lax.axis_size("group"), lax.axis_size("chip")
    group = lax.axis_index("group")
    place = sum(jnp.where(group == g, k, 0) for k, g in enumerate(GROUP_ORDER))
    return (chips - 1 - lax.axis_index("chip")) * groups + place


def select(parts, rows):
    owner = lax.rem(lanes(1) // 8, len(parts))
    out = jnp.broadcast_to(parts[0], (rows, 128))
    for g in range(1, len(parts)):
        out = jnp.where(owner == g, parts[g], out)
    return out


def exponentials(packed, core, blocks, inverse):
    groups, _, width = blocks.shape
    digits = jnp.sum(
        packed[:, width:].astype(jnp.float32).reshape(128 // 8, 8, 128), axis=0
    ).astype(jnp.int32)
    labels = digits[0:1] + (digits[1:2] << 7) + (digits[2:3] << 14)
    member = 2 * lax.axis_index("chip") + core
    first = (member * groups + lax.axis_index("group")) * BLK
    onehot = lax.broadcasted_iota(jnp.int32, (BLK, 128), 0) == labels - first
    units = packed[:, :width]
    dots = contract(blocks[...].reshape(groups * BLK, width), units, 1, 1)
    cosine = inverse * select([dots[g * BLK : (g + 1) * BLK] for g in range(groups)], BLK)
    expo = jnp.exp(logit_scale * (cosine - jnp.where(onehot, cos_margin, 0.0)))
    return jnp.where(inverse > 0.0, expo, 0.0), onehot, cosine * inverse


def sums(parts):
    rest = [jnp.where(onehot, 0.0, expo) for expo, onehot, _ in parts]
    at_label = [jnp.where(onehot, expo, 0.0) for expo, onehot, _ in parts]
    return [jnp.sum(sum(part), axis=0, keepdims=True) for part in (rest, at_label)]


def forward(packed, own_blocks, pair_blocks, expo_out, scaled_out, inverse_out, sums_out):
    core = lax.axis_index("core")
    parts = []
    for k, blocks in enumerate((own_blocks, pair_blocks)):
        norms = [inverse_norm(blocks[g].astype(jnp.float32)) for g in range(blocks.shape[0])]
        inverse = select(norms, BLK)
        inverse_out[k] = inverse
        part = exponentials(packed, core if k == 0 else 1 - core, blocks, inverse)
        expo_out[k] = jnp.where(part[1], -1.0, part[0])
        parts.append(part)
    scaled_out[...] = parts[0][2]
    sums_out[0:1, :], sums_out[1:2, :] = sums(parts)


def forward_other(packed, own_blocks, inverse, expo_out, scaled_out):
    expo, onehot, scaled = exponentials(packed, lax.axis_index("core"), own_blocks, inverse[0])
    expo_out[...] = jnp.where(onehot, -1.0, expo)
    scaled_out[...] = scaled


def with_sums(shares, own_sums, other_sums, other_expo, sent_out):
    del other_expo
    rows, wide = shares.shape
    sent_out[:, :wide] = shares[...]
    total = jnp.concatenate([own_sums[...], other_sums[...]], axis=0)
    high = total.astype(jnp.bfloat16)
    low = (total - high.astype(jnp.float32)).astype(jnp.bfloat16)
    tile = jnp.concatenate([high.astype(jnp.float32), low.astype(jnp.float32)], axis=0)
    tile = jnp.broadcast_to(tile[None], (rows // 8, 8, 128))
    sent_out[:, wide:] = tile.reshape(rows, 128).astype(jnp.bfloat16)


def shares(expo, inverse, own_blocks, pair_blocks, shares_out):
    groups, _, width = own_blocks.shape
    others, label = [], []
    for k in range(2):
        others.append((jnp.maximum(expo[k], 0.0) * inverse[k]).T)
        label.append(jnp.where(expo[k] < 0.0, 1.0, 0.0).T)
    others = jnp.concatenate(others, axis=1)
    label = jnp.concatenate(label, axis=1)
    places = [[] for _ in range(groups)]
    for g in range(groups):
        rows = [part[p * 8 : p * 8 + 8] for part in (others, label) for p in range(g, 16, groups)]
        blocks = jnp.concatenate([own_blocks[g], pair_blocks[g]], axis=0)
        both = contract(jnp.concatenate(rows, axis=0).astype(jnp.bfloat16), blocks, 1, 0)
        places[g] = [both[i * 8 : i * 8 + 8] for i in range(len(rows))]
    for part in range(2):
        count = 16 // groups
        rows = [places[g][part * count + i] for i in range(count) for g in range(groups)]
        rows = jnp.concatenate(rows, axis=0).astype(jnp.bfloat16)
        shares_out[:, part * width : (part + 1) * width] = rows


def backward(
    named,
    received,
    expo,
    other_expo,
    scaled,
    other_scaled,
    inverse,
    own_packed,
    other_packed,
    features,
    centres,
    grad_out,
    feature_out,
    loss_out,
    grad,
    feature_grad,
    loss_row,
    left,
):
    held = centres.shape[0]
    tok_dev, width = features.shape

    def total_of(columns):
        total = received[0, :, columns].astype(jnp.float32)
        for i in range(1, received.shape[0]):
            total = total + received[i, :, columns].astype(jnp.float32)
        return total

    tile = total_of(pl.ds(2 * width, 128))
    tile = tile[:4] + tile[4:]
    own_rest, own_label = tile[0:1], tile[1:2]
    other_rest, other_label = tile[2:3], tile[3:4]

    units = jnp.concatenate([own_packed[:, :width], other_packed[:, :width]], axis=0)
    own_scale = logit_scale / (own_rest + own_label)
    other_scale = logit_scale / (other_rest + other_label)
    own = expo[0]
    other = other_expo[...]
    own = jnp.where(own < 0.0, -own_rest, own) * (own_scale * inverse[0])
    other = jnp.where(other < 0.0, -other_rest, other) * (other_scale * inverse[0])
    weights = jnp.concatenate([own, other], axis=1)
    pulls = weights * jnp.concatenate([scaled[...], other_scaled[...]], axis=1)
    named = jnp.concatenate([named[...], named[...]], axis=1)
    moves = []

    def leave(source, target):
        move = pltpu.make_async_copy(source, target, left.at[len(moves)])
        move.start()
        moves.append(move)

    def block_out(b):
        mine = jnp.where(named == b, weights, 0.0).astype(jnp.bfloat16)
        back = jnp.sum(jnp.where(named == b, pulls, 0.0), axis=1, keepdims=True)
        grad[b] = contract(mine, units, 1, 0) - back * centres[b].astype(jnp.float32)
        for part in (pl.ds(0, BLK // 2), pl.ds(BLK // 2, BLK // 2)):
            leave(grad.at[b, part], grad_out.at[b, part])

    for b in range(held // 2):
        block_out(b)

    sums = total_of(pl.ds(0, 2 * width))
    sample = lax.broadcasted_iota(jnp.int32, (tok_dev, 128), 0) + own_place() * tok_dev
    mine = lanes(tok_dev) == sample
    rest = jnp.sum(jnp.where(mine, own_rest, 0.0), axis=1, keepdims=True)
    label = jnp.sum(jnp.where(mine, own_label, 0.0), axis=1, keepdims=True)
    total = rest + label
    loss = jnp.log(total) - jnp.log(label)
    square = (tok_dev, tok_dev)
    diagonal = lax.broadcasted_iota(jnp.int32, square, 0) == lax.broadcasted_iota(
        jnp.int32, square, 1
    )
    loss_row[...] = jnp.sum(jnp.where(diagonal, loss, 0.0), axis=0, keepdims=True)
    rows = features[...].astype(jnp.float32)
    inv_norm = inverse_norm(rows)
    unit = rows * inv_norm
    cand = sums[:, width : 2 * width]
    cand = (cand * inverse_norm(cand)).astype(jnp.bfloat16).astype(jnp.float32)
    unit_grad = logit_scale / total * (sums[:, :width] - rest * cand)
    along = jnp.sum(unit_grad * unit, axis=1, keepdims=True)
    feature_grad[...] = inv_norm * (unit_grad - along * unit)

    leave(feature_grad, feature_out)
    leave(loss_row, loss_out)
    for b in range(held // 2, held):
        block_out(b)
    for move in moves:
        move.wait()


def exchange(pieces, axes, order=None):
    return lax.all_to_all(
        pieces, axes, split_axis=0, concat_axis=0, axis_index_groups=order, tiled=True
    )


def exchange_chips(pieces):
    chips = lax.axis_size("chip")
    order = [g * chips + chip for chip in reversed(range(chips)) for g in GROUP_ORDER]
    return exchange(pieces, CHIPS, [order])


def with_partner(value):
    return lax.ppermute(value, "core", [(0, 1), (1, 0)])


def on_device(features, labels, centres, block_ids, listed):
    groups = lax.axis_size("group")
    chips = groups * lax.axis_size("chip")
    tok_dev, width = features.shape
    held = centres.shape[0] // BLK
    half = chips * tok_dev
    bf16, f32 = jnp.bfloat16, jnp.float32
    shape = jax.ShapeDtypeStruct

    copies, own_blocks, blocks, named, own_features = run(
        load,
        (
            shape((chips, tok_dev, width + 128), bf16),
            shape((groups, BLK, width), bf16),
            shape((held, BLK, width), bf16),
            shape((1, 128), block_ids.dtype),
            shape(features.shape, bf16),
        ),
        [HBM] * 5,
        *(
            pltpu.with_memory_space_constraint(array, pltpu.HBM)
            for array in (
                features,
                labels.reshape(1, -1),
                centres.reshape(held, BLK, width),
                block_ids.reshape(1, groups),
                listed.reshape(1, groups),
            )
        ),
        scratch=[
            pltpu.VMEM((1, labels.shape[0]), labels.dtype),
            pltpu.SMEM((1, groups), block_ids.dtype),
            pltpu.SMEM((1, groups), listed.dtype),
            pltpu.SemaphoreType.DMA((5,)),
        ],
    )
    pair_blocks = with_partner(own_blocks)
    own_packed = exchange_chips(copies).reshape(half, width + 128)
    other_packed = with_partner(own_packed)
    expo, scaled, inverse, own_sums = run(
        forward,
        (
            shape((2, BLK, half), f32),
            shape((BLK, half), f32),
            shape((2, BLK, half), f32),
            shape((2, half), f32),
        ),
        [VMEM] * 3,
        own_packed,
        own_blocks,
        pair_blocks,
    )
    other_sums = with_partner(own_sums)
    going = run(
        shares,
        shape((half, 2 * width), bf16),
        [VMEM] * 4,
        expo,
        inverse,
        own_blocks,
        pair_blocks,
    )
    other_expo, other_scaled = run(
        forward_other,
        (shape((BLK, half), f32), shape((BLK, half), f32)),
        [VMEM] * 3,
        other_packed,
        own_blocks,
        inverse,
    )
    sent = run(
        with_sums,
        shape((half, 2 * width + 128), bf16),
        [VMEM] * 3 + [pl.BlockSpec(memory_space=pl.ANY)],
        going,
        own_sums,
        other_sums,
        other_expo,
    )
    received = exchange_chips(sent.reshape(chips, tok_dev, 2 * width + 128))
    outs = (shape((held, BLK, width), f32), shape((tok_dev, width), f32), shape((1, tok_dev), f32))
    centre_grad, feature_grad, loss = run(
        backward,
        outs,
        [VMEM] * 11,
        named,
        received,
        expo,
        other_expo,
        scaled,
        other_scaled,
        inverse,
        own_packed,
        other_packed,
        own_features,
        blocks,
        out_spec=HBM,
        scratch=[
            *(pltpu.VMEM(out.shape, out.dtype) for out in outs),
            pltpu.SemaphoreType.DMA((2 * held + 2,)),
        ],
    )
    return (loss.reshape(tok_dev), feature_grad, centre_grad.reshape(held * BLK, width))


def on_device_of_many(features, labels, centres, block_ids, listed):
    groups = lax.axis_size("group")
    members = lax.axis_size("member")
    devices = groups * members
    group = lax.axis_index("group")
    member = lax.axis_index("member")
    tok_dev, width = features.shape
    group_tok = members * tok_dev
    held = centres.shape[0] // BLK

    vectors = features.astype(jnp.float32)
    inv_norm = inverse_norm(vectors)
    unit_rows = vectors * inv_norm
    copies = jnp.broadcast_to(unit_rows.astype(jnp.bfloat16), (devices, tok_dev, width))
    units = exchange(copies, AXES).reshape(groups, group_tok, width)
    all_labels = exchange(jnp.broadcast_to(labels[None], (groups, group_tok)), "group")

    picked = centres.reshape(held, BLK, width)[block_ids[:, 0]].astype(jnp.float32)
    inv_cand = inverse_norm(picked)
    unit_cand = picked * inv_cand
    cand_half = unit_cand.astype(jnp.bfloat16)
    cosine = jnp.einsum("gsd,gcd->gsc", units, cand_half, preferred_element_type=jnp.float32)
    local_label = all_labels - (member * groups + group) * BLK
    onehot = (lax.broadcasted_iota(jnp.int32, (1, 1, BLK), 2) == local_label[:, :, None]).astype(
        jnp.float32
    )
    logits = logit_scale * (cosine - cos_margin * onehot)
    exp_logits = jnp.exp(logits) * listed.astype(jnp.float32)[:, :, None]
    totals, label_logit = lax.psum(
        (jnp.sum(exp_logits, axis=2), jnp.sum(logits * onehot, axis=2)), AXES
    )
    loss_all = (jnp.log(totals) - label_logit).reshape(devices, tok_dev)
    sample_loss = lax.dynamic_slice_in_dim(loss_all, group * members + member, 1, 0)[0]

    weights = (logit_scale * (exp_logits / totals[:, :, None] - onehot)).astype(jnp.bfloat16)
    partial = jnp.einsum("gsc,gcd->gsd", weights, cand_half, preferred_element_type=jnp.float32)
    home = exchange(partial.astype(jnp.bfloat16).reshape(devices, tok_dev, width), AXES)
    unit_grad = jnp.sum(home.astype(jnp.float32), axis=0)
    feature_grad = inv_norm * (
        unit_grad - jnp.sum(unit_grad * unit_rows, axis=1, keepdims=True) * unit_rows
    )
    slot_grad = jnp.einsum("gsc,gsd->gcd", weights, units, preferred_element_type=jnp.float32)
    cand_grad = inv_cand * (
        slot_grad - jnp.sum(slot_grad * unit_cand, axis=2, keepdims=True) * unit_cand
    )
    cand_grad = cand_grad.astype(jnp.bfloat16).astype(jnp.float32)
    names = block_ids == jnp.arange(held, dtype=jnp.int32)[None, :]
    centre_grad = jnp.sum(
        jnp.where(names[:, :, None, None], cand_grad[:, None], 0.0), axis=0
    ).reshape(held * BLK, width)
    return (sample_loss, feature_grad, centre_grad)


def on_axes(body, mesh, axes):
    split = P(axes)
    return jax.shard_map(
        body,
        mesh=mesh,
        in_specs=(split, P("group"), split, P(None, axes), P(None, axes)),
        out_specs=(split, split, split),
        check_vma=False,
    )


def solution(mesh):
    groups, members = mesh.shape["group"], mesh.shape["member"]
    by_core = jax.sharding.Mesh(
        mesh.devices.reshape(groups, members // 2, 2), ("group", "chip", "core")
    )

    def program(features, *others):
        half = features.shape[0] // 2
        if half == 128 and 2 * groups == features.shape[0] // mesh.size == 8:
            return on_axes(on_device, by_core, (*CHIPS, "core"))(features, *others)
        return on_axes(on_device_of_many, mesh, AXES)(features, *others)

    return program
```

```python
import jax
import jax.numpy as jnp
from jax import lax
from jax.experimental import pallas as pl
from jax.experimental.pallas import tpu as pltpu
from jax.sharding import PartitionSpec as P

BLK = 128
AXES = ("group", "member")
CHIPS = ("group", "chip")

logit_scale = 32.0
cos_margin = 0.35
norm_epsilon = 1e-06
GROUP_ORDER = (2, 0, 3, 1)
UNLISTED = 1e19

VMEM = pl.BlockSpec(memory_space=pltpu.VMEM)
HBM = pl.BlockSpec(memory_space=pltpu.HBM)


def inverse_norm(rows):
    return lax.rsqrt(jnp.sum(rows * rows, axis=-1, keepdims=True) + norm_epsilon)


def contract(left, right, left_dim, right_dim):
    dims = (((left_dim,), (right_dim,)), ((), ()))
    return lax.dot_general(left, right, dims, preferred_element_type=jnp.float32)


def lanes(rows):
    return lax.broadcasted_iota(jnp.int32, (rows, 128), 1)


def run(kernel, out_shape, in_specs, *operands, out_spec=VMEM, scratch=()):
    shapes = jax.tree.leaves(out_shape)
    return pl.pallas_call(
        kernel,
        out_shape=out_shape,
        in_specs=in_specs,
        out_specs=jax.tree.map(lambda _: out_spec, out_shape),
        scratch_shapes=scratch,
        compiler_params=pltpu.CompilerParams(vmem_limit_bytes=48 * 1024 * 1024),
        cost_estimate=pl.CostEstimate(
            flops=0,
            transcendentals=0,
            bytes_accessed=sum(a.size * a.dtype.itemsize for a in (*shapes, *operands)),
        ),
    )(*operands)


def load(
    features,
    labels,
    centres,
    ids,
    listed,
    copies_out,
    blocks_out,
    centres_out,
    named_out,
    held_features,
    held_labels,
    held_ids,
    held_listed,
    arrived,
):
    moves = [
        pltpu.make_async_copy(source, target, arrived.at[i])
        for i, (source, target) in enumerate(
            (
                (features, held_features),
                (labels, held_labels),
                (ids, held_ids),
                (listed, held_listed),
                (centres, centres_out),
            )
        )
    ]
    for move in moves:
        move.start()
    moves[0].wait()
    moves[1].wait()
    chip = lax.axis_index("chip")
    member = 2 * chip + lax.axis_index("core")
    copies, tok_dev, _ = copies_out.shape
    width = features.shape[1]
    rows = held_features[...].astype(jnp.float32)
    unit = (rows * inverse_norm(rows)).astype(jnp.bfloat16)
    copies_out[:, :, :width] = jnp.broadcast_to(unit[None], (copies, tok_dev, width))

    place = own_place() * tok_dev
    row = held_labels[...]
    row = jnp.concatenate([row, jnp.zeros((1, 128 - row.shape[1]), jnp.int32)], axis=1)
    row = jnp.broadcast_to(row, (tok_dev, 128))
    row = pltpu.roll(row, lax.rem(place - member * tok_dev + 128, 128), 1)
    digit = lax.broadcasted_iota(jnp.int32, (tok_dev, 128), 0)
    digits = (row >> (7 * jnp.minimum(digit, 3))) & 127
    lane = lanes(tok_dev)
    digits = jnp.where((lane >= place) & (lane < place + tok_dev), digits, 0)
    copies_out[:, :, width:] = jnp.broadcast_to(
        digits.astype(jnp.float32).astype(jnp.bfloat16)[None], (copies, tok_dev, 128)
    )
    for move in moves[2:]:
        move.wait()
    named_out[...] = select([held_ids[0, group] for group in GROUP_ORDER], 1)
    for g, group in enumerate(GROUP_ORDER):
        block = centres_out[held_ids[0, group]]
        blocks_out[g] = jnp.where(held_listed[0, group] > 0, block, jnp.full_like(block, UNLISTED))


def own_place():
    groups, chips = lax.axis_size("group"), lax.axis_size("chip")
    group = lax.axis_index("group")
    place = sum(jnp.where(group == g, k, 0) for k, g in enumerate(GROUP_ORDER))
    return (chips - 1 - lax.axis_index("chip")) * groups + place


def select(parts, rows):
    owner = lax.rem(lanes(1) // 8, len(parts))
    out = jnp.broadcast_to(parts[0], (rows, 128))
    for g in range(1, len(parts)):
        out = jnp.where(owner == g, parts[g], out)
    return out


def exponentials(packed, core, blocks, inverse):
    groups, _, width = blocks.shape
    digits = jnp.sum(
        packed[:, width:].astype(jnp.float32).reshape(128 // 8, 8, 128), axis=0
    ).astype(jnp.int32)
    labels = digits[0:1] + (digits[1:2] << 7) + (digits[2:3] << 14)
    member = 2 * lax.axis_index("chip") + core
    first = (member * groups + lax.axis_index("group")) * BLK
    onehot = lax.broadcasted_iota(jnp.int32, (BLK, 128), 0) == labels - first
    units = packed[:, :width]
    dots = contract(blocks[...].reshape(groups * BLK, width), units, 1, 1)
    cosine = inverse * select([dots[g * BLK : (g + 1) * BLK] for g in range(groups)], BLK)
    expo = jnp.exp(logit_scale * (cosine - jnp.where(onehot, cos_margin, 0.0)))
    return jnp.where(inverse > 0.0, expo, 0.0), onehot, cosine * inverse


def sums(parts):
    rest = [jnp.where(onehot, 0.0, expo) for expo, onehot, _ in parts]
    at_label = [jnp.where(onehot, expo, 0.0) for expo, onehot, _ in parts]
    return [jnp.sum(sum(part), axis=0, keepdims=True) for part in (rest, at_label)]


def forward(packed, own_blocks, pair_blocks, expo_out, scaled_out, inverse_out, sums_out):
    core = lax.axis_index("core")
    parts = []
    for k, blocks in enumerate((own_blocks, pair_blocks)):
        norms = [inverse_norm(blocks[g].astype(jnp.float32)) for g in range(blocks.shape[0])]
        inverse = select(norms, BLK)
        inverse_out[k] = inverse
        part = exponentials(packed, core if k == 0 else 1 - core, blocks, inverse)
        expo_out[k] = jnp.where(part[1], -1.0, part[0])
        parts.append(part)
    scaled_out[...] = parts[0][2]
    sums_out[0:1, :], sums_out[1:2, :] = sums(parts)


def forward_other(
    packed, own_blocks, pair_blocks, inverse, own_sums, shares, expo_out, scaled_out, sent_out
):
    core = lax.axis_index("core")
    own = exponentials(packed, core, own_blocks, inverse[0])
    pair = exponentials(packed, 1 - core, pair_blocks, inverse[1])
    expo_out[...] = jnp.where(own[1], -1.0, own[0])
    scaled_out[...] = own[2]
    rows, wide = shares.shape
    sent_out[:, :wide] = shares[...]
    total = jnp.concatenate([own_sums[...], *sums([own, pair])], axis=0)
    high = total.astype(jnp.bfloat16)
    low = (total - high.astype(jnp.float32)).astype(jnp.bfloat16)
    tile = jnp.concatenate([high.astype(jnp.float32), low.astype(jnp.float32)], axis=0)
    tile = jnp.broadcast_to(tile[None], (rows // 8, 8, 128))
    sent_out[:, wide:] = tile.reshape(rows, 128).astype(jnp.bfloat16)


def shares(expo, inverse, own_blocks, pair_blocks, shares_out):
    groups, _, width = own_blocks.shape
    others, label = [], []
    for k in range(2):
        others.append((jnp.maximum(expo[k], 0.0) * inverse[k]).T)
        label.append(jnp.where(expo[k] < 0.0, 1.0, 0.0).T)
    others = jnp.concatenate(others, axis=1)
    label = jnp.concatenate(label, axis=1)
    places = [[] for _ in range(groups)]
    for g in range(groups):
        rows = [part[p * 8 : p * 8 + 8] for part in (others, label) for p in range(g, 16, groups)]
        blocks = jnp.concatenate([own_blocks[g], pair_blocks[g]], axis=0)
        both = contract(jnp.concatenate(rows, axis=0).astype(jnp.bfloat16), blocks, 1, 0)
        places[g] = [both[i * 8 : i * 8 + 8] for i in range(len(rows))]
    for part in range(2):
        count = 16 // groups
        rows = [places[g][part * count + i] for i in range(count) for g in range(groups)]
        rows = jnp.concatenate(rows, axis=0).astype(jnp.bfloat16)
        shares_out[:, part * width : (part + 1) * width] = rows


def backward(
    named,
    received,
    expo,
    other_expo,
    scaled,
    other_scaled,
    inverse,
    own_packed,
    other_packed,
    features,
    centres,
    grad_out,
    feature_out,
    loss_out,
    grad,
    feature_grad,
    loss_row,
    left,
):
    held = centres.shape[0]
    tok_dev, width = features.shape

    def total_of(columns):
        total = received[0, :, columns].astype(jnp.float32)
        for i in range(1, received.shape[0]):
            total = total + received[i, :, columns].astype(jnp.float32)
        return total

    tile = total_of(pl.ds(2 * width, 128))
    tile = tile[:4] + tile[4:]
    own_rest, own_label = tile[0:1], tile[1:2]
    other_rest, other_label = tile[2:3], tile[3:4]

    units = jnp.concatenate([own_packed[:, :width], other_packed[:, :width]], axis=0)
    own_scale = logit_scale / (own_rest + own_label)
    other_scale = logit_scale / (other_rest + other_label)
    own = expo[0]
    other = other_expo[...]
    own = jnp.where(own < 0.0, -own_rest, own) * own_scale
    other = jnp.where(other < 0.0, -other_rest, other) * other_scale
    weights = jnp.concatenate([own, other], axis=1).astype(jnp.bfloat16).astype(jnp.float32)
    pulls = weights * jnp.concatenate([scaled[...], other_scaled[...]], axis=1)
    own_named = named[...]
    named = jnp.concatenate([own_named, own_named], axis=1)
    moves = []

    def leave(source, target):
        move = pltpu.make_async_copy(source, target, left.at[len(moves)])
        move.start()
        moves.append(move)

    def block_out(b):
        mine = jnp.where(named == b, weights, 0.0).astype(jnp.bfloat16)
        factor = jnp.max(jnp.where(own_named == b, inverse[0], 0.0), axis=1, keepdims=True)
        back = factor * jnp.sum(jnp.where(named == b, pulls, 0.0), axis=1, keepdims=True)
        slot_grad = contract(mine, units, 1, 0)
        grad[b] = factor * slot_grad - back * centres[b].astype(jnp.float32)
        for part in (pl.ds(0, BLK // 2), pl.ds(BLK // 2, BLK // 2)):
            leave(grad.at[b, part], grad_out.at[b, part])

    for b in range(held // 2):
        block_out(b)

    sums = total_of(pl.ds(0, 2 * width))
    sample = lax.broadcasted_iota(jnp.int32, (tok_dev, 128), 0) + own_place() * tok_dev
    mine = lanes(tok_dev) == sample
    rest = jnp.sum(jnp.where(mine, own_rest, 0.0), axis=1, keepdims=True)
    label = jnp.sum(jnp.where(mine, own_label, 0.0), axis=1, keepdims=True)
    total = rest + label
    loss = jnp.log(total) - jnp.log(label)
    square = (tok_dev, tok_dev)
    diagonal = lax.broadcasted_iota(jnp.int32, square, 0) == lax.broadcasted_iota(
        jnp.int32, square, 1
    )
    loss_row[...] = jnp.sum(jnp.where(diagonal, loss, 0.0), axis=0, keepdims=True)
    rows = features[...].astype(jnp.float32)
    inv_norm = inverse_norm(rows)
    unit = rows * inv_norm
    cand = sums[:, width : 2 * width]
    cand = (cand * inverse_norm(cand)).astype(jnp.bfloat16).astype(jnp.float32)
    unit_grad = logit_scale / total * (sums[:, :width] - rest * cand)
    along = jnp.sum(unit_grad * unit, axis=1, keepdims=True)
    feature_grad[...] = inv_norm * (unit_grad - along * unit)

    leave(feature_grad, feature_out)
    leave(loss_row, loss_out)
    for b in range(held // 2, held):
        block_out(b)
    for move in moves:
        move.wait()


def exchange(pieces, axes, order=None):
    return lax.all_to_all(
        pieces, axes, split_axis=0, concat_axis=0, axis_index_groups=order, tiled=True
    )


def exchange_chips(pieces):
    chips = lax.axis_size("chip")
    order = [g * chips + chip for chip in reversed(range(chips)) for g in GROUP_ORDER]
    return exchange(pieces, CHIPS, [order])


def with_partner(value):
    return lax.ppermute(value, "core", [(0, 1), (1, 0)])


def on_device(features, labels, centres, block_ids, listed):
    groups = lax.axis_size("group")
    chips = groups * lax.axis_size("chip")
    tok_dev, width = features.shape
    held = centres.shape[0] // BLK
    half = chips * tok_dev
    bf16, f32 = jnp.bfloat16, jnp.float32
    shape = jax.ShapeDtypeStruct

    copies, own_blocks, blocks, named, own_features = run(
        load,
        (
            shape((chips, tok_dev, width + 128), bf16),
            shape((groups, BLK, width), bf16),
            shape((held, BLK, width), bf16),
            shape((1, 128), block_ids.dtype),
            shape(features.shape, bf16),
        ),
        [HBM] * 5,
        *(
            pltpu.with_memory_space_constraint(array, pltpu.HBM)
            for array in (
                features,
                labels.reshape(1, -1),
                centres.reshape(held, BLK, width),
                block_ids.reshape(1, groups),
                listed.reshape(1, groups),
            )
        ),
        scratch=[
            pltpu.VMEM((1, labels.shape[0]), labels.dtype),
            pltpu.SMEM((1, groups), block_ids.dtype),
            pltpu.SMEM((1, groups), listed.dtype),
            pltpu.SemaphoreType.DMA((5,)),
        ],
    )
    pair_blocks = with_partner(own_blocks)
    own_packed = exchange_chips(copies).reshape(half, width + 128)
    other_packed = with_partner(own_packed)
    expo, scaled, inverse, own_sums = run(
        forward,
        (
            shape((2, BLK, half), f32),
            shape((BLK, half), f32),
            shape((2, BLK, half), f32),
            shape((2, half), f32),
        ),
        [VMEM] * 3,
        own_packed,
        own_blocks,
        pair_blocks,
    )
    going = run(
        shares,
        shape((half, 2 * width), bf16),
        [VMEM] * 4,
        expo,
        inverse,
        own_blocks,
        pair_blocks,
    )
    other_expo, other_scaled, sent = run(
        forward_other,
        (
            shape((BLK, half), f32),
            shape((BLK, half), f32),
            shape((half, 2 * width + 128), bf16),
        ),
        [VMEM] * 6,
        other_packed,
        own_blocks,
        pair_blocks,
        inverse,
        own_sums,
        going,
    )
    received = exchange_chips(sent.reshape(chips, tok_dev, 2 * width + 128))
    outs = (shape((held, BLK, width), f32), shape((tok_dev, width), f32), shape((1, tok_dev), f32))
    centre_grad, feature_grad, loss = run(
        backward,
        outs,
        [VMEM] * 11,
        named,
        received,
        expo,
        other_expo,
        scaled,
        other_scaled,
        inverse,
        own_packed,
        other_packed,
        own_features,
        blocks,
        out_spec=HBM,
        scratch=[
            *(pltpu.VMEM(out.shape, out.dtype) for out in outs),
            pltpu.SemaphoreType.DMA((2 * held + 2,)),
        ],
    )
    return (loss.reshape(tok_dev), feature_grad, centre_grad.reshape(held * BLK, width))


def on_device_of_many(features, labels, centres, block_ids, listed):
    groups = lax.axis_size("group")
    members = lax.axis_size("member")
    devices = groups * members
    group = lax.axis_index("group")
    member = lax.axis_index("member")
    tok_dev, width = features.shape
    group_tok = members * tok_dev
    held = centres.shape[0] // BLK

    vectors = features.astype(jnp.float32)
    inv_norm = inverse_norm(vectors)
    unit_rows = vectors * inv_norm
    copies = jnp.broadcast_to(unit_rows.astype(jnp.bfloat16), (devices, tok_dev, width))
    units = exchange(copies, AXES).reshape(groups, group_tok, width)
    all_labels = exchange(jnp.broadcast_to(labels[None], (groups, group_tok)), "group")

    picked = centres.reshape(held, BLK, width)[block_ids[:, 0]].astype(jnp.float32)
    inv_cand = inverse_norm(picked)
    unit_cand = picked * inv_cand
    cand_half = unit_cand.astype(jnp.bfloat16)
    cosine = jnp.einsum("gsd,gcd->gsc", units, cand_half, preferred_element_type=jnp.float32)
    local_label = all_labels - (member * groups + group) * BLK
    onehot = (lax.broadcasted_iota(jnp.int32, (1, 1, BLK), 2) == local_label[:, :, None]).astype(
        jnp.float32
    )
    logits = logit_scale * (cosine - cos_margin * onehot)
    exp_logits = jnp.exp(logits) * listed.astype(jnp.float32)[:, :, None]
    totals, label_logit = lax.psum(
        (jnp.sum(exp_logits, axis=2), jnp.sum(logits * onehot, axis=2)), AXES
    )
    loss_all = (jnp.log(totals) - label_logit).reshape(devices, tok_dev)
    sample_loss = lax.dynamic_slice_in_dim(loss_all, group * members + member, 1, 0)[0]

    weights = (logit_scale * (exp_logits / totals[:, :, None] - onehot)).astype(jnp.bfloat16)
    partial = jnp.einsum("gsc,gcd->gsd", weights, cand_half, preferred_element_type=jnp.float32)
    home = exchange(partial.astype(jnp.bfloat16).reshape(devices, tok_dev, width), AXES)
    unit_grad = jnp.sum(home.astype(jnp.float32), axis=0)
    feature_grad = inv_norm * (
        unit_grad - jnp.sum(unit_grad * unit_rows, axis=1, keepdims=True) * unit_rows
    )
    slot_grad = jnp.einsum("gsc,gsd->gcd", weights, units, preferred_element_type=jnp.float32)
    cand_grad = inv_cand * (
        slot_grad - jnp.sum(slot_grad * unit_cand, axis=2, keepdims=True) * unit_cand
    )
    cand_grad = cand_grad.astype(jnp.bfloat16).astype(jnp.float32)
    names = block_ids == jnp.arange(held, dtype=jnp.int32)[None, :]
    centre_grad = jnp.sum(
        jnp.where(names[:, :, None, None], cand_grad[:, None], 0.0), axis=0
    ).reshape(held * BLK, width)
    return (sample_loss, feature_grad, centre_grad)


def on_axes(body, mesh, axes):
    split = P(axes)
    return jax.shard_map(
        body,
        mesh=mesh,
        in_specs=(split, P("group"), split, P(None, axes), P(None, axes)),
        out_specs=(split, split, split),
        check_vma=False,
    )


def solution(mesh):
    groups, members = mesh.shape["group"], mesh.shape["member"]
    by_core = jax.sharding.Mesh(
        mesh.devices.reshape(groups, members // 2, 2), ("group", "chip", "core")
    )

    def program(features, *others):
        half = features.shape[0] // 2
        if half == 128 and 2 * groups == features.shape[0] // mesh.size == 8:
            return on_axes(on_device, by_core, (*CHIPS, "core"))(features, *others)
        return on_axes(on_device_of_many, mesh, AXES)(features, *others)

    return program
```

```python
import jax
import jax.numpy as jnp
from jax import lax
from jax.experimental import pallas as pl
from jax.experimental.pallas import tpu as pltpu
from jax.sharding import PartitionSpec as P

BLK = 128
AXES = ("group", "member")
CHIPS = ("group", "chip")

logit_scale = 32.0
cos_margin = 0.35
norm_epsilon = 1e-06
GROUP_ORDER = (2, 0, 3, 1)
UNLISTED = 1e19

VMEM = pl.BlockSpec(memory_space=pltpu.VMEM)
HBM = pl.BlockSpec(memory_space=pltpu.HBM)


def inverse_norm(rows):
    return lax.rsqrt(jnp.sum(rows * rows, axis=-1, keepdims=True) + norm_epsilon)


def contract(left, right, left_dim, right_dim):
    dims = (((left_dim,), (right_dim,)), ((), ()))
    return lax.dot_general(left, right, dims, preferred_element_type=jnp.float32)


def lanes(rows):
    return lax.broadcasted_iota(jnp.int32, (rows, 128), 1)


def run(kernel, out_shape, in_specs, *operands, out_spec=VMEM, scratch=()):
    shapes = jax.tree.leaves(out_shape)
    return pl.pallas_call(
        kernel,
        out_shape=out_shape,
        in_specs=in_specs,
        out_specs=jax.tree.map(lambda _: out_spec, out_shape),
        scratch_shapes=scratch,
        compiler_params=pltpu.CompilerParams(vmem_limit_bytes=48 * 1024 * 1024),
        cost_estimate=pl.CostEstimate(
            flops=0,
            transcendentals=0,
            bytes_accessed=sum(a.size * a.dtype.itemsize for a in (*shapes, *operands)),
        ),
    )(*operands)


def load(
    features,
    labels,
    centres,
    ids,
    listed,
    copies_out,
    blocks_out,
    centres_out,
    named_out,
    held_features,
    held_labels,
    held_ids,
    held_listed,
    arrived,
):
    moves = [
        pltpu.make_async_copy(source, target, arrived.at[i])
        for i, (source, target) in enumerate(
            (
                (features, held_features),
                (labels, held_labels),
                (ids, held_ids),
                (listed, held_listed),
                *((centres.at[b], centres_out.at[b]) for b in range(centres.shape[0])),
            )
        )
    ]
    for i, move in enumerate(moves):
        move.start(priority=i % 2)
    moves[0].wait()
    moves[1].wait()
    chip = lax.axis_index("chip")
    member = 2 * chip + lax.axis_index("core")
    copies, tok_dev, _ = copies_out.shape
    width = features.shape[1]
    rows = held_features[...].astype(jnp.float32)
    unit = (rows * inverse_norm(rows)).astype(jnp.bfloat16)
    copies_out[:, :, :width] = jnp.broadcast_to(unit[None], (copies, tok_dev, width))

    place = own_place() * tok_dev
    row = held_labels[...]
    row = jnp.concatenate([row, jnp.zeros((1, 128 - row.shape[1]), jnp.int32)], axis=1)
    row = jnp.broadcast_to(row, (tok_dev, 128))
    row = pltpu.roll(row, lax.rem(place - member * tok_dev + 128, 128), 1)
    digit = lax.broadcasted_iota(jnp.int32, (tok_dev, 128), 0)
    digits = (row >> (7 * jnp.minimum(digit, 3))) & 127
    lane = lanes(tok_dev)
    digits = jnp.where((lane >= place) & (lane < place + tok_dev), digits, 0)
    copies_out[:, :, width:] = jnp.broadcast_to(
        digits.astype(jnp.float32).astype(jnp.bfloat16)[None], (copies, tok_dev, 128)
    )
    for move in moves[2:]:
        move.wait()
    named_out[...] = select([held_ids[0, group] for group in GROUP_ORDER], 1)
    for g, group in enumerate(GROUP_ORDER):
        block = centres_out[held_ids[0, group]]
        blocks_out[g] = jnp.where(held_listed[0, group] > 0, block, jnp.full_like(block, UNLISTED))


def own_place():
    groups, chips = lax.axis_size("group"), lax.axis_size("chip")
    group = lax.axis_index("group")
    place = sum(jnp.where(group == g, k, 0) for k, g in enumerate(GROUP_ORDER))
    return (chips - 1 - lax.axis_index("chip")) * groups + place


def select(parts, rows):
    owner = lax.rem(lanes(1) // 8, len(parts))
    out = jnp.broadcast_to(parts[0], (rows, 128))
    for g in range(1, len(parts)):
        out = jnp.where(owner == g, parts[g], out)
    return out


def exponentials(packed, core, blocks, inverse):
    groups, _, width = blocks.shape
    digits = jnp.sum(
        packed[:, width:].astype(jnp.float32).reshape(128 // 8, 8, 128), axis=0
    ).astype(jnp.int32)
    labels = digits[0:1] + (digits[1:2] << 7) + (digits[2:3] << 14)
    member = 2 * lax.axis_index("chip") + core
    first = (member * groups + lax.axis_index("group")) * BLK
    onehot = lax.broadcasted_iota(jnp.int32, (BLK, 128), 0) == labels - first
    units = packed[:, :width]
    dots = contract(blocks[...].reshape(groups * BLK, width), units, 1, 1)
    cosine = inverse * select([dots[g * BLK : (g + 1) * BLK] for g in range(groups)], BLK)
    expo = jnp.exp(logit_scale * (cosine - jnp.where(onehot, cos_margin, 0.0)))
    return jnp.where(inverse > 0.0, expo, 0.0), onehot, cosine * inverse


def sums(parts):
    rest = [jnp.where(onehot, 0.0, expo) for expo, onehot, _ in parts]
    at_label = [jnp.where(onehot, expo, 0.0) for expo, onehot, _ in parts]
    return [jnp.sum(sum(part), axis=0, keepdims=True) for part in (rest, at_label)]


def forward(packed, own_blocks, pair_blocks, expo_out, scaled_out, inverse_out, sums_out):
    core = lax.axis_index("core")
    parts = []
    for k, blocks in enumerate((own_blocks, pair_blocks)):
        norms = [inverse_norm(blocks[g].astype(jnp.float32)) for g in range(blocks.shape[0])]
        inverse = select(norms, BLK)
        inverse_out[k] = inverse
        part = exponentials(packed, core if k == 0 else 1 - core, blocks, inverse)
        expo_out[k] = jnp.where(part[1], -1.0, part[0])
        parts.append(part)
    scaled_out[...] = parts[0][2]
    sums_out[0:1, :], sums_out[1:2, :] = sums(parts)


def forward_other(
    packed, own_blocks, pair_blocks, inverse, own_sums, shares, expo_out, scaled_out, sent_out
):
    core = lax.axis_index("core")
    own = exponentials(packed, core, own_blocks, inverse[0])
    pair = exponentials(packed, 1 - core, pair_blocks, inverse[1])
    expo_out[...] = jnp.where(own[1], -1.0, own[0])
    scaled_out[...] = own[2]
    rows, wide = shares.shape
    sent_out[:, :wide] = shares[...]
    total = jnp.concatenate([own_sums[...], *sums([own, pair])], axis=0)
    high = total.astype(jnp.bfloat16)
    low = (total - high.astype(jnp.float32)).astype(jnp.bfloat16)
    tile = jnp.concatenate([high.astype(jnp.float32), low.astype(jnp.float32)], axis=0)
    tile = jnp.broadcast_to(tile[None], (rows // 8, 8, 128))
    sent_out[:, wide:] = tile.reshape(rows, 128).astype(jnp.bfloat16)


def shares(expo, inverse, own_blocks, pair_blocks, shares_out):
    groups, _, width = own_blocks.shape
    others, label = [], []
    for k in range(2):
        others.append((jnp.maximum(expo[k], 0.0) * inverse[k]).T)
        label.append(jnp.where(expo[k] < 0.0, 1.0, 0.0).T)
    others = jnp.concatenate(others, axis=1)
    label = jnp.concatenate(label, axis=1)
    places = [[] for _ in range(groups)]
    for g in range(groups):
        rows = [part[p * 8 : p * 8 + 8] for part in (others, label) for p in range(g, 16, groups)]
        blocks = jnp.concatenate([own_blocks[g], pair_blocks[g]], axis=0)
        both = contract(jnp.concatenate(rows, axis=0).astype(jnp.bfloat16), blocks, 1, 0)
        places[g] = [both[i * 8 : i * 8 + 8] for i in range(len(rows))]
    for part in range(2):
        count = 16 // groups
        rows = [places[g][part * count + i] for i in range(count) for g in range(groups)]
        rows = jnp.concatenate(rows, axis=0).astype(jnp.bfloat16)
        shares_out[:, part * width : (part + 1) * width] = rows


def backward(
    named,
    received,
    expo,
    other_expo,
    scaled,
    other_scaled,
    inverse,
    own_packed,
    other_packed,
    features,
    centres,
    grad_out,
    feature_out,
    loss_out,
    grad,
    feature_grad,
    loss_row,
    left,
):
    held = centres.shape[0]
    tok_dev, width = features.shape

    def total_of(columns):
        total = received[0, :, columns].astype(jnp.float32)
        for i in range(1, received.shape[0]):
            total = total + received[i, :, columns].astype(jnp.float32)
        return total

    tile = total_of(pl.ds(2 * width, 128))
    tile = tile[:4] + tile[4:]
    own_rest, own_label = tile[0:1], tile[1:2]
    other_rest, other_label = tile[2:3], tile[3:4]

    units = jnp.concatenate([own_packed[:, :width], other_packed[:, :width]], axis=0)
    own_scale = logit_scale / (own_rest + own_label)
    other_scale = logit_scale / (other_rest + other_label)
    own = expo[0]
    other = other_expo[...]
    own = jnp.where(own < 0.0, -own_rest, own) * own_scale
    other = jnp.where(other < 0.0, -other_rest, other) * other_scale
    weights = jnp.concatenate([own, other], axis=1).astype(jnp.bfloat16).astype(jnp.float32)
    pulls = weights * jnp.concatenate([scaled[...], other_scaled[...]], axis=1)
    own_named = named[...]
    named = jnp.concatenate([own_named, own_named], axis=1)
    moves = []

    def leave(source, target):
        move = pltpu.make_async_copy(source, target, left.at[len(moves)])
        move.start(priority=len(moves) % 2)
        moves.append(move)

    def block_out(b):
        mine = jnp.where(named == b, weights, 0.0).astype(jnp.bfloat16)
        factor = jnp.max(jnp.where(own_named == b, inverse[0], 0.0), axis=1, keepdims=True)
        back = factor * jnp.sum(jnp.where(named == b, pulls, 0.0), axis=1, keepdims=True)
        slot_grad = contract(mine, units, 1, 0)
        grad[b] = factor * slot_grad - back * centres[b].astype(jnp.float32)
        for part in (pl.ds(0, BLK // 2), pl.ds(BLK // 2, BLK // 2)):
            leave(grad.at[b, part], grad_out.at[b, part])

    for b in range(held // 2):
        block_out(b)

    sums = total_of(pl.ds(0, 2 * width))
    sample = lax.broadcasted_iota(jnp.int32, (tok_dev, 128), 0) + own_place() * tok_dev
    mine = lanes(tok_dev) == sample
    rest = jnp.sum(jnp.where(mine, own_rest, 0.0), axis=1, keepdims=True)
    label = jnp.sum(jnp.where(mine, own_label, 0.0), axis=1, keepdims=True)
    total = rest + label
    loss = jnp.log(total) - jnp.log(label)
    square = (tok_dev, tok_dev)
    diagonal = lax.broadcasted_iota(jnp.int32, square, 0) == lax.broadcasted_iota(
        jnp.int32, square, 1
    )
    loss_row[...] = jnp.sum(jnp.where(diagonal, loss, 0.0), axis=0, keepdims=True)
    rows = features[...].astype(jnp.float32)
    inv_norm = inverse_norm(rows)
    unit = rows * inv_norm
    cand = sums[:, width : 2 * width]
    cand = (cand * inverse_norm(cand)).astype(jnp.bfloat16).astype(jnp.float32)
    unit_grad = logit_scale / total * (sums[:, :width] - rest * cand)
    along = jnp.sum(unit_grad * unit, axis=1, keepdims=True)
    feature_grad[...] = inv_norm * (unit_grad - along * unit)

    leave(feature_grad, feature_out)
    leave(loss_row, loss_out)
    for b in range(held // 2, held):
        block_out(b)
    for move in moves:
        move.wait()


def exchange(pieces, axes, order=None):
    return lax.all_to_all(
        pieces, axes, split_axis=0, concat_axis=0, axis_index_groups=order, tiled=True
    )


def exchange_chips(pieces):
    chips = lax.axis_size("chip")
    order = [g * chips + chip for chip in reversed(range(chips)) for g in GROUP_ORDER]
    return exchange(pieces, CHIPS, [order])


def with_partner(value):
    return lax.ppermute(value, "core", [(0, 1), (1, 0)])


def on_device(features, labels, centres, block_ids, listed):
    groups = lax.axis_size("group")
    chips = groups * lax.axis_size("chip")
    tok_dev, width = features.shape
    held = centres.shape[0] // BLK
    half = chips * tok_dev
    bf16, f32 = jnp.bfloat16, jnp.float32
    shape = jax.ShapeDtypeStruct

    copies, own_blocks, blocks, named, own_features = run(
        load,
        (
            shape((chips, tok_dev, width + 128), bf16),
            shape((groups, BLK, width), bf16),
            shape((held, BLK, width), bf16),
            shape((1, 128), block_ids.dtype),
            shape(features.shape, bf16),
        ),
        [HBM] * 5,
        *(
            pltpu.with_memory_space_constraint(array, pltpu.HBM)
            for array in (
                features,
                labels.reshape(1, -1),
                centres.reshape(held, BLK, width),
                block_ids.reshape(1, groups),
                listed.reshape(1, groups),
            )
        ),
        scratch=[
            pltpu.VMEM((1, labels.shape[0]), labels.dtype),
            pltpu.SMEM((1, groups), block_ids.dtype),
            pltpu.SMEM((1, groups), listed.dtype),
            pltpu.SemaphoreType.DMA((4 + held,)),
        ],
    )
    pair_blocks = with_partner(own_blocks)
    own_packed = exchange_chips(copies).reshape(half, width + 128)
    other_packed = with_partner(own_packed)
    expo, scaled, inverse, own_sums = run(
        forward,
        (
            shape((2, BLK, half), f32),
            shape((BLK, half), f32),
            shape((2, BLK, half), f32),
            shape((2, half), f32),
        ),
        [VMEM] * 3,
        own_packed,
        own_blocks,
        pair_blocks,
    )
    going = run(
        shares,
        shape((half, 2 * width), bf16),
        [VMEM] * 4,
        expo,
        inverse,
        own_blocks,
        pair_blocks,
    )
    other_expo, other_scaled, sent = run(
        forward_other,
        (
            shape((BLK, half), f32),
            shape((BLK, half), f32),
            shape((half, 2 * width + 128), bf16),
        ),
        [VMEM] * 6,
        other_packed,
        own_blocks,
        pair_blocks,
        inverse,
        own_sums,
        going,
    )
    received = exchange_chips(sent.reshape(chips, tok_dev, 2 * width + 128))
    outs = (shape((held, BLK, width), f32), shape((tok_dev, width), f32), shape((1, tok_dev), f32))
    centre_grad, feature_grad, loss = run(
        backward,
        outs,
        [VMEM] * 11,
        named,
        received,
        expo,
        other_expo,
        scaled,
        other_scaled,
        inverse,
        own_packed,
        other_packed,
        own_features,
        blocks,
        out_spec=HBM,
        scratch=[
            *(pltpu.VMEM(out.shape, out.dtype) for out in outs),
            pltpu.SemaphoreType.DMA((2 * held + 2,)),
        ],
    )
    return (loss.reshape(tok_dev), feature_grad, centre_grad.reshape(held * BLK, width))


def on_device_of_many(features, labels, centres, block_ids, listed):
    groups = lax.axis_size("group")
    members = lax.axis_size("member")
    devices = groups * members
    group = lax.axis_index("group")
    member = lax.axis_index("member")
    tok_dev, width = features.shape
    group_tok = members * tok_dev
    held = centres.shape[0] // BLK

    vectors = features.astype(jnp.float32)
    inv_norm = inverse_norm(vectors)
    unit_rows = vectors * inv_norm
    copies = jnp.broadcast_to(unit_rows.astype(jnp.bfloat16), (devices, tok_dev, width))
    units = exchange(copies, AXES).reshape(groups, group_tok, width)
    all_labels = exchange(jnp.broadcast_to(labels[None], (groups, group_tok)), "group")

    picked = centres.reshape(held, BLK, width)[block_ids[:, 0]].astype(jnp.float32)
    inv_cand = inverse_norm(picked)
    unit_cand = picked * inv_cand
    cand_half = unit_cand.astype(jnp.bfloat16)
    cosine = jnp.einsum("gsd,gcd->gsc", units, cand_half, preferred_element_type=jnp.float32)
    local_label = all_labels - (member * groups + group) * BLK
    onehot = (lax.broadcasted_iota(jnp.int32, (1, 1, BLK), 2) == local_label[:, :, None]).astype(
        jnp.float32
    )
    logits = logit_scale * (cosine - cos_margin * onehot)
    exp_logits = jnp.exp(logits) * listed.astype(jnp.float32)[:, :, None]
    totals, label_logit = lax.psum(
        (jnp.sum(exp_logits, axis=2), jnp.sum(logits * onehot, axis=2)), AXES
    )
    loss_all = (jnp.log(totals) - label_logit).reshape(devices, tok_dev)
    sample_loss = lax.dynamic_slice_in_dim(loss_all, group * members + member, 1, 0)[0]

    weights = (logit_scale * (exp_logits / totals[:, :, None] - onehot)).astype(jnp.bfloat16)
    partial = jnp.einsum("gsc,gcd->gsd", weights, cand_half, preferred_element_type=jnp.float32)
    home = exchange(partial.astype(jnp.bfloat16).reshape(devices, tok_dev, width), AXES)
    unit_grad = jnp.sum(home.astype(jnp.float32), axis=0)
    feature_grad = inv_norm * (
        unit_grad - jnp.sum(unit_grad * unit_rows, axis=1, keepdims=True) * unit_rows
    )
    slot_grad = jnp.einsum("gsc,gsd->gcd", weights, units, preferred_element_type=jnp.float32)
    cand_grad = inv_cand * (
        slot_grad - jnp.sum(slot_grad * unit_cand, axis=2, keepdims=True) * unit_cand
    )
    cand_grad = cand_grad.astype(jnp.bfloat16).astype(jnp.float32)
    names = block_ids == jnp.arange(held, dtype=jnp.int32)[None, :]
    centre_grad = jnp.sum(
        jnp.where(names[:, :, None, None], cand_grad[:, None], 0.0), axis=0
    ).reshape(held * BLK, width)
    return (sample_loss, feature_grad, centre_grad)


def on_axes(body, mesh, axes):
    split = P(axes)
    return jax.shard_map(
        body,
        mesh=mesh,
        in_specs=(split, P("group"), split, P(None, axes), P(None, axes)),
        out_specs=(split, split, split),
        check_vma=False,
    )


def solution(mesh):
    groups, members = mesh.shape["group"], mesh.shape["member"]
    by_core = jax.sharding.Mesh(
        mesh.devices.reshape(groups, members // 2, 2), ("group", "chip", "core")
    )

    def program(features, *others):
        half = features.shape[0] // 2
        if half == 128 and 2 * groups == features.shape[0] // mesh.size == 8:
            return on_axes(on_device, by_core, (*CHIPS, "core"))(features, *others)
        return on_axes(on_device_of_many, mesh, AXES)(features, *others)

    return program
```

```python
import jax
import jax.numpy as jnp
from jax import lax
from jax.experimental import pallas as pl
from jax.experimental.pallas import tpu as pltpu
from jax.sharding import PartitionSpec as P

BLK = 128
AXES = ("group", "member")
CHIPS = ("group", "chip")

logit_scale = 32.0
cos_margin = 0.35
norm_epsilon = 1e-06
GROUP_ORDER = (2, 0, 3, 1)
UNLISTED = 1e19

VMEM = pl.BlockSpec(memory_space=pltpu.VMEM)
HBM = pl.BlockSpec(memory_space=pltpu.HBM)


def inverse_norm(rows):
    return lax.rsqrt(jnp.sum(rows * rows, axis=-1, keepdims=True) + norm_epsilon)


def contract(left, right, left_dim, right_dim):
    dims = (((left_dim,), (right_dim,)), ((), ()))
    return lax.dot_general(left, right, dims, preferred_element_type=jnp.float32)


def lanes(rows):
    return lax.broadcasted_iota(jnp.int32, (rows, 128), 1)


def run(kernel, out_shape, in_specs, *operands, out_spec=VMEM, scratch=()):
    shapes = jax.tree.leaves(out_shape)
    return pl.pallas_call(
        kernel,
        out_shape=out_shape,
        in_specs=in_specs,
        out_specs=jax.tree.map(lambda _: out_spec, out_shape),
        scratch_shapes=scratch,
        compiler_params=pltpu.CompilerParams(vmem_limit_bytes=48 * 1024 * 1024),
        cost_estimate=pl.CostEstimate(
            flops=0,
            transcendentals=0,
            bytes_accessed=sum(a.size * a.dtype.itemsize for a in (*shapes, *operands)),
        ),
    )(*operands)


def load(
    features,
    labels,
    centres,
    ids,
    listed,
    copies_out,
    blocks_out,
    centres_out,
    named_out,
    held_features,
    held_labels,
    held_ids,
    held_listed,
    arrived,
):
    moves = [
        pltpu.make_async_copy(source, target, arrived.at[i])
        for i, (source, target) in enumerate(
            (
                (features, held_features),
                (labels, held_labels),
                (ids, held_ids),
                (listed, held_listed),
                (centres, centres_out),
            )
        )
    ]
    for move in moves:
        move.start()
    moves[0].wait()
    moves[1].wait()
    chip = lax.axis_index("chip")
    member = 2 * chip + lax.axis_index("core")
    copies, tok_dev, _ = copies_out.shape
    width = features.shape[1]
    rows = held_features[...].astype(jnp.float32)
    unit = (rows * inverse_norm(rows)).astype(jnp.bfloat16)
    copies_out[:, :, :width] = jnp.broadcast_to(unit[None], (copies, tok_dev, width))

    place = own_place() * tok_dev
    row = held_labels[...]
    row = jnp.concatenate([row, jnp.zeros((1, 128 - row.shape[1]), jnp.int32)], axis=1)
    row = jnp.broadcast_to(row, (tok_dev, 128))
    row = pltpu.roll(row, lax.rem(place - member * tok_dev + 128, 128), 1)
    digit = lax.broadcasted_iota(jnp.int32, (tok_dev, 128), 0)
    digits = (row >> (7 * jnp.minimum(digit, 3))) & 127
    lane = lanes(tok_dev)
    digits = jnp.where((lane >= place) & (lane < place + tok_dev), digits, 0)
    copies_out[:, :, width:] = jnp.broadcast_to(
        digits.astype(jnp.float32).astype(jnp.bfloat16)[None], (copies, tok_dev, 128)
    )
    for move in moves[2:]:
        move.wait()
    named_out[...] = select([held_ids[0, group] for group in GROUP_ORDER], 1)
    for g, group in enumerate(GROUP_ORDER):
        block = centres_out[held_ids[0, group]]
        blocks_out[g] = jnp.where(held_listed[0, group] > 0, block, jnp.full_like(block, UNLISTED))


def own_place():
    groups, chips = lax.axis_size("group"), lax.axis_size("chip")
    group = lax.axis_index("group")
    place = sum(jnp.where(group == g, k, 0) for k, g in enumerate(GROUP_ORDER))
    return (chips - 1 - lax.axis_index("chip")) * groups + place


def select(parts, rows):
    owner = lax.rem(lanes(1) // 8, len(parts))
    out = jnp.broadcast_to(parts[0], (rows, 128))
    for g in range(1, len(parts)):
        out = jnp.where(owner == g, parts[g], out)
    return out


def exponentials(packed, core, blocks, inverse):
    groups, _, width = blocks.shape
    digits = jnp.sum(
        packed[:, width:].astype(jnp.float32).reshape(128 // 8, 8, 128), axis=0
    ).astype(jnp.int32)
    labels = digits[0:1] + (digits[1:2] << 7) + (digits[2:3] << 14)
    member = 2 * lax.axis_index("chip") + core
    first = (member * groups + lax.axis_index("group")) * BLK
    onehot = lax.broadcasted_iota(jnp.int32, (BLK, 128), 0) == labels - first
    units = packed[:, :width]
    dots = contract(blocks[...].reshape(groups * BLK, width), units, 1, 1)
    cosine = inverse * select([dots[g * BLK : (g + 1) * BLK] for g in range(groups)], BLK)
    expo = jnp.exp(logit_scale * (cosine - jnp.where(onehot, cos_margin, 0.0)))
    return jnp.where(inverse > 0.0, expo, 0.0), onehot, cosine * inverse


def sums(parts):
    rest = [jnp.where(onehot, 0.0, expo) for expo, onehot, _ in parts]
    at_label = [jnp.where(onehot, expo, 0.0) for expo, onehot, _ in parts]
    return [jnp.sum(sum(part), axis=0, keepdims=True) for part in (rest, at_label)]


def forward(packed, own_blocks, pair_blocks, expo_out, scaled_out, inverse_out, sums_out):
    core = lax.axis_index("core")
    parts = []
    for k, blocks in enumerate((own_blocks, pair_blocks)):
        norms = [inverse_norm(blocks[g].astype(jnp.float32)) for g in range(blocks.shape[0])]
        inverse = select(norms, BLK)
        inverse_out[k] = inverse
        part = exponentials(packed, core if k == 0 else 1 - core, blocks, inverse)
        expo_out[k] = jnp.where(part[1], -1.0, part[0])
        parts.append(part)
    scaled_out[...] = parts[0][2]
    sums_out[0:1, :], sums_out[1:2, :] = sums(parts)


def forward_other(
    packed, own_blocks, pair_blocks, inverse, own_sums, shares, expo_out, scaled_out, sent_out
):
    core = lax.axis_index("core")
    own = exponentials(packed, core, own_blocks, inverse[0])
    pair = exponentials(packed, 1 - core, pair_blocks, inverse[1])
    expo_out[...] = jnp.where(own[1], -1.0, own[0])
    scaled_out[...] = own[2]
    rows, wide = shares.shape
    sent_out[:, :wide] = shares[...]
    total = jnp.concatenate([own_sums[...], *sums([own, pair])], axis=0)
    high = total.astype(jnp.bfloat16)
    low = (total - high.astype(jnp.float32)).astype(jnp.bfloat16)
    tile = jnp.concatenate([high.astype(jnp.float32), low.astype(jnp.float32)], axis=0)
    tile = jnp.broadcast_to(tile[None], (rows // 8, 8, 128))
    sent_out[:, wide:] = tile.reshape(rows, 128).astype(jnp.bfloat16)


def shares(expo, inverse, own_blocks, pair_blocks, shares_out):
    groups, _, width = own_blocks.shape
    others, label = [], []
    for k in range(2):
        others.append((jnp.maximum(expo[k], 0.0) * inverse[k]).T)
        label.append(jnp.where(expo[k] < 0.0, 1.0, 0.0).T)
    others = jnp.concatenate(others, axis=1)
    label = jnp.concatenate(label, axis=1)
    places = [[] for _ in range(groups)]
    for g in range(groups):
        rows = [part[p * 8 : p * 8 + 8] for part in (others, label) for p in range(g, 16, groups)]
        blocks = jnp.concatenate([own_blocks[g], pair_blocks[g]], axis=0)
        both = contract(jnp.concatenate(rows, axis=0).astype(jnp.bfloat16), blocks, 1, 0)
        places[g] = [both[i * 8 : i * 8 + 8] for i in range(len(rows))]
    for part in range(2):
        count = 16 // groups
        rows = [places[g][part * count + i] for i in range(count) for g in range(groups)]
        rows = jnp.concatenate(rows, axis=0).astype(jnp.bfloat16)
        shares_out[:, part * width : (part + 1) * width] = rows


def backward(
    named,
    received,
    expo,
    other_expo,
    scaled,
    other_scaled,
    inverse,
    own_packed,
    other_packed,
    features,
    centres,
    grad_out,
    feature_out,
    loss_out,
    grad,
    feature_grad,
    loss_row,
    left,
):
    held = centres.shape[0]
    tok_dev, width = features.shape

    def total_of(columns):
        total = received[0, :, columns].astype(jnp.float32)
        for i in range(1, received.shape[0]):
            total = total + received[i, :, columns].astype(jnp.float32)
        return total

    tile = total_of(pl.ds(2 * width, 128))
    tile = tile[:4] + tile[4:]
    own_rest, own_label = tile[0:1], tile[1:2]
    other_rest, other_label = tile[2:3], tile[3:4]

    units = jnp.concatenate([own_packed[:, :width], other_packed[:, :width]], axis=0)
    own_scale = logit_scale / (own_rest + own_label)
    other_scale = logit_scale / (other_rest + other_label)
    own = expo[0]
    other = other_expo[...]
    own = jnp.where(own < 0.0, -own_rest, own) * own_scale
    other = jnp.where(other < 0.0, -other_rest, other) * other_scale
    weights = jnp.concatenate([own, other], axis=1).astype(jnp.bfloat16).astype(jnp.float32)
    pulls = weights * jnp.concatenate([scaled[...], other_scaled[...]], axis=1)
    own_named = named[...]
    named = jnp.concatenate([own_named, own_named], axis=1)
    moves = []

    def leave(source, target):
        move = pltpu.make_async_copy(source, target, left.at[len(moves)])
        move.start()
        moves.append(move)

    def block_out(b):
        mine = jnp.where(named == b, weights, 0.0).astype(jnp.bfloat16)
        factor = jnp.max(jnp.where(own_named == b, inverse[0], 0.0), axis=1, keepdims=True)
        back = factor * jnp.sum(jnp.where(named == b, pulls, 0.0), axis=1, keepdims=True)
        slot_grad = contract(mine, units, 1, 0)
        grad[b] = factor * slot_grad - back * centres[b].astype(jnp.float32)
        leave(grad.at[b], grad_out.at[b])

    for b in range(held // 2):
        block_out(b)

    sums = total_of(pl.ds(0, 2 * width))
    sample = lax.broadcasted_iota(jnp.int32, (tok_dev, 128), 0) + own_place() * tok_dev
    mine = lanes(tok_dev) == sample
    rest = jnp.sum(jnp.where(mine, own_rest, 0.0), axis=1, keepdims=True)
    label = jnp.sum(jnp.where(mine, own_label, 0.0), axis=1, keepdims=True)
    total = rest + label
    loss = jnp.log(total) - jnp.log(label)
    square = (tok_dev, tok_dev)
    diagonal = lax.broadcasted_iota(jnp.int32, square, 0) == lax.broadcasted_iota(
        jnp.int32, square, 1
    )
    loss_row[...] = jnp.sum(jnp.where(diagonal, loss, 0.0), axis=0, keepdims=True)
    rows = features[...].astype(jnp.float32)
    inv_norm = inverse_norm(rows)
    unit = rows * inv_norm
    cand = sums[:, width : 2 * width]
    cand = (cand * inverse_norm(cand)).astype(jnp.bfloat16).astype(jnp.float32)
    unit_grad = logit_scale / total * (sums[:, :width] - rest * cand)
    along = jnp.sum(unit_grad * unit, axis=1, keepdims=True)
    feature_grad[...] = inv_norm * (unit_grad - along * unit)

    leave(feature_grad, feature_out)
    leave(loss_row, loss_out)
    for b in range(held // 2, held):
        block_out(b)
    for move in moves:
        move.wait()


def exchange(pieces, axes, order=None):
    return lax.all_to_all(
        pieces, axes, split_axis=0, concat_axis=0, axis_index_groups=order, tiled=True
    )


def exchange_chips(pieces):
    chips = lax.axis_size("chip")
    order = [g * chips + chip for chip in reversed(range(chips)) for g in GROUP_ORDER]
    return exchange(pieces, CHIPS, [order])


def with_partner(value):
    return lax.ppermute(value, "core", [(0, 1), (1, 0)])


def on_device(features, labels, centres, block_ids, listed):
    groups = lax.axis_size("group")
    chips = groups * lax.axis_size("chip")
    tok_dev, width = features.shape
    held = centres.shape[0] // BLK
    half = chips * tok_dev
    bf16, f32 = jnp.bfloat16, jnp.float32
    shape = jax.ShapeDtypeStruct

    copies, own_blocks, blocks, named, own_features = run(
        load,
        (
            shape((chips, tok_dev, width + 128), bf16),
            shape((groups, BLK, width), bf16),
            shape((held, BLK, width), bf16),
            shape((1, 128), block_ids.dtype),
            shape(features.shape, bf16),
        ),
        [HBM] * 5,
        *(
            pltpu.with_memory_space_constraint(array, pltpu.HBM)
            for array in (
                features,
                labels.reshape(1, -1),
                centres.reshape(held, BLK, width),
                block_ids.reshape(1, groups),
                listed.reshape(1, groups),
            )
        ),
        scratch=[
            pltpu.VMEM((1, labels.shape[0]), labels.dtype),
            pltpu.SMEM((1, groups), block_ids.dtype),
            pltpu.SMEM((1, groups), listed.dtype),
            pltpu.SemaphoreType.DMA((5,)),
        ],
    )
    pair_blocks = with_partner(own_blocks)
    own_packed = exchange_chips(copies).reshape(half, width + 128)
    other_packed = with_partner(own_packed)
    expo, scaled, inverse, own_sums = run(
        forward,
        (
            shape((2, BLK, half), f32),
            shape((BLK, half), f32),
            shape((2, BLK, half), f32),
            shape((2, half), f32),
        ),
        [VMEM] * 3,
        own_packed,
        own_blocks,
        pair_blocks,
    )
    going = run(
        shares,
        shape((half, 2 * width), bf16),
        [VMEM] * 4,
        expo,
        inverse,
        own_blocks,
        pair_blocks,
    )
    other_expo, other_scaled, sent = run(
        forward_other,
        (
            shape((BLK, half), f32),
            shape((BLK, half), f32),
            shape((half, 2 * width + 128), bf16),
        ),
        [VMEM] * 6,
        other_packed,
        own_blocks,
        pair_blocks,
        inverse,
        own_sums,
        going,
    )
    received = exchange_chips(sent.reshape(chips, tok_dev, 2 * width + 128))
    outs = (shape((held, BLK, width), f32), shape((tok_dev, width), f32), shape((1, tok_dev), f32))
    centre_grad, feature_grad, loss = run(
        backward,
        outs,
        [VMEM] * 11,
        named,
        received,
        expo,
        other_expo,
        scaled,
        other_scaled,
        inverse,
        own_packed,
        other_packed,
        own_features,
        blocks,
        out_spec=HBM,
        scratch=[
            *(pltpu.VMEM(out.shape, out.dtype) for out in outs),
            pltpu.SemaphoreType.DMA((held + 2,)),
        ],
    )
    return (loss.reshape(tok_dev), feature_grad, centre_grad.reshape(held * BLK, width))


def on_device_of_many(features, labels, centres, block_ids, listed):
    groups = lax.axis_size("group")
    members = lax.axis_size("member")
    devices = groups * members
    group = lax.axis_index("group")
    member = lax.axis_index("member")
    tok_dev, width = features.shape
    group_tok = members * tok_dev
    held = centres.shape[0] // BLK

    vectors = features.astype(jnp.float32)
    inv_norm = inverse_norm(vectors)
    unit_rows = vectors * inv_norm
    copies = jnp.broadcast_to(unit_rows.astype(jnp.bfloat16), (devices, tok_dev, width))
    units = exchange(copies, AXES).reshape(groups, group_tok, width)
    all_labels = exchange(jnp.broadcast_to(labels[None], (groups, group_tok)), "group")

    picked = centres.reshape(held, BLK, width)[block_ids[:, 0]].astype(jnp.float32)
    inv_cand = inverse_norm(picked)
    unit_cand = picked * inv_cand
    cand_half = unit_cand.astype(jnp.bfloat16)
    cosine = jnp.einsum("gsd,gcd->gsc", units, cand_half, preferred_element_type=jnp.float32)
    local_label = all_labels - (member * groups + group) * BLK
    onehot = (lax.broadcasted_iota(jnp.int32, (1, 1, BLK), 2) == local_label[:, :, None]).astype(
        jnp.float32
    )
    logits = logit_scale * (cosine - cos_margin * onehot)
    exp_logits = jnp.exp(logits) * listed.astype(jnp.float32)[:, :, None]
    totals, label_logit = lax.psum(
        (jnp.sum(exp_logits, axis=2), jnp.sum(logits * onehot, axis=2)), AXES
    )
    loss_all = (jnp.log(totals) - label_logit).reshape(devices, tok_dev)
    sample_loss = lax.dynamic_slice_in_dim(loss_all, group * members + member, 1, 0)[0]

    weights = (logit_scale * (exp_logits / totals[:, :, None] - onehot)).astype(jnp.bfloat16)
    partial = jnp.einsum("gsc,gcd->gsd", weights, cand_half, preferred_element_type=jnp.float32)
    home = exchange(partial.astype(jnp.bfloat16).reshape(devices, tok_dev, width), AXES)
    unit_grad = jnp.sum(home.astype(jnp.float32), axis=0)
    feature_grad = inv_norm * (
        unit_grad - jnp.sum(unit_grad * unit_rows, axis=1, keepdims=True) * unit_rows
    )
    slot_grad = jnp.einsum("gsc,gsd->gcd", weights, units, preferred_element_type=jnp.float32)
    cand_grad = inv_cand * (
        slot_grad - jnp.sum(slot_grad * unit_cand, axis=2, keepdims=True) * unit_cand
    )
    cand_grad = cand_grad.astype(jnp.bfloat16).astype(jnp.float32)
    names = block_ids == jnp.arange(held, dtype=jnp.int32)[None, :]
    centre_grad = jnp.sum(
        jnp.where(names[:, :, None, None], cand_grad[:, None], 0.0), axis=0
    ).reshape(held * BLK, width)
    return (sample_loss, feature_grad, centre_grad)


def on_axes(body, mesh, axes):
    split = P(axes)
    return jax.shard_map(
        body,
        mesh=mesh,
        in_specs=(split, P("group"), split, P(None, axes), P(None, axes)),
        out_specs=(split, split, split),
        check_vma=False,
    )


def solution(mesh):
    groups, members = mesh.shape["group"], mesh.shape["member"]
    by_core = jax.sharding.Mesh(
        mesh.devices.reshape(groups, members // 2, 2), ("group", "chip", "core")
    )

    def program(features, *others):
        half = features.shape[0] // 2
        if half == 128 and 2 * groups == features.shape[0] // mesh.size == 8:
            return on_axes(on_device, by_core, (*CHIPS, "core"))(features, *others)
        return on_axes(on_device_of_many, mesh, AXES)(features, *others)

    return program
```

```python
import jax
import jax.numpy as jnp
from jax import lax
from jax.experimental import pallas as pl
from jax.experimental.pallas import tpu as pltpu
from jax.sharding import PartitionSpec as P

BLK = 128
AXES = ("group", "member")
CHIPS = ("group", "chip")

logit_scale = 32.0
cos_margin = 0.35
norm_epsilon = 1e-06
GROUP_ORDER = (2, 0, 3, 1)
UNLISTED = 1e19

VMEM = pl.BlockSpec(memory_space=pltpu.VMEM)
HBM = pl.BlockSpec(memory_space=pltpu.HBM)


def inverse_norm(rows):
    return lax.rsqrt(jnp.sum(rows * rows, axis=-1, keepdims=True) + norm_epsilon)


def contract(left, right, left_dim, right_dim):
    dims = (((left_dim,), (right_dim,)), ((), ()))
    return lax.dot_general(left, right, dims, preferred_element_type=jnp.float32)


def lanes(rows):
    return lax.broadcasted_iota(jnp.int32, (rows, 128), 1)


def run(kernel, out_shape, in_specs, *operands, out_spec=VMEM, scratch=()):
    shapes = jax.tree.leaves(out_shape)
    return pl.pallas_call(
        kernel,
        out_shape=out_shape,
        in_specs=in_specs,
        out_specs=jax.tree.map(lambda _: out_spec, out_shape),
        scratch_shapes=scratch,
        compiler_params=pltpu.CompilerParams(vmem_limit_bytes=48 * 1024 * 1024),
        cost_estimate=pl.CostEstimate(
            flops=0,
            transcendentals=0,
            bytes_accessed=sum(a.size * a.dtype.itemsize for a in (*shapes, *operands)),
        ),
    )(*operands)


def load(
    features,
    labels,
    centres,
    ids,
    listed,
    copies_out,
    blocks_out,
    centres_out,
    named_out,
    held_features,
    held_labels,
    held_ids,
    held_listed,
    arrived,
):
    moves = [
        pltpu.make_async_copy(source, target, arrived.at[i])
        for i, (source, target) in enumerate(
            (
                (features, held_features),
                (labels, held_labels),
                (ids, held_ids),
                (listed, held_listed),
                (centres, centres_out),
            )
        )
    ]
    for move in moves:
        move.start()
    moves[0].wait()
    moves[1].wait()
    chip = lax.axis_index("chip")
    member = 2 * chip + lax.axis_index("core")
    copies, tok_dev, _ = copies_out.shape
    width = features.shape[1]
    rows = held_features[...].astype(jnp.float32)
    unit = (rows * inverse_norm(rows)).astype(jnp.bfloat16)
    copies_out[:, :, :width] = jnp.broadcast_to(unit[None], (copies, tok_dev, width))

    place = own_place() * tok_dev
    row = held_labels[...]
    row = jnp.concatenate([row, jnp.zeros((1, 128 - row.shape[1]), jnp.int32)], axis=1)
    row = jnp.broadcast_to(row, (tok_dev, 128))
    row = pltpu.roll(row, lax.rem(place - member * tok_dev + 128, 128), 1)
    digit = lax.broadcasted_iota(jnp.int32, (tok_dev, 128), 0)
    digits = (row >> (7 * jnp.minimum(digit, 3))) & 127
    lane = lanes(tok_dev)
    digits = jnp.where((lane >= place) & (lane < place + tok_dev), digits, 0)
    copies_out[:, :, width:] = jnp.broadcast_to(
        digits.astype(jnp.float32).astype(jnp.bfloat16)[None], (copies, tok_dev, 128)
    )
    for move in moves[2:]:
        move.wait()
    named_out[...] = select([held_ids[0, group] for group in GROUP_ORDER], 1)
    for g, group in enumerate(GROUP_ORDER):
        block = centres_out[held_ids[0, group]]
        blocks_out[g] = jnp.where(held_listed[0, group] > 0, block, jnp.full_like(block, UNLISTED))


def own_place():
    groups, chips = lax.axis_size("group"), lax.axis_size("chip")
    group = lax.axis_index("group")
    place = sum(jnp.where(group == g, k, 0) for k, g in enumerate(GROUP_ORDER))
    return (chips - 1 - lax.axis_index("chip")) * groups + place


def select(parts, rows):
    owner = lax.rem(lanes(1) // 8, len(parts))
    out = jnp.broadcast_to(parts[0], (rows, 128))
    for g in range(1, len(parts)):
        out = jnp.where(owner == g, parts[g], out)
    return out


def exponentials(packed, core, blocks, inverse):
    groups, _, width = blocks.shape
    digits = jnp.sum(
        packed[:, width:].astype(jnp.float32).reshape(128 // 8, 8, 128), axis=0
    ).astype(jnp.int32)
    labels = digits[0:1] + (digits[1:2] << 7) + (digits[2:3] << 14)
    member = 2 * lax.axis_index("chip") + core
    first = (member * groups + lax.axis_index("group")) * BLK
    onehot = lax.broadcasted_iota(jnp.int32, (BLK, 128), 0) == labels - first
    units = packed[:, :width]
    dots = contract(blocks[...].reshape(groups * BLK, width), units, 1, 1)
    cosine = inverse * select([dots[g * BLK : (g + 1) * BLK] for g in range(groups)], BLK)
    expo = jnp.exp(logit_scale * (cosine - jnp.where(onehot, cos_margin, 0.0)))
    return jnp.where(inverse > 0.0, expo, 0.0), onehot, cosine * inverse


def sums(parts):
    rest = [jnp.where(onehot, 0.0, expo) for expo, onehot, _ in parts]
    at_label = [jnp.where(onehot, expo, 0.0) for expo, onehot, _ in parts]
    return [jnp.sum(sum(part), axis=0, keepdims=True) for part in (rest, at_label)]


def forward(packed, own_blocks, pair_blocks, expo_out, scaled_out, inverse_out, sums_out):
    core = lax.axis_index("core")
    parts = []
    for k, blocks in enumerate((own_blocks, pair_blocks)):
        norms = [inverse_norm(blocks[g].astype(jnp.float32)) for g in range(blocks.shape[0])]
        inverse = select(norms, BLK)
        inverse_out[k] = inverse
        part = exponentials(packed, core if k == 0 else 1 - core, blocks, inverse)
        expo_out[k] = jnp.where(part[1], -1.0, part[0])
        parts.append(part)
    scaled_out[...] = parts[0][2]
    sums_out[0:1, :], sums_out[1:2, :] = sums(parts)


def forward_other(
    packed, own_blocks, pair_blocks, inverse, own_sums, shares, expo_out, scaled_out, sent_out
):
    core = lax.axis_index("core")
    own = exponentials(packed, core, own_blocks, inverse[0])
    pair = exponentials(packed, 1 - core, pair_blocks, inverse[1])
    expo_out[...] = jnp.where(own[1], -1.0, own[0])
    scaled_out[...] = own[2]
    rows, wide = shares.shape
    sent_out[:, :wide] = shares[...]
    total = jnp.concatenate([own_sums[...], *sums([own, pair])], axis=0)
    high = total.astype(jnp.bfloat16)
    low = (total - high.astype(jnp.float32)).astype(jnp.bfloat16)
    tile = jnp.concatenate([high.astype(jnp.float32), low.astype(jnp.float32)], axis=0)
    tile = jnp.broadcast_to(tile[None], (rows // 8, 8, 128))
    sent_out[:, wide:] = tile.reshape(rows, 128).astype(jnp.bfloat16)


def shares(expo, inverse, own_blocks, pair_blocks, named, shares_out, factors_out):
    groups, _, width = own_blocks.shape
    others, label = [], []
    for k in range(2):
        others.append((jnp.maximum(expo[k], 0.0) * inverse[k]).T)
        label.append(jnp.where(expo[k] < 0.0, 1.0, 0.0).T)
    others = jnp.concatenate(others, axis=1)
    label = jnp.concatenate(label, axis=1)
    places = [[] for _ in range(groups)]
    for g in range(groups):
        rows = [part[p * 8 : p * 8 + 8] for part in (others, label) for p in range(g, 16, groups)]
        blocks = jnp.concatenate([own_blocks[g], pair_blocks[g]], axis=0)
        both = contract(jnp.concatenate(rows, axis=0).astype(jnp.bfloat16), blocks, 1, 0)
        places[g] = [both[i * 8 : i * 8 + 8] for i in range(len(rows))]
    for part in range(2):
        count = 16 // groups
        rows = [places[g][part * count + i] for i in range(count) for g in range(groups)]
        rows = jnp.concatenate(rows, axis=0).astype(jnp.bfloat16)
        shares_out[:, part * width : (part + 1) * width] = rows
    factors = [jnp.where(named[...] == b, inverse[0], 0.0) for b in range(groups)]
    factors_out[...] = select([jnp.max(part, axis=1, keepdims=True) for part in factors], BLK)


def backward(
    named,
    received,
    expo,
    other_expo,
    scaled,
    other_scaled,
    factors,
    own_packed,
    other_packed,
    features,
    centres,
    grad_out,
    feature_out,
    loss_out,
    grad,
    feature_grad,
    loss_row,
    left,
):
    held = centres.shape[0]
    tok_dev, width = features.shape

    def total_of(columns):
        total = received[0, :, columns].astype(jnp.float32)
        for i in range(1, received.shape[0]):
            total = total + received[i, :, columns].astype(jnp.float32)
        return total

    tile = total_of(pl.ds(2 * width, 128))
    tile = tile[:4] + tile[4:]
    own_rest, own_label = tile[0:1], tile[1:2]
    other_rest, other_label = tile[2:3], tile[3:4]

    units = jnp.concatenate([own_packed[:, :width], other_packed[:, :width]], axis=0)
    own_scale = logit_scale / (own_rest + own_label)
    other_scale = logit_scale / (other_rest + other_label)
    own = expo[0]
    other = other_expo[...]
    own = jnp.where(own < 0.0, -own_rest, own) * own_scale
    other = jnp.where(other < 0.0, -other_rest, other) * other_scale
    weights = jnp.concatenate([own, other], axis=1).astype(jnp.bfloat16).astype(jnp.float32)
    pulls = weights * jnp.concatenate([scaled[...], other_scaled[...]], axis=1)
    named = jnp.concatenate([named[...], named[...]], axis=1)
    moves = []

    def leave(source, target):
        move = pltpu.make_async_copy(source, target, left.at[len(moves)])
        move.start()
        moves.append(move)

    def block_out(b):
        mine = jnp.where(named == b, weights, 0.0).astype(jnp.bfloat16)
        factor = factors[:, b * 8 : b * 8 + 1]
        back = factor * jnp.sum(jnp.where(named == b, pulls, 0.0), axis=1, keepdims=True)
        slot_grad = contract(mine, units, 1, 0)
        grad[b] = factor * slot_grad - back * centres[b].astype(jnp.float32)
        leave(grad.at[b], grad_out.at[b])

    for b in range(held // 2):
        block_out(b)

    sums = total_of(pl.ds(0, 2 * width))
    sample = lax.broadcasted_iota(jnp.int32, (tok_dev, 128), 0) + own_place() * tok_dev
    mine = lanes(tok_dev) == sample
    rest = jnp.sum(jnp.where(mine, own_rest, 0.0), axis=1, keepdims=True)
    label = jnp.sum(jnp.where(mine, own_label, 0.0), axis=1, keepdims=True)
    total = rest + label
    loss = jnp.log(total) - jnp.log(label)
    square = (tok_dev, tok_dev)
    diagonal = lax.broadcasted_iota(jnp.int32, square, 0) == lax.broadcasted_iota(
        jnp.int32, square, 1
    )
    loss_row[...] = jnp.sum(jnp.where(diagonal, loss, 0.0), axis=0, keepdims=True)
    rows = features[...].astype(jnp.float32)
    inv_norm = inverse_norm(rows)
    unit = rows * inv_norm
    cand = sums[:, width : 2 * width]
    cand = (cand * inverse_norm(cand)).astype(jnp.bfloat16).astype(jnp.float32)
    unit_grad = logit_scale / total * (sums[:, :width] - rest * cand)
    along = jnp.sum(unit_grad * unit, axis=1, keepdims=True)
    feature_grad[...] = inv_norm * (unit_grad - along * unit)

    leave(feature_grad, feature_out)
    leave(loss_row, loss_out)
    for b in range(held // 2, held):
        block_out(b)
    for move in moves:
        move.wait()


def exchange(pieces, axes, order=None):
    return lax.all_to_all(
        pieces, axes, split_axis=0, concat_axis=0, axis_index_groups=order, tiled=True
    )


def exchange_chips(pieces):
    chips = lax.axis_size("chip")
    order = [g * chips + chip for chip in reversed(range(chips)) for g in GROUP_ORDER]
    return exchange(pieces, CHIPS, [order])


def with_partner(value):
    return lax.ppermute(value, "core", [(0, 1), (1, 0)])


def on_device(features, labels, centres, block_ids, listed):
    groups = lax.axis_size("group")
    chips = groups * lax.axis_size("chip")
    tok_dev, width = features.shape
    held = centres.shape[0] // BLK
    half = chips * tok_dev
    bf16, f32 = jnp.bfloat16, jnp.float32
    shape = jax.ShapeDtypeStruct

    copies, own_blocks, blocks, named, own_features = run(
        load,
        (
            shape((chips, tok_dev, width + 128), bf16),
            shape((groups, BLK, width), bf16),
            shape((held, BLK, width), bf16),
            shape((1, 128), block_ids.dtype),
            shape(features.shape, bf16),
        ),
        [HBM] * 5,
        *(
            pltpu.with_memory_space_constraint(array, pltpu.HBM)
            for array in (
                features,
                labels.reshape(1, -1),
                centres.reshape(held, BLK, width),
                block_ids.reshape(1, groups),
                listed.reshape(1, groups),
            )
        ),
        scratch=[
            pltpu.VMEM((1, labels.shape[0]), labels.dtype),
            pltpu.SMEM((1, groups), block_ids.dtype),
            pltpu.SMEM((1, groups), listed.dtype),
            pltpu.SemaphoreType.DMA((5,)),
        ],
    )
    pair_blocks = with_partner(own_blocks)
    own_packed = exchange_chips(copies).reshape(half, width + 128)
    other_packed = with_partner(own_packed)
    expo, scaled, inverse, own_sums = run(
        forward,
        (
            shape((2, BLK, half), f32),
            shape((BLK, half), f32),
            shape((2, BLK, half), f32),
            shape((2, half), f32),
        ),
        [VMEM] * 3,
        own_packed,
        own_blocks,
        pair_blocks,
    )
    going, factors = run(
        shares,
        (shape((half, 2 * width), bf16), shape((BLK, 128), f32)),
        [VMEM] * 5,
        expo,
        inverse,
        own_blocks,
        pair_blocks,
        named,
    )
    other_expo, other_scaled, sent = run(
        forward_other,
        (
            shape((BLK, half), f32),
            shape((BLK, half), f32),
            shape((half, 2 * width + 128), bf16),
        ),
        [VMEM] * 6,
        other_packed,
        own_blocks,
        pair_blocks,
        inverse,
        own_sums,
        going,
    )
    received = exchange_chips(sent.reshape(chips, tok_dev, 2 * width + 128))
    outs = (shape((held, BLK, width), f32), shape((tok_dev, width), f32), shape((1, tok_dev), f32))
    centre_grad, feature_grad, loss = run(
        backward,
        outs,
        [VMEM] * 11,
        named,
        received,
        expo,
        other_expo,
        scaled,
        other_scaled,
        factors,
        own_packed,
        other_packed,
        own_features,
        blocks,
        out_spec=HBM,
        scratch=[
            *(pltpu.VMEM(out.shape, out.dtype) for out in outs),
            pltpu.SemaphoreType.DMA((held + 2,)),
        ],
    )
    return (loss.reshape(tok_dev), feature_grad, centre_grad.reshape(held * BLK, width))


def on_device_of_many(features, labels, centres, block_ids, listed):
    groups = lax.axis_size("group")
    members = lax.axis_size("member")
    devices = groups * members
    group = lax.axis_index("group")
    member = lax.axis_index("member")
    tok_dev, width = features.shape
    group_tok = members * tok_dev
    held = centres.shape[0] // BLK

    vectors = features.astype(jnp.float32)
    inv_norm = inverse_norm(vectors)
    unit_rows = vectors * inv_norm
    copies = jnp.broadcast_to(unit_rows.astype(jnp.bfloat16), (devices, tok_dev, width))
    units = exchange(copies, AXES).reshape(groups, group_tok, width)
    all_labels = exchange(jnp.broadcast_to(labels[None], (groups, group_tok)), "group")

    picked = centres.reshape(held, BLK, width)[block_ids[:, 0]].astype(jnp.float32)
    inv_cand = inverse_norm(picked)
    unit_cand = picked * inv_cand
    cand_half = unit_cand.astype(jnp.bfloat16)
    cosine = jnp.einsum("gsd,gcd->gsc", units, cand_half, preferred_element_type=jnp.float32)
    local_label = all_labels - (member * groups + group) * BLK
    onehot = (lax.broadcasted_iota(jnp.int32, (1, 1, BLK), 2) == local_label[:, :, None]).astype(
        jnp.float32
    )
    logits = logit_scale * (cosine - cos_margin * onehot)
    exp_logits = jnp.exp(logits) * listed.astype(jnp.float32)[:, :, None]
    totals, label_logit = lax.psum(
        (jnp.sum(exp_logits, axis=2), jnp.sum(logits * onehot, axis=2)), AXES
    )
    loss_all = (jnp.log(totals) - label_logit).reshape(devices, tok_dev)
    sample_loss = lax.dynamic_slice_in_dim(loss_all, group * members + member, 1, 0)[0]

    weights = (logit_scale * (exp_logits / totals[:, :, None] - onehot)).astype(jnp.bfloat16)
    partial = jnp.einsum("gsc,gcd->gsd", weights, cand_half, preferred_element_type=jnp.float32)
    home = exchange(partial.astype(jnp.bfloat16).reshape(devices, tok_dev, width), AXES)
    unit_grad = jnp.sum(home.astype(jnp.float32), axis=0)
    feature_grad = inv_norm * (
        unit_grad - jnp.sum(unit_grad * unit_rows, axis=1, keepdims=True) * unit_rows
    )
    slot_grad = jnp.einsum("gsc,gsd->gcd", weights, units, preferred_element_type=jnp.float32)
    cand_grad = inv_cand * (
        slot_grad - jnp.sum(slot_grad * unit_cand, axis=2, keepdims=True) * unit_cand
    )
    cand_grad = cand_grad.astype(jnp.bfloat16).astype(jnp.float32)
    names = block_ids == jnp.arange(held, dtype=jnp.int32)[None, :]
    centre_grad = jnp.sum(
        jnp.where(names[:, :, None, None], cand_grad[:, None], 0.0), axis=0
    ).reshape(held * BLK, width)
    return (sample_loss, feature_grad, centre_grad)


def on_axes(body, mesh, axes):
    split = P(axes)
    return jax.shard_map(
        body,
        mesh=mesh,
        in_specs=(split, P("group"), split, P(None, axes), P(None, axes)),
        out_specs=(split, split, split),
        check_vma=False,
    )


def solution(mesh):
    groups, members = mesh.shape["group"], mesh.shape["member"]
    by_core = jax.sharding.Mesh(
        mesh.devices.reshape(groups, members // 2, 2), ("group", "chip", "core")
    )

    def program(features, *others):
        half = features.shape[0] // 2
        if half == 128 and (groups, features.shape[0] // mesh.size) == (4, 8):
            return on_axes(on_device, by_core, (*CHIPS, "core"))(features, *others)
        return on_axes(on_device_of_many, mesh, AXES)(features, *others)

    return program
```

```python
import jax
import jax.numpy as jnp
from jax import lax
from jax.experimental import pallas as pl
from jax.experimental.pallas import tpu as pltpu
from jax.sharding import PartitionSpec as P

BLK = 128
AXES = ("group", "member")
CHIPS = ("group", "chip")

logit_scale = 32.0
cos_margin = 0.35
norm_epsilon = 1e-06
GROUP_ORDER = (2, 0, 3, 1)
UNLISTED = 1e19

VMEM = pl.BlockSpec(memory_space=pltpu.VMEM)
HBM = pl.BlockSpec(memory_space=pltpu.HBM)


def inverse_norm(rows):
    return lax.rsqrt(jnp.sum(rows * rows, axis=-1, keepdims=True) + norm_epsilon)


def contract(left, right, left_dim, right_dim):
    dims = (((left_dim,), (right_dim,)), ((), ()))
    return lax.dot_general(left, right, dims, preferred_element_type=jnp.float32)


def lanes(rows):
    return lax.broadcasted_iota(jnp.int32, (rows, 128), 1)


def run(kernel, out_shape, in_specs, *operands, out_spec=VMEM, scratch=()):
    shapes = jax.tree.leaves(out_shape)
    return pl.pallas_call(
        kernel,
        out_shape=out_shape,
        in_specs=in_specs,
        out_specs=jax.tree.map(lambda _: out_spec, out_shape),
        scratch_shapes=scratch,
        compiler_params=pltpu.CompilerParams(vmem_limit_bytes=48 * 1024 * 1024),
        cost_estimate=pl.CostEstimate(
            flops=0,
            transcendentals=0,
            bytes_accessed=sum(a.size * a.dtype.itemsize for a in (*shapes, *operands)),
        ),
    )(*operands)


def load(
    features,
    labels,
    centres,
    ids,
    listed,
    copies_out,
    blocks_out,
    centres_out,
    named_out,
    held_features,
    held_labels,
    held_ids,
    held_listed,
    arrived,
):
    moves = [
        pltpu.make_async_copy(source, target, arrived.at[i])
        for i, (source, target) in enumerate(
            (
                (features, held_features),
                (labels, held_labels),
                (ids, held_ids),
                (listed, held_listed),
                (centres, centres_out),
            )
        )
    ]
    for move in moves:
        move.start()
    moves[0].wait()
    moves[1].wait()
    chip = lax.axis_index("chip")
    member = 2 * chip + lax.axis_index("core")
    copies, tok_dev, _ = copies_out.shape
    width = features.shape[1]
    rows = held_features[...].astype(jnp.float32)
    unit = (rows * inverse_norm(rows)).astype(jnp.bfloat16)
    copies_out[:, :, :width] = jnp.broadcast_to(unit[None], (copies, tok_dev, width))

    place = own_place() * tok_dev
    row = held_labels[...]
    row = jnp.concatenate([row, jnp.zeros((1, 128 - row.shape[1]), jnp.int32)], axis=1)
    row = jnp.broadcast_to(row, (tok_dev, 128))
    row = pltpu.roll(row, lax.rem(place - member * tok_dev + 128, 128), 1)
    digit = lax.broadcasted_iota(jnp.int32, (tok_dev, 128), 0)
    digits = (row >> (7 * jnp.minimum(digit, 3))) & 127
    lane = lanes(tok_dev)
    digits = jnp.where((lane >= place) & (lane < place + tok_dev), digits, 0)
    copies_out[:, :, width:] = jnp.broadcast_to(
        digits.astype(jnp.float32).astype(jnp.bfloat16)[None], (copies, tok_dev, 128)
    )
    for move in moves[2:]:
        move.wait()
    named_out[...] = select([held_ids[0, group] for group in GROUP_ORDER], 1)
    for g, group in enumerate(GROUP_ORDER):
        block = centres_out[held_ids[0, group]]
        blocks_out[g] = jnp.where(held_listed[0, group] > 0, block, jnp.full_like(block, UNLISTED))


def own_place():
    groups, chips = lax.axis_size("group"), lax.axis_size("chip")
    group = lax.axis_index("group")
    place = sum(jnp.where(group == g, k, 0) for k, g in enumerate(GROUP_ORDER))
    return (chips - 1 - lax.axis_index("chip")) * groups + place


def select(parts, rows):
    owner = lax.rem(lanes(1) // 8, len(parts))
    out = jnp.broadcast_to(parts[0], (rows, 128))
    for g in range(1, len(parts)):
        out = jnp.where(owner == g, parts[g], out)
    return out


def all_dots(packed, own_blocks, pair_blocks):
    groups, _, width = own_blocks.shape
    rows = jnp.concatenate([own_blocks[...], pair_blocks[...]], axis=0)
    dots = contract(rows.reshape(2 * groups * BLK, width), packed[:, :width], 1, 1)
    return dots[: groups * BLK], dots[groups * BLK :]


def exponentials(packed, core, dots, inverse):
    groups = dots.shape[0] // BLK
    width = packed.shape[1] - 128
    digits = jnp.sum(
        packed[:, width:].astype(jnp.float32).reshape(128 // 8, 8, 128), axis=0
    ).astype(jnp.int32)
    labels = digits[0:1] + (digits[1:2] << 7) + (digits[2:3] << 14)
    member = 2 * lax.axis_index("chip") + core
    first = (member * groups + lax.axis_index("group")) * BLK
    onehot = lax.broadcasted_iota(jnp.int32, (BLK, 128), 0) == labels - first
    cosine = inverse * select([dots[g * BLK : (g + 1) * BLK] for g in range(groups)], BLK)
    expo = jnp.exp(logit_scale * (cosine - jnp.where(onehot, cos_margin, 0.0)))
    return jnp.where(inverse > 0.0, expo, 0.0), onehot, cosine * inverse


def sums(parts):
    rest = [jnp.where(onehot, 0.0, expo) for expo, onehot, _ in parts]
    at_label = [jnp.where(onehot, expo, 0.0) for expo, onehot, _ in parts]
    return [jnp.sum(sum(part), axis=0, keepdims=True) for part in (rest, at_label)]


def forward(packed, own_blocks, pair_blocks, expo_out, scaled_out, inverse_out, sums_out):
    core = lax.axis_index("core")
    parts = []
    dots = all_dots(packed, own_blocks, pair_blocks)
    for k, blocks in enumerate((own_blocks, pair_blocks)):
        norms = [inverse_norm(blocks[g].astype(jnp.float32)) for g in range(blocks.shape[0])]
        inverse = select(norms, BLK)
        inverse_out[k] = inverse
        part = exponentials(packed, core if k == 0 else 1 - core, dots[k], inverse)
        expo_out[k] = jnp.where(part[1], -1.0, part[0])
        parts.append(part)
    scaled_out[...] = parts[0][2]
    sums_out[0:1, :], sums_out[1:2, :] = sums(parts)


def forward_other(
    packed, own_blocks, pair_blocks, inverse, own_sums, shares, expo_out, scaled_out, sent_out
):
    core = lax.axis_index("core")
    dots = all_dots(packed, own_blocks, pair_blocks)
    own = exponentials(packed, core, dots[0], inverse[0])
    pair = exponentials(packed, 1 - core, dots[1], inverse[1])
    expo_out[...] = jnp.where(own[1], -1.0, own[0])
    scaled_out[...] = own[2]
    rows, wide = shares.shape
    sent_out[:, :wide] = shares[...]
    total = jnp.concatenate([own_sums[...], *sums([own, pair])], axis=0)
    high = total.astype(jnp.bfloat16)
    low = (total - high.astype(jnp.float32)).astype(jnp.bfloat16)
    tile = jnp.concatenate([high.astype(jnp.float32), low.astype(jnp.float32)], axis=0)
    tile = jnp.broadcast_to(tile[None], (rows // 8, 8, 128))
    sent_out[:, wide:] = tile.reshape(rows, 128).astype(jnp.bfloat16)


def shares(expo, inverse, own_blocks, pair_blocks, shares_out):
    groups, _, width = own_blocks.shape
    others, label = [], []
    for k in range(2):
        others.append((jnp.maximum(expo[k], 0.0) * inverse[k]).T)
        label.append(jnp.where(expo[k] < 0.0, 1.0, 0.0).T)
    others = jnp.concatenate(others, axis=1)
    label = jnp.concatenate(label, axis=1)
    places = [[] for _ in range(groups)]
    for g in range(groups):
        rows = [part[p * 8 : p * 8 + 8] for part in (others, label) for p in range(g, 16, groups)]
        blocks = jnp.concatenate([own_blocks[g], pair_blocks[g]], axis=0)
        both = contract(jnp.concatenate(rows, axis=0).astype(jnp.bfloat16), blocks, 1, 0)
        places[g] = [both[i * 8 : i * 8 + 8] for i in range(len(rows))]
    for part in range(2):
        count = 16 // groups
        rows = [places[g][part * count + i] for i in range(count) for g in range(groups)]
        rows = jnp.concatenate(rows, axis=0).astype(jnp.bfloat16)
        shares_out[:, part * width : (part + 1) * width] = rows


def backward(
    named,
    received,
    expo,
    other_expo,
    scaled,
    other_scaled,
    inverse,
    own_packed,
    other_packed,
    features,
    centres,
    grad_out,
    feature_out,
    loss_out,
    grad,
    feature_grad,
    loss_row,
    left,
):
    held = centres.shape[0]
    tok_dev, width = features.shape

    def total_of(columns):
        total = received[0, :, columns].astype(jnp.float32)
        for i in range(1, received.shape[0]):
            total = total + received[i, :, columns].astype(jnp.float32)
        return total

    tile = total_of(pl.ds(2 * width, 128))
    tile = tile[:4] + tile[4:]
    own_rest, own_label = tile[0:1], tile[1:2]
    other_rest, other_label = tile[2:3], tile[3:4]

    units = jnp.concatenate([own_packed[:, :width], other_packed[:, :width]], axis=0)
    own_scale = logit_scale / (own_rest + own_label)
    other_scale = logit_scale / (other_rest + other_label)
    own = expo[0]
    other = other_expo[...]
    own = jnp.where(own < 0.0, -own_rest, own) * own_scale
    other = jnp.where(other < 0.0, -other_rest, other) * other_scale
    weights = jnp.concatenate([own, other], axis=1).astype(jnp.bfloat16).astype(jnp.float32)
    pulls = weights * jnp.concatenate([scaled[...], other_scaled[...]], axis=1)
    own_named = named[...]
    named = jnp.concatenate([own_named, own_named], axis=1)
    moves = []

    def leave(source, target):
        move = pltpu.make_async_copy(source, target, left.at[len(moves)])
        move.start()
        moves.append(move)

    def block_out(b):
        mine = jnp.where(named == b, weights, 0.0).astype(jnp.bfloat16)
        factor = jnp.max(jnp.where(own_named == b, inverse[0], 0.0), axis=1, keepdims=True)
        back = factor * jnp.sum(jnp.where(named == b, pulls, 0.0), axis=1, keepdims=True)
        slot_grad = contract(mine, units, 1, 0)
        grad[b] = factor * slot_grad - back * centres[b].astype(jnp.float32)
        leave(grad.at[b], grad_out.at[b])

    for b in range(held // 2):
        block_out(b)

    sums = total_of(pl.ds(0, 2 * width))
    sample = lax.broadcasted_iota(jnp.int32, (tok_dev, 128), 0) + own_place() * tok_dev
    mine = lanes(tok_dev) == sample
    rest = jnp.sum(jnp.where(mine, own_rest, 0.0), axis=1, keepdims=True)
    label = jnp.sum(jnp.where(mine, own_label, 0.0), axis=1, keepdims=True)
    total = rest + label
    loss = jnp.log(total) - jnp.log(label)
    square = (tok_dev, tok_dev)
    diagonal = lax.broadcasted_iota(jnp.int32, square, 0) == lax.broadcasted_iota(
        jnp.int32, square, 1
    )
    loss_row[...] = jnp.sum(jnp.where(diagonal, loss, 0.0), axis=0, keepdims=True)
    rows = features[...].astype(jnp.float32)
    inv_norm = inverse_norm(rows)
    unit = rows * inv_norm
    cand = sums[:, width : 2 * width]
    cand = (cand * inverse_norm(cand)).astype(jnp.bfloat16).astype(jnp.float32)
    unit_grad = logit_scale / total * (sums[:, :width] - rest * cand)
    along = jnp.sum(unit_grad * unit, axis=1, keepdims=True)
    feature_grad[...] = inv_norm * (unit_grad - along * unit)

    leave(feature_grad, feature_out)
    leave(loss_row, loss_out)
    for b in range(held // 2, held):
        block_out(b)
    for move in moves:
        move.wait()


def exchange(pieces, axes, order=None):
    return lax.all_to_all(
        pieces, axes, split_axis=0, concat_axis=0, axis_index_groups=order, tiled=True
    )


def exchange_chips(pieces):
    chips = lax.axis_size("chip")
    order = [g * chips + chip for chip in reversed(range(chips)) for g in GROUP_ORDER]
    return exchange(pieces, CHIPS, [order])


def with_partner(value):
    return lax.ppermute(value, "core", [(0, 1), (1, 0)])


def on_device(features, labels, centres, block_ids, listed):
    groups = lax.axis_size("group")
    chips = groups * lax.axis_size("chip")
    tok_dev, width = features.shape
    held = centres.shape[0] // BLK
    half = chips * tok_dev
    bf16, f32 = jnp.bfloat16, jnp.float32
    shape = jax.ShapeDtypeStruct

    copies, own_blocks, blocks, named, own_features = run(
        load,
        (
            shape((chips, tok_dev, width + 128), bf16),
            shape((groups, BLK, width), bf16),
            shape((held, BLK, width), bf16),
            shape((1, 128), block_ids.dtype),
            shape(features.shape, bf16),
        ),
        [HBM] * 5,
        *(
            pltpu.with_memory_space_constraint(array, pltpu.HBM)
            for array in (
                features,
                labels.reshape(1, -1),
                centres.reshape(held, BLK, width),
                block_ids.reshape(1, groups),
                listed.reshape(1, groups),
            )
        ),
        scratch=[
            pltpu.VMEM((1, labels.shape[0]), labels.dtype),
            pltpu.SMEM((1, groups), block_ids.dtype),
            pltpu.SMEM((1, groups), listed.dtype),
            pltpu.SemaphoreType.DMA((5,)),
        ],
    )
    pair_blocks = with_partner(own_blocks)
    own_packed = exchange_chips(copies).reshape(half, width + 128)
    other_packed = with_partner(own_packed)
    expo, scaled, inverse, own_sums = run(
        forward,
        (
            shape((2, BLK, half), f32),
            shape((BLK, half), f32),
            shape((2, BLK, half), f32),
            shape((2, half), f32),
        ),
        [VMEM] * 3,
        own_packed,
        own_blocks,
        pair_blocks,
    )
    going = run(
        shares,
        shape((half, 2 * width), bf16),
        [VMEM] * 4,
        expo,
        inverse,
        own_blocks,
        pair_blocks,
    )
    other_expo, other_scaled, sent = run(
        forward_other,
        (
            shape((BLK, half), f32),
            shape((BLK, half), f32),
            shape((half, 2 * width + 128), bf16),
        ),
        [VMEM] * 6,
        other_packed,
        own_blocks,
        pair_blocks,
        inverse,
        own_sums,
        going,
    )
    received = exchange_chips(sent.reshape(chips, tok_dev, 2 * width + 128))
    outs = (shape((held, BLK, width), f32), shape((tok_dev, width), f32), shape((1, tok_dev), f32))
    centre_grad, feature_grad, loss = run(
        backward,
        outs,
        [VMEM] * 11,
        named,
        received,
        expo,
        other_expo,
        scaled,
        other_scaled,
        inverse,
        own_packed,
        other_packed,
        own_features,
        blocks,
        out_spec=HBM,
        scratch=[
            *(pltpu.VMEM(out.shape, out.dtype) for out in outs),
            pltpu.SemaphoreType.DMA((held + 2,)),
        ],
    )
    return (loss.reshape(tok_dev), feature_grad, centre_grad.reshape(held * BLK, width))


def on_device_of_many(features, labels, centres, block_ids, listed):
    groups = lax.axis_size("group")
    members = lax.axis_size("member")
    devices = groups * members
    group = lax.axis_index("group")
    member = lax.axis_index("member")
    tok_dev, width = features.shape
    group_tok = members * tok_dev
    held = centres.shape[0] // BLK

    vectors = features.astype(jnp.float32)
    inv_norm = inverse_norm(vectors)
    unit_rows = vectors * inv_norm
    copies = jnp.broadcast_to(unit_rows.astype(jnp.bfloat16), (devices, tok_dev, width))
    units = exchange(copies, AXES).reshape(groups, group_tok, width)
    all_labels = exchange(jnp.broadcast_to(labels[None], (groups, group_tok)), "group")

    picked = centres.reshape(held, BLK, width)[block_ids[:, 0]].astype(jnp.float32)
    inv_cand = inverse_norm(picked)
    unit_cand = picked * inv_cand
    cand_half = unit_cand.astype(jnp.bfloat16)
    cosine = jnp.einsum("gsd,gcd->gsc", units, cand_half, preferred_element_type=jnp.float32)
    local_label = all_labels - (member * groups + group) * BLK
    onehot = (lax.broadcasted_iota(jnp.int32, (1, 1, BLK), 2) == local_label[:, :, None]).astype(
        jnp.float32
    )
    logits = logit_scale * (cosine - cos_margin * onehot)
    exp_logits = jnp.exp(logits) * listed.astype(jnp.float32)[:, :, None]
    totals, label_logit = lax.psum(
        (jnp.sum(exp_logits, axis=2), jnp.sum(logits * onehot, axis=2)), AXES
    )
    loss_all = (jnp.log(totals) - label_logit).reshape(devices, tok_dev)
    sample_loss = lax.dynamic_slice_in_dim(loss_all, group * members + member, 1, 0)[0]

    weights = (logit_scale * (exp_logits / totals[:, :, None] - onehot)).astype(jnp.bfloat16)
    partial = jnp.einsum("gsc,gcd->gsd", weights, cand_half, preferred_element_type=jnp.float32)
    home = exchange(partial.astype(jnp.bfloat16).reshape(devices, tok_dev, width), AXES)
    unit_grad = jnp.sum(home.astype(jnp.float32), axis=0)
    feature_grad = inv_norm * (
        unit_grad - jnp.sum(unit_grad * unit_rows, axis=1, keepdims=True) * unit_rows
    )
    slot_grad = jnp.einsum("gsc,gsd->gcd", weights, units, preferred_element_type=jnp.float32)
    cand_grad = inv_cand * (
        slot_grad - jnp.sum(slot_grad * unit_cand, axis=2, keepdims=True) * unit_cand
    )
    cand_grad = cand_grad.astype(jnp.bfloat16).astype(jnp.float32)
    names = block_ids == jnp.arange(held, dtype=jnp.int32)[None, :]
    centre_grad = jnp.sum(
        jnp.where(names[:, :, None, None], cand_grad[:, None], 0.0), axis=0
    ).reshape(held * BLK, width)
    return (sample_loss, feature_grad, centre_grad)


def on_axes(body, mesh, axes):
    split = P(axes)
    return jax.shard_map(
        body,
        mesh=mesh,
        in_specs=(split, P("group"), split, P(None, axes), P(None, axes)),
        out_specs=(split, split, split),
        check_vma=False,
    )


def solution(mesh):
    groups, members = mesh.shape["group"], mesh.shape["member"]
    by_core = jax.sharding.Mesh(
        mesh.devices.reshape(groups, members // 2, 2), ("group", "chip", "core")
    )

    def program(features, *others):
        half = features.shape[0] // 2
        if half == 128 and 2 * groups == features.shape[0] // mesh.size == 8:
            return on_axes(on_device, by_core, (*CHIPS, "core"))(features, *others)
        return on_axes(on_device_of_many, mesh, AXES)(features, *others)

    return program
```

```python
import jax
import jax.numpy as jnp
from jax import lax
from jax.experimental import pallas as pl
from jax.experimental.pallas import tpu as pltpu
from jax.sharding import PartitionSpec as P

BLK = 128
AXES = ("group", "member")
CHIPS = ("group", "chip")

logit_scale = 32.0
cos_margin = 0.35
norm_epsilon = 1e-06
GROUP_ORDER = (2, 0, 3, 1)
UNLISTED = 1e19

VMEM = pl.BlockSpec(memory_space=pltpu.VMEM)
HBM = pl.BlockSpec(memory_space=pltpu.HBM)


def inverse_norm(rows):
    return lax.rsqrt(jnp.sum(rows * rows, axis=-1, keepdims=True) + norm_epsilon)


def contract(left, right, left_dim, right_dim):
    dims = (((left_dim,), (right_dim,)), ((), ()))
    return lax.dot_general(left, right, dims, preferred_element_type=jnp.float32)


def lanes(rows):
    return lax.broadcasted_iota(jnp.int32, (rows, 128), 1)


def run(kernel, out_shape, in_specs, *operands, out_spec=VMEM, scratch=()):
    shapes = jax.tree.leaves(out_shape)
    return pl.pallas_call(
        kernel,
        out_shape=out_shape,
        in_specs=in_specs,
        out_specs=jax.tree.map(lambda _: out_spec, out_shape),
        scratch_shapes=scratch,
        compiler_params=pltpu.CompilerParams(vmem_limit_bytes=48 * 1024 * 1024),
        cost_estimate=pl.CostEstimate(
            flops=0,
            transcendentals=0,
            bytes_accessed=sum(a.size * a.dtype.itemsize for a in (*shapes, *operands)),
        ),
    )(*operands)


def load(
    features,
    labels,
    centres,
    ids,
    listed,
    copies_out,
    blocks_out,
    centres_out,
    named_out,
    held_features,
    held_labels,
    held_ids,
    held_listed,
    arrived,
):
    moves = [
        pltpu.make_async_copy(source, target, arrived.at[i])
        for i, (source, target) in enumerate(
            (
                (features, held_features),
                (labels, held_labels),
                (ids, held_ids),
                (listed, held_listed),
                (centres, centres_out),
            )
        )
    ]
    for move in moves:
        move.start()
    moves[0].wait()
    moves[1].wait()
    chip = lax.axis_index("chip")
    member = 2 * chip + lax.axis_index("core")
    copies, tok_dev, _ = copies_out.shape
    width = features.shape[1]
    rows = held_features[...].astype(jnp.float32)
    unit = (rows * inverse_norm(rows)).astype(jnp.bfloat16)
    copies_out[:, :, :width] = jnp.broadcast_to(unit[None], (copies, tok_dev, width))

    place = own_place() * tok_dev
    row = held_labels[...]
    row = jnp.concatenate([row, jnp.zeros((1, 128 - row.shape[1]), jnp.int32)], axis=1)
    row = jnp.broadcast_to(row, (tok_dev, 128))
    row = pltpu.roll(row, lax.rem(place - member * tok_dev + 128, 128), 1)
    digit = lax.broadcasted_iota(jnp.int32, (tok_dev, 128), 0)
    digits = (row >> (7 * jnp.minimum(digit, 3))) & 127
    lane = lanes(tok_dev)
    digits = jnp.where((lane >= place) & (lane < place + tok_dev), digits, 0)
    copies_out[:, :, width:] = jnp.broadcast_to(
        digits.astype(jnp.float32).astype(jnp.bfloat16)[None], (copies, tok_dev, 128)
    )
    for move in moves[2:]:
        move.wait()
    named_out[...] = select([held_ids[0, group] for group in GROUP_ORDER], 1)
    for g, group in enumerate(GROUP_ORDER):
        block = centres_out[held_ids[0, group]]
        blocks_out[g] = jnp.where(held_listed[0, group] > 0, block, jnp.full_like(block, UNLISTED))


def own_place():
    groups, chips = lax.axis_size("group"), lax.axis_size("chip")
    group = lax.axis_index("group")
    place = sum(jnp.where(group == g, k, 0) for k, g in enumerate(GROUP_ORDER))
    return (chips - 1 - lax.axis_index("chip")) * groups + place


def select(parts, rows):
    owner = lax.rem(lanes(1) // 8, len(parts))
    out = jnp.broadcast_to(parts[0], (rows, 128))
    for g in range(1, len(parts)):
        out = jnp.where(owner == g, parts[g], out)
    return out


def all_dots(packed, own_blocks, pair_blocks):
    groups, _, width = own_blocks.shape
    rows = jnp.concatenate([own_blocks[...], pair_blocks[...]], axis=0)
    dots = contract(rows.reshape(2 * groups * BLK, width), packed[:, :width], 1, 1)
    return dots[: groups * BLK], dots[groups * BLK :]


def exponentials(packed, core, dots, inverse):
    groups = dots.shape[0] // BLK
    width = packed.shape[1] - 128
    digits = jnp.sum(
        packed[:, width:].astype(jnp.float32).reshape(128 // 8, 8, 128), axis=0
    ).astype(jnp.int32)
    labels = digits[0:1] + (digits[1:2] << 7) + (digits[2:3] << 14)
    member = 2 * lax.axis_index("chip") + core
    first = (member * groups + lax.axis_index("group")) * BLK
    onehot = lax.broadcasted_iota(jnp.int32, (BLK, 128), 0) == labels - first
    cosine = inverse * select([dots[g * BLK : (g + 1) * BLK] for g in range(groups)], BLK)
    expo = jnp.exp(logit_scale * (cosine - jnp.where(onehot, cos_margin, 0.0)))
    return jnp.where(inverse > 0.0, expo, 0.0), onehot, cosine * inverse


def sums(parts):
    rest = [jnp.where(onehot, 0.0, expo) for expo, onehot, _ in parts]
    at_label = [jnp.where(onehot, expo, 0.0) for expo, onehot, _ in parts]
    return [jnp.sum(sum(part), axis=0, keepdims=True) for part in (rest, at_label)]


def forward(packed, own_blocks, pair_blocks, expo_out, scaled_out, inverse_out, sums_out):
    core = lax.axis_index("core")
    parts = []
    dots = all_dots(packed, own_blocks, pair_blocks)
    for k, blocks in enumerate((own_blocks, pair_blocks)):
        norms = [inverse_norm(blocks[g].astype(jnp.float32)) for g in range(blocks.shape[0])]
        inverse = select(norms, BLK)
        inverse_out[k] = inverse
        part = exponentials(packed, core if k == 0 else 1 - core, dots[k], inverse)
        expo_out[k] = jnp.where(part[1], -1.0, part[0])
        parts.append(part)
    scaled_out[...] = parts[0][2]
    sums_out[0:1, :], sums_out[1:2, :] = sums(parts)


def forward_other(
    packed, own_blocks, pair_blocks, inverse, own_sums, shares, expo_out, scaled_out, sent_out
):
    core = lax.axis_index("core")
    dots = all_dots(packed, own_blocks, pair_blocks)
    own = exponentials(packed, core, dots[0], inverse[0])
    pair = exponentials(packed, 1 - core, dots[1], inverse[1])
    expo_out[...] = jnp.where(own[1], -1.0, own[0])
    scaled_out[...] = own[2]
    rows, wide = shares.shape
    sent_out[:, :wide] = shares[...]
    total = jnp.concatenate([own_sums[...], *sums([own, pair])], axis=0)
    high = total.astype(jnp.bfloat16)
    low = (total - high.astype(jnp.float32)).astype(jnp.bfloat16)
    tile = jnp.concatenate([high.astype(jnp.float32), low.astype(jnp.float32)], axis=0)
    tile = jnp.broadcast_to(tile[None], (rows // 8, 8, 128))
    sent_out[:, wide:] = tile.reshape(rows, 128).astype(jnp.bfloat16)


def shares(expo, inverse, own_blocks, pair_blocks, shares_out):
    groups, _, width = own_blocks.shape
    others, label = [], []
    for k in range(2):
        others.append((jnp.maximum(expo[k], 0.0) * inverse[k]).T)
        label.append(jnp.where(expo[k] < 0.0, 1.0, 0.0).T)
    others = jnp.concatenate(others, axis=1)
    label = jnp.concatenate(label, axis=1)
    places = [[] for _ in range(groups)]
    for g in range(groups):
        rows = [part[p * 8 : p * 8 + 8] for part in (others, label) for p in range(g, 16, groups)]
        blocks = jnp.concatenate([own_blocks[g], pair_blocks[g]], axis=0)
        both = contract(jnp.concatenate(rows, axis=0).astype(jnp.bfloat16), blocks, 1, 0)
        places[g] = [both[i * 8 : i * 8 + 8] for i in range(len(rows))]
    for part in range(2):
        count = 16 // groups
        rows = [places[g][part * count + i] for i in range(count) for g in range(groups)]
        rows = jnp.concatenate(rows, axis=0).astype(jnp.bfloat16)
        shares_out[:, part * width : (part + 1) * width] = rows


def backward(
    named,
    received,
    expo,
    other_expo,
    scaled,
    other_scaled,
    inverse,
    own_packed,
    other_packed,
    features,
    centres,
    grad_out,
    feature_out,
    loss_out,
    grad,
    feature_grad,
    loss_row,
    left,
):
    held = centres.shape[0]
    tok_dev, width = features.shape

    def total_of(columns):
        total = received[0, :, columns].astype(jnp.float32)
        for i in range(1, received.shape[0]):
            total = total + received[i, :, columns].astype(jnp.float32)
        return total

    tile = total_of(pl.ds(2 * width, 128))
    tile = tile[:4] + tile[4:]
    own_rest, own_label = tile[0:1], tile[1:2]
    other_rest, other_label = tile[2:3], tile[3:4]

    units = jnp.concatenate([own_packed[:, :width], other_packed[:, :width]], axis=0)
    own_scale = logit_scale / (own_rest + own_label)
    other_scale = logit_scale / (other_rest + other_label)
    own = expo[0]
    other = other_expo[...]
    own = jnp.where(own < 0.0, -own_rest, own) * own_scale
    other = jnp.where(other < 0.0, -other_rest, other) * other_scale
    weights = jnp.concatenate([own, other], axis=1).astype(jnp.bfloat16).astype(jnp.float32)
    pulls = weights * jnp.concatenate([scaled[...], other_scaled[...]], axis=1)
    own_named = named[...]
    named = jnp.concatenate([own_named, own_named], axis=1)
    masked = [jnp.where(named == b, weights, 0.0).astype(jnp.bfloat16) for b in range(held)]
    slot_grads = contract(jnp.concatenate(masked, axis=0), units, 1, 0)
    moves = []

    def leave(source, target):
        move = pltpu.make_async_copy(source, target, left.at[len(moves)])
        move.start()
        moves.append(move)

    def block_out(b):
        factor = jnp.max(jnp.where(own_named == b, inverse[0], 0.0), axis=1, keepdims=True)
        back = factor * jnp.sum(jnp.where(named == b, pulls, 0.0), axis=1, keepdims=True)
        slot_grad = slot_grads[b * BLK : (b + 1) * BLK]
        grad[b] = factor * slot_grad - back * centres[b].astype(jnp.float32)
        leave(grad.at[b], grad_out.at[b])

    for b in range(held // 2):
        block_out(b)

    sums = total_of(pl.ds(0, 2 * width))
    sample = lax.broadcasted_iota(jnp.int32, (tok_dev, 128), 0) + own_place() * tok_dev
    mine = lanes(tok_dev) == sample
    rest = jnp.sum(jnp.where(mine, own_rest, 0.0), axis=1, keepdims=True)
    label = jnp.sum(jnp.where(mine, own_label, 0.0), axis=1, keepdims=True)
    total = rest + label
    loss = jnp.log(total) - jnp.log(label)
    square = (tok_dev, tok_dev)
    diagonal = lax.broadcasted_iota(jnp.int32, square, 0) == lax.broadcasted_iota(
        jnp.int32, square, 1
    )
    loss_row[...] = jnp.sum(jnp.where(diagonal, loss, 0.0), axis=0, keepdims=True)
    rows = features[...].astype(jnp.float32)
    inv_norm = inverse_norm(rows)
    unit = rows * inv_norm
    cand = sums[:, width : 2 * width]
    cand = (cand * inverse_norm(cand)).astype(jnp.bfloat16).astype(jnp.float32)
    unit_grad = logit_scale / total * (sums[:, :width] - rest * cand)
    along = jnp.sum(unit_grad * unit, axis=1, keepdims=True)
    feature_grad[...] = inv_norm * (unit_grad - along * unit)

    leave(feature_grad, feature_out)
    leave(loss_row, loss_out)
    for b in range(held // 2, held):
        block_out(b)
    for move in moves:
        move.wait()


def exchange(pieces, axes, order=None):
    return lax.all_to_all(
        pieces, axes, split_axis=0, concat_axis=0, axis_index_groups=order, tiled=True
    )


def exchange_chips(pieces):
    chips = lax.axis_size("chip")
    order = [g * chips + chip for chip in reversed(range(chips)) for g in GROUP_ORDER]
    return exchange(pieces, CHIPS, [order])


def with_partner(value):
    return lax.ppermute(value, "core", [(0, 1), (1, 0)])


def on_device(features, labels, centres, block_ids, listed):
    groups = lax.axis_size("group")
    chips = groups * lax.axis_size("chip")
    tok_dev, width = features.shape
    held = centres.shape[0] // BLK
    half = chips * tok_dev
    bf16, f32 = jnp.bfloat16, jnp.float32
    shape = jax.ShapeDtypeStruct

    copies, own_blocks, blocks, named, own_features = run(
        load,
        (
            shape((chips, tok_dev, width + 128), bf16),
            shape((groups, BLK, width), bf16),
            shape((held, BLK, width), bf16),
            shape((1, 128), block_ids.dtype),
            shape(features.shape, bf16),
        ),
        [HBM] * 5,
        *(
            pltpu.with_memory_space_constraint(array, pltpu.HBM)
            for array in (
                features,
                labels.reshape(1, -1),
                centres.reshape(held, BLK, width),
                block_ids.reshape(1, groups),
                listed.reshape(1, groups),
            )
        ),
        scratch=[
            pltpu.VMEM((1, labels.shape[0]), labels.dtype),
            pltpu.SMEM((1, groups), block_ids.dtype),
            pltpu.SMEM((1, groups), listed.dtype),
            pltpu.SemaphoreType.DMA((5,)),
        ],
    )
    pair_blocks = with_partner(own_blocks)
    own_packed = exchange_chips(copies).reshape(half, width + 128)
    other_packed = with_partner(own_packed)
    expo, scaled, inverse, own_sums = run(
        forward,
        (
            shape((2, BLK, half), f32),
            shape((BLK, half), f32),
            shape((2, BLK, half), f32),
            shape((2, half), f32),
        ),
        [VMEM] * 3,
        own_packed,
        own_blocks,
        pair_blocks,
    )
    going = run(
        shares,
        shape((half, 2 * width), bf16),
        [VMEM] * 4,
        expo,
        inverse,
        own_blocks,
        pair_blocks,
    )
    other_expo, other_scaled, sent = run(
        forward_other,
        (
            shape((BLK, half), f32),
            shape((BLK, half), f32),
            shape((half, 2 * width + 128), bf16),
        ),
        [VMEM] * 6,
        other_packed,
        own_blocks,
        pair_blocks,
        inverse,
        own_sums,
        going,
    )
    received = exchange_chips(sent.reshape(chips, tok_dev, 2 * width + 128))
    outs = (shape((held, BLK, width), f32), shape((tok_dev, width), f32), shape((1, tok_dev), f32))
    centre_grad, feature_grad, loss = run(
        backward,
        outs,
        [VMEM] * 11,
        named,
        received,
        expo,
        other_expo,
        scaled,
        other_scaled,
        inverse,
        own_packed,
        other_packed,
        own_features,
        blocks,
        out_spec=HBM,
        scratch=[
            *(pltpu.VMEM(out.shape, out.dtype) for out in outs),
            pltpu.SemaphoreType.DMA((held + 2,)),
        ],
    )
    return (loss.reshape(tok_dev), feature_grad, centre_grad.reshape(held * BLK, width))


def on_device_of_many(features, labels, centres, block_ids, listed):
    groups = lax.axis_size("group")
    members = lax.axis_size("member")
    devices = groups * members
    group = lax.axis_index("group")
    member = lax.axis_index("member")
    tok_dev, width = features.shape
    group_tok = members * tok_dev
    held = centres.shape[0] // BLK

    vectors = features.astype(jnp.float32)
    inv_norm = inverse_norm(vectors)
    unit_rows = vectors * inv_norm
    copies = jnp.broadcast_to(unit_rows.astype(jnp.bfloat16), (devices, tok_dev, width))
    units = exchange(copies, AXES).reshape(groups, group_tok, width)
    all_labels = exchange(jnp.broadcast_to(labels[None], (groups, group_tok)), "group")

    picked = centres.reshape(held, BLK, width)[block_ids[:, 0]].astype(jnp.float32)
    inv_cand = inverse_norm(picked)
    unit_cand = picked * inv_cand
    cand_half = unit_cand.astype(jnp.bfloat16)
    cosine = jnp.einsum("gsd,gcd->gsc", units, cand_half, preferred_element_type=jnp.float32)
    local_label = all_labels - (member * groups + group) * BLK
    onehot = (lax.broadcasted_iota(jnp.int32, (1, 1, BLK), 2) == local_label[:, :, None]).astype(
        jnp.float32
    )
    logits = logit_scale * (cosine - cos_margin * onehot)
    exp_logits = jnp.exp(logits) * listed.astype(jnp.float32)[:, :, None]
    totals, label_logit = lax.psum(
        (jnp.sum(exp_logits, axis=2), jnp.sum(logits * onehot, axis=2)), AXES
    )
    loss_all = (jnp.log(totals) - label_logit).reshape(devices, tok_dev)
    sample_loss = lax.dynamic_slice_in_dim(loss_all, group * members + member, 1, 0)[0]

    weights = (logit_scale * (exp_logits / totals[:, :, None] - onehot)).astype(jnp.bfloat16)
    partial = jnp.einsum("gsc,gcd->gsd", weights, cand_half, preferred_element_type=jnp.float32)
    home = exchange(partial.astype(jnp.bfloat16).reshape(devices, tok_dev, width), AXES)
    unit_grad = jnp.sum(home.astype(jnp.float32), axis=0)
    feature_grad = inv_norm * (
        unit_grad - jnp.sum(unit_grad * unit_rows, axis=1, keepdims=True) * unit_rows
    )
    slot_grad = jnp.einsum("gsc,gsd->gcd", weights, units, preferred_element_type=jnp.float32)
    cand_grad = inv_cand * (
        slot_grad - jnp.sum(slot_grad * unit_cand, axis=2, keepdims=True) * unit_cand
    )
    cand_grad = cand_grad.astype(jnp.bfloat16).astype(jnp.float32)
    names = block_ids == jnp.arange(held, dtype=jnp.int32)[None, :]
    centre_grad = jnp.sum(
        jnp.where(names[:, :, None, None], cand_grad[:, None], 0.0), axis=0
    ).reshape(held * BLK, width)
    return (sample_loss, feature_grad, centre_grad)


def on_axes(body, mesh, axes):
    split = P(axes)
    return jax.shard_map(
        body,
        mesh=mesh,
        in_specs=(split, P("group"), split, P(None, axes), P(None, axes)),
        out_specs=(split, split, split),
        check_vma=False,
    )


def solution(mesh):
    groups, members = mesh.shape["group"], mesh.shape["member"]
    by_core = jax.sharding.Mesh(
        mesh.devices.reshape(groups, members // 2, 2), ("group", "chip", "core")
    )

    def program(features, *others):
        half = features.shape[0] // 2
        if half == 128 and 2 * groups == features.shape[0] // mesh.size == 8:
            return on_axes(on_device, by_core, (*CHIPS, "core"))(features, *others)
        return on_axes(on_device_of_many, mesh, AXES)(features, *others)

    return program
```

```python
import jax
import jax.numpy as jnp
from jax import lax
from jax.experimental import pallas as pl
from jax.experimental.pallas import tpu as pltpu
from jax.sharding import PartitionSpec as P

BLK = 128
AXES = ("group", "member")
CHIPS = ("group", "chip")

logit_scale = 32.0
cos_margin = 0.35
norm_epsilon = 1e-06
GROUP_ORDER = (2, 0, 3, 1)
UNLISTED = 1e19

VMEM = pl.BlockSpec(memory_space=pltpu.VMEM)
HBM = pl.BlockSpec(memory_space=pltpu.HBM)


def inverse_norm(rows):
    return lax.rsqrt(jnp.sum(rows * rows, axis=-1, keepdims=True) + norm_epsilon)


def contract(left, right, left_dim, right_dim):
    dims = (((left_dim,), (right_dim,)), ((), ()))
    return lax.dot_general(left, right, dims, preferred_element_type=jnp.float32)


def lanes(rows):
    return lax.broadcasted_iota(jnp.int32, (rows, 128), 1)


def run(kernel, out_shape, in_specs, *operands, out_spec=VMEM, scratch=()):
    shapes = jax.tree.leaves(out_shape)
    return pl.pallas_call(
        kernel,
        out_shape=out_shape,
        in_specs=in_specs,
        out_specs=jax.tree.map(lambda _: out_spec, out_shape),
        scratch_shapes=scratch,
        compiler_params=pltpu.CompilerParams(vmem_limit_bytes=48 * 1024 * 1024),
        cost_estimate=pl.CostEstimate(
            flops=0,
            transcendentals=0,
            bytes_accessed=sum(a.size * a.dtype.itemsize for a in (*shapes, *operands)),
        ),
    )(*operands)


def load(
    features,
    labels,
    centres,
    ids,
    listed,
    copies_out,
    blocks_out,
    centres_out,
    named_out,
    held_features,
    held_labels,
    held_ids,
    held_listed,
    arrived,
):
    moves = [
        pltpu.make_async_copy(source, target, arrived.at[i])
        for i, (source, target) in enumerate(
            (
                (features, held_features),
                (labels, held_labels),
                (ids, held_ids),
                (listed, held_listed),
                (centres, centres_out),
            )
        )
    ]
    for move in moves:
        move.start()
    moves[0].wait()
    moves[1].wait()
    chip = lax.axis_index("chip")
    member = 2 * chip + lax.axis_index("core")
    copies, tok_dev, _ = copies_out.shape
    width = features.shape[1]
    rows = held_features[...].astype(jnp.float32)
    unit = (rows * inverse_norm(rows)).astype(jnp.bfloat16)
    copies_out[:, :, :width] = jnp.broadcast_to(unit[None], (copies, tok_dev, width))

    place = own_place() * tok_dev
    row = held_labels[...]
    row = jnp.concatenate([row, jnp.zeros((1, 128 - row.shape[1]), jnp.int32)], axis=1)
    row = jnp.broadcast_to(row, (tok_dev, 128))
    row = pltpu.roll(row, lax.rem(place - member * tok_dev + 128, 128), 1)
    digit = lax.broadcasted_iota(jnp.int32, (tok_dev, 128), 0)
    digits = (row >> (7 * jnp.minimum(digit, 3))) & 127
    lane = lanes(tok_dev)
    digits = jnp.where((lane >= place) & (lane < place + tok_dev), digits, 0)
    copies_out[:, :, width:] = jnp.broadcast_to(
        digits.astype(jnp.float32).astype(jnp.bfloat16)[None], (copies, tok_dev, 128)
    )
    for move in moves[2:]:
        move.wait()
    named_out[...] = select([held_ids[0, group] for group in GROUP_ORDER], 1)
    for g, group in enumerate(GROUP_ORDER):
        block = centres_out[held_ids[0, group]]
        blocks_out[g] = jnp.where(held_listed[0, group] > 0, block, jnp.full_like(block, UNLISTED))


def own_place():
    groups, chips = lax.axis_size("group"), lax.axis_size("chip")
    group = lax.axis_index("group")
    place = sum(jnp.where(group == g, k, 0) for k, g in enumerate(GROUP_ORDER))
    return (chips - 1 - lax.axis_index("chip")) * groups + place


def select(parts, rows):
    owner = lax.rem(lanes(1) // 8, len(parts))
    out = jnp.broadcast_to(parts[0], (rows, 128))
    for g in range(1, len(parts)):
        out = jnp.where(owner == g, parts[g], out)
    return out


def all_dots(packed, own_blocks, pair_blocks):
    groups, _, width = own_blocks.shape
    rows = jnp.concatenate([own_blocks[...], pair_blocks[...]], axis=0)
    dots = contract(rows.reshape(2 * groups * BLK, width), packed[:, :width], 1, 1)
    return dots[: groups * BLK], dots[groups * BLK :]


def exponentials(packed, core, dots, inverse):
    groups = dots.shape[0] // BLK
    width = packed.shape[1] - 128
    digits = jnp.sum(
        packed[:, width:].astype(jnp.float32).reshape(128 // 8, 8, 128), axis=0
    ).astype(jnp.int32)
    labels = digits[0:1] + (digits[1:2] << 7) + (digits[2:3] << 14)
    member = 2 * lax.axis_index("chip") + core
    first = (member * groups + lax.axis_index("group")) * BLK
    onehot = lax.broadcasted_iota(jnp.int32, (BLK, 128), 0) == labels - first
    cosine = inverse * select([dots[g * BLK : (g + 1) * BLK] for g in range(groups)], BLK)
    expo = jnp.exp(logit_scale * (cosine - jnp.where(onehot, cos_margin, 0.0)))
    return jnp.where(inverse > 0.0, expo, 0.0), onehot, cosine * inverse


def sums(parts):
    rest = [jnp.where(onehot, 0.0, expo) for expo, onehot, _ in parts]
    at_label = [jnp.where(onehot, expo, 0.0) for expo, onehot, _ in parts]
    return [jnp.sum(sum(part), axis=0, keepdims=True) for part in (rest, at_label)]


def forward(packed, own_blocks, pair_blocks, expo_out, scaled_out, inverse_out, sums_out):
    core = lax.axis_index("core")
    parts = []
    dots = all_dots(packed, own_blocks, pair_blocks)
    for k, blocks in enumerate((own_blocks, pair_blocks)):
        norms = [inverse_norm(blocks[g].astype(jnp.float32)) for g in range(blocks.shape[0])]
        inverse = select(norms, BLK)
        inverse_out[k] = inverse
        part = exponentials(packed, core if k == 0 else 1 - core, dots[k], inverse)
        expo_out[k] = jnp.where(part[1], -1.0, part[0])
        parts.append(part)
    scaled_out[...] = parts[0][2]
    sums_out[0:1, :], sums_out[1:2, :] = sums(parts)


def forward_other(
    packed, own_blocks, pair_blocks, inverse, own_sums, shares, expo_out, scaled_out, sent_out
):
    core = lax.axis_index("core")
    dots = all_dots(packed, own_blocks, pair_blocks)
    own = exponentials(packed, core, dots[0], inverse[0])
    pair = exponentials(packed, 1 - core, dots[1], inverse[1])
    expo_out[...] = jnp.where(own[1], -1.0, own[0])
    scaled_out[...] = own[2]
    rows, wide = shares.shape
    sent_out[:, :wide] = shares[...]
    total = jnp.concatenate([own_sums[...], *sums([own, pair])], axis=0)
    high = total.astype(jnp.bfloat16)
    low = (total - high.astype(jnp.float32)).astype(jnp.bfloat16)
    tile = jnp.concatenate([high.astype(jnp.float32), low.astype(jnp.float32)], axis=0)
    tile = jnp.broadcast_to(tile[None], (rows // 8, 8, 128))
    sent_out[:, wide:] = tile.reshape(rows, 128).astype(jnp.bfloat16)


def shares(expo, inverse, own_blocks, pair_blocks, shares_out):
    groups, _, width = own_blocks.shape
    others, label = [], []
    for k in range(2):
        others.append((jnp.maximum(expo[k], 0.0) * inverse[k]).T)
        label.append(jnp.where(expo[k] < 0.0, 1.0, 0.0).T)
    others = jnp.concatenate(others, axis=1)
    label = jnp.concatenate(label, axis=1)
    places = [[] for _ in range(groups)]
    for g in range(groups):
        rows = [part[p * 8 : p * 8 + 8] for part in (others, label) for p in range(g, 16, groups)]
        blocks = jnp.concatenate([own_blocks[g], pair_blocks[g]], axis=0)
        both = contract(jnp.concatenate(rows, axis=0).astype(jnp.bfloat16), blocks, 1, 0)
        places[g] = [both[i * 8 : i * 8 + 8] for i in range(len(rows))]
    for part in range(2):
        count = 16 // groups
        rows = [places[g][part * count + i] for i in range(count) for g in range(groups)]
        rows = jnp.concatenate(rows, axis=0).astype(jnp.bfloat16)
        shares_out[:, part * width : (part + 1) * width] = rows


def backward(
    named,
    received,
    expo,
    other_expo,
    scaled,
    other_scaled,
    inverse,
    own_packed,
    other_packed,
    features,
    centres,
    grad_out,
    feature_out,
    loss_out,
    grad,
    feature_grad,
    loss_row,
    left,
):
    held = centres.shape[0]
    tok_dev, width = features.shape

    def total_of(columns):
        total = received[0, :, columns].astype(jnp.float32)
        for i in range(1, received.shape[0]):
            total = total + received[i, :, columns].astype(jnp.float32)
        return total

    tile = total_of(pl.ds(2 * width, 128))
    tile = tile[:4] + tile[4:]
    own_rest, own_label = tile[0:1], tile[1:2]
    other_rest, other_label = tile[2:3], tile[3:4]

    units = jnp.concatenate([own_packed[:, :width], other_packed[:, :width]], axis=0)
    own_scale = logit_scale / (own_rest + own_label)
    other_scale = logit_scale / (other_rest + other_label)
    own = expo[0]
    other = other_expo[...]
    own = jnp.where(own < 0.0, -own_rest, own) * own_scale
    other = jnp.where(other < 0.0, -other_rest, other) * other_scale
    weights = jnp.concatenate([own, other], axis=1).astype(jnp.bfloat16).astype(jnp.float32)
    pulls = weights * jnp.concatenate([scaled[...], other_scaled[...]], axis=1)
    own_named = named[...]
    named = jnp.concatenate([own_named, own_named], axis=1)
    masked = [jnp.where(named == b, weights, 0.0).astype(jnp.bfloat16) for b in range(held)]
    slot_grads = contract(jnp.concatenate(masked, axis=0), units, 1, 0)
    moves = []

    def leave(source, target):
        move = pltpu.make_async_copy(source, target, left.at[len(moves)])
        move.start()
        moves.append(move)

    def block_out(b):
        factor = jnp.max(jnp.where(own_named == b, inverse[0], 0.0), axis=1, keepdims=True)
        back = factor * jnp.sum(jnp.where(named == b, pulls, 0.0), axis=1, keepdims=True)
        slot_grad = slot_grads[b * BLK : (b + 1) * BLK]
        grad[b] = factor * slot_grad - back * centres[b].astype(jnp.float32)
        leave(grad.at[b], grad_out.at[b])

    for b in range(1):
        block_out(b)

    sums = total_of(pl.ds(0, 2 * width))
    sample = lax.broadcasted_iota(jnp.int32, (tok_dev, 128), 0) + own_place() * tok_dev
    mine = lanes(tok_dev) == sample
    rest = jnp.sum(jnp.where(mine, own_rest, 0.0), axis=1, keepdims=True)
    label = jnp.sum(jnp.where(mine, own_label, 0.0), axis=1, keepdims=True)
    total = rest + label
    loss = jnp.log(total) - jnp.log(label)
    square = (tok_dev, tok_dev)
    diagonal = lax.broadcasted_iota(jnp.int32, square, 0) == lax.broadcasted_iota(
        jnp.int32, square, 1
    )
    loss_row[...] = jnp.sum(jnp.where(diagonal, loss, 0.0), axis=0, keepdims=True)
    rows = features[...].astype(jnp.float32)
    inv_norm = inverse_norm(rows)
    unit = rows * inv_norm
    cand = sums[:, width : 2 * width]
    cand = (cand * inverse_norm(cand)).astype(jnp.bfloat16).astype(jnp.float32)
    unit_grad = logit_scale / total * (sums[:, :width] - rest * cand)
    along = jnp.sum(unit_grad * unit, axis=1, keepdims=True)
    feature_grad[...] = inv_norm * (unit_grad - along * unit)

    leave(feature_grad, feature_out)
    leave(loss_row, loss_out)
    for b in range(1, held):
        block_out(b)
    for move in moves:
        move.wait()


def exchange(pieces, axes, order=None):
    return lax.all_to_all(
        pieces, axes, split_axis=0, concat_axis=0, axis_index_groups=order, tiled=True
    )


def exchange_chips(pieces):
    chips = lax.axis_size("chip")
    order = [g * chips + chip for chip in reversed(range(chips)) for g in GROUP_ORDER]
    return exchange(pieces, CHIPS, [order])


def with_partner(value):
    return lax.ppermute(value, "core", [(0, 1), (1, 0)])


def on_device(features, labels, centres, block_ids, listed):
    groups = lax.axis_size("group")
    chips = groups * lax.axis_size("chip")
    tok_dev, width = features.shape
    held = centres.shape[0] // BLK
    half = chips * tok_dev
    bf16, f32 = jnp.bfloat16, jnp.float32
    shape = jax.ShapeDtypeStruct

    copies, own_blocks, blocks, named, own_features = run(
        load,
        (
            shape((chips, tok_dev, width + 128), bf16),
            shape((groups, BLK, width), bf16),
            shape((held, BLK, width), bf16),
            shape((1, 128), block_ids.dtype),
            shape(features.shape, bf16),
        ),
        [HBM] * 5,
        *(
            pltpu.with_memory_space_constraint(array, pltpu.HBM)
            for array in (
                features,
                labels.reshape(1, -1),
                centres.reshape(held, BLK, width),
                block_ids.reshape(1, groups),
                listed.reshape(1, groups),
            )
        ),
        scratch=[
            pltpu.VMEM((1, labels.shape[0]), labels.dtype),
            pltpu.SMEM((1, groups), block_ids.dtype),
            pltpu.SMEM((1, groups), listed.dtype),
            pltpu.SemaphoreType.DMA((5,)),
        ],
    )
    pair_blocks = with_partner(own_blocks)
    own_packed = exchange_chips(copies).reshape(half, width + 128)
    other_packed = with_partner(own_packed)
    expo, scaled, inverse, own_sums = run(
        forward,
        (
            shape((2, BLK, half), f32),
            shape((BLK, half), f32),
            shape((2, BLK, half), f32),
            shape((2, half), f32),
        ),
        [VMEM] * 3,
        own_packed,
        own_blocks,
        pair_blocks,
    )
    going = run(
        shares,
        shape((half, 2 * width), bf16),
        [VMEM] * 4,
        expo,
        inverse,
        own_blocks,
        pair_blocks,
    )
    other_expo, other_scaled, sent = run(
        forward_other,
        (
            shape((BLK, half), f32),
            shape((BLK, half), f32),
            shape((half, 2 * width + 128), bf16),
        ),
        [VMEM] * 6,
        other_packed,
        own_blocks,
        pair_blocks,
        inverse,
        own_sums,
        going,
    )
    received = exchange_chips(sent.reshape(chips, tok_dev, 2 * width + 128))
    outs = (shape((held, BLK, width), f32), shape((tok_dev, width), f32), shape((1, tok_dev), f32))
    centre_grad, feature_grad, loss = run(
        backward,
        outs,
        [VMEM] * 11,
        named,
        received,
        expo,
        other_expo,
        scaled,
        other_scaled,
        inverse,
        own_packed,
        other_packed,
        own_features,
        blocks,
        out_spec=HBM,
        scratch=[
            *(pltpu.VMEM(out.shape, out.dtype) for out in outs),
            pltpu.SemaphoreType.DMA((held + 2,)),
        ],
    )
    return (loss.reshape(tok_dev), feature_grad, centre_grad.reshape(held * BLK, width))


def on_device_of_many(features, labels, centres, block_ids, listed):
    groups = lax.axis_size("group")
    members = lax.axis_size("member")
    devices = groups * members
    group = lax.axis_index("group")
    member = lax.axis_index("member")
    tok_dev, width = features.shape
    group_tok = members * tok_dev
    held = centres.shape[0] // BLK

    vectors = features.astype(jnp.float32)
    inv_norm = inverse_norm(vectors)
    unit_rows = vectors * inv_norm
    copies = jnp.broadcast_to(unit_rows.astype(jnp.bfloat16), (devices, tok_dev, width))
    units = exchange(copies, AXES).reshape(groups, group_tok, width)
    all_labels = exchange(jnp.broadcast_to(labels[None], (groups, group_tok)), "group")

    picked = centres.reshape(held, BLK, width)[block_ids[:, 0]].astype(jnp.float32)
    inv_cand = inverse_norm(picked)
    unit_cand = picked * inv_cand
    cand_half = unit_cand.astype(jnp.bfloat16)
    cosine = jnp.einsum("gsd,gcd->gsc", units, cand_half, preferred_element_type=jnp.float32)
    local_label = all_labels - (member * groups + group) * BLK
    onehot = (lax.broadcasted_iota(jnp.int32, (1, 1, BLK), 2) == local_label[:, :, None]).astype(
        jnp.float32
    )
    logits = logit_scale * (cosine - cos_margin * onehot)
    exp_logits = jnp.exp(logits) * listed.astype(jnp.float32)[:, :, None]
    totals, label_logit = lax.psum(
        (jnp.sum(exp_logits, axis=2), jnp.sum(logits * onehot, axis=2)), AXES
    )
    loss_all = (jnp.log(totals) - label_logit).reshape(devices, tok_dev)
    sample_loss = lax.dynamic_slice_in_dim(loss_all, group * members + member, 1, 0)[0]

    weights = (logit_scale * (exp_logits / totals[:, :, None] - onehot)).astype(jnp.bfloat16)
    partial = jnp.einsum("gsc,gcd->gsd", weights, cand_half, preferred_element_type=jnp.float32)
    home = exchange(partial.astype(jnp.bfloat16).reshape(devices, tok_dev, width), AXES)
    unit_grad = jnp.sum(home.astype(jnp.float32), axis=0)
    feature_grad = inv_norm * (
        unit_grad - jnp.sum(unit_grad * unit_rows, axis=1, keepdims=True) * unit_rows
    )
    slot_grad = jnp.einsum("gsc,gsd->gcd", weights, units, preferred_element_type=jnp.float32)
    cand_grad = inv_cand * (
        slot_grad - jnp.sum(slot_grad * unit_cand, axis=2, keepdims=True) * unit_cand
    )
    cand_grad = cand_grad.astype(jnp.bfloat16).astype(jnp.float32)
    names = block_ids == jnp.arange(held, dtype=jnp.int32)[None, :]
    centre_grad = jnp.sum(
        jnp.where(names[:, :, None, None], cand_grad[:, None], 0.0), axis=0
    ).reshape(held * BLK, width)
    return (sample_loss, feature_grad, centre_grad)


def on_axes(body, mesh, axes):
    split = P(axes)
    return jax.shard_map(
        body,
        mesh=mesh,
        in_specs=(split, P("group"), split, P(None, axes), P(None, axes)),
        out_specs=(split, split, split),
        check_vma=False,
    )


def solution(mesh):
    groups, members = mesh.shape["group"], mesh.shape["member"]
    by_core = jax.sharding.Mesh(
        mesh.devices.reshape(groups, members // 2, 2), ("group", "chip", "core")
    )

    def program(features, *others):
        half = features.shape[0] // 2
        if half == 128 and 2 * groups == features.shape[0] // mesh.size == 8:
            return on_axes(on_device, by_core, (*CHIPS, "core"))(features, *others)
        return on_axes(on_device_of_many, mesh, AXES)(features, *others)

    return program
```
